128 devices in a mesh: gx: 16 (over x, z), gy: 8 (over y, core).
Axes of the slice: x: 4, y: 4, z: 4, core: 2. Of those that a mesh axis runs over, the one named last changes fastest.
Arguments:
- test_vectors: float32 [48, 64, 128, 128], P(None, 'gx', 'gy'), may hold values from -6 to 6
- coef_x: float32 [64, 128, 128], P('gx', 'gy'), may hold values from 0.3 to 3
- coef_y: float32 [64, 128, 128], P('gx', 'gy'), may hold values from 0.3 to 3
- coef_z: float32 [64, 128, 128], P('gx', 'gy'), may hold values from 0.05 to 0.5
- shift: float32 [64, 128, 128], P('gx', 'gy'), may hold values from 0.1 to 1
- cf_split: int32 [64, 128, 1], P('gx', 'gy'), may hold values from 0 to 1, as said below
- nbr_count: int32 [64, 128, 1], P('gx', 'gy'), may hold values from 1 to 4, as said below
- nbr_owner: int32 [64, 128, 1, 4], P('gx', 'gy'), may hold values from 0 to 127, as said below
- nbr_block: int32 [64, 128, 1, 4], P('gx', 'gy'), may hold values from 0 to 63, as said below
Outputs:
- smoothed: float32 [48, 64, 128, 128], P(None, 'gx', 'gy')
- interp_weights: float32 [4, 64, 128, 128], P(None, 'gx', 'gy')
The draws below stay inside these ranges and needn't reach their ends.
Inputs may be any that keep to these rules, and one draw needn't show every extreme that they name: `cf_split`: each device holds exactly 16 C blocks. Only the first nbr_count slots of an F block are live; the other slots, and all slots of C blocks, are filler. `nbr_owner`: owner ids are i * 8 + j for the mesh position (i, j). Among the live slots of one device's blocks at most 2 name the same owner, and in every draw some owner is named by exactly 2 live slots of every device. `nbr_block`: A live slot names a C block of its owner.
All inputs are finite; a program needn't handle non-finite values.
Results may differ from the reference program's by a relative error of at most 0.0039.
Values may be sent and summed in bfloat16 or wider, within the bound.
A program may use at most 64 MiB of HBM per device.

```python
import math
import jax
import jax.numpy as jnp
from jax import lax

CELLS_X = 4
CELLS_Y = 16
DEPTH = 128
VECS = 48
SLOTS = 4
SWEEPS = 3
BLOCK_ROWS = 128
GRID_X = 64
GRID_Y = 128
ZBLOCKS = 1
BLOCKS_DEV = 64
COARSE_DEV = 16
CAPACITY = 2


def to_grid(per_device, row_devs, col_devs):
    tail = per_device.shape[2:]
    shaped = per_device.reshape((row_devs, col_devs, CELLS_X, CELLS_Y, ZBLOCKS) + tail)
    moved = jnp.moveaxis(shaped, 2, 1)
    return moved.reshape((GRID_X, GRID_Y, ZBLOCKS) + tail)


def neighbour_tables(key):
    row_devs = GRID_X // CELLS_X
    col_devs = GRID_Y // CELLS_Y
    devices = row_devs * col_devs
    blocks = BLOCKS_DEV
    entries = blocks * SLOTS
    key_list = jax.random.split(key, 6)
    coarse_order = jax.vmap(lambda subkey: jax.random.permutation(subkey, blocks))(jax.random.split(key_list[0], devices))
    placed = jnp.argsort(coarse_order, axis=1)
    is_coarse = placed < COARSE_DEV
    counts = jax.random.randint(key_list[1], (devices, blocks), 1, SLOTS + 1)
    first_fine = coarse_order[:, COARSE_DEV]
    counts = counts.at[jnp.arange(devices), first_fine].set(SLOTS)
    is_live = jnp.logical_not(is_coarse)[:, :, None] & (jnp.arange(SLOTS)[None, None, :] < counts[:, :, None])
    is_live = is_live.reshape(devices, entries)
    shuffle = jax.vmap(lambda subkey: jax.random.permutation(subkey, entries))(jax.random.split(key_list[2], devices))
    scores = jnp.where(is_live, shuffle, shuffle + entries)
    ordering = jnp.argsort(scores, axis=1)
    ranking = jnp.argsort(ordering, axis=1)
    common = jax.random.randint(key_list[3], (), 0, devices)
    owners_perm = jax.vmap(lambda subkey: jax.random.permutation(subkey, devices))(jax.random.split(key_list[4], devices))
    where_common = jnp.argmax(owners_perm == common, axis=1)
    leading = owners_perm[:, 0]
    owners_perm = owners_perm.at[jnp.arange(devices), where_common].set(leading)
    owners_perm = owners_perm.at[:, 0].set(common)
    group_at = jnp.minimum(ranking // CAPACITY, devices - 1)
    owner_ids = jnp.take_along_axis(owners_perm, group_at, axis=1)
    owner_ids = jnp.where(is_live, owner_ids, 0)
    picked = jax.random.randint(key_list[5], (devices, entries), 0, COARSE_DEV)
    chosen = coarse_order[owner_ids, picked]
    chosen = jnp.where(is_live, chosen, 0)
    split_grid = to_grid(is_coarse.astype(jnp.int32), row_devs, col_devs)
    count_grid = to_grid(counts.astype(jnp.int32), row_devs, col_devs)
    owner_grid = to_grid(owner_ids.reshape(devices, blocks, SLOTS).astype(jnp.int32), row_devs, col_devs)
    block_grid = to_grid(chosen.reshape(devices, blocks, SLOTS).astype(jnp.int32), row_devs, col_devs)
    return (split_grid, count_grid, owner_grid, block_grid)


def draw_cf_split(key, part):
    return neighbour_tables(key)[0]


def draw_nbr_count(key, part):
    return neighbour_tables(key)[1]


def draw_nbr_owner(key, part):
    return neighbour_tables(key)[2]


def draw_nbr_block(key, part):
    return neighbour_tables(key)[3]


def level_of(stream_key, shape, pieces, low, largest):
    def one(position, blocks):
        heights = jax.random.uniform(jax.random.fold_in(jax.random.fold_in(stream_key, 6), position), (blocks,), jnp.float32, low / len(pieces), largest / len(pieces))
        return jnp.repeat(jnp.exp(heights), shape[position] // blocks).reshape((-1,) + (1,) * (len(shape) - position - 1))

    gain = one(*pieces[0])
    for cut in pieces[1:]:
        gain = gain * one(*cut)
    return gain


def gaussian(key, shape, scale, limit, pieces=(), kind=jnp.bfloat16):
    values = scale * jax.random.normal(key, shape, jnp.float32)
    if pieces:
        values = values * level_of(key, shape, pieces, -0.22, 0.18)
    return jnp.clip(values, -limit, limit).astype(kind)


def setup_inputs(seed: int = 0) -> dict:
    streams_of = jax.random.split(jax.random.key(seed), 10)
    return {
        "test_vectors": gaussian(streams_of[0], (VECS, GRID_X, GRID_Y, DEPTH), 1.0, 6.0, ((1, 16), (2, 8)), jnp.float32),
        "coef_x": jnp.clip(jnp.exp(math.log(3.0) - 2.3025851 * jax.random.uniform(streams_of[1], (GRID_X, GRID_Y, DEPTH), jnp.float32) ** level_of(streams_of[1], (GRID_X, GRID_Y, DEPTH), ((0, 16), (1, 8)), -0.2, 0.2)), 0.3, 3.0),
        "coef_y": jnp.clip(jnp.exp(math.log(3.0) - 2.3025851 * jax.random.uniform(streams_of[2], (GRID_X, GRID_Y, DEPTH), jnp.float32) ** level_of(streams_of[2], (GRID_X, GRID_Y, DEPTH), ((0, 16), (1, 8)), -0.2, 0.2)), 0.3, 3.0),
        "coef_z": jnp.clip(jnp.exp(math.log(0.5) - 2.3025851 * jax.random.uniform(streams_of[3], (GRID_X, GRID_Y, DEPTH), jnp.float32) ** level_of(streams_of[3], (GRID_X, GRID_Y, DEPTH), ((0, 16), (1, 8)), -0.2, 0.2)), 0.05, 0.5),
        "shift": jnp.clip(jnp.exp(math.log(1.0) - 2.3025851 * jax.random.uniform(streams_of[4], (GRID_X, GRID_Y, DEPTH), jnp.float32) ** level_of(streams_of[4], (GRID_X, GRID_Y, DEPTH), ((0, 16), (1, 8)), -0.2, 0.2)), 0.1, 1.0),
        "cf_split": draw_cf_split(jax.random.fold_in(streams_of[9], 71), 0),
        "nbr_count": draw_nbr_count(jax.random.fold_in(streams_of[9], 71), 0),
        "nbr_owner": draw_nbr_owner(jax.random.fold_in(streams_of[9], 71), 0),
        "nbr_block": draw_nbr_block(jax.random.fold_in(streams_of[9], 71), 0),
    }


OMEGA = 0.8
RIDGE = 0.05

def couple(padded, weight_x, weight_y, weight_z):
    along_x = padded[:, 2:, 1:-1, 1:-1] + padded[:, :-2, 1:-1, 1:-1]
    along_y = padded[:, 1:-1, 2:, 1:-1] + padded[:, 1:-1, :-2, 1:-1]
    along_z = padded[:, 1:-1, 1:-1, 2:] + padded[:, 1:-1, 1:-1, :-2]
    return weight_x * along_x + weight_y * along_y + weight_z * along_z

def relax_step(values, summed, diagonal):
    return (1.0 - OMEGA) * values + OMEGA * (summed / diagonal)

def solve_small(gram_rows, right_side):
    extent = len(right_side)
    factor = [[None] * extent for unused in range(extent)]
    for row_at in range(extent):
        for col_at in range(row_at + 1):
            residual_sum = gram_rows[row_at][col_at]
            for mid_at in range(col_at):
                residual_sum = residual_sum - factor[row_at][mid_at] * factor[col_at][mid_at]
            if row_at == col_at:
                factor[row_at][row_at] = jnp.sqrt(residual_sum)
            else:
                factor[row_at][col_at] = residual_sum / factor[col_at][col_at]
    forward = []
    for row_at in range(extent):
        residual_sum = right_side[row_at]
        for mid_at in range(row_at):
            residual_sum = residual_sum - factor[row_at][mid_at] * forward[mid_at]
        forward.append(residual_sum / factor[row_at][row_at])
    result = [None] * extent
    for row_at in reversed(range(extent)):
        residual_sum = forward[row_at]
        for mid_at in range(row_at + 1, extent):
            residual_sum = residual_sum - factor[mid_at][row_at] * result[mid_at]
        result[row_at] = residual_sum / factor[row_at][row_at]
    return result

def reference(test_vectors, coef_x, coef_y, coef_z, shift, cf_split, nbr_count, nbr_owner, nbr_block):
    diagonal = 2.0 * (coef_x + coef_y + coef_z) + shift

    def smooth_one(vector):
        values = vector[None]
        for repeat in range(SWEEPS):
            padded = jnp.pad(values, ((0, 0), (1, 1), (1, 1), (1, 1)))
            values = relax_step(values, couple(padded, coef_x, coef_y, coef_z), diagonal)
        return values[0]
    smoothed = lax.map(smooth_one, test_vectors)
    rounded = smoothed.astype(jnp.bfloat16)
    all_blocks = jnp.transpose(rounded.reshape(VECS, GRID_X, GRID_Y, ZBLOCKS, BLOCK_ROWS), (1, 2, 3, 0, 4))
    col_devs = GRID_Y // CELLS_Y
    slot_ids = jnp.arange(SLOTS)

    def fit_row(row_x):
        owner_ids = nbr_owner[row_x]
        local_ids = nbr_block[row_x]
        source_x = owner_ids // col_devs * CELLS_X + local_ids // (CELLS_Y * ZBLOCKS)
        source_y = owner_ids % col_devs * CELLS_Y + local_ids // ZBLOCKS % CELLS_Y
        source_z = local_ids % ZBLOCKS
        is_live = (cf_split[row_x] == 0)[:, :, None] & (slot_ids[None, None, :] < nbr_count[row_x][:, :, None])
        coarse = all_blocks[source_x, source_y, source_z]
        coarse = jnp.where(is_live[..., None, None], coarse, jnp.zeros((), jnp.bfloat16))
        fine_block = all_blocks[row_x]
        coarse_wide = coarse.astype(jnp.float32)
        fine_wide = fine_block.astype(jnp.float32)
        gram_full = jnp.einsum('abskr,abtkr->abstr', coarse_wide, coarse_wide) / VECS
        rhs_full = jnp.einsum('abskr,abkr->absr', coarse_wide, fine_wide) / VECS
        gram_rows = [[gram_full[:, :, first, second] + (RIDGE if first == second else 0.0) for second in range(SLOTS)] for first in range(SLOTS)]
        weights = solve_small(gram_rows, [rhs_full[:, :, first] for first in range(SLOTS)])
        return jnp.stack(weights, 0)
    fitted = lax.map(fit_row, jnp.arange(GRID_X))
    interp_weights = jnp.transpose(fitted, (1, 0, 2, 3, 4)).reshape(SLOTS, GRID_X, GRID_Y, DEPTH)
    return (smoothed, interp_weights)
```

```python
import jax
import jax.numpy as jnp
from jax import lax
from jax.experimental import pallas as pl
from jax.experimental.pallas import tpu as pltpu
from jax.sharding import PartitionSpec as P

SLOTS = 4
SWEEPS = 3
ROWS = 128
OMEGA = 0.8
RIDGE = 0.05
VECS = 48
CHUNKS = 3
KV = VECS // CHUNKS
NX = 4
NY = 16
SITES = NX * NY
XROW = (NY + 2) * KV
EXT = (NX + 2) * XROW
GX = 16
GY = 8
MESH = pl.DeviceIdType.MESH
F32 = jnp.float32
BF16 = jnp.bfloat16


def site_row(x, y):
    return (x + 1) * XROW + (y + 1) * KV


def smooth_kernel(
    tv, cx, cy, cz, sh, sm_out, blk, stage, wa, wb, ka, kb, km, kp, fxs, fxr, fys, fyr,
    in_sem, out_sem, send_sem, recv_sem
):
    i = lax.axis_index("gx")
    j = lax.axis_index("gy")
    peers = (
        (lax.rem(i + GX - 1, GX), j),
        (lax.rem(i + 1, GX), j),
        (i, lax.rem(j + GY - 1, GY)),
        (i, lax.rem(j + 1, GY)),
    )
    loads = []
    for c in range(CHUNKS):
        part = pl.ds(c * KV, KV)
        load = pltpu.make_async_copy(tv.at[part], stage.at[part], in_sem.at[c])
        load.start()
        loads.append(load)
    barrier = pltpu.get_barrier_semaphore()
    for peer in peers:
        pl.semaphore_signal(barrier, inc=1, device_id=peer, device_id_type=MESH)

    ax, ay, az = cx[...], cy[...], cz[...]
    scale = OMEGA / (2.0 * (ax + ay + az) + sh[...])
    ka[...] = ax * scale
    kb[...] = ay * scale
    az = az * scale
    lane = lax.broadcasted_iota(jnp.int32, az.shape, 2)
    km[...] = jnp.where(lane == 0, 0.0, az)
    kp[...] = jnp.where(lane == ROWS - 1, 0.0, az)
    keep = (
        (i > 0).astype(F32),
        (i < GX - 1).astype(F32),
        (j > 0).astype(F32),
        (j < GY - 1).astype(F32),
    )

    def copies(s, c):
        out = []
        for d in range(4):
            src, dst = (fxs, fxr) if d < 2 else (fys, fyr)
            out.append(
                pltpu.make_async_remote_copy(
                    src_ref=src.at[s, c, d % 2],
                    dst_ref=dst.at[s, c, 1 - d % 2],
                    send_sem=send_sem.at[s, c, d],
                    recv_sem=recv_sem.at[s, c, d],
                    device_id=peers[d],
                    device_id_type=MESH,
                )
            )
        return out

    def send_faces(s, c, w):
        for side in range(2):
            x = side * (NX - 1)
            fxs[s, c, side] = w[c, pl.ds(site_row(x, 0), NY * KV)].astype(BF16)
            y = side * (NY - 1)
            for x in range(NX):
                fys[s, c, side, pl.ds(x * KV, KV)] = w[c, pl.ds(site_row(x, y), KV)].astype(BF16)
        for copy in copies(s, c):
            copy.start()

    def fill_halo(s, c, w):
        for copy in copies(s, c):
            copy.wait_recv()
        for side in range(2):
            x = -1 if side == 0 else NX
            w[c, pl.ds(site_row(x, 0), NY * KV)] = fxr[s, c, side].astype(F32) * keep[side]
            y = -1 if side == 0 else NY
            for x in range(NX):
                w[c, pl.ds(site_row(x, y), KV)] = (
                    fyr[s, c, side, pl.ds(x * KV, KV)].astype(F32) * keep[2 + side]
                )

    def sweep(c, src, dst, last):
        def plane(x, carry):
            base = pl.multiple_of(x * XROW, 16)

            def cell(dx, y):
                return src[c, pl.ds(base + site_row(dx, y), KV)]

            below, here = cell(0, -1), cell(0, 0)
            for y in range(NY):
                above = cell(0, y + 1)
                row = slice(y, y + 1)
                new = (
                    ka[x, row] * (cell(-1, y) + cell(1, y))
                    + kb[x, row] * (below + above)
                    + km[x, row] * pltpu.roll(here, 1, 1)
                    + kp[x, row] * pltpu.roll(here, ROWS - 1, 1)
                    + (1.0 - OMEGA) * here
                )
                dst[c, pl.ds(base + site_row(0, y), KV)] = new
                if last:
                    blk[x * NY + y, pl.ds(c * KV, KV)] = new.astype(BF16)
                below, here = here, above
            return carry

        lax.fori_loop(0, NX, plane, 0)

    buffers = (wa, wb)
    for c in range(CHUNKS):
        loads[c].wait()
        for x in range(NX):
            for half in range(NY // 8):
                for k in range(KV):
                    wa[c, pl.ds(site_row(x, half * 8) + k, 8, stride=KV), :] = stage[
                        c * KV + k, x, pl.ds(half * 8, 8), :
                    ]
        if c == 0:
            pl.semaphore_wait(barrier, 4)
        send_faces(0, c, wa)
    stores = []
    for s in range(SWEEPS):
        src, dst = buffers[s % 2], buffers[(s + 1) % 2]
        for c in range(CHUNKS):
            fill_halo(s, c, src)
            sweep(c, src, dst, s == SWEEPS - 1)
            if s < SWEEPS - 1:
                send_faces(s + 1, c, dst)
            else:
                for x in range(NX):
                    for half in range(NY // 8):
                        for k in range(KV):
                            stage[c * KV + k, x, pl.ds(half * 8, 8), :] = dst[
                                c, pl.ds(site_row(x, half * 8) + k, 8, stride=KV), :
                            ]
                part = pl.ds(c * KV, KV)
                store = pltpu.make_async_copy(stage.at[part], sm_out.at[part], out_sem.at[c])
                store.start()
                stores.append(store)
    for s in range(SWEEPS):
        for c in range(CHUNKS):
            for copy in copies(s, c):
                copy.wait_send()
    for store in stores:
        store.wait()


def smooth(test_vectors, coef_x, coef_y, coef_z, shift):
    vmem = pl.BlockSpec(memory_space=pltpu.VMEM)
    anywhere = pl.BlockSpec(memory_space=pl.ANY)
    return pl.pallas_call(
        smooth_kernel,
        out_shape=(
            jax.ShapeDtypeStruct((VECS, NX, NY, ROWS), F32),
            jax.ShapeDtypeStruct((SITES, VECS, ROWS), BF16),
        ),
        in_specs=[anywhere, vmem, vmem, vmem, vmem],
        out_specs=(anywhere, vmem),
        scratch_shapes=[
            pltpu.VMEM((VECS, NX, NY, ROWS), F32),
            pltpu.VMEM((CHUNKS, EXT, ROWS), F32),
            pltpu.VMEM((CHUNKS, EXT, ROWS), F32),
            pltpu.VMEM((NX, NY, ROWS), F32),
            pltpu.VMEM((NX, NY, ROWS), F32),
            pltpu.VMEM((NX, NY, ROWS), F32),
            pltpu.VMEM((NX, NY, ROWS), F32),
            pltpu.VMEM((SWEEPS, CHUNKS, 2, NY * KV, ROWS), BF16),
            pltpu.VMEM((SWEEPS, CHUNKS, 2, NY * KV, ROWS), BF16),
            pltpu.VMEM((SWEEPS, CHUNKS, 2, NX * KV, ROWS), BF16),
            pltpu.VMEM((SWEEPS, CHUNKS, 2, NX * KV, ROWS), BF16),
            pltpu.SemaphoreType.DMA((CHUNKS,)),
            pltpu.SemaphoreType.DMA((CHUNKS,)),
            pltpu.SemaphoreType.DMA((SWEEPS, CHUNKS, 4)),
            pltpu.SemaphoreType.DMA((SWEEPS, CHUNKS, 4)),
        ],
        compiler_params=pltpu.CompilerParams(
            collective_id=0, has_side_effects=True, vmem_limit_bytes=48 * 1024 * 1024
        ),
        name="smooth",
    )(test_vectors, coef_x, coef_y, coef_z, shift)


def solve_rows(gram, rhs):
    low = [[None] * SLOTS for _ in range(SLOTS)]
    inv = []
    for r in range(SLOTS):
        scaled = []
        diag = gram[r, r]
        for c in range(r):
            rest = gram[r, c]
            for m in range(c):
                rest = rest - scaled[m] * low[c][m]
            scaled.append(rest)
            low[r][c] = rest * inv[c]
            diag = diag - rest * low[r][c]
        inv.append(1.0 / diag)
    fwd = []
    for r in range(SLOTS):
        rest = rhs[r]
        for m in range(r):
            rest = rest - low[r][m] * fwd[m]
        fwd.append(rest)
    out = [None] * SLOTS
    for r in reversed(range(SLOTS)):
        rest = fwd[r] * inv[r]
        for m in range(r + 1, SLOTS):
            rest = rest - low[m][r] * out[m]
        out[r] = rest
    return out


PAIRS = [(s, t) for s in range(SLOTS) for t in range(s + 1)] + [
    (s, SLOTS) for s in range(SLOTS)
]


def weights_kernel(target, replies, blk, sm_in, w_out, sm_out, sums, copy_sem):
    move = pltpu.make_async_copy(sm_in, sm_out, copy_sem)
    move.start()

    def block(b, carry):
        values = []
        for s in range(SLOTS):
            at = target[b * SLOTS + s]
            live = at >= 0
            found = replies[jnp.maximum(at, 0)].astype(F32)
            values.append(jnp.where(live, found, 0.0))
        values.append(blk[b].astype(F32))
        for n, (s, t) in enumerate(PAIRS):
            prod = values[s] * values[t]
            acc = prod[0:8]
            for h in range(1, VECS // 8):
                acc = acc + prod[8 * h : 8 * h + 8]
            sums[n, pl.ds(pl.multiple_of(b * 8, 8), 8), :] = acc
        return carry

    lax.fori_loop(0, SITES, block, 0)
    for g in range(SITES // 8):
        total = {}
        for n, pair in enumerate(PAIRS):
            acc = sums[n, pl.ds(g * 64, 8, stride=8), :]
            for h in range(1, 8):
                acc = acc + sums[n, pl.ds(g * 64 + h, 8, stride=8), :]
            acc = acc * (1.0 / VECS)
            if pair[0] == pair[1]:
                acc = acc + RIDGE
            total[pair] = acc
        out = solve_rows(total, [total[s, SLOTS] for s in range(SLOTS)])
        for s in range(SLOTS):
            w_out[s, g // 2, pl.ds((g % 2) * 8, 8), :] = out[s]
    move.wait()


def fit(target, replies, blk, sm):
    vmem = pl.BlockSpec(memory_space=pltpu.VMEM)
    anywhere = pl.BlockSpec(memory_space=pl.ANY)
    return pl.pallas_call(
        weights_kernel,
        out_shape=(
            jax.ShapeDtypeStruct((SLOTS, NX, NY, ROWS), F32),
            jax.ShapeDtypeStruct((VECS, NX, NY, ROWS), F32),
        ),
        in_specs=[pl.BlockSpec(memory_space=pltpu.SMEM), vmem, vmem, anywhere],
        out_specs=(vmem, anywhere),
        scratch_shapes=[
            pltpu.VMEM((len(PAIRS), SITES * 8, ROWS), F32),
            pltpu.SemaphoreType.DMA,
        ],
        compiler_params=pltpu.CompilerParams(vmem_limit_bytes=48 * 1024 * 1024),
        name="fit",
    )(target, replies, blk, sm)


def per_device(
    test_vectors, coef_x, coef_y, coef_z, shift, cf_split, nbr_count, nbr_owner, nbr_block
):
    devices = GX * GY
    entries = SITES * SLOTS
    capacity = 2
    live = ((cf_split == 0)[..., None] & (jnp.arange(SLOTS) < nbr_count[..., None])).reshape(entries)
    owner = nbr_owner.reshape(entries)
    local = nbr_block.reshape(entries)
    member = (owner[:, None] == jnp.arange(devices)[None, :]) & live[:, None]
    key = jnp.arange(entries) * SITES + local
    first = jnp.min(jnp.where(member, key[:, None], entries * SITES), axis=0)
    second = jnp.max(jnp.where(member, key[:, None], -1), axis=0)
    table = jnp.stack([first % SITES, jnp.maximum(second, 0) % SITES], axis=1)
    first_here = jnp.sum(jnp.where(member, first[None, :], 0), axis=1)
    target = jnp.where(live, owner * capacity + (key != first_here), -1)
    sm, blk = smooth(test_vectors, coef_x, coef_y, coef_z, shift)
    wanted = lax.all_to_all(table, ("gx", "gy"), split_axis=0, concat_axis=0, tiled=True)
    found = blk[wanted.reshape(-1)].reshape(devices, capacity, VECS, ROWS)
    replies = lax.all_to_all(found, ("gx", "gy"), split_axis=0, concat_axis=0, tiled=True)
    replies = replies.reshape(devices * capacity, VECS, ROWS)
    weights, smoothed = fit(target, replies, blk, sm)
    return (smoothed, weights)


def solution(mesh):
    cells = P("gx", "gy", None)
    lists = P("gx", "gy", None, None)
    vectors = P(None, "gx", "gy", None)
    return jax.shard_map(
        per_device,
        mesh=mesh,
        in_specs=(vectors, cells, cells, cells, cells, cells, cells, lists, lists),
        out_specs=(vectors, vectors),
        check_vma=False,
    )
```

```python
import jax
import jax.numpy as jnp
from jax import lax
from jax.experimental import pallas as pl
from jax.experimental.pallas import tpu as pltpu
from jax.sharding import PartitionSpec as P

SLOTS = 4
SWEEPS = 3
ROWS = 128
OMEGA = 0.8
RIDGE = 0.05
VECS = 48
CHUNKS = 3
KV = VECS // CHUNKS
NX = 4
NY = 16
SITES = NX * NY
XROW = (NY + 2) * KV
EXT = (NX + 2) * XROW
GX = 16
GY = 8
MESH = pl.DeviceIdType.MESH
F32 = jnp.float32
BF16 = jnp.bfloat16


def site_row(x, y):
    return (x + 1) * XROW + (y + 1) * KV


AXES = "xyz"
LINE = 4
CORES = 2
COARSE = 16
PLANE = LINE * LINE
ROUTES = (("x", "z", "y"), ("y", "z", "x"), ("z", "x", "y"))


def lists_of(meta):
    lane = lax.broadcasted_iota(jnp.int32, (ROWS, ROWS), 1)
    sub = lax.broadcasted_iota(jnp.int32, (ROWS, ROWS), 0)
    diag = lane == sub
    none = 1 << 20

    def column(row):
        return jnp.sum(jnp.where(diag, row, 0), axis=1, keepdims=True)

    def line(col):
        return jnp.sum(jnp.where(diag, col, 0), axis=0, keepdims=True)

    members, keys, owners = [], [], []
    for h in range(2):
        entry = meta[h : h + 1]
        owner = entry >> 6
        key = (lane[:1] + h * ROWS) * SITES + (entry & (SITES - 1))
        owners.append(owner)
        keys.append(key)
        members.append(owner == sub)
    first = jnp.minimum(*[jnp.where(m, k, none) for m, k in zip(members, keys)])
    first = jnp.min(first, axis=1, keepdims=True)
    first = jnp.where(first >= none, 0, first)
    second = jnp.maximum(*[jnp.where(m, k, 0) for m, k in zip(members, keys)])
    second = jnp.max(second, axis=1, keepdims=True)
    wanted = [line(v) & (SITES - 1) for v in (first, second)]
    targets = [[] for _ in ROUTES]
    for h in range(2):
        own = owners[h]
        at_first = jnp.sum(jnp.where(members[h], first, 0), axis=0, keepdims=True)
        place = jnp.where(keys[h] == at_first, 0, 1)
        at = {"x": (own >> 5) & 3, "z": (own >> 3) & 3, "y": (own >> 1) & 3}
        for c, (a, u, v) in enumerate(ROUTES):
            slot = ((at[a] * CORES + (own & 1)) * PLANE + at[v] * LINE + at[u]) * 2 + place
            targets[c].append(jnp.where(own < 0, -1, slot))
    coarse = meta[2:3]
    rank = jnp.sum(jnp.where(sub < lane, column(coarse), 0), axis=0, keepdims=True)
    hit = (rank == sub[:COARSE]) & (coarse > 0)
    ids = jnp.sum(jnp.where(hit, lane[:COARSE], 0), axis=1, keepdims=True)
    ids = jnp.broadcast_to(ids, (COARSE, ROWS))
    rank = jnp.minimum(rank, COARSE - 1)
    return wanted, targets, rank, ids


def smooth_kernel(
    tv, cx, cy, cz, sh, meta, sm_out, blk, rb, tgt,
    stage, coef, wa, wb, ka, kb, km, kp, fxs, fxr, fys, fyr,
    want, wants, ranks, idv, want_s, rank_s, id_s, pg0, pg1, pg2, sb,
    in_sem, coef_sem, out_sem, send_sem, recv_sem, want_send, want_recv, rank_send, rank_recv,
    cast_send, cast_recv, ans_send, ans_recv, own_sem, smem_sem,
):
    pg = (pg0, pg1, pg2)
    i = lax.axis_index("gx")
    j = lax.axis_index("gy")
    core = lax.rem(j, CORES)
    at = {"x": i // LINE, "z": lax.rem(i, LINE), "y": j // CORES}
    peers = (
        (lax.rem(i + GX - 1, GX), j),
        (lax.rem(i + 1, GX), j),
        (i, lax.rem(j + GY - 1, GY)),
        (i, lax.rem(j + 1, GY)),
    )

    def device(axis, d, e):
        moved = dict(at)
        moved[axis] = lax.rem(at[axis] + d, LINE)
        return (moved["x"] * LINE + moved["z"], moved["y"] * CORES + lax.rem(core + e, CORES))

    def remote(src, dst, send, recv, peer):
        return pltpu.make_async_remote_copy(
            src_ref=src, dst_ref=dst, send_sem=send, recv_sem=recv,
            device_id=peer, device_id_type=MESH,
        )

    loads = []
    for n, part in enumerate((cx, cy, cz, sh)):
        load = pltpu.make_async_copy(part, coef.at[n], coef_sem.at[n])
        load.start()
        loads.append(load)
    coef_loads, loads = loads, []
    for c in range(CHUNKS):
        part = pl.ds(c * KV, KV)
        load = pltpu.make_async_copy(tv.at[part], stage.at[part], in_sem.at[c])
        load.start()
        loads.append(load)
    barrier = pltpu.get_barrier_semaphore()
    for peer in peers[:2]:
        pl.semaphore_signal(barrier, inc=1, device_id=peer, device_id_type=MESH)
    pl.semaphore_signal(barrier, inc=1, device_id=device("x", 0, 1), device_id_type=MESH)
    for axis in AXES:
        for d in range(1, LINE):
            for e in range(CORES):
                pl.semaphore_signal(
                    barrier, inc=1, device_id=device(axis, d, e), device_id_type=MESH
                )
    greeted = 3 + len(AXES) * (LINE - 1) * CORES

    for load in coef_loads:
        load.wait()
    ax, ay, az = coef[0], coef[1], coef[2]
    scale = OMEGA / (2.0 * (ax + ay + az) + coef[3])
    ka[...] = ax * scale
    kb[...] = ay * scale
    az = az * scale
    lane = lax.broadcasted_iota(jnp.int32, az.shape, 2)
    km[...] = jnp.where(lane == 0, 0.0, az)
    kp[...] = jnp.where(lane == ROWS - 1, 0.0, az)
    keep = (
        (i > 0).astype(F32),
        (i < GX - 1).astype(F32),
        (j > 0).astype(F32),
        (j < GY - 1).astype(F32),
    )

    def copies(s, c):
        out = []
        for d in range(4):
            src, dst = (fxs, fxr) if d < 2 else (fys, fyr)
            out.append(
                remote(
                    src.at[s, c, d % 2], dst.at[s, c, 1 - d % 2],
                    send_sem.at[s, c, d], recv_sem.at[s, c, d], peers[d],
                )
            )
        return out

    def send_faces(s, c, w):
        for side in range(2):
            x = side * (NX - 1)
            fxs[s, c, side] = w[c, pl.ds(site_row(x, 0), NY * KV)].astype(BF16)
            y = side * (NY - 1)
            for x in range(NX):
                fys[s, c, side, pl.ds(x * KV, KV)] = w[c, pl.ds(site_row(x, y), KV)].astype(BF16)
        for copy in copies(s, c):
            copy.start()

    def fill_halo(s, c, w):
        for copy in copies(s, c):
            copy.wait_recv()
        for side in range(2):
            x = -1 if side == 0 else NX
            w[c, pl.ds(site_row(x, 0), NY * KV)] = fxr[s, c, side].astype(F32) * keep[side]
            y = -1 if side == 0 else NY
            for x in range(NX):
                w[c, pl.ds(site_row(x, y), KV)] = (
                    fyr[s, c, side, pl.ds(x * KV, KV)].astype(F32) * keep[2 + side]
                )

    def sweep(c, src, dst, last):
        def plane(x, carry):
            base = pl.multiple_of(x * XROW, 16)

            def cell(dx, y):
                return src[c, pl.ds(base + site_row(dx, y), KV)]

            below, here = cell(0, -1), cell(0, 0)
            for y in range(NY):
                above = cell(0, y + 1)
                row = slice(y, y + 1)
                new = (
                    ka[x, row] * (cell(-1, y) + cell(1, y))
                    + kb[x, row] * (below + above)
                    + km[x, row] * pltpu.roll(here, 1, 1)
                    + kp[x, row] * pltpu.roll(here, ROWS - 1, 1)
                    + (1.0 - OMEGA) * here
                )
                dst[c, pl.ds(base + site_row(0, y), KV)] = new
                if last:
                    blk[c, x * NY + y] = new.astype(BF16)
                below, here = here, above
            return carry

        lax.fori_loop(0, NX, plane, 0)

    def want_copies():
        out = []
        for n, axis in enumerate(AXES):
            for d in range(LINE):
                for e in range(CORES):
                    if d or e:
                        out.append(
                            remote(
                                want, wants.at[n, at[axis] * CORES + core],
                                want_send.at[n, d, e], want_recv.at[n, d, e], device(axis, d, e),
                            )
                        )
        return out

    def rank_copies(c, step):
        a, u, v = ROUTES[c]
        out = []
        for d in range(1, LINE):
            if step == 0:
                ref, peer = ranks.at[c, at[v], at[u]], device(u, d, 0)
            else:
                ref, peer = ranks.at[c, at[v]], device(v, d, 0)
            out.append(
                remote(ref, ref, rank_send.at[c, step, d], rank_recv.at[c, step, d], peer)
            )
        return out

    def cast_copies(c, step):
        a, u, v = ROUTES[c]
        out = []
        for d in (2, 1, 3):
            if step == 0:
                ref, peer = pg[c].at[at[v], at[u]], device(u, d, 0)
            else:
                ref, peer = pg[c].at[at[v]], device(v, d, 0)
            out.append(
                remote(ref, ref, cast_send.at[c, step, d], cast_recv.at[c, step, d], peer)
            )
        return out

    def answer(c, d, e):
        a = ROUTES[c][0]
        slot = lax.rem(at[a] + d, LINE) * CORES + lax.rem(core + e, CORES)
        here = at[a] * CORES + core
        if d == 0 and e == 0:
            return pltpu.make_async_copy(sb.at[c, slot], rb.at[c, here], own_sem.at[c])
        return remote(
            sb.at[c, slot], rb.at[c, here],
            ans_send.at[c, d, e], ans_recv.at[c, d, e], device(a, d, e),
        )

    order = [(d, e) for d in (2, 1, 3, 0) for e in range(CORES)]

    def spread(c):
        a, u, v = ROUTES[c]
        for r in range(COARSE):
            pg[c][at[v], at[u], r] = blk[c, id_s[r, 0] & (SITES - 1)]
        for copy in cast_copies(c, 0):
            copy.start()

    def spread_more(c):
        for copy in cast_copies(c, 0):
            copy.wait_recv()
        for copy in cast_copies(c, 1):
            copy.start()

    def reply(c):
        a, u, v = ROUTES[c]
        n = AXES.index(a)
        for copy in cast_copies(c, 1):
            copy.wait_recv()
        for d, e in order:
            slot = lax.rem(at[a] + d, LINE) * CORES + lax.rem(core + e, CORES)
            for vv in range(LINE):
                for uu in range(LINE):
                    whose = {a: at[a], u: uu, v: vv}
                    owner = whose["x"] * 32 + whose["z"] * 8 + whose["y"] * 2 + core
                    for p in range(2):
                        block = want_s[n, slot, p, owner] & (SITES - 1)
                        rank = rank_s[c, vv, uu, 0, block] & (COARSE - 1)
                        sb[c, slot, (vv * LINE + uu) * 2 + p] = pg[c][vv, uu, rank]
            answer(c, d, e).start()

    def transpose_in(c):
        loads[c].wait()
        for x in range(NX):
            for half in range(NY // 8):
                for k in range(KV):
                    wa[c, pl.ds(site_row(x, half * 8) + k, 8, stride=KV), :] = stage[
                        c * KV + k, x, pl.ds(half * 8, 8), :
                    ]

    stores = []

    def transpose_out(c, w):
        for x in range(NX):
            for half in range(NY // 8):
                for k in range(KV):
                    stage[c * KV + k, x, pl.ds(half * 8, 8), :] = w[
                        c, pl.ds(site_row(x, half * 8) + k, 8, stride=KV), :
                    ]
        part = pl.ds(c * KV, KV)
        store = pltpu.make_async_copy(stage.at[part], sm_out.at[part], out_sem.at[c])
        store.start()
        stores.append(store)

    transpose_in(0)
    pl.semaphore_wait(barrier, greeted)
    send_faces(0, 0, wa)
    for c in range(1, CHUNKS):
        transpose_in(c)
        send_faces(0, c, wa)

    wanted, targets, rank, ids = lists_of(meta[...])
    idv[...] = ids
    id_copy = pltpu.make_async_copy(idv, id_s, smem_sem.at[0])
    id_copy.start()
    for p in range(2):
        want[p : p + 1] = wanted[p]
        for n, axis in enumerate(AXES):
            wants[n, at[axis] * CORES + core, p : p + 1] = wanted[p]
    tgt[...] = jnp.zeros_like(tgt)
    for c in range(CHUNKS):
        a, u, v = ROUTES[c]
        ranks[c, at[v], at[u]] = rank
        for h in range(2):
            tgt[2 * c + h : 2 * c + h + 1] = targets[c][h]
        for copy in rank_copies(c, 0):
            copy.start()
    for copy in want_copies():
        copy.start()

    for c in range(CHUNKS):
        fill_halo(0, c, wa)
        sweep(c, wa, wb, False)
        send_faces(1, c, wb)
    for c in range(CHUNKS):
        for copy in rank_copies(c, 0):
            copy.wait_recv()
        for copy in rank_copies(c, 1):
            copy.start()
    for c in range(CHUNKS):
        fill_halo(1, c, wb)
        sweep(c, wb, wa, False)
        send_faces(2, c, wa)
    for copy in want_copies():
        copy.wait_recv()
    want_copy = pltpu.make_async_copy(wants, want_s, smem_sem.at[1])
    want_copy.start()
    for c in range(CHUNKS):
        for copy in rank_copies(c, 1):
            copy.wait_recv()
    rank_copy = pltpu.make_async_copy(ranks, rank_s, smem_sem.at[2])
    rank_copy.start()
    id_copy.wait()
    for c in range(CHUNKS):
        fill_halo(2, c, wa)
        sweep(c, wa, wb, True)
        spread(c)
        if c > 0:
            spread_more(c - 1)
    want_copy.wait()
    rank_copy.wait()
    spread_more(CHUNKS - 1)
    for c in range(CHUNKS):
        reply(c)
        transpose_out(c, wb)

    for s in range(SWEEPS):
        for c in range(CHUNKS):
            for copy in copies(s, c):
                copy.wait_send()
    for copy in want_copies():
        copy.wait_send()
    for c in range(CHUNKS):
        for step in range(2):
            for copy in rank_copies(c, step) + cast_copies(c, step):
                copy.wait_send()
        for d, e in order:
            copy = answer(c, d, e)
            if d or e:
                copy.wait_send()
                copy.wait_recv()
            else:
                copy.wait()
    for store in stores:
        store.wait()


def smooth(test_vectors, coef_x, coef_y, coef_z, shift, meta):
    vmem = pl.BlockSpec(memory_space=pltpu.VMEM)
    anywhere = pl.BlockSpec(memory_space=pl.ANY)
    cells = pltpu.VMEM((NX, NY, ROWS), F32)
    plane = pltpu.VMEM((LINE, LINE, COARSE, KV, ROWS), BF16)
    dma = pltpu.SemaphoreType.DMA
    return pl.pallas_call(
        smooth_kernel,
        out_shape=(
            jax.ShapeDtypeStruct((VECS, NX, NY, ROWS), F32),
            jax.ShapeDtypeStruct((CHUNKS, SITES, KV, ROWS), BF16),
            jax.ShapeDtypeStruct((CHUNKS, LINE * CORES, 2 * PLANE, KV, ROWS), BF16),
            jax.ShapeDtypeStruct((8, ROWS), jnp.int32),
        ),
        in_specs=[anywhere] * 5 + [vmem],
        out_specs=(anywhere, vmem, anywhere, vmem),
        scratch_shapes=[
            pltpu.VMEM((VECS, NX, NY, ROWS), F32),
            pltpu.VMEM((4, NX, NY, ROWS), F32),
            pltpu.VMEM((CHUNKS, EXT, ROWS), F32),
            pltpu.VMEM((CHUNKS, EXT, ROWS), F32),
            cells, cells, cells, cells,
            pltpu.VMEM((SWEEPS, CHUNKS, 2, NY * KV, ROWS), BF16),
            pltpu.VMEM((SWEEPS, CHUNKS, 2, NY * KV, ROWS), BF16),
            pltpu.VMEM((SWEEPS, CHUNKS, 2, NX * KV, ROWS), BF16),
            pltpu.VMEM((SWEEPS, CHUNKS, 2, NX * KV, ROWS), BF16),
            pltpu.VMEM((2, ROWS), jnp.int32),
            pltpu.VMEM((len(AXES), LINE * CORES, 2, ROWS), jnp.int32),
            pltpu.VMEM((CHUNKS, LINE, LINE, 1, ROWS), jnp.int32),
            pltpu.VMEM((COARSE, ROWS), jnp.int32),
            pltpu.SMEM((len(AXES), LINE * CORES, 2, ROWS), jnp.int32),
            pltpu.SMEM((CHUNKS, LINE, LINE, 1, ROWS), jnp.int32),
            pltpu.SMEM((COARSE, ROWS), jnp.int32),
            plane, plane, plane,
            pltpu.VMEM((CHUNKS, LINE * CORES, 2 * PLANE, KV, ROWS), BF16),
            dma((CHUNKS,)),
            dma((4,)),
            dma((CHUNKS,)),
            dma((SWEEPS, CHUNKS, 4)),
            dma((SWEEPS, CHUNKS, 4)),
            dma((len(AXES), LINE, CORES)),
            dma((len(AXES), LINE, CORES)),
            dma((CHUNKS, 2, LINE)),
            dma((CHUNKS, 2, LINE)),
            dma((CHUNKS, 2, LINE)),
            dma((CHUNKS, 2, LINE)),
            dma((CHUNKS, LINE, CORES)),
            dma((CHUNKS, LINE, CORES)),
            dma((CHUNKS,)),
            dma((3,)),
        ],
        compiler_params=pltpu.CompilerParams(
            collective_id=0, has_side_effects=True, vmem_limit_bytes=48 * 1024 * 1024
        ),
        name="smooth",
    )(test_vectors, coef_x, coef_y, coef_z, shift, meta)


def solve_rows(gram, rhs):
    low = [[None] * SLOTS for _ in range(SLOTS)]
    inv = []
    for r in range(SLOTS):
        scaled = []
        diag = gram[r, r]
        for c in range(r):
            rest = gram[r, c]
            for m in range(c):
                rest = rest - scaled[m] * low[c][m]
            scaled.append(rest)
            low[r][c] = rest * inv[c]
            diag = diag - rest * low[r][c]
        inv.append(1.0 / diag)
    fwd = []
    for r in range(SLOTS):
        rest = rhs[r]
        for m in range(r):
            rest = rest - low[r][m] * fwd[m]
        fwd.append(rest)
    out = [None] * SLOTS
    for r in reversed(range(SLOTS)):
        rest = fwd[r] * inv[r]
        for m in range(r + 1, SLOTS):
            rest = rest - low[m][r] * out[m]
        out[r] = rest
    return out


PAIRS = [(s, t) for s in range(SLOTS) for t in range(s + 1)] + [
    (s, SLOTS) for s in range(SLOTS)
]


def weights_kernel(target, replies, blk, sm_in, w_out, sm_out, sums, copy_sem):
    move = pltpu.make_async_copy(sm_in, sm_out, copy_sem)
    move.start()

    def block(b, carry):
        accs = [None] * len(PAIRS)
        for c in range(CHUNKS):
            values = []
            for s in range(SLOTS):
                at = target[2 * c + b // 32, lax.rem(b, 32) * SLOTS + s]
                found = replies[c, jnp.maximum(at, 0)].astype(F32)
                values.append(jnp.where(at >= 0, found, 0.0))
            values.append(blk[c, b].astype(F32))
            for n, (s, t) in enumerate(PAIRS):
                prod = values[s] * values[t]
                part = prod[0:8] + prod[8:16]
                accs[n] = part if c == 0 else accs[n] + part
        for n, acc in enumerate(accs):
            sums[n, pl.ds(pl.multiple_of(b * 8, 8), 8), :] = acc
        return carry

    lax.fori_loop(0, SITES, block, 0)
    for g in range(SITES // 8):
        total = {}
        for n, pair in enumerate(PAIRS):
            acc = sums[n, pl.ds(g * 64, 8, stride=8), :]
            for h in range(1, 8):
                acc = acc + sums[n, pl.ds(g * 64 + h, 8, stride=8), :]
            acc = acc * (1.0 / VECS)
            if pair[0] == pair[1]:
                acc = acc + RIDGE
            total[pair] = acc
        out = solve_rows(total, [total[s, SLOTS] for s in range(SLOTS)])
        for s in range(SLOTS):
            w_out[s, g // 2, pl.ds((g % 2) * 8, 8), :] = out[s]
    move.wait()


def fit(target, replies, blk, sm):
    vmem = pl.BlockSpec(memory_space=pltpu.VMEM)
    anywhere = pl.BlockSpec(memory_space=pl.ANY)
    return pl.pallas_call(
        weights_kernel,
        out_shape=(
            jax.ShapeDtypeStruct((SLOTS, NX, NY, ROWS), F32),
            jax.ShapeDtypeStruct((VECS, NX, NY, ROWS), F32),
        ),
        in_specs=[pl.BlockSpec(memory_space=pltpu.SMEM), vmem, vmem, anywhere],
        out_specs=(vmem, anywhere),
        scratch_shapes=[
            pltpu.VMEM((len(PAIRS), SITES * 8, ROWS), F32),
            pltpu.SemaphoreType.DMA,
        ],
        compiler_params=pltpu.CompilerParams(vmem_limit_bytes=48 * 1024 * 1024),
        name="fit",
    )(target, replies, blk, sm)


def per_device(
    test_vectors, coef_x, coef_y, coef_z, shift, cf_split, nbr_count, nbr_owner, nbr_block
):
    entries = SITES * SLOTS
    live = (cf_split == 0)[..., None] & (jnp.arange(SLOTS) < nbr_count[..., None])
    listed = jnp.where(live, nbr_owner * SITES + nbr_block, -1).reshape(entries // ROWS, ROWS)
    coarse = jnp.pad(cf_split.reshape(1, SITES), ((0, 5), (0, ROWS - SITES)))
    meta = jnp.concatenate([listed, coarse], axis=0)
    sm, blk, replies, target = smooth(test_vectors, coef_x, coef_y, coef_z, shift, meta)
    replies = replies.reshape(CHUNKS, LINE * CORES * 2 * PLANE, KV, ROWS)
    weights, smoothed = fit(target, replies, blk, sm)
    return (smoothed, weights)


def solution(mesh):
    cells = P("gx", "gy", None)
    lists = P("gx", "gy", None, None)
    vectors = P(None, "gx", "gy", None)
    return jax.shard_map(
        per_device,
        mesh=mesh,
        in_specs=(vectors, cells, cells, cells, cells, cells, cells, lists, lists),
        out_specs=(vectors, vectors),
        check_vma=False,
    )
```

```python
import jax
import jax.numpy as jnp
from jax import lax
from jax.experimental import pallas as pl
from jax.experimental.pallas import tpu as pltpu
from jax.sharding import PartitionSpec as P

SLOTS = 4
SWEEPS = 3
ROWS = 128
OMEGA = 0.8
RIDGE = 0.05
VECS = 48
CHUNKS = 3
KV = VECS // CHUNKS
NX = 4
NY = 16
SITES = NX * NY
XROW = (NY + 2) * KV
EXT = (NX + 2) * XROW
GX = 16
GY = 8
MESH = pl.DeviceIdType.MESH
F32 = jnp.float32
BF16 = jnp.bfloat16


def site_row(x, y):
    return (x + 1) * XROW + (y + 1) * KV


AXES = "xyz"
LINE = 4
CORES = 2
COARSE = 16
PLANE = LINE * LINE
ROUTES = (("x", "z", "y"), ("y", "z", "x"), ("z", "x", "y"))


def lists_of(meta):
    lane = lax.broadcasted_iota(jnp.int32, (ROWS, ROWS), 1)
    sub = lax.broadcasted_iota(jnp.int32, (ROWS, ROWS), 0)
    diag = lane == sub
    none = 1 << 20

    def column(row):
        return jnp.sum(jnp.where(diag, row, 0), axis=1, keepdims=True)

    def line(col):
        return jnp.sum(jnp.where(diag, col, 0), axis=0, keepdims=True)

    members, keys, owners = [], [], []
    for h in range(2):
        entry = meta[h : h + 1]
        owner = entry >> 6
        key = (lane[:1] + h * ROWS) * SITES + (entry & (SITES - 1))
        owners.append(owner)
        keys.append(key)
        members.append(owner == sub)
    first = jnp.minimum(*[jnp.where(m, k, none) for m, k in zip(members, keys)])
    first = jnp.min(first, axis=1, keepdims=True)
    first = jnp.where(first >= none, 0, first)
    second = jnp.maximum(*[jnp.where(m, k, 0) for m, k in zip(members, keys)])
    second = jnp.max(second, axis=1, keepdims=True)
    wanted = [line(v) & (SITES - 1) for v in (first, second)]
    targets = [[] for _ in ROUTES]
    for h in range(2):
        own = owners[h]
        at_first = jnp.sum(jnp.where(members[h], first, 0), axis=0, keepdims=True)
        place = jnp.where(keys[h] == at_first, 0, 1)
        at = {"x": (own >> 5) & 3, "z": (own >> 3) & 3, "y": (own >> 1) & 3}
        for c, (a, u, v) in enumerate(ROUTES):
            slot = ((at[a] * CORES + (own & 1)) * PLANE + at[v] * LINE + at[u]) * 2 + place
            targets[c].append(jnp.where(own < 0, -1, slot))
    coarse = meta[2:3]
    rank = jnp.sum(jnp.where(sub < lane, column(coarse), 0), axis=0, keepdims=True)
    hit = (rank == sub[:COARSE]) & (coarse > 0)
    ids = jnp.sum(jnp.where(hit, lane[:COARSE], 0), axis=1, keepdims=True)
    ids = jnp.broadcast_to(ids, (COARSE, ROWS))
    rank = jnp.minimum(rank, COARSE - 1)
    return wanted, targets, rank, ids


def smooth_kernel(
    tv, cx, cy, cz, sh, meta, sm_out, blk, rb, tgt,
    stage, coef, wa, wb, ka, kb, km, kp, fxs, fxr, fys, fyr,
    want, wants, ranks, idv, want_s, rank_s, id_s, pg0, pg1, pg2, sb, fb,
    in_sem, coef_sem, out_sem, send_sem, recv_sem, want_send, want_recv, rank_send, rank_recv,
    cast_send, cast_recv, ans_send, ans_recv, fwd_send, fwd_recv, own_sem, smem_sem,
):
    pg = (pg0, pg1, pg2)
    i = lax.axis_index("gx")
    j = lax.axis_index("gy")
    core = lax.rem(j, CORES)
    at = {"x": i // LINE, "z": lax.rem(i, LINE), "y": j // CORES}
    peers = (
        (lax.rem(i + GX - 1, GX), j),
        (lax.rem(i + 1, GX), j),
        (i, lax.rem(j + GY - 1, GY)),
        (i, lax.rem(j + 1, GY)),
    )

    def device(axis, d, e):
        moved = dict(at)
        moved[axis] = lax.rem(at[axis] + d, LINE)
        return (moved["x"] * LINE + moved["z"], moved["y"] * CORES + lax.rem(core + e, CORES))

    def remote(src, dst, send, recv, peer):
        return pltpu.make_async_remote_copy(
            src_ref=src, dst_ref=dst, send_sem=send, recv_sem=recv,
            device_id=peer, device_id_type=MESH,
        )

    loads = []
    for n, part in enumerate((cx, cy, cz, sh)):
        load = pltpu.make_async_copy(part, coef.at[n], coef_sem.at[n])
        load.start()
        loads.append(load)
    coef_loads, loads = loads, []
    for c in range(CHUNKS):
        part = pl.ds(c * KV, KV)
        load = pltpu.make_async_copy(tv.at[part], stage.at[part], in_sem.at[c])
        load.start()
        loads.append(load)
    barrier = pltpu.get_barrier_semaphore()
    for peer in peers[:2]:
        pl.semaphore_signal(barrier, inc=1, device_id=peer, device_id_type=MESH)
    pl.semaphore_signal(barrier, inc=1, device_id=device("x", 0, 1), device_id_type=MESH)
    for axis in AXES:
        for d in range(1, LINE):
            for e in range(CORES):
                pl.semaphore_signal(
                    barrier, inc=1, device_id=device(axis, d, e), device_id_type=MESH
                )
    greeted = 3 + len(AXES) * (LINE - 1) * CORES

    for load in coef_loads:
        load.wait()
    ax, ay, az = coef[0], coef[1], coef[2]
    scale = OMEGA / (2.0 * (ax + ay + az) + coef[3])
    ka[...] = ax * scale
    kb[...] = ay * scale
    az = az * scale
    lane = lax.broadcasted_iota(jnp.int32, az.shape, 2)
    km[...] = jnp.where(lane == 0, 0.0, az)
    kp[...] = jnp.where(lane == ROWS - 1, 0.0, az)
    keep = (
        (i > 0).astype(F32),
        (i < GX - 1).astype(F32),
        (j > 0).astype(F32),
        (j < GY - 1).astype(F32),
    )

    def copies(s, c):
        out = []
        for d in range(4):
            src, dst = (fxs, fxr) if d < 2 else (fys, fyr)
            out.append(
                remote(
                    src.at[s, c, d % 2], dst.at[s, c, 1 - d % 2],
                    send_sem.at[s, c, d], recv_sem.at[s, c, d], peers[d],
                )
            )
        return out

    def send_faces(s, c, w):
        for side in range(2):
            x = side * (NX - 1)
            fxs[s, c, side] = w[c, pl.ds(site_row(x, 0), NY * KV)].astype(BF16)
            y = side * (NY - 1)
            for x in range(NX):
                fys[s, c, side, pl.ds(x * KV, KV)] = w[c, pl.ds(site_row(x, y), KV)].astype(BF16)
        for copy in copies(s, c):
            copy.start()

    def fill_halo(s, c, w):
        for copy in copies(s, c):
            copy.wait_recv()
        for side in range(2):
            x = -1 if side == 0 else NX
            w[c, pl.ds(site_row(x, 0), NY * KV)] = fxr[s, c, side].astype(F32) * keep[side]
            y = -1 if side == 0 else NY
            for x in range(NX):
                w[c, pl.ds(site_row(x, y), KV)] = (
                    fyr[s, c, side, pl.ds(x * KV, KV)].astype(F32) * keep[2 + side]
                )

    def sweep(c, src, dst, last):
        def plane(x, carry):
            base = pl.multiple_of(x * XROW, 16)

            def cell(dx, y):
                return src[c, pl.ds(base + site_row(dx, y), KV)]

            below, here = cell(0, -1), cell(0, 0)
            for y in range(NY):
                above = cell(0, y + 1)
                row = slice(y, y + 1)
                new = (
                    ka[x, row] * (cell(-1, y) + cell(1, y))
                    + kb[x, row] * (below + above)
                    + km[x, row] * pltpu.roll(here, 1, 1)
                    + kp[x, row] * pltpu.roll(here, ROWS - 1, 1)
                    + (1.0 - OMEGA) * here
                )
                dst[c, pl.ds(base + site_row(0, y), KV)] = new
                if last:
                    blk[c, x * NY + y] = new.astype(BF16)
                below, here = here, above
            return carry

        lax.fori_loop(0, NX, plane, 0)

    def want_copies():
        out = []
        for n, axis in enumerate(AXES):
            for d in range(LINE):
                for e in range(CORES):
                    if d or e:
                        out.append(
                            remote(
                                want, wants.at[n, at[axis] * CORES + core],
                                want_send.at[n, d, e], want_recv.at[n, d, e], device(axis, d, e),
                            )
                        )
        return out

    def rank_copies(c, step):
        a, u, v = ROUTES[c]
        out = []
        for d in range(1, LINE):
            if step == 0:
                ref, peer = ranks.at[c, at[v], at[u]], device(u, d, 0)
            else:
                ref, peer = ranks.at[c, at[v]], device(v, d, 0)
            out.append(
                remote(ref, ref, rank_send.at[c, step, d], rank_recv.at[c, step, d], peer)
            )
        return out

    def cast_copies(c, step):
        a, u, v = ROUTES[c]
        axis = v if step else u

        def part(back, half):
            pos = lax.rem(at[axis] + LINE - back, LINE)
            if step:
                return pg[c].at[pos, pl.ds(half * (LINE // 2), LINE // 2)]
            return pg[c].at[at[v], pos, pl.ds(half * (COARSE // 2), COARSE // 2)]

        plan = ((0, 0, 1), (0, 1, 3), (0, 1, 1), (0, 0, 3), (1, 0, 1), (3, 1, 3))
        return [
            remote(
                part(back, half), part(back, half),
                cast_send.at[c, step, n], cast_recv.at[c, step, n], device(axis, d, 0),
            )
            for n, (back, half, d) in enumerate(plan)
        ]

    def answer(c, d, e):
        a = ROUTES[c][0]
        slot = lax.rem(at[a] + d, LINE) * CORES + lax.rem(core + e, CORES)
        here = at[a] * CORES + core
        if d == 0 and e == 0:
            return pltpu.make_async_copy(sb.at[c, slot], rb.at[c, here], own_sem.at[c])
        dst, peer = rb.at[c, here], device(a, d, e)
        if d == 2:
            dst, peer = fb.at[c, e], device(a, 1 + 2 * e, 0)
        return remote(sb.at[c, slot], dst, ans_send.at[c, d, e], ans_recv.at[c, d, e], peer)

    def forward(c, e):
        a = ROUTES[c][0]
        origin = lax.rem(at[a] + 3 - 2 * e, LINE) * CORES + core
        return remote(
            fb.at[c, e], rb.at[c, origin], fwd_send.at[c, e], fwd_recv.at[c, e],
            device(a, 1 + 2 * e, e),
        )

    order = [(d, e) for d in (2, 1, 3, 0) for e in range(CORES)]

    def spread(c):
        a, u, v = ROUTES[c]
        for r in range(COARSE):
            pg[c][at[v], at[u], r] = blk[c, id_s[r, 0] & (SITES - 1)]
        for copy in cast_copies(c, 0)[:4]:
            copy.start()

    def pass_on(c, step):
        all_copies = cast_copies(c, step)
        for n in range(2):
            all_copies[n].wait_recv()
            all_copies[4 + n].start()

    def gathered(c, step):
        for copy in cast_copies(c, step)[2:]:
            copy.wait_recv()

    def spread_more(c):
        gathered(c, 0)
        for copy in cast_copies(c, 1)[:4]:
            copy.start()

    def reply(c):
        a, u, v = ROUTES[c]
        n = AXES.index(a)
        gathered(c, 1)
        for d, e in order:
            slot = lax.rem(at[a] + d, LINE) * CORES + lax.rem(core + e, CORES)
            for vv in range(LINE):
                for uu in range(LINE):
                    whose = {a: at[a], u: uu, v: vv}
                    owner = whose["x"] * 32 + whose["z"] * 8 + whose["y"] * 2 + core
                    for p in range(2):
                        block = want_s[n, slot, p, owner] & (SITES - 1)
                        rank = rank_s[c, vv, uu, 0, block] & (COARSE - 1)
                        sb[c, slot, (vv * LINE + uu) * 2 + p] = pg[c][vv, uu, rank]
            answer(c, d, e).start()

    def reply_on(c):
        for e in range(2):
            answer(c, 2, e).wait_recv()
            forward(c, e).start()

    def transpose_in(c):
        loads[c].wait()
        for x in range(NX):
            for half in range(NY // 8):
                for k in range(KV):
                    wa[c, pl.ds(site_row(x, half * 8) + k, 8, stride=KV), :] = stage[
                        c * KV + k, x, pl.ds(half * 8, 8), :
                    ]

    stores = []

    def transpose_out(c, w):
        for x in range(NX):
            for half in range(NY // 8):
                for k in range(KV):
                    stage[c * KV + k, x, pl.ds(half * 8, 8), :] = w[
                        c, pl.ds(site_row(x, half * 8) + k, 8, stride=KV), :
                    ]
        part = pl.ds(c * KV, KV)
        store = pltpu.make_async_copy(stage.at[part], sm_out.at[part], out_sem.at[c])
        store.start()
        stores.append(store)

    transpose_in(0)
    pl.semaphore_wait(barrier, greeted)
    send_faces(0, 0, wa)
    for c in range(1, CHUNKS):
        transpose_in(c)
        send_faces(0, c, wa)

    wanted, targets, rank, ids = lists_of(meta[...])
    idv[...] = ids
    id_copy = pltpu.make_async_copy(idv, id_s, smem_sem.at[0])
    id_copy.start()
    for p in range(2):
        want[p : p + 1] = wanted[p]
        for n, axis in enumerate(AXES):
            wants[n, at[axis] * CORES + core, p : p + 1] = wanted[p]
    tgt[...] = jnp.zeros_like(tgt)
    for c in range(CHUNKS):
        a, u, v = ROUTES[c]
        ranks[c, at[v], at[u]] = rank
        for h in range(2):
            tgt[2 * c + h : 2 * c + h + 1] = targets[c][h]
        for copy in rank_copies(c, 0):
            copy.start()
    for copy in want_copies():
        copy.start()

    for c in range(CHUNKS):
        fill_halo(0, c, wa)
        sweep(c, wa, wb, False)
        send_faces(1, c, wb)
    for c in range(CHUNKS):
        for copy in rank_copies(c, 0):
            copy.wait_recv()
        for copy in rank_copies(c, 1):
            copy.start()
    for c in range(CHUNKS):
        fill_halo(1, c, wb)
        sweep(c, wb, wa, False)
        send_faces(2, c, wa)
    for copy in want_copies():
        copy.wait_recv()
    want_copy = pltpu.make_async_copy(wants, want_s, smem_sem.at[1])
    want_copy.start()
    for c in range(CHUNKS):
        for copy in rank_copies(c, 1):
            copy.wait_recv()
    rank_copy = pltpu.make_async_copy(ranks, rank_s, smem_sem.at[2])
    rank_copy.start()
    id_copy.wait()
    for c in range(CHUNKS):
        fill_halo(2, c, wa)
        sweep(c, wa, wb, True)
        spread(c)
        if c > 0:
            pass_on(c - 1, 0)
        if c > 1:
            spread_more(c - 2)
    want_copy.wait()
    rank_copy.wait()
    pass_on(2, 0)
    spread_more(1)
    transpose_out(0, wb)
    pass_on(0, 1)
    spread_more(2)
    transpose_out(1, wb)
    pass_on(1, 1)
    reply(0)
    pass_on(2, 1)
    reply(1)
    reply_on(0)
    reply(2)
    reply_on(1)
    transpose_out(2, wb)
    reply_on(2)

    for s in range(SWEEPS):
        for c in range(CHUNKS):
            for copy in copies(s, c):
                copy.wait_send()
    for copy in want_copies():
        copy.wait_send()
    for c in range(CHUNKS):
        for step in range(2):
            for copy in rank_copies(c, step) + cast_copies(c, step):
                copy.wait_send()
        for d, e in order:
            copy = answer(c, d, e)
            if d or e:
                copy.wait_send()
                if d != 2:
                    copy.wait_recv()
            else:
                copy.wait()
        for e in range(2):
            forward(c, e).wait_send()
            forward(c, e).wait_recv()
    for store in stores:
        store.wait()


def smooth(test_vectors, coef_x, coef_y, coef_z, shift, meta):
    vmem = pl.BlockSpec(memory_space=pltpu.VMEM)
    anywhere = pl.BlockSpec(memory_space=pl.ANY)
    cells = pltpu.VMEM((NX, NY, ROWS), F32)
    plane = pltpu.VMEM((LINE, LINE, COARSE, KV, ROWS), BF16)
    dma = pltpu.SemaphoreType.DMA
    return pl.pallas_call(
        smooth_kernel,
        out_shape=(
            jax.ShapeDtypeStruct((VECS, NX, NY, ROWS), F32),
            jax.ShapeDtypeStruct((CHUNKS, SITES, KV, ROWS), BF16),
            jax.ShapeDtypeStruct((CHUNKS, LINE * CORES, 2 * PLANE, KV, ROWS), BF16),
            jax.ShapeDtypeStruct((8, ROWS), jnp.int32),
        ),
        in_specs=[anywhere] * 5 + [vmem],
        out_specs=(anywhere, vmem, anywhere, vmem),
        scratch_shapes=[
            pltpu.VMEM((VECS, NX, NY, ROWS), F32),
            pltpu.VMEM((4, NX, NY, ROWS), F32),
            pltpu.VMEM((CHUNKS, EXT, ROWS), F32),
            pltpu.VMEM((CHUNKS, EXT, ROWS), F32),
            cells, cells, cells, cells,
            pltpu.VMEM((SWEEPS, CHUNKS, 2, NY * KV, ROWS), BF16),
            pltpu.VMEM((SWEEPS, CHUNKS, 2, NY * KV, ROWS), BF16),
            pltpu.VMEM((SWEEPS, CHUNKS, 2, NX * KV, ROWS), BF16),
            pltpu.VMEM((SWEEPS, CHUNKS, 2, NX * KV, ROWS), BF16),
            pltpu.VMEM((2, ROWS), jnp.int32),
            pltpu.VMEM((len(AXES), LINE * CORES, 2, ROWS), jnp.int32),
            pltpu.VMEM((CHUNKS, LINE, LINE, 1, ROWS), jnp.int32),
            pltpu.VMEM((COARSE, ROWS), jnp.int32),
            pltpu.SMEM((len(AXES), LINE * CORES, 2, ROWS), jnp.int32),
            pltpu.SMEM((CHUNKS, LINE, LINE, 1, ROWS), jnp.int32),
            pltpu.SMEM((COARSE, ROWS), jnp.int32),
            plane, plane, plane,
            pltpu.VMEM((CHUNKS, LINE * CORES, 2 * PLANE, KV, ROWS), BF16),
            pltpu.VMEM((CHUNKS, CORES, 2 * PLANE, KV, ROWS), BF16),
            dma((CHUNKS,)),
            dma((4,)),
            dma((CHUNKS,)),
            dma((SWEEPS, CHUNKS, 4)),
            dma((SWEEPS, CHUNKS, 4)),
            dma((len(AXES), LINE, CORES)),
            dma((len(AXES), LINE, CORES)),
            dma((CHUNKS, 2, LINE)),
            dma((CHUNKS, 2, LINE)),
            dma((CHUNKS, 2, 6)),
            dma((CHUNKS, 2, 6)),
            dma((CHUNKS, LINE, CORES)),
            dma((CHUNKS, LINE, CORES)),
            dma((CHUNKS, CORES)),
            dma((CHUNKS, CORES)),
            dma((CHUNKS,)),
            dma((3,)),
        ],
        compiler_params=pltpu.CompilerParams(
            collective_id=0, has_side_effects=True, vmem_limit_bytes=60 * 1024 * 1024
        ),
        name="smooth",
    )(test_vectors, coef_x, coef_y, coef_z, shift, meta)


def solve_rows(gram, rhs):
    low = [[None] * SLOTS for _ in range(SLOTS)]
    inv = []
    for r in range(SLOTS):
        scaled = []
        diag = gram[r, r]
        for c in range(r):
            rest = gram[r, c]
            for m in range(c):
                rest = rest - scaled[m] * low[c][m]
            scaled.append(rest)
            low[r][c] = rest * inv[c]
            diag = diag - rest * low[r][c]
        inv.append(1.0 / diag)
    fwd = []
    for r in range(SLOTS):
        rest = rhs[r]
        for m in range(r):
            rest = rest - low[r][m] * fwd[m]
        fwd.append(rest)
    out = [None] * SLOTS
    for r in reversed(range(SLOTS)):
        rest = fwd[r] * inv[r]
        for m in range(r + 1, SLOTS):
            rest = rest - low[m][r] * out[m]
        out[r] = rest
    return out


PAIRS = [(s, t) for s in range(SLOTS) for t in range(s + 1)] + [
    (s, SLOTS) for s in range(SLOTS)
]


def weights_kernel(target, replies, blk, sm_in, w_out, sm_out, sums, copy_sem):
    move = pltpu.make_async_copy(sm_in, sm_out, copy_sem)
    move.start()

    def block(b, carry):
        accs = [None] * len(PAIRS)
        for c in range(CHUNKS):
            values = []
            for s in range(SLOTS):
                at = target[2 * c + b // 32, lax.rem(b, 32) * SLOTS + s]
                found = replies[c, jnp.maximum(at, 0)].astype(F32)
                values.append(jnp.where(at >= 0, found, 0.0))
            values.append(blk[c, b].astype(F32))
            for n, (s, t) in enumerate(PAIRS):
                prod = values[s] * values[t]
                part = prod[0:8] + prod[8:16]
                accs[n] = part if c == 0 else accs[n] + part
        for n, acc in enumerate(accs):
            sums[n, pl.ds(pl.multiple_of(b * 8, 8), 8), :] = acc
        return carry

    lax.fori_loop(0, SITES, block, 0)
    for g in range(SITES // 8):
        total = {}
        for n, pair in enumerate(PAIRS):
            acc = sums[n, pl.ds(g * 64, 8, stride=8), :]
            for h in range(1, 8):
                acc = acc + sums[n, pl.ds(g * 64 + h, 8, stride=8), :]
            acc = acc * (1.0 / VECS)
            if pair[0] == pair[1]:
                acc = acc + RIDGE
            total[pair] = acc
        out = solve_rows(total, [total[s, SLOTS] for s in range(SLOTS)])
        for s in range(SLOTS):
            w_out[s, g // 2, pl.ds((g % 2) * 8, 8), :] = out[s]
    move.wait()


def fit(target, replies, blk, sm):
    vmem = pl.BlockSpec(memory_space=pltpu.VMEM)
    anywhere = pl.BlockSpec(memory_space=pl.ANY)
    return pl.pallas_call(
        weights_kernel,
        out_shape=(
            jax.ShapeDtypeStruct((SLOTS, NX, NY, ROWS), F32),
            jax.ShapeDtypeStruct((VECS, NX, NY, ROWS), F32),
        ),
        in_specs=[pl.BlockSpec(memory_space=pltpu.SMEM), vmem, vmem, anywhere],
        out_specs=(vmem, anywhere),
        scratch_shapes=[
            pltpu.VMEM((len(PAIRS), SITES * 8, ROWS), F32),
            pltpu.SemaphoreType.DMA,
        ],
        compiler_params=pltpu.CompilerParams(vmem_limit_bytes=48 * 1024 * 1024),
        name="fit",
    )(target, replies, blk, sm)


def per_device(
    test_vectors, coef_x, coef_y, coef_z, shift, cf_split, nbr_count, nbr_owner, nbr_block
):
    entries = SITES * SLOTS
    live = (cf_split == 0)[..., None] & (jnp.arange(SLOTS) < nbr_count[..., None])
    listed = jnp.where(live, nbr_owner * SITES + nbr_block, -1).reshape(entries // ROWS, ROWS)
    coarse = jnp.pad(cf_split.reshape(1, SITES), ((0, 5), (0, ROWS - SITES)))
    meta = jnp.concatenate([listed, coarse], axis=0)
    sm, blk, replies, target = smooth(test_vectors, coef_x, coef_y, coef_z, shift, meta)
    replies = replies.reshape(CHUNKS, LINE * CORES * 2 * PLANE, KV, ROWS)
    weights, smoothed = fit(target, replies, blk, sm)
    return (smoothed, weights)


def solution(mesh):
    cells = P("gx", "gy", None)
    lists = P("gx", "gy", None, None)
    vectors = P(None, "gx", "gy", None)
    return jax.shard_map(
        per_device,
        mesh=mesh,
        in_specs=(vectors, cells, cells, cells, cells, cells, cells, lists, lists),
        out_specs=(vectors, vectors),
        check_vma=False,
    )
```

```python
import jax
import jax.numpy as jnp
from jax import lax
from jax.experimental import pallas as pl
from jax.experimental.pallas import tpu as pltpu
from jax.sharding import PartitionSpec as P

SLOTS = 4
SWEEPS = 3
ROWS = 128
OMEGA = 0.8
RIDGE = 0.05
VECS = 48
CHUNKS = 3
KV = VECS // CHUNKS
NX = 4
NY = 16
SITES = NX * NY
XROW = (NY + 2) * KV
EXT = (NX + 2) * XROW
GX = 16
GY = 8
MESH = pl.DeviceIdType.MESH
F32 = jnp.float32
BF16 = jnp.bfloat16


def site_row(x, y):
    return (x + 1) * XROW + (y + 1) * KV


AXES = "xyz"
LINE = 4
CORES = 2
COARSE = 16
PLANE = LINE * LINE
ROUTES = (("x", "z", "y"), ("y", "x", "z"), ("z", "y", "x"))


def lists_of(meta):
    lane = lax.broadcasted_iota(jnp.int32, (ROWS, ROWS), 1)
    sub = lax.broadcasted_iota(jnp.int32, (ROWS, ROWS), 0)
    diag = lane == sub
    none = 1 << 20

    def column(row):
        return jnp.sum(jnp.where(diag, row, 0), axis=1, keepdims=True)

    def line(col):
        return jnp.sum(jnp.where(diag, col, 0), axis=0, keepdims=True)

    members, keys, owners = [], [], []
    for h in range(2):
        entry = meta[h : h + 1]
        owner = entry >> 6
        key = (lane[:1] + h * ROWS) * SITES + (entry & (SITES - 1))
        owners.append(owner)
        keys.append(key)
        members.append(owner == sub)
    first = jnp.minimum(*[jnp.where(m, k, none) for m, k in zip(members, keys)])
    first = jnp.min(first, axis=1, keepdims=True)
    first = jnp.where(first >= none, 0, first)
    second = jnp.maximum(*[jnp.where(m, k, 0) for m, k in zip(members, keys)])
    second = jnp.max(second, axis=1, keepdims=True)
    wanted = [line(v) & (SITES - 1) for v in (first, second)]
    targets = [[] for _ in ROUTES]
    for h in range(2):
        own = owners[h]
        at_first = jnp.sum(jnp.where(members[h], first, 0), axis=0, keepdims=True)
        place = jnp.where(keys[h] == at_first, 0, 1)
        at = {"x": (own >> 5) & 3, "z": (own >> 3) & 3, "y": (own >> 1) & 3}
        for c, (a, u, v) in enumerate(ROUTES):
            slot = ((at[a] * CORES + (own & 1)) * PLANE + at[v] * LINE + at[u]) * 2 + place
            targets[c].append(jnp.where(own < 0, -1, slot))
    coarse = meta[2:3]
    rank = jnp.sum(jnp.where(sub < lane, column(coarse), 0), axis=0, keepdims=True)
    hit = (rank == sub[:COARSE]) & (coarse > 0)
    ids = jnp.sum(jnp.where(hit, lane[:COARSE], 0), axis=1, keepdims=True)
    ids = jnp.broadcast_to(ids, (COARSE, ROWS))
    rank = jnp.minimum(rank, COARSE - 1)
    return wanted, targets, rank, ids


def smooth_kernel(
    tv, cx, cy, cz, sh, meta, sm_out, blk, rb, tgt,
    stage, coef, wa, wb, ka, kb, km, kp, fxs, fxr, fys, fyr,
    want, wants, ranks, idv, want_s, rank_s, id_s, pg0, pg1, pg2, sb, fb,
    in_sem, coef_sem, out_sem, send_sem, recv_sem, want_send, want_recv, rank_send, rank_recv,
    cast_send, cast_recv, ans_send, ans_recv, fwd_send, fwd_recv, own_sem, smem_sem,
):
    pg = (pg0, pg1, pg2)
    i = lax.axis_index("gx")
    j = lax.axis_index("gy")
    core = lax.rem(j, CORES)
    at = {"x": i // LINE, "z": lax.rem(i, LINE), "y": j // CORES}
    peers = (
        (lax.rem(i + GX - 1, GX), j),
        (lax.rem(i + 1, GX), j),
        (i, lax.rem(j + GY - 1, GY)),
        (i, lax.rem(j + 1, GY)),
    )

    def device(axis, d, e):
        moved = dict(at)
        moved[axis] = lax.rem(at[axis] + d, LINE)
        return (moved["x"] * LINE + moved["z"], moved["y"] * CORES + lax.rem(core + e, CORES))

    def remote(src, dst, send, recv, peer):
        return pltpu.make_async_remote_copy(
            src_ref=src, dst_ref=dst, send_sem=send, recv_sem=recv,
            device_id=peer, device_id_type=MESH,
        )

    loads = []
    for n, part in enumerate((cx, cy, cz, sh)):
        load = pltpu.make_async_copy(part, coef.at[n], coef_sem.at[n])
        load.start()
        loads.append(load)
    coef_loads, loads = loads, []
    for c in range(CHUNKS):
        part = pl.ds(c * KV, KV)
        load = pltpu.make_async_copy(tv.at[part], stage.at[part], in_sem.at[c])
        load.start()
        loads.append(load)
    barrier = pltpu.get_barrier_semaphore()
    for peer in peers[:2]:
        pl.semaphore_signal(barrier, inc=1, device_id=peer, device_id_type=MESH)
    pl.semaphore_signal(barrier, inc=1, device_id=device("x", 0, 1), device_id_type=MESH)
    for axis in AXES:
        for d in range(1, LINE):
            for e in range(CORES):
                pl.semaphore_signal(
                    barrier, inc=1, device_id=device(axis, d, e), device_id_type=MESH
                )
    greeted = 3 + len(AXES) * (LINE - 1) * CORES

    for load in coef_loads:
        load.wait()
    ax, ay, az = coef[0], coef[1], coef[2]
    scale = OMEGA / (2.0 * (ax + ay + az) + coef[3])
    ka[...] = ax * scale
    kb[...] = ay * scale
    az = az * scale
    lane = lax.broadcasted_iota(jnp.int32, az.shape, 2)
    km[...] = jnp.where(lane == 0, 0.0, az)
    kp[...] = jnp.where(lane == ROWS - 1, 0.0, az)
    keep = (
        (i > 0).astype(F32),
        (i < GX - 1).astype(F32),
        (j > 0).astype(F32),
        (j < GY - 1).astype(F32),
    )

    def copies(s, c):
        out = []
        for d in range(4):
            src, dst = (fxs, fxr) if d < 2 else (fys, fyr)
            out.append(
                remote(
                    src.at[s, c, d % 2], dst.at[s, c, 1 - d % 2],
                    send_sem.at[s, c, d], recv_sem.at[s, c, d], peers[d],
                )
            )
        return out

    def send_faces(s, c, w):
        for side in range(2):
            x = side * (NX - 1)
            fxs[s, c, side] = w[c, pl.ds(site_row(x, 0), NY * KV)].astype(BF16)
            y = side * (NY - 1)
            for x in range(NX):
                fys[s, c, side, pl.ds(x * KV, KV)] = w[c, pl.ds(site_row(x, y), KV)].astype(BF16)
        for copy in copies(s, c):
            copy.start()

    def fill_halo(s, c, w):
        for copy in copies(s, c):
            copy.wait_recv()
        for side in range(2):
            x = -1 if side == 0 else NX
            w[c, pl.ds(site_row(x, 0), NY * KV)] = fxr[s, c, side].astype(F32) * keep[side]
            y = -1 if side == 0 else NY
            for x in range(NX):
                w[c, pl.ds(site_row(x, y), KV)] = (
                    fyr[s, c, side, pl.ds(x * KV, KV)].astype(F32) * keep[2 + side]
                )

    def sweep(c, src, dst, last):
        def plane(x, carry):
            base = pl.multiple_of(x * XROW, 16)

            def cell(dx, y):
                return src[c, pl.ds(base + site_row(dx, y), KV)]

            below, here = cell(0, -1), cell(0, 0)
            for y in range(NY):
                above = cell(0, y + 1)
                row = slice(y, y + 1)
                new = (
                    ka[x, row] * (cell(-1, y) + cell(1, y))
                    + kb[x, row] * (below + above)
                    + km[x, row] * pltpu.roll(here, 1, 1)
                    + kp[x, row] * pltpu.roll(here, ROWS - 1, 1)
                    + (1.0 - OMEGA) * here
                )
                dst[c, pl.ds(base + site_row(0, y), KV)] = new
                if last:
                    blk[c, x * NY + y] = new.astype(BF16)
                below, here = here, above
            return carry

        lax.fori_loop(0, NX, plane, 0)

    def want_copies():
        out = []
        for n, axis in enumerate(AXES):
            for d in range(LINE):
                for e in range(CORES):
                    if d or e:
                        out.append(
                            remote(
                                want, wants.at[n, at[axis] * CORES + core],
                                want_send.at[n, d, e], want_recv.at[n, d, e], device(axis, d, e),
                            )
                        )
        return out

    def rank_copies(c, step):
        a, u, v = ROUTES[c]
        out = []
        for d in range(1, LINE):
            if step == 0:
                ref, peer = ranks.at[c, at[v], at[u]], device(u, d, 0)
            else:
                ref, peer = ranks.at[c, at[v]], device(v, d, 0)
            out.append(
                remote(ref, ref, rank_send.at[c, step, d], rank_recv.at[c, step, d], peer)
            )
        return out

    def cast_copies(c, step):
        a, u, v = ROUTES[c]
        axis = v if step else u

        def part(back, half):
            pos = lax.rem(at[axis] + LINE - back, LINE)
            if step:
                return pg[c].at[pos, pl.ds(half * (LINE // 2), LINE // 2)]
            return pg[c].at[at[v], pos, pl.ds(half * (COARSE // 2), COARSE // 2)]

        plan = ((0, 0, 1), (0, 1, 3), (0, 1, 1), (0, 0, 3), (1, 0, 1), (3, 1, 3))
        return [
            remote(
                part(back, half), part(back, half),
                cast_send.at[c, step, n], cast_recv.at[c, step, n], device(axis, d, 0),
            )
            for n, (back, half, d) in enumerate(plan)
        ]

    def answer(c, d, e):
        a = ROUTES[c][0]
        slot = lax.rem(at[a] + d, LINE) * CORES + lax.rem(core + e, CORES)
        here = at[a] * CORES + core
        if d == 0 and e == 0:
            return pltpu.make_async_copy(sb.at[c, slot], rb.at[c, here], own_sem.at[c])
        dst, peer = rb.at[c, here], device(a, d, e)
        if d == 2:
            dst, peer = fb.at[c, e], device(a, 1 + 2 * e, 0)
        return remote(sb.at[c, slot], dst, ans_send.at[c, d, e], ans_recv.at[c, d, e], peer)

    def forward(c, e):
        a = ROUTES[c][0]
        origin = lax.rem(at[a] + 3 - 2 * e, LINE) * CORES + core
        return remote(
            fb.at[c, e], rb.at[c, origin], fwd_send.at[c, e], fwd_recv.at[c, e],
            device(a, 1 + 2 * e, e),
        )

    order = [(d, e) for d in (2, 1, 3, 0) for e in range(CORES)]

    def spread(c):
        a, u, v = ROUTES[c]
        for r in range(COARSE):
            pg[c][at[v], at[u], r] = blk[c, id_s[r, 0] & (SITES - 1)]
        for copy in cast_copies(c, 0)[:4]:
            copy.start()

    def pass_on(c, step):
        all_copies = cast_copies(c, step)
        for n in range(2):
            all_copies[n].wait_recv()
            all_copies[4 + n].start()

    def gathered(c, step):
        for copy in cast_copies(c, step)[2:]:
            copy.wait_recv()

    def spread_more(c):
        gathered(c, 0)
        for copy in cast_copies(c, 1)[:4]:
            copy.start()

    def reply(c):
        a, u, v = ROUTES[c]
        n = AXES.index(a)
        gathered(c, 1)
        for d, e in order:
            slot = lax.rem(at[a] + d, LINE) * CORES + lax.rem(core + e, CORES)
            for vv in range(LINE):
                for uu in range(LINE):
                    whose = {a: at[a], u: uu, v: vv}
                    owner = whose["x"] * 32 + whose["z"] * 8 + whose["y"] * 2 + core
                    for p in range(2):
                        block = want_s[n, slot, p, owner] & (SITES - 1)
                        rank = rank_s[c, vv, uu, 0, block] & (COARSE - 1)
                        sb[c, slot, (vv * LINE + uu) * 2 + p] = pg[c][vv, uu, rank]
            answer(c, d, e).start()

    def reply_on(c):
        for e in range(2):
            answer(c, 2, e).wait_recv()
            forward(c, e).start()

    def transpose_in(c):
        loads[c].wait()
        for x in range(NX):
            for half in range(NY // 8):
                for k in range(KV):
                    wa[c, pl.ds(site_row(x, half * 8) + k, 8, stride=KV), :] = stage[
                        c * KV + k, x, pl.ds(half * 8, 8), :
                    ]

    stores = []

    def transpose_out(c, w):
        for x in range(NX):
            for half in range(NY // 8):
                for k in range(KV):
                    stage[c * KV + k, x, pl.ds(half * 8, 8), :] = w[
                        c, pl.ds(site_row(x, half * 8) + k, 8, stride=KV), :
                    ]
        part = pl.ds(c * KV, KV)
        store = pltpu.make_async_copy(stage.at[part], sm_out.at[part], out_sem.at[c])
        store.start()
        stores.append(store)

    transpose_in(0)
    pl.semaphore_wait(barrier, greeted)
    send_faces(0, 0, wa)
    for c in range(1, CHUNKS):
        transpose_in(c)
        send_faces(0, c, wa)

    wanted, targets, rank, ids = lists_of(meta[...])
    idv[...] = ids
    id_copy = pltpu.make_async_copy(idv, id_s, smem_sem.at[0])
    id_copy.start()
    for p in range(2):
        want[p : p + 1] = wanted[p]
        for n, axis in enumerate(AXES):
            wants[n, at[axis] * CORES + core, p : p + 1] = wanted[p]
    tgt[...] = jnp.zeros_like(tgt)
    for c in range(CHUNKS):
        a, u, v = ROUTES[c]
        ranks[c, at[v], at[u]] = rank
        for h in range(2):
            tgt[2 * c + h : 2 * c + h + 1] = targets[c][h]
        for copy in rank_copies(c, 0):
            copy.start()
    for copy in want_copies():
        copy.start()

    for c in range(CHUNKS):
        fill_halo(0, c, wa)
        sweep(c, wa, wb, False)
        send_faces(1, c, wb)
    for c in range(CHUNKS):
        for copy in rank_copies(c, 0):
            copy.wait_recv()
        for copy in rank_copies(c, 1):
            copy.start()
    for c in range(CHUNKS):
        fill_halo(1, c, wb)
        sweep(c, wb, wa, False)
        send_faces(2, c, wa)
    for copy in want_copies():
        copy.wait_recv()
    want_copy = pltpu.make_async_copy(wants, want_s, smem_sem.at[1])
    want_copy.start()
    for c in range(CHUNKS):
        for copy in rank_copies(c, 1):
            copy.wait_recv()
    rank_copy = pltpu.make_async_copy(ranks, rank_s, smem_sem.at[2])
    rank_copy.start()
    id_copy.wait()
    for c in range(CHUNKS):
        fill_halo(2, c, wa)
        sweep(c, wa, wb, True)
        spread(c)
        if c > 0:
            pass_on(c - 1, 0)
        if c > 1:
            spread_more(c - 2)
    want_copy.wait()
    rank_copy.wait()
    pass_on(2, 0)
    spread_more(1)
    transpose_out(0, wb)
    pass_on(0, 1)
    spread_more(2)
    transpose_out(1, wb)
    pass_on(1, 1)
    reply(0)
    pass_on(2, 1)
    reply(1)
    reply_on(0)
    reply(2)
    reply_on(1)
    transpose_out(2, wb)
    reply_on(2)

    for s in range(SWEEPS):
        for c in range(CHUNKS):
            for copy in copies(s, c):
                copy.wait_send()
    for copy in want_copies():
        copy.wait_send()
    for c in range(CHUNKS):
        for step in range(2):
            for copy in rank_copies(c, step) + cast_copies(c, step):
                copy.wait_send()
        for d, e in order:
            copy = answer(c, d, e)
            if d or e:
                copy.wait_send()
                if d != 2:
                    copy.wait_recv()
            else:
                copy.wait()
        for e in range(2):
            forward(c, e).wait_send()
            forward(c, e).wait_recv()
    for store in stores:
        store.wait()


def smooth(test_vectors, coef_x, coef_y, coef_z, shift, meta):
    vmem = pl.BlockSpec(memory_space=pltpu.VMEM)
    anywhere = pl.BlockSpec(memory_space=pl.ANY)
    cells = pltpu.VMEM((NX, NY, ROWS), F32)
    plane = pltpu.VMEM((LINE, LINE, COARSE, KV, ROWS), BF16)
    dma = pltpu.SemaphoreType.DMA
    return pl.pallas_call(
        smooth_kernel,
        out_shape=(
            jax.ShapeDtypeStruct((VECS, NX, NY, ROWS), F32),
            jax.ShapeDtypeStruct((CHUNKS, SITES, KV, ROWS), BF16),
            jax.ShapeDtypeStruct((CHUNKS, LINE * CORES, 2 * PLANE, KV, ROWS), BF16),
            jax.ShapeDtypeStruct((8, ROWS), jnp.int32),
        ),
        in_specs=[anywhere] * 5 + [vmem],
        out_specs=(anywhere, vmem, anywhere, vmem),
        scratch_shapes=[
            pltpu.VMEM((VECS, NX, NY, ROWS), F32),
            pltpu.VMEM((4, NX, NY, ROWS), F32),
            pltpu.VMEM((CHUNKS, EXT, ROWS), F32),
            pltpu.VMEM((CHUNKS, EXT, ROWS), F32),
            cells, cells, cells, cells,
            pltpu.VMEM((SWEEPS, CHUNKS, 2, NY * KV, ROWS), BF16),
            pltpu.VMEM((SWEEPS, CHUNKS, 2, NY * KV, ROWS), BF16),
            pltpu.VMEM((SWEEPS, CHUNKS, 2, NX * KV, ROWS), BF16),
            pltpu.VMEM((SWEEPS, CHUNKS, 2, NX * KV, ROWS), BF16),
            pltpu.VMEM((2, ROWS), jnp.int32),
            pltpu.VMEM((len(AXES), LINE * CORES, 2, ROWS), jnp.int32),
            pltpu.VMEM((CHUNKS, LINE, LINE, 1, ROWS), jnp.int32),
            pltpu.VMEM((COARSE, ROWS), jnp.int32),
            pltpu.SMEM((len(AXES), LINE * CORES, 2, ROWS), jnp.int32),
            pltpu.SMEM((CHUNKS, LINE, LINE, 1, ROWS), jnp.int32),
            pltpu.SMEM((COARSE, ROWS), jnp.int32),
            plane, plane, plane,
            pltpu.VMEM((CHUNKS, LINE * CORES, 2 * PLANE, KV, ROWS), BF16),
            pltpu.VMEM((CHUNKS, CORES, 2 * PLANE, KV, ROWS), BF16),
            dma((CHUNKS,)),
            dma((4,)),
            dma((CHUNKS,)),
            dma((SWEEPS, CHUNKS, 4)),
            dma((SWEEPS, CHUNKS, 4)),
            dma((len(AXES), LINE, CORES)),
            dma((len(AXES), LINE, CORES)),
            dma((CHUNKS, 2, LINE)),
            dma((CHUNKS, 2, LINE)),
            dma((CHUNKS, 2, 6)),
            dma((CHUNKS, 2, 6)),
            dma((CHUNKS, LINE, CORES)),
            dma((CHUNKS, LINE, CORES)),
            dma((CHUNKS, CORES)),
            dma((CHUNKS, CORES)),
            dma((CHUNKS,)),
            dma((3,)),
        ],
        compiler_params=pltpu.CompilerParams(
            collective_id=0, has_side_effects=True, vmem_limit_bytes=60 * 1024 * 1024
        ),
        name="smooth",
    )(test_vectors, coef_x, coef_y, coef_z, shift, meta)


def solve_rows(gram, rhs):
    low = [[None] * SLOTS for _ in range(SLOTS)]
    inv = []
    for r in range(SLOTS):
        scaled = []
        diag = gram[r, r]
        for c in range(r):
            rest = gram[r, c]
            for m in range(c):
                rest = rest - scaled[m] * low[c][m]
            scaled.append(rest)
            low[r][c] = rest * inv[c]
            diag = diag - rest * low[r][c]
        inv.append(1.0 / diag)
    fwd = []
    for r in range(SLOTS):
        rest = rhs[r]
        for m in range(r):
            rest = rest - low[r][m] * fwd[m]
        fwd.append(rest)
    out = [None] * SLOTS
    for r in reversed(range(SLOTS)):
        rest = fwd[r] * inv[r]
        for m in range(r + 1, SLOTS):
            rest = rest - low[m][r] * out[m]
        out[r] = rest
    return out


PAIRS = [(s, t) for s in range(SLOTS) for t in range(s + 1)] + [
    (s, SLOTS) for s in range(SLOTS)
]


def weights_kernel(target, replies, blk, sm_in, w_out, sm_out, sums, copy_sem):
    move = pltpu.make_async_copy(sm_in, sm_out, copy_sem)
    move.start()

    def block(b, carry):
        accs = [None] * len(PAIRS)
        for c in range(CHUNKS):
            values = []
            for s in range(SLOTS):
                at = target[2 * c + b // 32, lax.rem(b, 32) * SLOTS + s]
                found = replies[c, jnp.maximum(at, 0)].astype(F32)
                values.append(jnp.where(at >= 0, found, 0.0))
            values.append(blk[c, b].astype(F32))
            for n, (s, t) in enumerate(PAIRS):
                prod = values[s] * values[t]
                part = prod[0:8] + prod[8:16]
                accs[n] = part if c == 0 else accs[n] + part
        for n, acc in enumerate(accs):
            sums[n, pl.ds(pl.multiple_of(b * 8, 8), 8), :] = acc
        return carry

    lax.fori_loop(0, SITES, block, 0)
    for g in range(SITES // 8):
        total = {}
        for n, pair in enumerate(PAIRS):
            acc = sums[n, pl.ds(g * 64, 8, stride=8), :]
            for h in range(1, 8):
                acc = acc + sums[n, pl.ds(g * 64 + h, 8, stride=8), :]
            acc = acc * (1.0 / VECS)
            if pair[0] == pair[1]:
                acc = acc + RIDGE
            total[pair] = acc
        out = solve_rows(total, [total[s, SLOTS] for s in range(SLOTS)])
        for s in range(SLOTS):
            w_out[s, g // 2, pl.ds((g % 2) * 8, 8), :] = out[s]
    move.wait()


def fit(target, replies, blk, sm):
    vmem = pl.BlockSpec(memory_space=pltpu.VMEM)
    anywhere = pl.BlockSpec(memory_space=pl.ANY)
    return pl.pallas_call(
        weights_kernel,
        out_shape=(
            jax.ShapeDtypeStruct((SLOTS, NX, NY, ROWS), F32),
            jax.ShapeDtypeStruct((VECS, NX, NY, ROWS), F32),
        ),
        in_specs=[pl.BlockSpec(memory_space=pltpu.SMEM), vmem, vmem, anywhere],
        out_specs=(vmem, anywhere),
        scratch_shapes=[
            pltpu.VMEM((len(PAIRS), SITES * 8, ROWS), F32),
            pltpu.SemaphoreType.DMA,
        ],
        compiler_params=pltpu.CompilerParams(vmem_limit_bytes=60 * 1024 * 1024),
        name="fit",
    )(target, replies, blk, sm)


def per_device(
    test_vectors, coef_x, coef_y, coef_z, shift, cf_split, nbr_count, nbr_owner, nbr_block
):
    entries = SITES * SLOTS
    live = (cf_split == 0)[..., None] & (jnp.arange(SLOTS) < nbr_count[..., None])
    listed = jnp.where(live, nbr_owner * SITES + nbr_block, -1).reshape(entries // ROWS, ROWS)
    coarse = jnp.pad(cf_split.reshape(1, SITES), ((0, 5), (0, ROWS - SITES)))
    meta = jnp.concatenate([listed, coarse], axis=0)
    sm, blk, replies, target = smooth(test_vectors, coef_x, coef_y, coef_z, shift, meta)
    replies = replies.reshape(CHUNKS, LINE * CORES * 2 * PLANE, KV, ROWS)
    weights, smoothed = fit(target, replies, blk, sm)
    return (smoothed, weights)


def solution(mesh):
    cells = P("gx", "gy", None)
    lists = P("gx", "gy", None, None)
    vectors = P(None, "gx", "gy", None)
    return jax.shard_map(
        per_device,
        mesh=mesh,
        in_specs=(vectors, cells, cells, cells, cells, cells, cells, lists, lists),
        out_specs=(vectors, vectors),
        check_vma=False,
    )
```

```python
import jax
import jax.numpy as jnp
from jax import lax
from jax.experimental import pallas as pl
from jax.experimental.pallas import tpu as pltpu
from jax.sharding import PartitionSpec as P

SLOTS = 4
SWEEPS = 3
ROWS = 128
OMEGA = 0.8
RIDGE = 0.05
VECS = 48
CHUNKS = 3
KV = VECS // CHUNKS
NX = 4
NY = 16
SITES = NX * NY
XROW = (NY + 2) * KV
EXT = (NX + 2) * XROW
GX = 16
GY = 8
MESH = pl.DeviceIdType.MESH
F32 = jnp.float32
BF16 = jnp.bfloat16


def site_row(x, y):
    return (x + 1) * XROW + (y + 1) * KV


AXES = "xyz"
LINE = 4
CORES = 2
COARSE = 16
PLANE = LINE * LINE
ROUTES = (("x", "z", "y"), ("y", "x", "z"), ("z", "y", "x"))
BACKS = (0, 1, 3, 2)
PARTS = ((0, 1), (1, 2), (3, 1))


def lists_of(meta, here):
    lane = lax.broadcasted_iota(jnp.int32, (ROWS, ROWS), 1)
    sub = lax.broadcasted_iota(jnp.int32, (ROWS, ROWS), 0)
    diag = lane == sub
    none = 1 << 20

    def column(row):
        return jnp.sum(jnp.where(diag, row, 0), axis=1, keepdims=True)

    def line(col):
        return jnp.sum(jnp.where(diag, col, 0), axis=0, keepdims=True)

    members, keys, owners = [], [], []
    for h in range(2):
        entry = meta[h : h + 1]
        owner = entry >> 6
        key = (lane[:1] + h * ROWS) * SITES + (entry & (SITES - 1))
        owners.append(owner)
        keys.append(key)
        members.append(owner == sub)
    first = jnp.minimum(*[jnp.where(m, k, none) for m, k in zip(members, keys)])
    first = jnp.min(first, axis=1, keepdims=True)
    first = jnp.where(first >= none, 0, first)
    second = jnp.maximum(*[jnp.where(m, k, 0) for m, k in zip(members, keys)])
    second = jnp.max(second, axis=1, keepdims=True)
    wanted = [line(v) & (SITES - 1) for v in (first, second)]
    targets = [[] for _ in ROUTES]
    for h in range(2):
        own = owners[h]
        at_first = jnp.sum(jnp.where(members[h], first, 0), axis=0, keepdims=True)
        place = jnp.where(keys[h] == at_first, 0, 1)
        at = {"x": (own >> 5) & 3, "z": (own >> 3) & 3, "y": (own >> 1) & 3}
        for c, (a, u, v) in enumerate(ROUTES):
            back = (at[v] - here[v]) & 3
            spot = jnp.where(back == 2, 3, jnp.where(back == 3, 2, back))
            slot = ((at[a] * CORES + (own & 1)) * PLANE + spot * LINE + at[u]) * 2 + place
            targets[c].append(jnp.where(own < 0, -1, slot))
    coarse = meta[2:3]
    rank = jnp.sum(jnp.where(sub < lane, column(coarse), 0), axis=0, keepdims=True)
    hit = (rank == sub[:COARSE]) & (coarse > 0)
    ids = jnp.sum(jnp.where(hit, lane[:COARSE], 0), axis=1, keepdims=True)
    ids = jnp.broadcast_to(ids, (COARSE, ROWS))
    rank = jnp.minimum(rank, COARSE - 1)
    return wanted, targets, rank, ids


def smooth_kernel(
    tv, cx, cy, cz, sh, meta, sm_out, blk, rb, tgt,
    stage, coef, wa, wb, ka, kb, km, kp, fxs, fxr, fys, fyr,
    want, wants, ranks, idv, want_s, rank_s, id_s, p00, p01, p02, p03, p10, p11, p12, p13, p20, p21, p22, p23, sb, fb,
    in_sem, coef_sem, out_sem, send_sem, recv_sem, want_send, want_recv, rank_send, rank_recv,
    near_send, near_recv, cast_send, cast_recv, ans_send, ans_recv, fwd_send, fwd_recv, own_sem, smem_sem,
):
    pg = ((p00, p01, p02, p03), (p10, p11, p12, p13), (p20, p21, p22, p23))
    i = lax.axis_index("gx")
    j = lax.axis_index("gy")
    core = lax.rem(j, CORES)
    at = {"x": i // LINE, "z": lax.rem(i, LINE), "y": j // CORES}
    peers = (
        (lax.rem(i + GX - 1, GX), j),
        (lax.rem(i + 1, GX), j),
        (i, lax.rem(j + GY - 1, GY)),
        (i, lax.rem(j + 1, GY)),
    )

    def device(axis, d, e):
        moved = dict(at)
        moved[axis] = lax.rem(at[axis] + d, LINE)
        return (moved["x"] * LINE + moved["z"], moved["y"] * CORES + lax.rem(core + e, CORES))

    def remote(src, dst, send, recv, peer):
        return pltpu.make_async_remote_copy(
            src_ref=src, dst_ref=dst, send_sem=send, recv_sem=recv,
            device_id=peer, device_id_type=MESH,
        )

    loads = []
    for n, part in enumerate((cx, cy, cz, sh)):
        load = pltpu.make_async_copy(part, coef.at[n], coef_sem.at[n])
        load.start()
        loads.append(load)
    coef_loads, loads = loads, []
    for c in range(CHUNKS):
        part = pl.ds(c * KV, KV)
        load = pltpu.make_async_copy(tv.at[part], stage.at[part], in_sem.at[c])
        load.start()
        loads.append(load)
    barrier = pltpu.get_barrier_semaphore()
    for peer in peers[:2]:
        pl.semaphore_signal(barrier, inc=1, device_id=peer, device_id_type=MESH)
    pl.semaphore_signal(barrier, inc=1, device_id=device("x", 0, 1), device_id_type=MESH)
    for axis in AXES:
        for d in range(1, LINE):
            for e in range(CORES):
                pl.semaphore_signal(
                    barrier, inc=1, device_id=device(axis, d, e), device_id_type=MESH
                )
    greeted = 3 + len(AXES) * (LINE - 1) * CORES

    keep = (
        (i > 0).astype(F32),
        (i < GX - 1).astype(F32),
        (j > 0).astype(F32),
        (j < GY - 1).astype(F32),
    )

    def copies(s, c):
        out = []
        for d in range(4):
            src, dst = (fxs, fxr) if d < 2 else (fys, fyr)
            out.append(
                remote(
                    src.at[s, c, d % 2], dst.at[s, c, 1 - d % 2],
                    send_sem.at[s, c, d], recv_sem.at[s, c, d], peers[d],
                )
            )
        return out

    def send_faces(s, c, w):
        for side in range(2):
            x = side * (NX - 1)
            fxs[s, c, side] = w[c, pl.ds(site_row(x, 0), NY * KV)].astype(BF16)
            y = side * (NY - 1)
            for x in range(NX):
                fys[s, c, side, pl.ds(x * KV, KV)] = w[c, pl.ds(site_row(x, y), KV)].astype(BF16)
        for copy in copies(s, c):
            copy.start()

    def fill_halo(s, c, w):
        for copy in copies(s, c):
            copy.wait_recv()
        for side in range(2):
            x = -1 if side == 0 else NX
            w[c, pl.ds(site_row(x, 0), NY * KV)] = fxr[s, c, side].astype(F32) * keep[side]
            y = -1 if side == 0 else NY
            for x in range(NX):
                w[c, pl.ds(site_row(x, y), KV)] = (
                    fyr[s, c, side, pl.ds(x * KV, KV)].astype(F32) * keep[2 + side]
                )

    def sweep(c, src, dst, last):
        def plane(x, carry):
            base = pl.multiple_of(x * XROW, 16)

            def cell(dx, y):
                return src[c, pl.ds(base + site_row(dx, y), KV)]

            below, here = cell(0, -1), cell(0, 0)
            for y in range(NY):
                above = cell(0, y + 1)
                row = slice(y, y + 1)
                new = (
                    ka[x, row] * (cell(-1, y) + cell(1, y))
                    + kb[x, row] * (below + above)
                    + km[x, row] * pltpu.roll(here, 1, 1)
                    + kp[x, row] * pltpu.roll(here, ROWS - 1, 1)
                    + (1.0 - OMEGA) * here
                )
                dst[c, pl.ds(base + site_row(0, y), KV)] = new
                if last:
                    blk[c, x * NY + y] = new.astype(BF16)
                below, here = here, above
            return carry

        lax.fori_loop(0, NX, plane, 0)

    def want_copies():
        out = []
        for n, axis in enumerate(AXES):
            for d in range(LINE):
                for e in range(CORES):
                    if d or e:
                        out.append(
                            remote(
                                want, wants.at[n, at[axis] * CORES + core],
                                want_send.at[n, d, e], want_recv.at[n, d, e], device(axis, d, e),
                            )
                        )
        return out

    def rank_copies(c, step):
        a, u, v = ROUTES[c]
        out = []
        for d in range(1, LINE):
            if step == 0:
                ref, peer = ranks.at[c, at[v], at[u]], device(u, d, 0)
            else:
                ref, peer = ranks.at[c, at[v]], device(v, d, 0)
            out.append(
                remote(ref, ref, rank_send.at[c, step, d], rank_recv.at[c, step, d], peer)
            )
        return out

    def spread_copies(c):
        a, u, v = ROUTES[c]
        ref = pg[c][0].at[at[u]]
        return [
            remote(ref, ref, near_send.at[c, d], near_recv.at[c, d], device(u, d, 0))
            for d in (2, 1, 3)
        ]

    def cast_copies(c):
        a, u, v = ROUTES[c]
        plan = ((0, 0, 3, 1), (0, 1, 1, 3), (0, 1, 3, 1), (0, 0, 1, 3), (3, 0, 2, 1), (1, 1, 2, 3))
        return [
            remote(
                pg[c][src].at[pl.ds(half * 2, 2)], pg[c][dst].at[pl.ds(half * 2, 2)],
                cast_send.at[c, n], cast_recv.at[c, n], device(v, d, 0),
            )
            for n, (src, half, dst, d) in enumerate(plan)
        ]

    def piece(ref, part):
        first, count = PARTS[part]
        return ref.at[pl.ds(first, count)]

    def answer(c, part, d, e):
        a = ROUTES[c][0]
        slot = lax.rem(at[a] + d, LINE) * CORES + lax.rem(core + e, CORES)
        here = at[a] * CORES + core
        src = piece(sb.at[c, slot], part)
        dst, peer = piece(rb.at[c, here], part), device(a, d, e)
        if d == 0 and e == 0:
            return pltpu.make_async_copy(src, dst, own_sem.at[c, part])
        if d == 2:
            dst, peer = piece(fb.at[c, e], part), device(a, 1 + 2 * e, 0)
        return remote(
            src, dst, ans_send.at[c, part, d, e], ans_recv.at[c, part, d, e], peer
        )

    def forward(c, part, e):
        a = ROUTES[c][0]
        origin = lax.rem(at[a] + 3 - 2 * e, LINE) * CORES + core
        return remote(
            piece(fb.at[c, e], part), piece(rb.at[c, origin], part),
            fwd_send.at[c, part, e], fwd_recv.at[c, part, e], device(a, 1 + 2 * e, e),
        )

    order = [(d, e) for d in (2, 1, 3, 0) for e in range(CORES)]

    def spread(c):
        a, u, v = ROUTES[c]
        for r in range(COARSE):
            pg[c][0][at[u], r] = blk[c, id_s[r, 0] & (SITES - 1)]
        for copy in spread_copies(c):
            copy.start()

    def cast(c):
        for copy in spread_copies(c):
            copy.wait_recv()
        for copy in cast_copies(c)[:4]:
            copy.start()

    def pass_on(c):
        all_copies = cast_copies(c)
        for n in range(2):
            all_copies[n].wait_recv()
            all_copies[4 + n].start()

    def reply(c, part):
        a, u, v = ROUTES[c]
        n = AXES.index(a)
        if part:
            for copy in cast_copies(c)[2:4] if part == 1 else cast_copies(c)[4:]:
                copy.wait_recv()
        first, count = PARTS[part]
        for d, e in order:
            slot = lax.rem(at[a] + d, LINE) * CORES + lax.rem(core + e, CORES)
            for place in range(first, first + count):
                back = BACKS[place]
                vv = lax.rem(at[v] + back, LINE)
                for uu in range(LINE):
                    whose = {a: at[a], u: uu, v: vv}
                    owner = whose["x"] * 32 + whose["z"] * 8 + whose["y"] * 2 + core
                    for p in range(2):
                        block = want_s[n, slot, p, owner] & (SITES - 1)
                        rank = rank_s[c, vv, uu, 0, block] & (COARSE - 1)
                        sb[c, slot, place, uu * 2 + p] = pg[c][back][uu, rank]
            answer(c, part, d, e).start()

    def reply_on(c, part):
        for e in range(2):
            answer(c, part, 2, e).wait_recv()
            forward(c, part, e).start()

    def transpose_in(c):
        loads[c].wait()
        for x in range(NX):
            for half in range(NY // 8):
                for k in range(KV):
                    wa[c, pl.ds(site_row(x, half * 8) + k, 8, stride=KV), :] = stage[
                        c * KV + k, x, pl.ds(half * 8, 8), :
                    ]

    stores = []

    def transpose_out(c, w):
        for x in range(NX):
            for half in range(NY // 8):
                for k in range(KV):
                    stage[c * KV + k, x, pl.ds(half * 8, 8), :] = w[
                        c, pl.ds(site_row(x, half * 8) + k, 8, stride=KV), :
                    ]
        part = pl.ds(c * KV, KV)
        store = pltpu.make_async_copy(stage.at[part], sm_out.at[part], out_sem.at[c])
        store.start()
        stores.append(store)

    for c in range(CHUNKS):
        transpose_in(c)
        if c == 0:
            pl.semaphore_wait(barrier, greeted)
        send_faces(0, c, wa)

    for load in coef_loads:
        load.wait()
    ax, ay, az = coef[0], coef[1], coef[2]
    scale = OMEGA / (2.0 * (ax + ay + az) + coef[3])
    ka[...] = ax * scale
    kb[...] = ay * scale
    az = az * scale
    lane = lax.broadcasted_iota(jnp.int32, az.shape, 2)
    km[...] = jnp.where(lane == 0, 0.0, az)
    kp[...] = jnp.where(lane == ROWS - 1, 0.0, az)

    wanted, targets, rank, ids = lists_of(meta[...], at)
    idv[...] = ids
    id_copy = pltpu.make_async_copy(idv, id_s, smem_sem.at[0])
    id_copy.start()
    for p in range(2):
        want[p : p + 1] = wanted[p]
        for n, axis in enumerate(AXES):
            wants[n, at[axis] * CORES + core, p : p + 1] = wanted[p]
    tgt[...] = jnp.zeros_like(tgt)
    for c in range(CHUNKS):
        a, u, v = ROUTES[c]
        ranks[c, at[v], at[u]] = rank
        for h in range(2):
            tgt[2 * c + h : 2 * c + h + 1] = targets[c][h]

    for c in range(CHUNKS):
        fill_halo(0, c, wa)
        sweep(c, wa, wb, False)
        send_faces(1, c, wb)
    for c in range(CHUNKS):
        for copy in rank_copies(c, 0):
            copy.start()
    for copy in want_copies():
        copy.start()
    for c in range(CHUNKS):
        fill_halo(1, c, wb)
        sweep(c, wb, wa, False)
        send_faces(2, c, wa)
    for c in range(CHUNKS):
        for copy in rank_copies(c, 0):
            copy.wait_recv()
        for copy in rank_copies(c, 1):
            copy.start()
    id_copy.wait()
    for c in range(CHUNKS):
        fill_halo(2, c, wa)
        sweep(c, wa, wb, True)
        spread(c)
    for copy in want_copies():
        copy.wait_recv()
    want_copy = pltpu.make_async_copy(wants, want_s, smem_sem.at[1])
    want_copy.start()
    for c in range(CHUNKS):
        for copy in rank_copies(c, 1):
            copy.wait_recv()
    rank_copy = pltpu.make_async_copy(ranks, rank_s, smem_sem.at[2])
    rank_copy.start()
    for c in range(CHUNKS):
        cast(c)
    want_copy.wait()
    rank_copy.wait()
    transpose_out(0, wb)
    for c in range(CHUNKS):
        pass_on(c)
    for c in range(CHUNKS):
        reply(c, 0)
    for c in range(CHUNKS):
        reply(c, 1)
        reply_on(c, 0)
    for c in range(CHUNKS):
        reply(c, 2)
        reply_on(c, 1)
    transpose_out(1, wb)
    for c in range(CHUNKS):
        reply_on(c, 2)
    transpose_out(2, wb)

    for s in range(SWEEPS):
        for c in range(CHUNKS):
            for copy in copies(s, c):
                copy.wait_send()
    for copy in want_copies():
        copy.wait_send()
    for c in range(CHUNKS):
        for copy in rank_copies(c, 0) + rank_copies(c, 1) + spread_copies(c) + cast_copies(c):
            copy.wait_send()
        for part in range(len(PARTS)):
            for d, e in order:
                copy = answer(c, part, d, e)
                if d or e:
                    copy.wait_send()
                    if d != 2:
                        copy.wait_recv()
                else:
                    copy.wait()
            for e in range(2):
                forward(c, part, e).wait_send()
                forward(c, part, e).wait_recv()
    for store in stores:
        store.wait()


def smooth(test_vectors, coef_x, coef_y, coef_z, shift, meta):
    vmem = pl.BlockSpec(memory_space=pltpu.VMEM)
    anywhere = pl.BlockSpec(memory_space=pl.ANY)
    cells = pltpu.VMEM((NX, NY, ROWS), F32)
    rows = pltpu.VMEM((LINE, COARSE, KV, ROWS), BF16)
    dma = pltpu.SemaphoreType.DMA
    return pl.pallas_call(
        smooth_kernel,
        out_shape=(
            jax.ShapeDtypeStruct((VECS, NX, NY, ROWS), F32),
            jax.ShapeDtypeStruct((CHUNKS, SITES, KV, ROWS), BF16),
            jax.ShapeDtypeStruct((CHUNKS, LINE * CORES, LINE, 2 * LINE, KV, ROWS), BF16),
            jax.ShapeDtypeStruct((8, ROWS), jnp.int32),
        ),
        in_specs=[anywhere] * 5 + [vmem],
        out_specs=(anywhere, vmem, anywhere, vmem),
        scratch_shapes=[
            pltpu.VMEM((VECS, NX, NY, ROWS), F32),
            pltpu.VMEM((4, NX, NY, ROWS), F32),
            pltpu.VMEM((CHUNKS, EXT, ROWS), F32),
            pltpu.VMEM((CHUNKS, EXT, ROWS), F32),
            cells, cells, cells, cells,
            pltpu.VMEM((SWEEPS, CHUNKS, 2, NY * KV, ROWS), BF16),
            pltpu.VMEM((SWEEPS, CHUNKS, 2, NY * KV, ROWS), BF16),
            pltpu.VMEM((SWEEPS, CHUNKS, 2, NX * KV, ROWS), BF16),
            pltpu.VMEM((SWEEPS, CHUNKS, 2, NX * KV, ROWS), BF16),
            pltpu.VMEM((2, ROWS), jnp.int32),
            pltpu.VMEM((len(AXES), LINE * CORES, 2, ROWS), jnp.int32),
            pltpu.VMEM((CHUNKS, LINE, LINE, 1, ROWS), jnp.int32),
            pltpu.VMEM((COARSE, ROWS), jnp.int32),
            pltpu.SMEM((len(AXES), LINE * CORES, 2, ROWS), jnp.int32),
            pltpu.SMEM((CHUNKS, LINE, LINE, 1, ROWS), jnp.int32),
            pltpu.SMEM((COARSE, ROWS), jnp.int32),
            *([rows] * (LINE * CHUNKS)),
            pltpu.VMEM((CHUNKS, LINE * CORES, LINE, 2 * LINE, KV, ROWS), BF16),
            pltpu.VMEM((CHUNKS, CORES, LINE, 2 * LINE, KV, ROWS), BF16),
            dma((CHUNKS,)),
            dma((4,)),
            dma((CHUNKS,)),
            dma((SWEEPS, CHUNKS, 4)),
            dma((SWEEPS, CHUNKS, 4)),
            dma((len(AXES), LINE, CORES)),
            dma((len(AXES), LINE, CORES)),
            dma((CHUNKS, 2, LINE)),
            dma((CHUNKS, 2, LINE)),
            dma((CHUNKS, LINE)),
            dma((CHUNKS, LINE)),
            dma((CHUNKS, 6)),
            dma((CHUNKS, 6)),
            dma((CHUNKS, len(PARTS), LINE, CORES)),
            dma((CHUNKS, len(PARTS), LINE, CORES)),
            dma((CHUNKS, len(PARTS), CORES)),
            dma((CHUNKS, len(PARTS), CORES)),
            dma((CHUNKS, len(PARTS))),
            dma((3,)),
        ],
        compiler_params=pltpu.CompilerParams(
            collective_id=0, has_side_effects=True, vmem_limit_bytes=60 * 1024 * 1024
        ),
        name="smooth",
    )(test_vectors, coef_x, coef_y, coef_z, shift, meta)


def solve_rows(gram, rhs):
    low = [[None] * SLOTS for _ in range(SLOTS)]
    inv = []
    for r in range(SLOTS):
        scaled = []
        diag = gram[r, r]
        for c in range(r):
            rest = gram[r, c]
            for m in range(c):
                rest = rest - scaled[m] * low[c][m]
            scaled.append(rest)
            low[r][c] = rest * inv[c]
            diag = diag - rest * low[r][c]
        inv.append(1.0 / diag)
    fwd = []
    for r in range(SLOTS):
        rest = rhs[r]
        for m in range(r):
            rest = rest - low[r][m] * fwd[m]
        fwd.append(rest)
    out = [None] * SLOTS
    for r in reversed(range(SLOTS)):
        rest = fwd[r] * inv[r]
        for m in range(r + 1, SLOTS):
            rest = rest - low[m][r] * out[m]
        out[r] = rest
    return out


PAIRS = [(s, t) for s in range(SLOTS) for t in range(s + 1)] + [
    (s, SLOTS) for s in range(SLOTS)
]


def weights_kernel(target, replies, blk, sm_in, w_out, sm_out, sums, copy_sem):
    move = pltpu.make_async_copy(sm_in, sm_out, copy_sem)
    move.start()

    def block(b, carry):
        accs = [None] * len(PAIRS)
        for c in range(CHUNKS):
            values = []
            for s in range(SLOTS):
                at = target[2 * c + b // 32, lax.rem(b, 32) * SLOTS + s]
                found = replies[c, jnp.maximum(at, 0)].astype(F32)
                values.append(jnp.where(at >= 0, found, 0.0))
            values.append(blk[c, b].astype(F32))
            for n, (s, t) in enumerate(PAIRS):
                prod = values[s] * values[t]
                part = prod[0:8] + prod[8:16]
                accs[n] = part if c == 0 else accs[n] + part
        for n, acc in enumerate(accs):
            sums[n, pl.ds(pl.multiple_of(b * 8, 8), 8), :] = acc
        return carry

    lax.fori_loop(0, SITES, block, 0)
    for g in range(SITES // 8):
        total = {}
        for n, pair in enumerate(PAIRS):
            acc = sums[n, pl.ds(g * 64, 8, stride=8), :]
            for h in range(1, 8):
                acc = acc + sums[n, pl.ds(g * 64 + h, 8, stride=8), :]
            acc = acc * (1.0 / VECS)
            if pair[0] == pair[1]:
                acc = acc + RIDGE
            total[pair] = acc
        out = solve_rows(total, [total[s, SLOTS] for s in range(SLOTS)])
        for s in range(SLOTS):
            w_out[s, g // 2, pl.ds((g % 2) * 8, 8), :] = out[s]
    move.wait()


def fit(target, replies, blk, sm):
    vmem = pl.BlockSpec(memory_space=pltpu.VMEM)
    anywhere = pl.BlockSpec(memory_space=pl.ANY)
    return pl.pallas_call(
        weights_kernel,
        out_shape=(
            jax.ShapeDtypeStruct((SLOTS, NX, NY, ROWS), F32),
            jax.ShapeDtypeStruct((VECS, NX, NY, ROWS), F32),
        ),
        in_specs=[pl.BlockSpec(memory_space=pltpu.SMEM), vmem, vmem, vmem],
        out_specs=(vmem, anywhere),
        scratch_shapes=[
            pltpu.VMEM((len(PAIRS), SITES * 8, ROWS), F32),
            pltpu.SemaphoreType.DMA,
        ],
        compiler_params=pltpu.CompilerParams(vmem_limit_bytes=60 * 1024 * 1024),
        name="fit",
    )(target, replies, blk, sm)


def per_device(
    test_vectors, coef_x, coef_y, coef_z, shift, cf_split, nbr_count, nbr_owner, nbr_block
):
    entries = SITES * SLOTS
    live = (cf_split == 0)[..., None] & (jnp.arange(SLOTS) < nbr_count[..., None])
    listed = jnp.where(live, nbr_owner * SITES + nbr_block, -1).reshape(entries // ROWS, ROWS)
    coarse = jnp.pad(cf_split.reshape(1, SITES), ((0, 5), (0, ROWS - SITES)))
    meta = jnp.concatenate([listed, coarse], axis=0)
    sm, blk, replies, target = smooth(test_vectors, coef_x, coef_y, coef_z, shift, meta)
    replies = replies.reshape(CHUNKS, LINE * CORES * 2 * PLANE, KV, ROWS)
    weights, smoothed = fit(target, replies, blk, sm)
    return (smoothed, weights)


def solution(mesh):
    cells = P("gx", "gy", None)
    lists = P("gx", "gy", None, None)
    vectors = P(None, "gx", "gy", None)
    return jax.shard_map(
        per_device,
        mesh=mesh,
        in_specs=(vectors, cells, cells, cells, cells, cells, cells, lists, lists),
        out_specs=(vectors, vectors),
        check_vma=False,
    )
```

```python
import jax
import jax.numpy as jnp
from jax import lax
from jax.experimental import pallas as pl
from jax.experimental.pallas import tpu as pltpu
from jax.sharding import PartitionSpec as P

SLOTS = 4
SWEEPS = 3
ROWS = 128
OMEGA = 0.8
RIDGE = 0.05
VECS = 48
CHUNKS = 3
KV = VECS // CHUNKS
NX = 4
NY = 16
SITES = NX * NY
XROW = (NY + 2) * KV
EXT = (NX + 2) * XROW
GX = 16
GY = 8
MESH = pl.DeviceIdType.MESH
F32 = jnp.float32
BF16 = jnp.bfloat16


def site_row(x, y):
    return (x + 1) * XROW + (y + 1) * KV


AXES = "xyz"
LINE = 4
CORES = 2
COARSE = 16
PLANE = LINE * LINE
ROUTES = (("x", "z", "y"), ("y", "x", "z"), ("z", "y", "x"))
BACKS = (0, 1, 3, 2)
PARTS = ((0, 3), (3, 1))


def lists_of(meta, here):
    lane = lax.broadcasted_iota(jnp.int32, (ROWS, ROWS), 1)
    sub = lax.broadcasted_iota(jnp.int32, (ROWS, ROWS), 0)
    diag = lane == sub
    none = 1 << 20

    def column(row):
        return jnp.sum(jnp.where(diag, row, 0), axis=1, keepdims=True)

    def line(col):
        return jnp.sum(jnp.where(diag, col, 0), axis=0, keepdims=True)

    members, keys, owners = [], [], []
    for h in range(2):
        entry = meta[h : h + 1]
        owner = entry >> 6
        key = (lane[:1] + h * ROWS) * SITES + (entry & (SITES - 1))
        owners.append(owner)
        keys.append(key)
        members.append(owner == sub)
    first = jnp.minimum(*[jnp.where(m, k, none) for m, k in zip(members, keys)])
    first = jnp.min(first, axis=1, keepdims=True)
    first = jnp.where(first >= none, 0, first)
    second = jnp.maximum(*[jnp.where(m, k, 0) for m, k in zip(members, keys)])
    second = jnp.max(second, axis=1, keepdims=True)
    wanted = [line(v) & (SITES - 1) for v in (first, second)]
    targets = [[] for _ in ROUTES]
    for h in range(2):
        own = owners[h]
        at_first = jnp.sum(jnp.where(members[h], first, 0), axis=0, keepdims=True)
        place = jnp.where(keys[h] == at_first, 0, 1)
        at = {"x": (own >> 5) & 3, "z": (own >> 3) & 3, "y": (own >> 1) & 3}
        for c, (a, u, v) in enumerate(ROUTES):
            back = (at[v] - here[v]) & 3
            spot = jnp.where(back == 2, 3, jnp.where(back == 3, 2, back))
            slot = ((at[a] * CORES + (own & 1)) * PLANE + spot * LINE + at[u]) * 2 + place
            targets[c].append(jnp.where(own < 0, -1, slot))
    coarse = meta[2:3]
    rank = jnp.sum(jnp.where(sub < lane, column(coarse), 0), axis=0, keepdims=True)
    hit = (rank == sub[:COARSE]) & (coarse > 0)
    ids = jnp.sum(jnp.where(hit, lane[:COARSE], 0), axis=1, keepdims=True)
    ids = jnp.broadcast_to(ids, (COARSE, ROWS))
    rank = jnp.minimum(rank, COARSE - 1)
    return wanted, targets, rank, ids


def smooth_kernel(
    tv, cx, cy, cz, sh, meta, sm_out, blk, rb, tgt,
    stage, coef, wa, wb, ka, kb, km, kp, fxs, fxr, fys, fyr,
    pair, lines, ranks, idv, line_s, rank_s, id_s, p00, p01, p02, p03, p10, p11, p12, p13, p20, p21, p22, p23, sb, fb,
    in_sem, coef_sem, out_sem, send_sem, recv_sem, pair_sem, table_sem,
    near_sem, cast_send, cast_recv, ans_send, ans_recv, hop_recv, fwd_send, own_sem, smem_sem,
):
    pg = ((p00, p01, p02, p03), (p10, p11, p12, p13), (p20, p21, p22, p23))
    i = lax.axis_index("gx")
    j = lax.axis_index("gy")
    core = lax.rem(j, CORES)
    at = {"x": i // LINE, "z": lax.rem(i, LINE), "y": j // CORES}
    peers = (
        (lax.rem(i + GX - 1, GX), j),
        (lax.rem(i + 1, GX), j),
        (i, lax.rem(j + GY - 1, GY)),
        (i, lax.rem(j + 1, GY)),
    )

    def device(axis, d, e):
        moved = dict(at)
        moved[axis] = lax.rem(at[axis] + d, LINE)
        return (moved["x"] * LINE + moved["z"], moved["y"] * CORES + lax.rem(core + e, CORES))

    def remote(src, dst, send, recv, peer):
        return pltpu.make_async_remote_copy(
            src_ref=src, dst_ref=dst, send_sem=send, recv_sem=recv,
            device_id=peer, device_id_type=MESH,
        )

    loads = []
    for n, part in enumerate((cx, cy, cz, sh)):
        load = pltpu.make_async_copy(part, coef.at[n], coef_sem.at[n])
        load.start()
        loads.append(load)
    coef_loads, loads = loads, []
    for c in range(CHUNKS):
        part = pl.ds(c * KV, KV)
        load = pltpu.make_async_copy(tv.at[part], stage.at[part], in_sem.at[c])
        load.start()
        loads.append(load)
    barrier = pltpu.get_barrier_semaphore()
    for peer in peers[:2]:
        pl.semaphore_signal(barrier, inc=1, device_id=peer, device_id_type=MESH)
    pl.semaphore_signal(barrier, inc=1, device_id=device("x", 0, 1), device_id_type=MESH)
    for axis in AXES:
        for d in range(1, LINE):
            for e in range(CORES):
                pl.semaphore_signal(
                    barrier, inc=1, device_id=device(axis, d, e), device_id_type=MESH
                )
    greeted = 3 + len(AXES) * (LINE - 1) * CORES

    keep = (
        (i > 0).astype(F32),
        (i < GX - 1).astype(F32),
        (j > 0).astype(F32),
        (j < GY - 1).astype(F32),
    )

    def drain(ref, sem):
        pltpu.make_async_copy(ref, ref, sem).wait()

    def copies(s, c):
        out = []
        for d in range(4):
            src, dst = (fxs, fxr) if d < 2 else (fys, fyr)
            out.append(
                remote(
                    src.at[s, c, d % 2], dst.at[s, c, 1 - d % 2],
                    send_sem.at[d // 2], recv_sem.at[s, c, d // 2], peers[d],
                )
            )
        return out

    def send_faces(s, c, w):
        for side in range(2):
            x = side * (NX - 1)
            fxs[s, c, side] = w[c, pl.ds(site_row(x, 0), NY * KV)].astype(BF16)
            y = side * (NY - 1)
            for x in range(NX):
                fys[s, c, side, pl.ds(x * KV, KV)] = w[c, pl.ds(site_row(x, y), KV)].astype(BF16)
        for copy in copies(s, c):
            copy.start()

    def fill_halo(s, c, w):
        drain(fxr.at[s, c], recv_sem.at[s, c, 0])
        drain(fyr.at[s, c], recv_sem.at[s, c, 1])
        for side in range(2):
            x = -1 if side == 0 else NX
            w[c, pl.ds(site_row(x, 0), NY * KV)] = fxr[s, c, side].astype(F32) * keep[side]
            y = -1 if side == 0 else NY
            for x in range(NX):
                w[c, pl.ds(site_row(x, y), KV)] = (
                    fyr[s, c, side, pl.ds(x * KV, KV)].astype(F32) * keep[2 + side]
                )

    def sweep(c, src, dst, last):
        def plane(x, carry):
            base = pl.multiple_of(x * XROW, 16)

            def cell(dx, y):
                return src[c, pl.ds(base + site_row(dx, y), KV)]

            below, here = cell(0, -1), cell(0, 0)
            for y in range(NY):
                above = cell(0, y + 1)
                row = slice(y, y + 1)
                new = (
                    ka[x, row] * (cell(-1, y) + cell(1, y))
                    + kb[x, row] * (below + above)
                    + km[x, row] * pltpu.roll(here, 1, 1)
                    + kp[x, row] * pltpu.roll(here, ROWS - 1, 1)
                    + (1.0 - OMEGA) * here
                )
                dst[c, pl.ds(base + site_row(0, y), KV)] = new
                if last:
                    blk[c, x * NY + y] = new.astype(BF16)
                below, here = here, above
            return carry

        lax.fori_loop(0, NX, plane, 0)

    def pair_copy():
        slot = pair.at[core]
        return remote(slot, slot, pair_sem.at[0], pair_sem.at[1], device("x", 0, 1))

    def line_copies():
        return [
            remote(
                pair, lines.at[n, at[axis]], table_sem.at[0, 0], table_sem.at[0, 1],
                device(axis, d, 0),
            )
            for n, axis in enumerate(AXES)
            for d in range(1, LINE)
        ]

    def rank_copies():
        out = []
        for c, (a, u, v) in enumerate(ROUTES):
            src = lines.at[AXES.index(u), :, core, 2]
            for d in range(1, LINE):
                out.append(
                    remote(
                        src, ranks.at[c, at[v]], table_sem.at[1, 0], table_sem.at[1, 1],
                        device(v, d, 0),
                    )
                )
        return out

    def spread_copies(c):
        a, u, v = ROUTES[c]
        ref = pg[c][0].at[at[u]]
        return [
            remote(ref, ref, near_sem.at[c, 0], near_sem.at[c, 1], device(u, d, 0))
            for d in (2, 1, 3)
        ]

    def cast_copies(c):
        a, u, v = ROUTES[c]
        plan = ((0, 0, 3, 1), (0, 1, 1, 3), (0, 1, 3, 1), (0, 0, 1, 3), (3, 0, 2, 1), (1, 1, 2, 3))
        return [
            remote(
                pg[c][src].at[pl.ds(half * 2, 2)], pg[c][dst].at[pl.ds(half * 2, 2)],
                cast_send.at[c, n // 2], cast_recv.at[c, min(n, 2 + n // 4)], device(v, d, 0),
            )
            for n, (src, half, dst, d) in enumerate(plan)
        ]

    def piece(ref, part):
        first, count = PARTS[part]
        return ref.at[pl.ds(first, count)]

    def answer(c, part, d, e):
        a = ROUTES[c][0]
        slot = lax.rem(at[a] + d, LINE) * CORES + lax.rem(core + e, CORES)
        here = at[a] * CORES + core
        src = piece(sb.at[c, slot], part)
        dst, peer = piece(rb.at[c, here], part), device(a, d, e)
        if d == 0 and e == 0:
            return pltpu.make_async_copy(src, dst, own_sem.at[c, part])
        if d == 2:
            dst, peer = piece(fb.at[c, e], part), device(a, 1 + 2 * e, 0)
            return remote(src, dst, ans_send.at[c, part], hop_recv.at[c, part, e], peer)
        return remote(src, dst, ans_send.at[c, part], ans_recv.at[c, part], peer)

    def forward(c, part, e):
        a = ROUTES[c][0]
        origin = lax.rem(at[a] + 3 - 2 * e, LINE) * CORES + core
        return remote(
            piece(fb.at[c, e], part), piece(rb.at[c, origin], part),
            fwd_send.at[c, part], ans_recv.at[c, part], device(a, 1 + 2 * e, e),
        )

    order = [(d, e) for d in (2, 1, 3, 0) for e in range(CORES)]

    def spread(c):
        a, u, v = ROUTES[c]
        for r in range(COARSE):
            pg[c][0][at[u], r] = blk[c, id_s[r, 0] & (SITES - 1)]
        for copy in spread_copies(c):
            copy.start()

    def cast(c):
        drain(pg[c][1].at[pl.ds(0, 3)], near_sem.at[c, 1])
        for copy in cast_copies(c)[:4]:
            copy.start()

    def pass_on(c):
        all_copies = cast_copies(c)
        for n in range(2):
            all_copies[n].wait_recv()
            all_copies[4 + n].start()

    def reply(c, part):
        a, u, v = ROUTES[c]
        n = AXES.index(a)
        drain(pg[c][0], cast_recv.at[c, 2 + part])
        first, count = PARTS[part]
        for d, e in order:
            q, to = lax.rem(at[a] + d, LINE), lax.rem(core + e, CORES)
            slot = q * CORES + to
            for place in range(first, first + count):
                back = BACKS[place]
                vv = lax.rem(at[v] + back, LINE)
                tiles = []
                for uu in range(LINE):
                    whose = {a: at[a], u: uu, v: vv}
                    owner = whose["x"] * 32 + whose["z"] * 8 + whose["y"] * 2 + core
                    for p in range(2):
                        block = line_s[n, q, to, p, 0, owner] & (SITES - 1)
                        rank = rank_s[c, vv, uu, 0, block] & (COARSE - 1)
                        tiles.append(pg[c][back][uu, rank])
                for t, tile in enumerate(tiles):
                    sb[c, slot, place, t] = tile
            answer(c, part, d, e).start()

    def reply_on(c, part):
        for e in range(2):
            answer(c, part, 2, e).wait_recv()
            forward(c, part, e).start()

    def transpose_in(c):
        loads[c].wait()
        for x in range(NX):
            for half in range(NY // 8):
                for k in range(KV):
                    wa[c, pl.ds(site_row(x, half * 8) + k, 8, stride=KV), :] = stage[
                        c * KV + k, x, pl.ds(half * 8, 8), :
                    ]

    stores = []

    def transpose_out(c, w):
        for x in range(NX):
            for half in range(NY // 8):
                for k in range(KV):
                    stage[c * KV + k, x, pl.ds(half * 8, 8), :] = w[
                        c, pl.ds(site_row(x, half * 8) + k, 8, stride=KV), :
                    ]
        part = pl.ds(c * KV, KV)
        store = pltpu.make_async_copy(stage.at[part], sm_out.at[part], out_sem.at[c])
        store.start()
        stores.append(store)

    for c in range(CHUNKS):
        transpose_in(c)
        if c == 0:
            pl.semaphore_wait(barrier, greeted)
        send_faces(0, c, wa)

    for load in coef_loads:
        load.wait()
    ax, ay, az = coef[0], coef[1], coef[2]
    scale = OMEGA / (2.0 * (ax + ay + az) + coef[3])
    ka[...] = ax * scale
    kb[...] = ay * scale
    az = az * scale
    lane = lax.broadcasted_iota(jnp.int32, az.shape, 2)
    km[...] = jnp.where(lane == 0, 0.0, az)
    kp[...] = jnp.where(lane == ROWS - 1, 0.0, az)

    wanted, targets, rank, ids = lists_of(meta[...], at)
    idv[...] = ids
    id_copy = pltpu.make_async_copy(idv, id_s, smem_sem.at[0])
    id_copy.start()
    for n, row in enumerate((*wanted, rank)):
        pair[core, n] = row
    pair_copy().start()
    tgt[...] = jnp.zeros_like(tgt)
    for c in range(CHUNKS):
        for h in range(2):
            tgt[2 * c + h : 2 * c + h + 1] = targets[c][h]

    for c in range(CHUNKS):
        fill_halo(0, c, wa)
        sweep(c, wa, wb, False)
        send_faces(1, c, wb)
    pair_copy().wait_recv()
    for copy in line_copies():
        copy.start()
    for n, axis in enumerate(AXES):
        lines[n, at[axis]] = pair[...]
    for c in range(CHUNKS):
        fill_halo(1, c, wb)
        sweep(c, wb, wa, False)
        send_faces(2, c, wa)
    drain(lines.at[:, pl.ds(0, 3)], table_sem.at[0, 1])
    for copy in rank_copies():
        copy.start()
    for c, (a, u, v) in enumerate(ROUTES):
        ranks[c, at[v]] = lines[AXES.index(u), :, core, 2]
    line_copy = pltpu.make_async_copy(lines, line_s, smem_sem.at[1])
    line_copy.start()
    id_copy.wait()
    for c in range(CHUNKS):
        fill_halo(2, c, wa)
        sweep(c, wa, wb, True)
        spread(c)
    drain(ranks.at[:, pl.ds(0, 3)], table_sem.at[1, 1])
    rank_copy = pltpu.make_async_copy(ranks, rank_s, smem_sem.at[2])
    rank_copy.start()
    for c in range(CHUNKS):
        cast(c)
    line_copy.wait()
    rank_copy.wait()
    transpose_out(0, wb)
    for c in range(CHUNKS):
        pass_on(c)
    for c in range(CHUNKS):
        reply(c, 0)
    for c in range(CHUNKS):
        reply(c, 1)
        reply_on(c, 0)
    transpose_out(1, wb)
    for c in range(CHUNKS):
        reply_on(c, 1)
    transpose_out(2, wb)

    drain(fxs, send_sem.at[0])
    drain(fys, send_sem.at[1])
    pair_copy().wait_send()
    drain(lines.at[:, pl.ds(0, 3)], table_sem.at[0, 0])
    drain(ranks.at[:, pl.ds(0, 3)], table_sem.at[1, 0])
    for c in range(CHUNKS):
        drain(pg[c][0].at[pl.ds(0, 3)], near_sem.at[c, 0])
        for n in range(3):
            drain(pg[c][0], cast_send.at[c, n])
        for part in range(len(PARTS)):
            answer(c, part, 0, 0).wait()
            first, count = PARTS[part]
            seven = sb.at[c, pl.ds(0, 7), pl.ds(first, count)]
            drain(seven, ans_send.at[c, part])
            drain(fb.at[c, :, pl.ds(first, count)], fwd_send.at[c, part])
            drain(seven, ans_recv.at[c, part])
    for store in stores:
        store.wait()


def smooth(test_vectors, coef_x, coef_y, coef_z, shift, meta):
    vmem = pl.BlockSpec(memory_space=pltpu.VMEM)
    anywhere = pl.BlockSpec(memory_space=pl.ANY)
    cells = pltpu.VMEM((NX, NY, ROWS), F32)
    rows = pltpu.VMEM((LINE, COARSE, KV, ROWS), BF16)
    dma = pltpu.SemaphoreType.DMA
    return pl.pallas_call(
        smooth_kernel,
        out_shape=(
            jax.ShapeDtypeStruct((VECS, NX, NY, ROWS), F32),
            jax.ShapeDtypeStruct((CHUNKS, SITES, KV, ROWS), BF16),
            jax.ShapeDtypeStruct((CHUNKS, LINE * CORES, LINE, 2 * LINE, KV, ROWS), BF16),
            jax.ShapeDtypeStruct((8, ROWS), jnp.int32),
        ),
        in_specs=[anywhere] * 5 + [vmem],
        out_specs=(anywhere, vmem, anywhere, vmem),
        scratch_shapes=[
            pltpu.VMEM((VECS, NX, NY, ROWS), F32),
            pltpu.VMEM((4, NX, NY, ROWS), F32),
            pltpu.VMEM((CHUNKS, EXT, ROWS), F32),
            pltpu.VMEM((CHUNKS, EXT, ROWS), F32),
            cells, cells, cells, cells,
            pltpu.VMEM((SWEEPS, CHUNKS, 2, NY * KV, ROWS), BF16),
            pltpu.VMEM((SWEEPS, CHUNKS, 2, NY * KV, ROWS), BF16),
            pltpu.VMEM((SWEEPS, CHUNKS, 2, NX * KV, ROWS), BF16),
            pltpu.VMEM((SWEEPS, CHUNKS, 2, NX * KV, ROWS), BF16),
            pltpu.VMEM((CORES, 3, 1, ROWS), jnp.int32),
            pltpu.VMEM((len(AXES), LINE, CORES, 3, 1, ROWS), jnp.int32),
            pltpu.VMEM((CHUNKS, LINE, LINE, 1, ROWS), jnp.int32),
            pltpu.VMEM((COARSE, ROWS), jnp.int32),
            pltpu.SMEM((len(AXES), LINE, CORES, 3, 1, ROWS), jnp.int32),
            pltpu.SMEM((CHUNKS, LINE, LINE, 1, ROWS), jnp.int32),
            pltpu.SMEM((COARSE, ROWS), jnp.int32),
            *([rows] * (LINE * CHUNKS)),
            pltpu.VMEM((CHUNKS, LINE * CORES, LINE, 2 * LINE, KV, ROWS), BF16),
            pltpu.VMEM((CHUNKS, CORES, LINE, 2 * LINE, KV, ROWS), BF16),
            dma((CHUNKS,)),
            dma((4,)),
            dma((CHUNKS,)),
            dma((2,)),
            dma((SWEEPS, CHUNKS, 2)),
            dma((2,)),
            dma((2, 2)),
            dma((CHUNKS, 2)),
            dma((CHUNKS, 3)),
            dma((CHUNKS, 4)),
            dma((CHUNKS, len(PARTS))),
            dma((CHUNKS, len(PARTS))),
            dma((CHUNKS, len(PARTS), CORES)),
            dma((CHUNKS, len(PARTS))),
            dma((CHUNKS, len(PARTS))),
            dma((3,)),
        ],
        compiler_params=pltpu.CompilerParams(
            collective_id=0, has_side_effects=True, vmem_limit_bytes=60 * 1024 * 1024
        ),
        name="smooth",
    )(test_vectors, coef_x, coef_y, coef_z, shift, meta)


def solve_rows(gram, rhs):
    low = [[None] * SLOTS for _ in range(SLOTS)]
    inv = []
    for r in range(SLOTS):
        scaled = []
        diag = gram[r, r]
        for c in range(r):
            rest = gram[r, c]
            for m in range(c):
                rest = rest - scaled[m] * low[c][m]
            scaled.append(rest)
            low[r][c] = rest * inv[c]
            diag = diag - rest * low[r][c]
        inv.append(1.0 / diag)
    fwd = []
    for r in range(SLOTS):
        rest = rhs[r]
        for m in range(r):
            rest = rest - low[r][m] * fwd[m]
        fwd.append(rest)
    out = [None] * SLOTS
    for r in reversed(range(SLOTS)):
        rest = fwd[r] * inv[r]
        for m in range(r + 1, SLOTS):
            rest = rest - low[m][r] * out[m]
        out[r] = rest
    return out


PAIRS = [(s, t) for s in range(SLOTS) for t in range(s + 1)] + [
    (s, SLOTS) for s in range(SLOTS)
]


def weights_kernel(target, replies, blk, sm_in, w_out, sm_out, sums, copy_sem):
    move = pltpu.make_async_copy(sm_in, sm_out, copy_sem)
    move.start()

    def block(b, carry):
        accs = [None] * len(PAIRS)
        for c in range(CHUNKS):
            values = []
            for s in range(SLOTS):
                at = target[2 * c + b // 32, lax.rem(b, 32) * SLOTS + s]
                found = replies[c, jnp.maximum(at, 0)].astype(F32)
                values.append(jnp.where(at >= 0, found, 0.0))
            values.append(blk[c, b].astype(F32))
            for n, (s, t) in enumerate(PAIRS):
                prod = values[s] * values[t]
                part = prod[0:8] + prod[8:16]
                accs[n] = part if c == 0 else accs[n] + part
        for n, acc in enumerate(accs):
            sums[n, pl.ds(pl.multiple_of(b * 8, 8), 8), :] = acc
        return carry

    lax.fori_loop(0, SITES, block, 0)
    for g in range(SITES // 8):
        total = {}
        for n, pair in enumerate(PAIRS):
            acc = sums[n, pl.ds(g * 64, 8, stride=8), :]
            for h in range(1, 8):
                acc = acc + sums[n, pl.ds(g * 64 + h, 8, stride=8), :]
            acc = acc * (1.0 / VECS)
            if pair[0] == pair[1]:
                acc = acc + RIDGE
            total[pair] = acc
        out = solve_rows(total, [total[s, SLOTS] for s in range(SLOTS)])
        for s in range(SLOTS):
            w_out[s, g // 2, pl.ds((g % 2) * 8, 8), :] = out[s]
    move.wait()


def fit(target, replies, blk, sm):
    vmem = pl.BlockSpec(memory_space=pltpu.VMEM)
    anywhere = pl.BlockSpec(memory_space=pl.ANY)
    return pl.pallas_call(
        weights_kernel,
        out_shape=(
            jax.ShapeDtypeStruct((SLOTS, NX, NY, ROWS), F32),
            jax.ShapeDtypeStruct((VECS, NX, NY, ROWS), F32),
        ),
        in_specs=[pl.BlockSpec(memory_space=pltpu.SMEM), vmem, vmem, vmem],
        out_specs=(vmem, anywhere),
        scratch_shapes=[
            pltpu.VMEM((len(PAIRS), SITES * 8, ROWS), F32),
            pltpu.SemaphoreType.DMA,
        ],
        compiler_params=pltpu.CompilerParams(vmem_limit_bytes=60 * 1024 * 1024),
        name="fit",
    )(target, replies, blk, sm)


def per_device(
    test_vectors, coef_x, coef_y, coef_z, shift, cf_split, nbr_count, nbr_owner, nbr_block
):
    entries = SITES * SLOTS
    live = (cf_split == 0)[..., None] & (jnp.arange(SLOTS) < nbr_count[..., None])
    listed = jnp.where(live, nbr_owner * SITES + nbr_block, -1).reshape(entries // ROWS, ROWS)
    coarse = jnp.pad(cf_split.reshape(1, SITES), ((0, 5), (0, ROWS - SITES)))
    meta = jnp.concatenate([listed, coarse], axis=0)
    sm, blk, replies, target = smooth(test_vectors, coef_x, coef_y, coef_z, shift, meta)
    replies = replies.reshape(CHUNKS, LINE * CORES * 2 * PLANE, KV, ROWS)
    weights, smoothed = fit(target, replies, blk, sm)
    return (smoothed, weights)


def solution(mesh):
    cells = P("gx", "gy", None)
    lists = P("gx", "gy", None, None)
    vectors = P(None, "gx", "gy", None)
    return jax.shard_map(
        per_device,
        mesh=mesh,
        in_specs=(vectors, cells, cells, cells, cells, cells, cells, lists, lists),
        out_specs=(vectors, vectors),
        check_vma=False,
    )
```

```python
import jax
import jax.numpy as jnp
from jax import lax
from jax.experimental import pallas as pl
from jax.experimental.pallas import tpu as pltpu
from jax.sharding import PartitionSpec as P

SLOTS = 4
SWEEPS = 3
ROWS = 128
OMEGA = 0.8
RIDGE = 0.05
VECS = 48
CHUNKS = 3
KV = VECS // CHUNKS
NX = 4
NY = 16
SITES = NX * NY
XROW = (NY + 2) * KV
EXT = (NX + 2) * XROW
GX = 16
GY = 8
MESH = pl.DeviceIdType.MESH
F32 = jnp.float32
BF16 = jnp.bfloat16


def site_row(x, y):
    return (x + 1) * XROW + (y + 1) * KV


PAIRS = [(s, t) for s in range(SLOTS) for t in range(s + 1)] + [(s, SLOTS) for s in range(SLOTS)]
AXES = "xyz"
LINE = 4
CORES = 2
COARSE = 16
PLANE = LINE * LINE
ROUTES = (("x", "z", "y"), ("y", "x", "z"), ("z", "y", "x"))
BACKS = (0, 1, 3, 2)
EMPTY = LINE * CORES * PLANE * 2
SPOT = 2 * LINE
REPLY = PLANE * 2
PARTS = ((0, 3), (3, 1))


def lists_of(meta, here):
    lane = lax.broadcasted_iota(jnp.int32, (ROWS, ROWS), 1)
    sub = lax.broadcasted_iota(jnp.int32, (ROWS, ROWS), 0)
    diag = lane == sub
    none = 1 << 20

    def column(row):
        return jnp.sum(jnp.where(diag, row, 0), axis=1, keepdims=True)

    def line(col):
        return jnp.sum(jnp.where(diag, col, 0), axis=0, keepdims=True)

    members, keys, owners = [], [], []
    for h in range(2):
        entry = meta[h : h + 1]
        owner = entry >> 6
        key = (lane[:1] + h * ROWS) * SITES + (entry & (SITES - 1))
        owners.append(owner)
        keys.append(key)
        members.append(owner == sub)
    first = jnp.minimum(*[jnp.where(m, k, none) for m, k in zip(members, keys)])
    first = jnp.min(first, axis=1, keepdims=True)
    first = jnp.where(first >= none, 0, first)
    second = jnp.maximum(*[jnp.where(m, k, 0) for m, k in zip(members, keys)])
    second = jnp.max(second, axis=1, keepdims=True)
    wanted = [line(v) & (SITES - 1) for v in (first, second)]
    targets = [[] for _ in ROUTES]
    for h in range(2):
        own = owners[h]
        at_first = jnp.sum(jnp.where(members[h], first, 0), axis=0, keepdims=True)
        place = jnp.where(keys[h] == at_first, 0, 1)
        at = {"x": (own >> 5) & 3, "z": (own >> 3) & 3, "y": (own >> 1) & 3}
        for c, (a, u, v) in enumerate(ROUTES):
            back = (at[v] - here[v]) & 3
            spot = jnp.where(back == 2, 3, jnp.where(back == 3, 2, back))
            slot = ((at[a] * CORES + (own & 1)) * PLANE + spot * LINE + at[u]) * 2 + place
            targets[c].append(jnp.where(own < 0, EMPTY, slot))
    coarse = meta[2:3]
    rank = jnp.sum(jnp.where(sub < lane, column(coarse), 0), axis=0, keepdims=True)
    hit = (rank == sub[:COARSE]) & (coarse > 0)
    ids = jnp.sum(jnp.where(hit, lane[:COARSE], 0), axis=1, keepdims=True)
    ids = jnp.broadcast_to(ids, (COARSE, ROWS))
    rank = jnp.minimum(rank, COARSE - 1)
    return wanted, targets, rank, ids


def smooth_kernel(
    tv, cx, cy, cz, sh, split, count, owner, local, sm_out, sums,
    split_v, count_v, owner_v, local_v, meta, tgt, tgt_s, blk, rb0, rb1, rb2, part_sums,
    stage, coef, wa, wb, ka, kb, km, kp, fxs, fxr, fys, fyr,
    pair, lines, ranks, idv, line_s, rank_s, id_s, p00, p01, p02, p03, p10, p11, p12, p13, p20, p21, p22, p23, sb, fb,
    in_sem, coef_sem, out_sem, send_sem, recv_sem, pair_sem, table_sem,
    near_sem, cast_send, cast_recv, ans_send, ans_recv, hop_recv, fwd_send, own_sem, smem_sem, list_sem,
):
    cells = (split_v, count_v, owner_v, local_v)
    rb = (rb0, rb1, rb2)
    pg = ((p00, p01, p02, p03), (p10, p11, p12, p13), (p20, p21, p22, p23))
    i = lax.axis_index("gx")
    j = lax.axis_index("gy")
    core = lax.rem(j, CORES)
    at = {"x": i // LINE, "z": lax.rem(i, LINE), "y": j // CORES}
    peers = (
        (lax.rem(i + GX - 1, GX), j),
        (lax.rem(i + 1, GX), j),
        (i, lax.rem(j + GY - 1, GY)),
        (i, lax.rem(j + 1, GY)),
    )

    def device(axis, d, e):
        moved = dict(at)
        moved[axis] = lax.rem(at[axis] + d, LINE)
        return (moved["x"] * LINE + moved["z"], moved["y"] * CORES + lax.rem(core + e, CORES))

    def remote(src, dst, send, recv, peer):
        return pltpu.make_async_remote_copy(
            src_ref=src, dst_ref=dst, send_sem=send, recv_sem=recv,
            device_id=peer, device_id_type=MESH,
        )

    loads = []
    for n, part in enumerate((cx, cy, cz, sh)):
        load = pltpu.make_async_copy(part, coef.at[n], coef_sem.at[n])
        load.start()
        loads.append(load)
    coef_loads, loads = loads, []
    lists = []
    for n, part in enumerate((split, count, owner, local)):
        load = pltpu.make_async_copy(part, cells[n], list_sem.at[n])
        load.start()
        lists.append(load)
    for c in range(CHUNKS):
        part = pl.ds(c * KV, KV)
        load = pltpu.make_async_copy(tv.at[part], stage.at[part], in_sem.at[c])
        load.start()
        loads.append(load)
    barrier = pltpu.get_barrier_semaphore()
    for peer in peers[:2]:
        pl.semaphore_signal(barrier, inc=1, device_id=peer, device_id_type=MESH)
    pl.semaphore_signal(barrier, inc=1, device_id=device("x", 0, 1), device_id_type=MESH)
    for axis in AXES:
        for d in range(1, LINE):
            for e in range(CORES):
                pl.semaphore_signal(
                    barrier, inc=1, device_id=device(axis, d, e), device_id_type=MESH
                )
    greeted = 3 + len(AXES) * (LINE - 1) * CORES

    keep = (
        (i > 0).astype(F32),
        (i < GX - 1).astype(F32),
        (j > 0).astype(F32),
        (j < GY - 1).astype(F32),
    )

    def drain(ref, sem):
        pltpu.make_async_copy(ref, ref, sem).wait()

    def copies(s, c):
        out = []
        for d in range(4):
            src, dst = (fxs, fxr) if d < 2 else (fys, fyr)
            out.append(
                remote(
                    src.at[s, c, d % 2], dst.at[s, c, 1 - d % 2],
                    send_sem.at[d // 2], recv_sem.at[s, c, d // 2], peers[d],
                )
            )
        return out

    def send_faces(s, c, w):
        for side in range(2):
            x = side * (NX - 1)
            fxs[s, c, side] = w[c, pl.ds(site_row(x, 0), NY * KV)].astype(BF16)
            y = side * (NY - 1)
            for x in range(NX):
                fys[s, c, side, pl.ds(x * KV, KV)] = w[c, pl.ds(site_row(x, y), KV)].astype(BF16)
        for copy in copies(s, c):
            copy.start()

    def fill_halo(s, c, w):
        drain(fxr.at[s, c], recv_sem.at[s, c, 0])
        drain(fyr.at[s, c], recv_sem.at[s, c, 1])
        for side in range(2):
            x = -1 if side == 0 else NX
            w[c, pl.ds(site_row(x, 0), NY * KV)] = fxr[s, c, side].astype(F32) * keep[side]
            y = -1 if side == 0 else NY
            for x in range(NX):
                w[c, pl.ds(site_row(x, y), KV)] = (
                    fyr[s, c, side, pl.ds(x * KV, KV)].astype(F32) * keep[2 + side]
                )

    def sweep(c, src, dst, last):
        def plane(x, carry):
            base = pl.multiple_of(x * XROW, 16)

            def cell(dx, y):
                return src[c, pl.ds(base + site_row(dx, y), KV)]

            below, here = cell(0, -1), cell(0, 0)
            for y in range(NY):
                above = cell(0, y + 1)
                row = slice(y, y + 1)
                new = (
                    ka[x, row] * (cell(-1, y) + cell(1, y))
                    + kb[x, row] * (below + above)
                    + km[x, row] * pltpu.roll(here, 1, 1)
                    + kp[x, row] * pltpu.roll(here, ROWS - 1, 1)
                    + (1.0 - OMEGA) * here
                )
                dst[c, pl.ds(base + site_row(0, y), KV)] = new
                if last:
                    blk[c, x * NY + y] = new.astype(BF16)
                below, here = here, above
            return carry

        lax.fori_loop(0, NX, plane, 0)

    def pair_copy():
        slot = pair.at[core]
        return remote(slot, slot, pair_sem.at[0], pair_sem.at[1], device("x", 0, 1))

    def line_copies():
        return [
            remote(
                pair, lines.at[n, at[axis]], table_sem.at[0, 0], table_sem.at[0, 1],
                device(axis, d, 0),
            )
            for n, axis in enumerate(AXES)
            for d in range(1, LINE)
        ]

    def rank_copies():
        out = []
        for c, (a, u, v) in enumerate(ROUTES):
            src = lines.at[AXES.index(u), :, core, 2]
            for d in range(1, LINE):
                out.append(
                    remote(
                        src, ranks.at[c, at[v]], table_sem.at[1, 0], table_sem.at[1, 1],
                        device(v, d, 0),
                    )
                )
        return out

    def spread_copies(c):
        a, u, v = ROUTES[c]
        ref = pg[c][0].at[at[u]]
        return [
            remote(ref, ref, near_sem.at[c, 0], near_sem.at[c, 1], device(u, d, 0))
            for d in (2, 1, 3)
        ]

    def cast_copies(c):
        a, u, v = ROUTES[c]
        plan = ((0, 0, 3, 1), (0, 1, 1, 3), (0, 1, 3, 1), (0, 0, 1, 3), (3, 0, 2, 1), (1, 1, 2, 3))
        return [
            remote(
                pg[c][src].at[pl.ds(half * 2, 2)], pg[c][dst].at[pl.ds(half * 2, 2)],
                cast_send.at[c, n // 2], cast_recv.at[c, min(n, 2 + n // 4)], device(v, d, 0),
            )
            for n, (src, half, dst, d) in enumerate(plan)
        ]

    def piece(slot, part):
        first, count = PARTS[part]
        return pl.ds(slot * REPLY + first * SPOT, count * SPOT)

    def answer(c, part, d, e):
        a = ROUTES[c][0]
        slot = lax.rem(at[a] + d, LINE) * CORES + lax.rem(core + e, CORES)
        here = at[a] * CORES + core
        src = sb.at[c, piece(slot, part)]
        dst, peer = rb[c].at[piece(here, part)], device(a, d, e)
        if d == 0 and e == 0:
            return pltpu.make_async_copy(src, dst, own_sem.at[c, part])
        if d == 2:
            dst, peer = fb.at[c, e, piece(0, part)], device(a, 1 + 2 * e, 0)
            return remote(src, dst, ans_send.at[c, part], hop_recv.at[c, part, e], peer)
        return remote(src, dst, ans_send.at[c, part], ans_recv.at[c, part], peer)

    def forward(c, part, e):
        a = ROUTES[c][0]
        origin = lax.rem(at[a] + 3 - 2 * e, LINE) * CORES + core
        return remote(
            fb.at[c, e, piece(0, part)], rb[c].at[piece(origin, part)],
            fwd_send.at[c, part], ans_recv.at[c, part], device(a, 1 + 2 * e, e),
        )

    order = [(d, e) for d in (2, 1, 3, 0) for e in range(CORES)]

    def spread(c):
        a, u, v = ROUTES[c]
        for r in range(COARSE):
            pg[c][0][at[u], r] = blk[c, id_s[r, 0] & (SITES - 1)]
        for copy in spread_copies(c):
            copy.start()

    def cast(c):
        drain(pg[c][1].at[pl.ds(0, 3)], near_sem.at[c, 1])
        for copy in cast_copies(c)[:4]:
            copy.start()

    def pass_on(c):
        all_copies = cast_copies(c)
        for n in range(2):
            all_copies[n].wait_recv()
            all_copies[4 + n].start()

    def reply(c, part):
        a, u, v = ROUTES[c]
        n = AXES.index(a)
        drain(pg[c][0], cast_recv.at[c, 2 + part])
        first, count = PARTS[part]
        for d, e in order:
            q, to = lax.rem(at[a] + d, LINE), lax.rem(core + e, CORES)
            slot = q * CORES + to
            for place in range(first, first + count):
                back = BACKS[place]
                vv = lax.rem(at[v] + back, LINE)
                tiles = []
                for uu in range(LINE):
                    whose = {a: at[a], u: uu, v: vv}
                    owner = whose["x"] * 32 + whose["z"] * 8 + whose["y"] * 2 + core
                    for p in range(2):
                        block = line_s[n, q, to, p, 0, owner] & (SITES - 1)
                        rank = rank_s[c, vv, uu, 0, block] & (COARSE - 1)
                        tiles.append(pg[c][back][uu, rank])
                for t, tile in enumerate(tiles):
                    sb[c, slot * REPLY + place * SPOT + t] = tile
            answer(c, part, d, e).start()

    def reply_on(c, part):
        for e in range(2):
            answer(c, part, 2, e).wait_recv()
            forward(c, part, e).start()

    def transpose_in(c):
        loads[c].wait()
        for x in range(NX):
            for half in range(NY // 8):
                for k in range(KV):
                    wa[c, pl.ds(site_row(x, half * 8) + k, 8, stride=KV), :] = stage[
                        c * KV + k, x, pl.ds(half * 8, 8), :
                    ]

    def add_products(c):
        def step(g, carry):
            for m in range(4):
                b = g * 4 + m
                column = ((b >> 4) & 1) * (ROWS // 2) + (b & (NY - 1))
                values = []
                for t in range(SLOTS):
                    found = tgt_s[2 * c + (b >> 5), column + t * NY]
                    values.append(rb[c][found].astype(F32))
                values.append(blk[c, b].astype(F32))
                row = pl.ds(pl.multiple_of(b * 8, 8), 8)
                for n, (p, q) in enumerate(PAIRS):
                    product = values[p] * values[q]
                    product = product[0:8] + product[8:16]
                    if c:
                        product = product + part_sums[n, row, :]
                    part_sums[n, row, :] = product
            return carry

        lax.fori_loop(0, SITES // 4, step, 0)

    stores = []

    def transpose_out(c, w):
        for x in range(NX):
            for half in range(NY // 8):
                for k in range(KV):
                    stage[c * KV + k, x, pl.ds(half * 8, 8), :] = w[
                        c, pl.ds(site_row(x, half * 8) + k, 8, stride=KV), :
                    ]
        part = pl.ds(c * KV, KV)
        store = pltpu.make_async_copy(stage.at[part], sm_out.at[part], out_sem.at[c])
        store.start()
        stores.append(store)

    for c in range(CHUNKS):
        transpose_in(c)
        if c == 0:
            pl.semaphore_wait(barrier, greeted)
        send_faces(0, c, wa)

    for load in coef_loads:
        load.wait()
    ax, ay, az = coef[0], coef[1], coef[2]
    scale = OMEGA / (2.0 * (ax + ay + az) + coef[3])
    ka[...] = ax * scale
    kb[...] = ay * scale
    az = az * scale
    lane = lax.broadcasted_iota(jnp.int32, az.shape, 2)
    km[...] = jnp.where(lane == 0, 0.0, az)
    kp[...] = jnp.where(lane == ROWS - 1, 0.0, az)

    for load in lists:
        load.wait()
    meta[...] = jnp.zeros_like(meta)
    slots = lax.broadcasted_iota(jnp.int32, (SLOTS, NY), 0)
    for x in range(NX):
        live = (cells[0][x] == 0) & (slots < cells[1][x])
        listed = jnp.where(live, cells[2][x] * SITES + cells[3][x], -1)
        for t in range(SLOTS):
            where = pl.ds((x % 2) * (ROWS // 2) + t * NY, NY)
            meta[x // 2 : x // 2 + 1, where] = listed[t : t + 1]
        meta[2:3, pl.ds(x * NY, NY)] = cells[0][x]
    wanted, targets, rank, ids = lists_of(meta[...], at)
    idv[...] = ids
    id_copy = pltpu.make_async_copy(idv, id_s, smem_sem.at[0])
    id_copy.start()
    for n, row in enumerate((*wanted, rank)):
        pair[core, n] = row
    pair_copy().start()
    tgt[...] = jnp.zeros_like(tgt)
    for c in range(CHUNKS):
        for h in range(2):
            tgt[2 * c + h : 2 * c + h + 1] = targets[c][h]
        rb[c][EMPTY] = jnp.zeros((KV, ROWS), BF16)
    tgt_copy = pltpu.make_async_copy(tgt, tgt_s, smem_sem.at[3])
    tgt_copy.start()

    for c in range(CHUNKS):
        fill_halo(0, c, wa)
        sweep(c, wa, wb, False)
        send_faces(1, c, wb)
    pair_copy().wait_recv()
    for copy in line_copies():
        copy.start()
    for n, axis in enumerate(AXES):
        lines[n, at[axis]] = pair[...]
    for c in range(CHUNKS):
        fill_halo(1, c, wb)
        sweep(c, wb, wa, False)
        send_faces(2, c, wa)
    drain(lines.at[:, pl.ds(0, 3)], table_sem.at[0, 1])
    for copy in rank_copies():
        copy.start()
    for c, (a, u, v) in enumerate(ROUTES):
        ranks[c, at[v]] = lines[AXES.index(u), :, core, 2]
    line_copy = pltpu.make_async_copy(lines, line_s, smem_sem.at[1])
    line_copy.start()
    id_copy.wait()
    for c in range(CHUNKS):
        fill_halo(2, c, wa)
        sweep(c, wa, wb, True)
        spread(c)
    drain(ranks.at[:, pl.ds(0, 3)], table_sem.at[1, 1])
    rank_copy = pltpu.make_async_copy(ranks, rank_s, smem_sem.at[2])
    rank_copy.start()
    for c in range(CHUNKS):
        cast(c)
    line_copy.wait()
    rank_copy.wait()
    transpose_out(0, wb)
    for c in range(CHUNKS):
        pass_on(c)
    for c in range(CHUNKS):
        reply(c, 0)
    for c in range(CHUNKS):
        reply(c, 1)
        reply_on(c, 0)
    transpose_out(1, wb)
    for c in range(CHUNKS):
        reply_on(c, 1)
    transpose_out(2, wb)
    tgt_copy.wait()
    for c in range(CHUNKS):
        for part in range(len(PARTS)):
            answer(c, part, 0, 0).wait()
            drain(sb.at[c, pl.ds(0, 7 * PARTS[part][1] * SPOT)], ans_recv.at[c, part])
        add_products(c)
    for g in range(SITES // 8):
        for n in range(len(PAIRS)):
            acc = part_sums[n, pl.ds(g * 64, 8, stride=8), :]
            for h in range(1, 8):
                acc = acc + part_sums[n, pl.ds(g * 64 + h, 8, stride=8), :]
            sums[n, pl.ds(g * 8, 8), :] = acc

    drain(fxs, send_sem.at[0])
    drain(fys, send_sem.at[1])
    pair_copy().wait_send()
    drain(lines.at[:, pl.ds(0, 3)], table_sem.at[0, 0])
    drain(ranks.at[:, pl.ds(0, 3)], table_sem.at[1, 0])
    for c in range(CHUNKS):
        drain(pg[c][0].at[pl.ds(0, 3)], near_sem.at[c, 0])
        for n in range(3):
            drain(pg[c][0], cast_send.at[c, n])
        for part in range(len(PARTS)):
            count = PARTS[part][1]
            drain(sb.at[c, pl.ds(0, 7 * count * SPOT)], ans_send.at[c, part])
            drain(fb.at[c, :, pl.ds(0, count * SPOT)], fwd_send.at[c, part])
    for store in stores:
        store.wait()


def smooth(test_vectors, coef_x, coef_y, coef_z, shift, split, count, owner, local):
    vmem = pl.BlockSpec(memory_space=pltpu.VMEM)
    anywhere = pl.BlockSpec(memory_space=pl.ANY)
    cells = pltpu.VMEM((NX, NY, ROWS), F32)
    rows = pltpu.VMEM((LINE, COARSE, KV, ROWS), BF16)
    dma = pltpu.SemaphoreType.DMA
    return pl.pallas_call(
        smooth_kernel,
        out_shape=(
            jax.ShapeDtypeStruct((VECS, NX, NY, ROWS), F32),
            jax.ShapeDtypeStruct((len(PAIRS), SITES, ROWS), F32),
        ),
        in_specs=[anywhere] * 9,
        out_specs=(anywhere, vmem),
        scratch_shapes=[
            pltpu.VMEM((NX, 1, NY), jnp.int32),
            pltpu.VMEM((NX, 1, NY), jnp.int32),
            pltpu.VMEM((NX, SLOTS, NY), jnp.int32),
            pltpu.VMEM((NX, SLOTS, NY), jnp.int32),
            pltpu.VMEM((8, ROWS), jnp.int32),
            pltpu.VMEM((8, ROWS), jnp.int32),
            pltpu.SMEM((8, ROWS), jnp.int32),
            pltpu.VMEM((CHUNKS, SITES, KV, ROWS), BF16),
            *([pltpu.VMEM((EMPTY + 8, KV, ROWS), BF16)] * CHUNKS),
            pltpu.VMEM((len(PAIRS), SITES * 8, ROWS), F32),
            pltpu.VMEM((VECS, NX, NY, ROWS), F32),
            pltpu.VMEM((4, NX, NY, ROWS), F32),
            pltpu.VMEM((CHUNKS, EXT, ROWS), F32),
            pltpu.VMEM((CHUNKS, EXT, ROWS), F32),
            cells, cells, cells, cells,
            pltpu.VMEM((SWEEPS, CHUNKS, 2, NY * KV, ROWS), BF16),
            pltpu.VMEM((SWEEPS, CHUNKS, 2, NY * KV, ROWS), BF16),
            pltpu.VMEM((SWEEPS, CHUNKS, 2, NX * KV, ROWS), BF16),
            pltpu.VMEM((SWEEPS, CHUNKS, 2, NX * KV, ROWS), BF16),
            pltpu.VMEM((CORES, 3, 1, ROWS), jnp.int32),
            pltpu.VMEM((len(AXES), LINE, CORES, 3, 1, ROWS), jnp.int32),
            pltpu.VMEM((CHUNKS, LINE, LINE, 1, ROWS), jnp.int32),
            pltpu.VMEM((COARSE, ROWS), jnp.int32),
            pltpu.SMEM((len(AXES), LINE, CORES, 3, 1, ROWS), jnp.int32),
            pltpu.SMEM((CHUNKS, LINE, LINE, 1, ROWS), jnp.int32),
            pltpu.SMEM((COARSE, ROWS), jnp.int32),
            *([rows] * (LINE * CHUNKS)),
            pltpu.VMEM((CHUNKS, EMPTY, KV, ROWS), BF16),
            pltpu.VMEM((CHUNKS, CORES, REPLY, KV, ROWS), BF16),
            dma((CHUNKS,)),
            dma((4,)),
            dma((CHUNKS,)),
            dma((2,)),
            dma((SWEEPS, CHUNKS, 2)),
            dma((2,)),
            dma((2, 2)),
            dma((CHUNKS, 2)),
            dma((CHUNKS, 3)),
            dma((CHUNKS, 4)),
            dma((CHUNKS, len(PARTS))),
            dma((CHUNKS, len(PARTS))),
            dma((CHUNKS, len(PARTS), CORES)),
            dma((CHUNKS, len(PARTS))),
            dma((CHUNKS, len(PARTS))),
            dma((4,)),
            dma((4,)),
        ],
        compiler_params=pltpu.CompilerParams(
            collective_id=0, has_side_effects=True, vmem_limit_bytes=60 * 1024 * 1024
        ),
        name="smooth",
    )(test_vectors, coef_x, coef_y, coef_z, shift, split, count, owner, local)


def solve_rows(gram, rhs):
    low = [[None] * SLOTS for _ in range(SLOTS)]
    inv = []
    for r in range(SLOTS):
        scaled = []
        diag = gram[r, r]
        for c in range(r):
            rest = gram[r, c]
            for m in range(c):
                rest = rest - scaled[m] * low[c][m]
            scaled.append(rest)
            low[r][c] = rest * inv[c]
            diag = diag - rest * low[r][c]
        inv.append(1.0 / diag)
    fwd = []
    for r in range(SLOTS):
        rest = rhs[r]
        for m in range(r):
            rest = rest - low[r][m] * fwd[m]
        fwd.append(rest)
    out = [None] * SLOTS
    for r in reversed(range(SLOTS)):
        rest = fwd[r] * inv[r]
        for m in range(r + 1, SLOTS):
            rest = rest - low[m][r] * out[m]
        out[r] = rest
    return out


def solve_kernel(sums, sm_in, w_out, sm_out, copy_sem):
    move = pltpu.make_async_copy(sm_in, sm_out, copy_sem)
    move.start()
    for g in range(SITES // 8):
        total = {}
        for n, pair in enumerate(PAIRS):
            total[pair] = sums[n, pl.ds(g * 8, 8), :] * (1.0 / VECS)
            if pair[0] == pair[1]:
                total[pair] = total[pair] + RIDGE
        out = solve_rows(total, [total[s, SLOTS] for s in range(SLOTS)])
        for s in range(SLOTS):
            w_out[s, g // 2, pl.ds((g % 2) * 8, 8), :] = out[s]
    move.wait()


def fit(sums, sm):
    vmem = pl.BlockSpec(memory_space=pltpu.VMEM)
    return pl.pallas_call(
        solve_kernel,
        out_shape=(
            jax.ShapeDtypeStruct((SLOTS, NX, NY, ROWS), F32),
            jax.ShapeDtypeStruct((VECS, NX, NY, ROWS), F32),
        ),
        in_specs=[vmem, vmem],
        out_specs=(vmem, pl.BlockSpec(memory_space=pl.ANY)),
        scratch_shapes=[pltpu.SemaphoreType.DMA],
        compiler_params=pltpu.CompilerParams(vmem_limit_bytes=60 * 1024 * 1024),
        name="fit",
    )(sums, sm)


def per_device(
    test_vectors, coef_x, coef_y, coef_z, shift, cf_split, nbr_count, nbr_owner, nbr_block
):
    sm, sums = smooth(
        test_vectors, coef_x, coef_y, coef_z, shift,
        jnp.swapaxes(cf_split, 1, 2),
        jnp.swapaxes(nbr_count, 1, 2),
        jnp.transpose(nbr_owner, (0, 2, 3, 1)).reshape(NX, SLOTS, NY),
        jnp.transpose(nbr_block, (0, 2, 3, 1)).reshape(NX, SLOTS, NY),
    )
    weights, smoothed = fit(sums, sm)
    return (smoothed, weights)


def solution(mesh):
    cells = P("gx", "gy", None)
    lists = P("gx", "gy", None, None)
    vectors = P(None, "gx", "gy", None)
    return jax.shard_map(
        per_device,
        mesh=mesh,
        in_specs=(vectors, cells, cells, cells, cells, cells, cells, lists, lists),
        out_specs=(vectors, vectors),
        check_vma=False,
    )
```

```python
import jax
import jax.numpy as jnp
from jax import lax
from jax.experimental import pallas as pl
from jax.experimental.pallas import tpu as pltpu
from jax.sharding import PartitionSpec as P

SLOTS = 4
SWEEPS = 3
ROWS = 128
OMEGA = 0.8
RIDGE = 0.05
VECS = 48
CHUNKS = 3
KV = VECS // CHUNKS
NX = 4
NY = 16
SITES = NX * NY
XROW = (NY + 2) * KV
EXT = (NX + 2) * XROW
GX = 16
GY = 8
MESH = pl.DeviceIdType.MESH
F32 = jnp.float32
BF16 = jnp.bfloat16


def site_row(x, y):
    return (x + 1) * XROW + (y + 1) * KV


def solve_rows(gram, rhs):
    low = [[None] * SLOTS for _ in range(SLOTS)]
    inv = []
    for r in range(SLOTS):
        scaled = []
        diag = gram[r, r]
        for c in range(r):
            rest = gram[r, c]
            for m in range(c):
                rest = rest - scaled[m] * low[c][m]
            scaled.append(rest)
            low[r][c] = rest * inv[c]
            diag = diag - rest * low[r][c]
        inv.append(1.0 / diag)
    fwd = []
    for r in range(SLOTS):
        rest = rhs[r]
        for m in range(r):
            rest = rest - low[r][m] * fwd[m]
        fwd.append(rest)
    out = [None] * SLOTS
    for r in reversed(range(SLOTS)):
        rest = fwd[r] * inv[r]
        for m in range(r + 1, SLOTS):
            rest = rest - low[m][r] * out[m]
        out[r] = rest
    return out


PAIRS = [(s, t) for s in range(SLOTS) for t in range(s + 1)] + [(s, SLOTS) for s in range(SLOTS)]
AXES = "xyz"
LINE = 4
CORES = 2
COARSE = 16
PLANE = LINE * LINE
ROUTES = (("x", "z", "y"), ("y", "x", "z"), ("z", "y", "x"))
BACKS = (0, 1, 3, 2)
EMPTY = LINE * CORES * PLANE * 2
SPOT = 2 * LINE
REPLY = PLANE * 2
PARTS = ((0, 3), (3, 1))


def lists_of(meta, here):
    lane = lax.broadcasted_iota(jnp.int32, (ROWS, ROWS), 1)
    sub = lax.broadcasted_iota(jnp.int32, (ROWS, ROWS), 0)
    diag = lane == sub
    none = 1 << 20

    def column(row):
        return jnp.sum(jnp.where(diag, row, 0), axis=1, keepdims=True)

    def line(col):
        return jnp.sum(jnp.where(diag, col, 0), axis=0, keepdims=True)

    members, keys, owners = [], [], []
    for h in range(2):
        entry = meta[h : h + 1]
        owner = entry >> 6
        key = (lane[:1] + h * ROWS) * SITES + (entry & (SITES - 1))
        owners.append(owner)
        keys.append(key)
        members.append(owner == sub)
    first = jnp.minimum(*[jnp.where(m, k, none) for m, k in zip(members, keys)])
    first = jnp.min(first, axis=1, keepdims=True)
    first = jnp.where(first >= none, 0, first)
    second = jnp.maximum(*[jnp.where(m, k, 0) for m, k in zip(members, keys)])
    second = jnp.max(second, axis=1, keepdims=True)
    wanted = [line(v) & (SITES - 1) for v in (first, second)]
    targets = [[] for _ in ROUTES]
    for h in range(2):
        own = owners[h]
        at_first = jnp.sum(jnp.where(members[h], first, 0), axis=0, keepdims=True)
        place = jnp.where(keys[h] == at_first, 0, 1)
        at = {"x": (own >> 5) & 3, "z": (own >> 3) & 3, "y": (own >> 1) & 3}
        for c, (a, u, v) in enumerate(ROUTES):
            back = (at[v] - here[v]) & 3
            spot = jnp.where(back == 2, 3, jnp.where(back == 3, 2, back))
            slot = ((at[a] * CORES + (own & 1)) * PLANE + spot * LINE + at[u]) * 2 + place
            targets[c].append(jnp.where(own < 0, EMPTY, slot))
    coarse = meta[2:3]
    rank = jnp.sum(jnp.where(sub < lane, column(coarse), 0), axis=0, keepdims=True)
    hit = (rank == sub[:COARSE]) & (coarse > 0)
    ids = jnp.sum(jnp.where(hit, lane[:COARSE], 0), axis=1, keepdims=True)
    ids = jnp.broadcast_to(ids, (COARSE, ROWS))
    rank = jnp.minimum(rank, COARSE - 1)
    return wanted, targets, rank, ids


def smooth_kernel(
    tv, cx, cy, cz, sh, split, count, owner, local, sm_out, w_out,
    split_v, count_v, owner_v, local_v, meta, tgt, tgt_s, blk, rb0, rb1, rb2, part_sums,
    stage, coef, wa, wb, ka, kb, km, kp, fxs, fxr, fys, fyr,
    pair, lines, ranks, idv, line_s, rank_s, id_s, p00, p01, p02, p03, p10, p11, p12, p13, p20, p21, p22, p23, sb, fb,
    in_sem, coef_sem, out_sem, send_sem, recv_sem, pair_sem, table_sem,
    near_sem, cast_send, cast_recv, ans_send, ans_recv, hop_recv, fwd_send, own_sem, smem_sem, list_sem,
):
    cells = (split_v, count_v, owner_v, local_v)
    rb = (rb0, rb1, rb2)
    pg = ((p00, p01, p02, p03), (p10, p11, p12, p13), (p20, p21, p22, p23))
    i = lax.axis_index("gx")
    j = lax.axis_index("gy")
    core = lax.rem(j, CORES)
    at = {"x": i // LINE, "z": lax.rem(i, LINE), "y": j // CORES}
    peers = (
        (lax.rem(i + GX - 1, GX), j),
        (lax.rem(i + 1, GX), j),
        (i, lax.rem(j + GY - 1, GY)),
        (i, lax.rem(j + 1, GY)),
    )

    def device(axis, d, e):
        moved = dict(at)
        moved[axis] = lax.rem(at[axis] + d, LINE)
        return (moved["x"] * LINE + moved["z"], moved["y"] * CORES + lax.rem(core + e, CORES))

    def remote(src, dst, send, recv, peer):
        return pltpu.make_async_remote_copy(
            src_ref=src, dst_ref=dst, send_sem=send, recv_sem=recv,
            device_id=peer, device_id_type=MESH,
        )

    loads = []
    for c in range(CHUNKS):
        part = pl.ds(c * KV, KV)
        loads.append(pltpu.make_async_copy(tv.at[part], stage.at[part], in_sem.at[c]))
    loads[0].start()
    barrier = pltpu.get_barrier_semaphore()
    for peer in peers[:2]:
        pl.semaphore_signal(barrier, inc=1, device_id=peer, device_id_type=MESH)
    pl.semaphore_signal(barrier, inc=1, device_id=device("x", 0, 1), device_id_type=MESH)
    for axis in AXES:
        for d in range(1, LINE):
            for e in range(CORES):
                pl.semaphore_signal(
                    barrier, inc=1, device_id=device(axis, d, e), device_id_type=MESH
                )
    greeted = 3 + len(AXES) * (LINE - 1) * CORES
    for load in loads[1:]:
        load.start()
    coef_loads = []
    for n, part in enumerate((cx, cy, cz, sh)):
        load = pltpu.make_async_copy(part, coef.at[n], coef_sem.at[n])
        load.start()
        coef_loads.append(load)
    lists = []
    for n, part in enumerate((split, count, owner, local)):
        load = pltpu.make_async_copy(part, cells[n], list_sem.at[n])
        load.start()
        lists.append(load)

    keep = (
        (i > 0).astype(F32),
        (i < GX - 1).astype(F32),
        (j > 0).astype(F32),
        (j < GY - 1).astype(F32),
    )

    def drain(ref, sem):
        pltpu.make_async_copy(ref, ref, sem).wait()

    def copies(s, c):
        out = []
        for d in range(4):
            src, dst = (fxs, fxr) if d < 2 else (fys, fyr)
            out.append(
                remote(
                    src.at[s, c, d % 2], dst.at[s, c, 1 - d % 2],
                    send_sem.at[d // 2], recv_sem.at[s, c, d // 2], peers[d],
                )
            )
        return out

    def send_faces(s, c, w):
        for side in range(2):
            x = side * (NX - 1)
            fxs[s, c, side] = w[c, pl.ds(site_row(x, 0), NY * KV)].astype(BF16)
            y = side * (NY - 1)
            for x in range(NX):
                fys[s, c, side, pl.ds(x * KV, KV)] = w[c, pl.ds(site_row(x, y), KV)].astype(BF16)
        for copy in copies(s, c):
            copy.start()

    def fill_halo(s, c, w):
        drain(fxr.at[s, c], recv_sem.at[s, c, 0])
        drain(fyr.at[s, c], recv_sem.at[s, c, 1])
        for side in range(2):
            x = -1 if side == 0 else NX
            w[c, pl.ds(site_row(x, 0), NY * KV)] = fxr[s, c, side].astype(F32) * keep[side]
            y = -1 if side == 0 else NY
            for x in range(NX):
                w[c, pl.ds(site_row(x, y), KV)] = (
                    fyr[s, c, side, pl.ds(x * KV, KV)].astype(F32) * keep[2 + side]
                )

    def sweep(c, src, dst, last):
        def plane(x, carry):
            base = pl.multiple_of(x * XROW, 16)

            def cell(dx, y):
                return src[c, pl.ds(base + site_row(dx, y), KV)]

            below, here = cell(0, -1), cell(0, 0)
            for y in range(NY):
                above = cell(0, y + 1)
                row = slice(y, y + 1)
                new = (
                    ka[x, row] * (cell(-1, y) + cell(1, y))
                    + kb[x, row] * (below + above)
                    + km[x, row] * pltpu.roll(here, 1, 1)
                    + kp[x, row] * pltpu.roll(here, ROWS - 1, 1)
                    + (1.0 - OMEGA) * here
                )
                dst[c, pl.ds(base + site_row(0, y), KV)] = new
                if last:
                    blk[c, x * NY + y] = new.astype(BF16)
                below, here = here, above
            return carry

        lax.fori_loop(0, NX, plane, 0)

    def pair_copy():
        slot = pair.at[core]
        return remote(slot, slot, pair_sem.at[0], pair_sem.at[1], device("x", 0, 1))

    def line_copies():
        return [
            remote(
                pair, lines.at[n, at[axis]], table_sem.at[0, 0], table_sem.at[0, 1],
                device(axis, d, 0),
            )
            for n, axis in enumerate(AXES)
            for d in range(1, LINE)
        ]

    def rank_copies():
        out = []
        for c, (a, u, v) in enumerate(ROUTES):
            src = lines.at[AXES.index(u), :, core, 2]
            for d in range(1, LINE):
                out.append(
                    remote(
                        src, ranks.at[c, at[v]], table_sem.at[1, 0], table_sem.at[1, 1],
                        device(v, d, 0),
                    )
                )
        return out

    def spread_copies(c):
        a, u, v = ROUTES[c]
        ref = pg[c][0].at[at[u]]
        return [
            remote(ref, ref, near_sem.at[c, 0], near_sem.at[c, 1], device(u, d, 0))
            for d in (2, 1, 3)
        ]

    def cast_copies(c):
        a, u, v = ROUTES[c]
        plan = ((0, 0, 3, 1), (0, 1, 1, 3), (0, 1, 3, 1), (0, 0, 1, 3), (3, 0, 2, 1), (1, 1, 2, 3))
        return [
            remote(
                pg[c][src].at[pl.ds(half * 2, 2)], pg[c][dst].at[pl.ds(half * 2, 2)],
                cast_send.at[c, n // 2], cast_recv.at[c, min(n, 2 + n // 4)], device(v, d, 0),
            )
            for n, (src, half, dst, d) in enumerate(plan)
        ]

    def piece(slot, part):
        first, count = PARTS[part]
        return pl.ds(slot * REPLY + first * SPOT, count * SPOT)

    def answer(c, part, d, e):
        a = ROUTES[c][0]
        slot = lax.rem(at[a] + d, LINE) * CORES + lax.rem(core + e, CORES)
        here = at[a] * CORES + core
        src = sb.at[c, piece(slot, part)]
        dst, peer = rb[c].at[piece(here, part)], device(a, d, e)
        if d == 0 and e == 0:
            return pltpu.make_async_copy(src, dst, own_sem.at[c, part])
        if d == 2 and part == 0:
            dst, peer = fb.at[c, e, piece(0, part)], device(a, 1 + 2 * e, 0)
            return remote(src, dst, ans_send.at[c, part], hop_recv.at[c, e], peer)
        return remote(src, dst, ans_send.at[c, part], ans_recv.at[c, part], peer)

    def forward(c, part, e):
        a = ROUTES[c][0]
        origin = lax.rem(at[a] + 3 - 2 * e, LINE) * CORES + core
        return remote(
            fb.at[c, e, piece(0, part)], rb[c].at[piece(origin, part)],
            fwd_send.at[c], ans_recv.at[c, part], device(a, 1 + 2 * e, e),
        )

    order = [(d, e) for d in (2, 1, 3, 0) for e in range(CORES)]

    def spread(c):
        a, u, v = ROUTES[c]
        for r in range(COARSE):
            pg[c][0][at[u], r] = blk[c, id_s[r, 0] & (SITES - 1)]
        for copy in spread_copies(c):
            copy.start()

    def cast(c):
        drain(pg[c][1].at[pl.ds(0, 3)], near_sem.at[c, 1])
        for copy in cast_copies(c)[:4]:
            copy.start()

    def pass_on(c):
        all_copies = cast_copies(c)
        for n in range(2):
            all_copies[n].wait_recv()
            all_copies[4 + n].start()

    def reply(c, part):
        a, u, v = ROUTES[c]
        n = AXES.index(a)
        drain(pg[c][0], cast_recv.at[c, 2 + part])
        first, count = PARTS[part]
        for d, e in order:
            q, to = lax.rem(at[a] + d, LINE), lax.rem(core + e, CORES)
            slot = q * CORES + to
            for place in range(first, first + count):
                back = BACKS[place]
                vv = lax.rem(at[v] + back, LINE)
                tiles = []
                for uu in range(LINE):
                    whose = {a: at[a], u: uu, v: vv}
                    owner = whose["x"] * 32 + whose["z"] * 8 + whose["y"] * 2 + core
                    for p in range(2):
                        block = line_s[n, q, to, p, 0, owner] & (SITES - 1)
                        rank = rank_s[c, vv, uu, 0, block] & (COARSE - 1)
                        tiles.append(pg[c][back][uu, rank])
                for t, tile in enumerate(tiles):
                    sb[c, slot * REPLY + place * SPOT + t] = tile
            answer(c, part, d, e).start()

    def reply_on(c, part):
        for e in range(2):
            answer(c, part, 2, e).wait_recv()
            forward(c, part, e).start()

    def transpose_in(c):
        loads[c].wait()
        for x in range(NX):
            for half in range(NY // 8):
                for k in range(KV):
                    wa[c, pl.ds(site_row(x, half * 8) + k, 8, stride=KV), :] = stage[
                        c * KV + k, x, pl.ds(half * 8, 8), :
                    ]

    def products(c, b):
        column = ((b >> 4) & 1) * (ROWS // 2) + (b & (NY - 1))
        values = []
        for t in range(SLOTS):
            found = tgt_s[2 * c + (b >> 5), column + t * NY]
            values.append(rb[c][found].astype(F32))
        values.append(blk[c, b].astype(F32))
        for n, (p, q) in enumerate(PAIRS):
            product = values[p] * values[q]
            product = product[0:8] + product[8:16]
            row = pl.ds(pl.multiple_of(b * 8, 8), 8)
            if c:
                product = product + part_sums[n, row, :]
            part_sums[n, row, :] = product

    def add_products(c):
        def step(g, carry):
            for m in range(4):
                products(c, g * 4 + m)
            return carry

        lax.fori_loop(0, SITES // 4, step, 0)

    def finish():
        sub = lax.broadcasted_iota(jnp.int32, (8, ROWS), 0)
        low4, low2, low1 = sub < 4, (sub & 2) == 0, (sub & 1) == 0

        def merge(first, second, keep_first, shift):
            first = first + pltpu.roll(first, 8 - shift, 0)
            second = second + pltpu.roll(second, shift, 0)
            return jnp.where(keep_first, first, second)

        def group(g, carry):
            total = {}
            for n, pair in enumerate(PAIRS):
                rows = [
                    part_sums[n, pl.ds(pl.multiple_of(g * 64, 64) + 8 * m, 8), :]
                    for m in range(8)
                ]
                rows = [
                    jnp.where(low4, rows[m], rows[m + 4])
                    + pltpu.roll(jnp.where(low4, rows[m + 4], rows[m]), 4, 0)
                    for m in range(4)
                ]
                rows = [merge(rows[m], rows[m + 2], low2, 2) for m in range(2)]
                total[pair] = merge(rows[0], rows[1], low1, 1) * (1.0 / VECS)
                if pair[0] == pair[1]:
                    total[pair] = total[pair] + RIDGE
            out = solve_rows(total, [total[s, SLOTS] for s in range(SLOTS)])
            for s in range(SLOTS):
                w_out[s, pl.ds(pl.multiple_of(g * 8, 8), 8), :] = out[s]
            return carry

        lax.fori_loop(0, SITES // 8, group, 0)

    stores = []

    def transpose_out(c, w):
        for x in range(NX):
            for half in range(NY // 8):
                for k in range(KV):
                    stage[c * KV + k, x, pl.ds(half * 8, 8), :] = w[
                        c, pl.ds(site_row(x, half * 8) + k, 8, stride=KV), :
                    ]
        part = pl.ds(c * KV, KV)
        store = pltpu.make_async_copy(stage.at[part], sm_out.at[part], out_sem.at[c])
        store.start()
        stores.append(store)

    for c in range(CHUNKS):
        transpose_in(c)
        if c == 0:
            pl.semaphore_wait(barrier, greeted)
        send_faces(0, c, wa)

    for load in coef_loads:
        load.wait()
    ax, ay, az = coef[0], coef[1], coef[2]
    scale = OMEGA / (2.0 * (ax + ay + az) + coef[3])
    ka[...] = ax * scale
    kb[...] = ay * scale
    az = az * scale
    lane = lax.broadcasted_iota(jnp.int32, az.shape, 2)
    km[...] = jnp.where(lane == 0, 0.0, az)
    kp[...] = jnp.where(lane == ROWS - 1, 0.0, az)

    for load in lists:
        load.wait()
    meta[...] = jnp.zeros_like(meta)
    slots = lax.broadcasted_iota(jnp.int32, (SLOTS, NY), 0)
    for x in range(NX):
        live = (cells[0][x] == 0) & (slots < cells[1][x])
        listed = jnp.where(live, cells[2][x] * SITES + cells[3][x], -1)
        for t in range(SLOTS):
            where = pl.ds((x % 2) * (ROWS // 2) + t * NY, NY)
            meta[x // 2 : x // 2 + 1, where] = listed[t : t + 1]
        meta[2:3, pl.ds(x * NY, NY)] = cells[0][x]
    wanted, targets, rank, ids = lists_of(meta[...], at)
    idv[...] = ids
    id_copy = pltpu.make_async_copy(idv, id_s, smem_sem.at[0])
    id_copy.start()
    for n, row in enumerate((*wanted, rank)):
        pair[core, n] = row
    pair_copy().start()
    tgt[...] = jnp.zeros_like(tgt)
    for c in range(CHUNKS):
        for h in range(2):
            tgt[2 * c + h : 2 * c + h + 1] = targets[c][h]
        rb[c][EMPTY] = jnp.zeros((KV, ROWS), BF16)
    tgt_copy = pltpu.make_async_copy(tgt, tgt_s, smem_sem.at[3])
    tgt_copy.start()

    for c in range(CHUNKS):
        fill_halo(0, c, wa)
        sweep(c, wa, wb, False)
        send_faces(1, c, wb)
    pair_copy().wait_recv()
    for copy in line_copies():
        copy.start()
    for n, axis in enumerate(AXES):
        lines[n, at[axis]] = pair[...]
    for c in range(CHUNKS):
        fill_halo(1, c, wb)
        sweep(c, wb, wa, False)
        send_faces(2, c, wa)
    drain(lines.at[:, pl.ds(0, 3)], table_sem.at[0, 1])
    for copy in rank_copies():
        copy.start()
    for c, (a, u, v) in enumerate(ROUTES):
        ranks[c, at[v]] = lines[AXES.index(u), :, core, 2]
    line_copy = pltpu.make_async_copy(lines, line_s, smem_sem.at[1])
    line_copy.start()
    id_copy.wait()
    for c in range(CHUNKS):
        fill_halo(2, c, wa)
        sweep(c, wa, wb, True)
        spread(c)
    drain(ranks.at[:, pl.ds(0, 3)], table_sem.at[1, 1])
    rank_copy = pltpu.make_async_copy(ranks, rank_s, smem_sem.at[2])
    rank_copy.start()
    for c in range(CHUNKS):
        cast(c)
    line_copy.wait()
    rank_copy.wait()
    transpose_out(0, wb)
    for c in range(CHUNKS):
        pass_on(c)
    for c in range(CHUNKS):
        reply(c, 0)
    for c in range(CHUNKS):
        reply_on(c, 0)
        reply(c, 1)
    transpose_out(1, wb)
    transpose_out(2, wb)
    tgt_copy.wait()
    for c in range(CHUNKS):
        for part in range(len(PARTS)):
            answer(c, part, 0, 0).wait()
            drain(sb.at[c, pl.ds(0, 7 * PARTS[part][1] * SPOT)], ans_recv.at[c, part])
        add_products(c)
    finish()

    drain(fxs, send_sem.at[0])
    drain(fys, send_sem.at[1])
    pair_copy().wait_send()
    drain(lines.at[:, pl.ds(0, 3)], table_sem.at[0, 0])
    drain(ranks.at[:, pl.ds(0, 3)], table_sem.at[1, 0])
    for c in range(CHUNKS):
        drain(pg[c][0].at[pl.ds(0, 3)], near_sem.at[c, 0])
        for n in range(3):
            drain(pg[c][0], cast_send.at[c, n])
        for part in range(len(PARTS)):
            count = PARTS[part][1]
            drain(sb.at[c, pl.ds(0, 7 * count * SPOT)], ans_send.at[c, part])
        drain(fb.at[c, :, pl.ds(0, PARTS[0][1] * SPOT)], fwd_send.at[c])
    for store in stores:
        store.wait()


def smooth(test_vectors, coef_x, coef_y, coef_z, shift, split, count, owner, local):
    vmem = pl.BlockSpec(memory_space=pltpu.VMEM)
    anywhere = pl.BlockSpec(memory_space=pl.ANY)
    cells = pltpu.VMEM((NX, NY, ROWS), F32)
    rows = pltpu.VMEM((LINE, COARSE, KV, ROWS), BF16)
    dma = pltpu.SemaphoreType.DMA
    return pl.pallas_call(
        smooth_kernel,
        out_shape=(
            jax.ShapeDtypeStruct((VECS, NX, NY, ROWS), F32),
            jax.ShapeDtypeStruct((SLOTS, SITES, ROWS), F32),
        ),
        in_specs=[anywhere] * 9,
        out_specs=(anywhere, vmem),
        scratch_shapes=[
            pltpu.VMEM((NX, 1, NY), jnp.int32),
            pltpu.VMEM((NX, 1, NY), jnp.int32),
            pltpu.VMEM((NX, SLOTS, NY), jnp.int32),
            pltpu.VMEM((NX, SLOTS, NY), jnp.int32),
            pltpu.VMEM((8, ROWS), jnp.int32),
            pltpu.VMEM((8, ROWS), jnp.int32),
            pltpu.SMEM((8, ROWS), jnp.int32),
            pltpu.VMEM((CHUNKS, SITES, KV, ROWS), BF16),
            *([pltpu.VMEM((EMPTY + 8, KV, ROWS), BF16)] * CHUNKS),
            pltpu.VMEM((len(PAIRS), SITES * 8, ROWS), F32),
            pltpu.VMEM((VECS, NX, NY, ROWS), F32),
            pltpu.VMEM((4, NX, NY, ROWS), F32),
            pltpu.VMEM((CHUNKS, EXT, ROWS), F32),
            pltpu.VMEM((CHUNKS, EXT, ROWS), F32),
            cells, cells, cells, cells,
            pltpu.VMEM((SWEEPS, CHUNKS, 2, NY * KV, ROWS), BF16),
            pltpu.VMEM((SWEEPS, CHUNKS, 2, NY * KV, ROWS), BF16),
            pltpu.VMEM((SWEEPS, CHUNKS, 2, NX * KV, ROWS), BF16),
            pltpu.VMEM((SWEEPS, CHUNKS, 2, NX * KV, ROWS), BF16),
            pltpu.VMEM((CORES, 3, 1, ROWS), jnp.int32),
            pltpu.VMEM((len(AXES), LINE, CORES, 3, 1, ROWS), jnp.int32),
            pltpu.VMEM((CHUNKS, LINE, LINE, 1, ROWS), jnp.int32),
            pltpu.VMEM((COARSE, ROWS), jnp.int32),
            pltpu.SMEM((len(AXES), LINE, CORES, 3, 1, ROWS), jnp.int32),
            pltpu.SMEM((CHUNKS, LINE, LINE, 1, ROWS), jnp.int32),
            pltpu.SMEM((COARSE, ROWS), jnp.int32),
            *([rows] * (LINE * CHUNKS)),
            pltpu.VMEM((CHUNKS, EMPTY, KV, ROWS), BF16),
            pltpu.VMEM((CHUNKS, CORES, REPLY, KV, ROWS), BF16),
            dma((CHUNKS,)),
            dma((4,)),
            dma((CHUNKS,)),
            dma((2,)),
            dma((SWEEPS, CHUNKS, 2)),
            dma((2,)),
            dma((2, 2)),
            dma((CHUNKS, 2)),
            dma((CHUNKS, 3)),
            dma((CHUNKS, 4)),
            dma((CHUNKS, len(PARTS))),
            dma((CHUNKS, len(PARTS))),
            dma((CHUNKS, CORES)),
            dma((CHUNKS,)),
            dma((CHUNKS, len(PARTS))),
            dma((4,)),
            dma((4,)),
        ],
        compiler_params=pltpu.CompilerParams(
            collective_id=0, has_side_effects=True, vmem_limit_bytes=60 * 1024 * 1024
        ),
        name="smooth",
    )(test_vectors, coef_x, coef_y, coef_z, shift, split, count, owner, local)


def pass_kernel(w_in, sm_in, w_out, sm_out, w_hold, sm_hold, in_sem, out_sem):
    parts = [(w_in, w_hold, w_out)]
    for c in range(CHUNKS):
        part = pl.ds(c * KV, KV)
        parts.append((sm_in.at[part], sm_hold.at[part], sm_out.at[part]))
    ins = [pltpu.make_async_copy(a, b, in_sem.at[n]) for n, (a, b, _) in enumerate(parts)]
    outs = [pltpu.make_async_copy(b, d, out_sem.at[n]) for n, (_, b, d) in enumerate(parts)]
    for copy in ins:
        copy.start()
    for load, store in zip(ins, outs):
        load.wait()
        store.start()
    for store in outs:
        store.wait()


def pass_on_results(weights, sm):
    anywhere = pl.BlockSpec(memory_space=pl.ANY)
    dma = pltpu.SemaphoreType.DMA
    return pl.pallas_call(
        pass_kernel,
        out_shape=(
            jax.ShapeDtypeStruct(weights.shape, F32),
            jax.ShapeDtypeStruct(sm.shape, F32),
        ),
        in_specs=[anywhere, anywhere],
        out_specs=(anywhere, anywhere),
        scratch_shapes=[
            pltpu.VMEM(weights.shape, F32),
            pltpu.VMEM(sm.shape, F32),
            dma((CHUNKS + 1,)),
            dma((CHUNKS + 1,)),
        ],
        compiler_params=pltpu.CompilerParams(vmem_limit_bytes=60 * 1024 * 1024),
        name="fit",
    )(weights, sm)


def per_device(
    test_vectors, coef_x, coef_y, coef_z, shift, cf_split, nbr_count, nbr_owner, nbr_block
):
    sm, weights = smooth(
        test_vectors, coef_x, coef_y, coef_z, shift,
        jnp.swapaxes(cf_split, 1, 2),
        jnp.swapaxes(nbr_count, 1, 2),
        jnp.transpose(nbr_owner, (0, 2, 3, 1)).reshape(NX, SLOTS, NY),
        jnp.transpose(nbr_block, (0, 2, 3, 1)).reshape(NX, SLOTS, NY),
    )
    weights, smoothed = pass_on_results(weights.reshape(SLOTS, NX, NY, ROWS), sm)
    return (smoothed, weights)


def solution(mesh):
    cells = P("gx", "gy", None)
    lists = P("gx", "gy", None, None)
    vectors = P(None, "gx", "gy", None)
    return jax.shard_map(
        per_device,
        mesh=mesh,
        in_specs=(vectors, cells, cells, cells, cells, cells, cells, lists, lists),
        out_specs=(vectors, vectors),
        check_vma=False,
    )
```

```python
import jax
import jax.numpy as jnp
from jax import lax
from jax.experimental import pallas as pl
from jax.experimental.pallas import tpu as pltpu
from jax.sharding import PartitionSpec as P

SLOTS = 4
SWEEPS = 3
ROWS = 128
OMEGA = 0.8
RIDGE = 0.05
VECS = 48
CHUNKS = 3
KV = VECS // CHUNKS
NX = 4
NY = 16
SITES = NX * NY
XROW = (NY + 2) * KV
EXT = (NX + 2) * XROW
GX = 16
GY = 8
MESH = pl.DeviceIdType.MESH
F32 = jnp.float32
BF16 = jnp.bfloat16


def site_row(x, y):
    return (x + 1) * XROW + (y + 1) * KV


def solve_rows(gram, rhs):
    low = [[None] * SLOTS for _ in range(SLOTS)]
    inv = []
    for r in range(SLOTS):
        scaled = []
        diag = gram[r, r]
        for c in range(r):
            rest = gram[r, c]
            for m in range(c):
                rest = rest - scaled[m] * low[c][m]
            scaled.append(rest)
            low[r][c] = rest * inv[c]
            diag = diag - rest * low[r][c]
        inv.append(1.0 / diag)
    fwd = []
    for r in range(SLOTS):
        rest = rhs[r]
        for m in range(r):
            rest = rest - low[r][m] * fwd[m]
        fwd.append(rest)
    out = [None] * SLOTS
    for r in reversed(range(SLOTS)):
        rest = fwd[r] * inv[r]
        for m in range(r + 1, SLOTS):
            rest = rest - low[m][r] * out[m]
        out[r] = rest
    return out


PAIRS = [(s, t) for s in range(SLOTS) for t in range(s + 1)] + [(s, SLOTS) for s in range(SLOTS)]
AXES = "xyz"
LINE = 4
CORES = 2
COARSE = 16
PLANE = LINE * LINE
ROUTES = (("x", "z", "y"), ("y", "x", "z"), ("z", "y", "x"))
BACKS = (0, 1, 3, 2)
EMPTY = LINE * CORES * PLANE * 2
SPOT = 2 * LINE
GRAM_ORDER = (1, 2, 0)
REPLY = PLANE * 2
PARTS = ((0, 3), (3, 1))


def lists_of(meta, here):
    lane = lax.broadcasted_iota(jnp.int32, (ROWS, ROWS), 1)
    sub = lax.broadcasted_iota(jnp.int32, (ROWS, ROWS), 0)
    diag = lane == sub
    none = 1 << 20

    def column(row):
        return jnp.sum(jnp.where(diag, row, 0), axis=1, keepdims=True)

    def line(col):
        return jnp.sum(jnp.where(diag, col, 0), axis=0, keepdims=True)

    members, keys, owners = [], [], []
    for h in range(2):
        entry = meta[h : h + 1]
        owner = entry >> 6
        key = (lane[:1] + h * ROWS) * SITES + (entry & (SITES - 1))
        owners.append(owner)
        keys.append(key)
        members.append(owner == sub)
    first = jnp.minimum(*[jnp.where(m, k, none) for m, k in zip(members, keys)])
    first = jnp.min(first, axis=1, keepdims=True)
    first = jnp.where(first >= none, 0, first)
    second = jnp.maximum(*[jnp.where(m, k, 0) for m, k in zip(members, keys)])
    second = jnp.max(second, axis=1, keepdims=True)
    wanted = [line(v) & (SITES - 1) for v in (first, second)]
    targets = [[] for _ in ROUTES]
    for h in range(2):
        own = owners[h]
        at_first = jnp.sum(jnp.where(members[h], first, 0), axis=0, keepdims=True)
        place = jnp.where(keys[h] == at_first, 0, 1)
        at = {"x": (own >> 5) & 3, "z": (own >> 3) & 3, "y": (own >> 1) & 3}
        for c, (a, u, v) in enumerate(ROUTES):
            back = (at[v] - here[v]) & 3
            spot = jnp.where(back == 2, 3, jnp.where(back == 3, 2, back))
            slot = ((at[a] * CORES + (own & 1)) * PLANE + spot * LINE + ((at[u] - here[u]) & 3)) * 2 + place
            targets[c].append(jnp.where(own < 0, EMPTY, slot))
    coarse = meta[2:3]
    rank = jnp.sum(jnp.where(sub < lane, column(coarse), 0), axis=0, keepdims=True)
    hit = (rank == sub[:COARSE]) & (coarse > 0)
    ids = jnp.sum(jnp.where(hit, lane[:COARSE], 0), axis=1, keepdims=True)
    ids = jnp.broadcast_to(ids, (COARSE, ROWS))
    rank = jnp.minimum(rank, COARSE - 1)
    return wanted, targets, rank, ids


def smooth_kernel(
    tv, cx, cy, cz, sh, split, count, owner, local, sm_out, w_out,
    split_v, count_v, owner_v, local_v, meta, tgt, tgt_s, blk, rb0, rb1, rb2, part_sums,
    stage, coef, wa, wb, ka, kb, km, kp, fxs, fxr, fys, fyr,
    pair, lines, ranks, idv, line_s, rank_s, id_s, tile_s, p00, p01, p02, p03, p10, p11, p12, p13, p20, p21, p22, p23, sb, fb,
    in_sem, coef_sem, out_sem, send_sem, recv_sem, pair_sem, table_sem,
    near_sem, cast_send, cast_recv, ans_send, ans_recv, hop_recv, fwd_send, own_sem, smem_sem, list_sem,
):
    cells = (split_v, count_v, owner_v, local_v)
    rb = (rb0, rb1, rb2)
    pg = ((p00, p01, p02, p03), (p10, p11, p12, p13), (p20, p21, p22, p23))
    i = lax.axis_index("gx")
    j = lax.axis_index("gy")
    core = lax.rem(j, CORES)
    at = {"x": i // LINE, "z": lax.rem(i, LINE), "y": j // CORES}
    peers = (
        (lax.rem(i + GX - 1, GX), j),
        (lax.rem(i + 1, GX), j),
        (i, lax.rem(j + GY - 1, GY)),
        (i, lax.rem(j + 1, GY)),
    )

    def device(axis, d, e):
        moved = dict(at)
        moved[axis] = lax.rem(at[axis] + d, LINE)
        return (moved["x"] * LINE + moved["z"], moved["y"] * CORES + lax.rem(core + e, CORES))

    def remote(src, dst, send, recv, peer):
        return pltpu.make_async_remote_copy(
            src_ref=src, dst_ref=dst, send_sem=send, recv_sem=recv,
            device_id=peer, device_id_type=MESH,
        )

    loads = []
    for c in range(CHUNKS):
        part = pl.ds(c * KV, KV)
        loads.append(pltpu.make_async_copy(tv.at[part], stage.at[part], in_sem.at[c]))
    loads[0].start()
    barrier = pltpu.get_barrier_semaphore()
    for peer in peers[:2]:
        pl.semaphore_signal(barrier, inc=1, device_id=peer, device_id_type=MESH)
    pl.semaphore_signal(barrier, inc=1, device_id=device("x", 0, 1), device_id_type=MESH)
    for axis in AXES:
        for d in range(1, LINE):
            for e in range(CORES):
                pl.semaphore_signal(
                    barrier, inc=1, device_id=device(axis, d, e), device_id_type=MESH
                )
    greeted = 3 + len(AXES) * (LINE - 1) * CORES
    for load in loads[1:]:
        load.start()
    coef_loads = []
    for n, part in enumerate((cx, cy, cz, sh)):
        load = pltpu.make_async_copy(part, coef.at[n], coef_sem.at[n])
        load.start()
        coef_loads.append(load)
    lists = []
    for n, part in enumerate((split, count, owner, local)):
        load = pltpu.make_async_copy(part, cells[n], list_sem.at[n])
        load.start()
        lists.append(load)

    keep = (
        (i > 0).astype(F32),
        (i < GX - 1).astype(F32),
        (j > 0).astype(F32),
        (j < GY - 1).astype(F32),
    )

    def drain(ref, sem):
        pltpu.make_async_copy(ref, ref, sem).wait()

    def copies(s, c):
        out = []
        for d in range(4):
            src, dst = (fxs, fxr) if d < 2 else (fys, fyr)
            out.append(
                remote(
                    src.at[s, c, d % 2], dst.at[s, c, 1 - d % 2],
                    send_sem.at[d // 2], recv_sem.at[s, c, d // 2], peers[d],
                )
            )
        return out

    def send_faces(s, c, w):
        for side in range(2):
            x = side * (NX - 1)
            fxs[s, c, side] = w[c, pl.ds(site_row(x, 0), NY * KV)].astype(BF16)
            y = side * (NY - 1)
            for x in range(NX):
                fys[s, c, side, pl.ds(x * KV, KV)] = w[c, pl.ds(site_row(x, y), KV)].astype(BF16)
        for copy in copies(s, c):
            copy.start()

    def fill_halo(s, c, w):
        drain(fxr.at[s, c], recv_sem.at[s, c, 0])
        drain(fyr.at[s, c], recv_sem.at[s, c, 1])
        for side in range(2):
            x = -1 if side == 0 else NX
            w[c, pl.ds(site_row(x, 0), NY * KV)] = fxr[s, c, side].astype(F32) * keep[side]
            y = -1 if side == 0 else NY
            for x in range(NX):
                w[c, pl.ds(site_row(x, y), KV)] = (
                    fyr[s, c, side, pl.ds(x * KV, KV)].astype(F32) * keep[2 + side]
                )

    def sweep(c, src, dst, last):
        def plane(x, carry):
            base = pl.multiple_of(x * XROW, 16)

            def cell(dx, y):
                return src[c, pl.ds(base + site_row(dx, y), KV)]

            below, here = cell(0, -1), cell(0, 0)
            for y in range(NY):
                above = cell(0, y + 1)
                row = slice(y, y + 1)
                new = (
                    ka[x, row] * (cell(-1, y) + cell(1, y))
                    + kb[x, row] * (below + above)
                    + km[x, row] * pltpu.roll(here, 1, 1)
                    + kp[x, row] * pltpu.roll(here, ROWS - 1, 1)
                    + (1.0 - OMEGA) * here
                )
                dst[c, pl.ds(base + site_row(0, y), KV)] = new
                if last:
                    blk[c, x * NY + y] = new.astype(BF16)
                below, here = here, above
            return carry

        lax.fori_loop(0, NX, plane, 0)

    def pair_copy():
        slot = pair.at[core]
        return remote(slot, slot, pair_sem.at[0], pair_sem.at[1], device("x", 0, 1))

    def line_copies():
        return [
            remote(
                pair, lines.at[n, at[axis]], table_sem.at[0, 0], table_sem.at[0, 1],
                device(axis, d, 0),
            )
            for n, axis in enumerate(AXES)
            for d in range(1, LINE)
        ]

    def rank_copies():
        out = []
        for c, (a, u, v) in enumerate(ROUTES):
            src = lines.at[AXES.index(u), :, core, 2]
            for d in range(1, LINE):
                out.append(
                    remote(
                        src, ranks.at[c, at[v]], table_sem.at[1, 0], table_sem.at[1, 1],
                        device(v, d, 0),
                    )
                )
        return out

    def spread_copies(c):
        a, u, v = ROUTES[c]
        return [
            remote(
                pg[c][0].at[0], pg[c][0].at[LINE - d],
                near_sem.at[c, 0], near_sem.at[c, 1], device(u, d, 0),
            )
            for d in (2, 1, 3)
        ]

    def cast_copies(c):
        a, u, v = ROUTES[c]
        plan = (
            (0, 0, 1, 3, 1, 0, 0),
            (0, 0, 1, 1, 3, 1, 2),
            (0, 1, 1, 3, 1, 0, 0),
            (0, 2, 2, 1, 3, 1, 1),
            (0, 2, 2, 3, 1, 0, 2),
            (0, 1, 1, 1, 3, 1, 2),
            (3, 0, 2, 2, 1, 2, 3),
            (1, 2, 2, 2, 3, 2, 3),
        )
        return [
            remote(
                pg[c][src].at[pl.ds(first, size)], pg[c][dst].at[pl.ds(first, size)],
                cast_send.at[c, out], cast_recv.at[c, into], device(v, d, 0),
            )
            for src, first, size, dst, d, out, into in plan
        ]

    def piece(slot, part):
        first, count = PARTS[part]
        return pl.ds(slot * REPLY + first * SPOT, count * SPOT)

    def answer(c, part, d, e):
        a = ROUTES[c][0]
        slot = lax.rem(at[a] + d, LINE) * CORES + lax.rem(core + e, CORES)
        here = at[a] * CORES + core
        src = sb.at[c, piece(slot, part)]
        dst, peer = rb[c].at[piece(here, part)], device(a, d, e)
        if d == 0 and e == 0:
            return pltpu.make_async_copy(src, dst, own_sem.at[c, part])
        if d == 2 and part == 0:
            dst, peer = fb.at[c, e, piece(0, part)], device(a, 1 + 2 * e, 0)
            return remote(src, dst, ans_send.at[c, part], hop_recv.at[c, e], peer)
        return remote(src, dst, ans_send.at[c, part], ans_recv.at[c, part], peer)

    def forward(c, part, e):
        a = ROUTES[c][0]
        origin = lax.rem(at[a] + 3 - 2 * e, LINE) * CORES + core
        return remote(
            fb.at[c, e, piece(0, part)], rb[c].at[piece(origin, part)],
            fwd_send.at[c], ans_recv.at[c, part], device(a, 1 + 2 * e, e),
        )

    order = [(d, e) for d in (2, 1, 3, 0) for e in range(CORES)]

    def spread(c):
        a, u, v = ROUTES[c]
        for r in range(COARSE):
            pg[c][0][0, r] = blk[c, id_s[r, 0] & (SITES - 1)]
        for copy in spread_copies(c) + cast_copies(c)[:2]:
            copy.start()

    def cast(c):
        drain(pg[c][1].at[pl.ds(0, 3)], near_sem.at[c, 1])
        for copy in cast_copies(c)[2:6]:
            copy.start()

    def pass_on(c):
        for n in range(2):
            drain(pg[c][0].at[pl.ds(0, 2)], cast_recv.at[c, n])
            cast_copies(c)[6 + n].start()

    def find_tiles(c):
        a, u, v = ROUTES[c]
        n = AXES.index(a)

        def one(slot, carry):
            q, to = slot // CORES, lax.rem(slot, CORES)
            for place, back in enumerate(BACKS):
                vv = lax.rem(at[v] + back, LINE)
                for ahead in range(LINE):
                    uu = lax.rem(at[u] + ahead, LINE)
                    whose = {a: at[a], u: uu, v: vv}
                    owner = whose["x"] * 32 + whose["z"] * 8 + whose["y"] * 2 + core
                    for p in range(2):
                        block = line_s[n, q, to, p, 0, owner] & (SITES - 1)
                        rank = rank_s[c, vv, uu, 0, block] & (COARSE - 1)
                        tile_s[c, slot, place * SPOT + ahead * 2 + p] = rank
            return carry

        lax.fori_loop(0, LINE * CORES, one, 0)

    def reply(c, part):
        a, u, v = ROUTES[c]
        drain(pg[c][0], cast_recv.at[c, 2 + part])
        first, count = PARTS[part]
        for d, e in order:
            slot = lax.rem(at[a] + d, LINE) * CORES + lax.rem(core + e, CORES)
            for place in range(first, first + count):
                tiles = []
                for t in range(SPOT):
                    rank = tile_s[c, slot, place * SPOT + t] & (COARSE - 1)
                    tiles.append(pg[c][BACKS[place]][t // 2, rank])
                for t, tile in enumerate(tiles):
                    sb[c, slot * REPLY + place * SPOT + t] = tile
            answer(c, part, d, e).start()

    def reply_on(c, part):
        for e in range(2):
            answer(c, part, 2, e).wait_recv()
            forward(c, part, e).start()

    def transpose_in(c):
        loads[c].wait()
        for x in range(NX):
            for half in range(NY // 8):
                for k in range(KV):
                    wa[c, pl.ds(site_row(x, half * 8) + k, 8, stride=KV), :] = stage[
                        c * KV + k, x, pl.ds(half * 8, 8), :
                    ]

    def products(c, b):
        column = ((b >> 4) & 1) * (ROWS // 2) + (b & (NY - 1))
        values = []
        for t in range(SLOTS):
            found = tgt_s[2 * c + (b >> 5), column + t * NY]
            values.append(rb[c][found].astype(F32))
        values.append(blk[c, b].astype(F32))
        for n, (p, q) in enumerate(PAIRS):
            product = values[p] * values[q]
            product = product[0:8] + product[8:16]
            row = pl.ds(pl.multiple_of(b * 8, 8), 8)
            if c != GRAM_ORDER[0]:
                product = product + part_sums[n, row, :]
            part_sums[n, row, :] = product

    def add_products(c):
        def step(g, carry):
            for m in range(4):
                products(c, g * 4 + m)
            return carry

        lax.fori_loop(0, SITES // 4, step, 0)

    def finish():
        sub = lax.broadcasted_iota(jnp.int32, (8, ROWS), 0)
        low4, low2, low1 = sub < 4, (sub & 2) == 0, (sub & 1) == 0

        def merge(first, second, keep_first, shift):
            first = first + pltpu.roll(first, 8 - shift, 0)
            second = second + pltpu.roll(second, shift, 0)
            return jnp.where(keep_first, first, second)

        def group(g, carry):
            total = {}
            for n, pair in enumerate(PAIRS):
                rows = [
                    part_sums[n, pl.ds(pl.multiple_of(g * 64, 64) + 8 * m, 8), :]
                    for m in range(8)
                ]
                rows = [
                    jnp.where(low4, rows[m], rows[m + 4])
                    + pltpu.roll(jnp.where(low4, rows[m + 4], rows[m]), 4, 0)
                    for m in range(4)
                ]
                rows = [merge(rows[m], rows[m + 2], low2, 2) for m in range(2)]
                total[pair] = merge(rows[0], rows[1], low1, 1) * (1.0 / VECS)
                if pair[0] == pair[1]:
                    total[pair] = total[pair] + RIDGE
            out = solve_rows(total, [total[s, SLOTS] for s in range(SLOTS)])
            for s in range(SLOTS):
                w_out[s, pl.ds(pl.multiple_of(g * 8, 8), 8), :] = out[s]
            return carry

        lax.fori_loop(0, SITES // 8, group, 0)

    stores = []

    def transpose_out(c, w):
        for x in range(NX):
            for half in range(NY // 8):
                for k in range(KV):
                    stage[c * KV + k, x, pl.ds(half * 8, 8), :] = w[
                        c, pl.ds(site_row(x, half * 8) + k, 8, stride=KV), :
                    ]
        part = pl.ds(c * KV, KV)
        store = pltpu.make_async_copy(stage.at[part], sm_out.at[part], out_sem.at[c])
        store.start()
        stores.append(store)

    for c in range(CHUNKS):
        transpose_in(c)
        if c == 0:
            pl.semaphore_wait(barrier, greeted)
        send_faces(0, c, wa)

    for load in coef_loads:
        load.wait()
    ax, ay, az = coef[0], coef[1], coef[2]
    scale = OMEGA / (2.0 * (ax + ay + az) + coef[3])
    ka[...] = ax * scale
    kb[...] = ay * scale
    az = az * scale
    lane = lax.broadcasted_iota(jnp.int32, az.shape, 2)
    km[...] = jnp.where(lane == 0, 0.0, az)
    kp[...] = jnp.where(lane == ROWS - 1, 0.0, az)

    for load in lists:
        load.wait()
    meta[...] = jnp.zeros_like(meta)
    slots = lax.broadcasted_iota(jnp.int32, (SLOTS, NY), 0)
    for x in range(NX):
        live = (cells[0][x] == 0) & (slots < cells[1][x])
        listed = jnp.where(live, cells[2][x] * SITES + cells[3][x], -1)
        for t in range(SLOTS):
            where = pl.ds((x % 2) * (ROWS // 2) + t * NY, NY)
            meta[x // 2 : x // 2 + 1, where] = listed[t : t + 1]
        meta[2:3, pl.ds(x * NY, NY)] = cells[0][x]
    wanted, targets, rank, ids = lists_of(meta[...], at)
    idv[...] = ids
    id_copy = pltpu.make_async_copy(idv, id_s, smem_sem.at[0])
    id_copy.start()
    for n, row in enumerate((*wanted, rank)):
        pair[core, n] = row
    pair_copy().start()
    tgt[...] = jnp.zeros_like(tgt)
    for c in range(CHUNKS):
        for h in range(2):
            tgt[2 * c + h : 2 * c + h + 1] = targets[c][h]
        rb[c][EMPTY] = jnp.zeros((KV, ROWS), BF16)
    tgt_copy = pltpu.make_async_copy(tgt, tgt_s, smem_sem.at[3])
    tgt_copy.start()

    for c in range(CHUNKS):
        fill_halo(0, c, wa)
        sweep(c, wa, wb, False)
        send_faces(1, c, wb)
    pair_copy().wait_recv()
    for copy in line_copies():
        copy.start()
    for n, axis in enumerate(AXES):
        lines[n, at[axis]] = pair[...]
    for c in range(CHUNKS):
        fill_halo(1, c, wb)
        sweep(c, wb, wa, False)
        send_faces(2, c, wa)
    drain(lines.at[:, pl.ds(0, 3)], table_sem.at[0, 1])
    for copy in rank_copies():
        copy.start()
    for c, (a, u, v) in enumerate(ROUTES):
        ranks[c, at[v]] = lines[AXES.index(u), :, core, 2]
    line_copy = pltpu.make_async_copy(lines, line_s, smem_sem.at[1])
    line_copy.start()
    id_copy.wait()
    for c in range(CHUNKS):
        fill_halo(2, c, wa)
        sweep(c, wa, wb, True)
        spread(c)
    drain(ranks.at[:, pl.ds(0, 3)], table_sem.at[1, 1])
    rank_copy = pltpu.make_async_copy(ranks, rank_s, smem_sem.at[2])
    rank_copy.start()
    cast(0)
    cast(1)
    line_copy.wait()
    rank_copy.wait()
    find_tiles(1)
    cast(2)
    find_tiles(0)
    find_tiles(2)
    for c in range(CHUNKS):
        pass_on(c)
    for c in (1, 2, 0):
        reply(c, 0)
    for c in (1, 0, 2):
        reply_on(c, 0)
        reply(c, 1)
    for c in range(CHUNKS):
        transpose_out(c, wb)
    tgt_copy.wait()
    for c in GRAM_ORDER:
        for part in range(len(PARTS)):
            answer(c, part, 0, 0).wait()
            drain(sb.at[c, pl.ds(0, 7 * PARTS[part][1] * SPOT)], ans_recv.at[c, part])
        add_products(c)
    finish()

    drain(fxs, send_sem.at[0])
    drain(fys, send_sem.at[1])
    pair_copy().wait_send()
    drain(lines.at[:, pl.ds(0, 3)], table_sem.at[0, 0])
    drain(ranks.at[:, pl.ds(0, 3)], table_sem.at[1, 0])
    for c in range(CHUNKS):
        drain(pg[c][0].at[pl.ds(0, 3)], near_sem.at[c, 0])
        for n in range(3):
            drain(pg[c][0], cast_send.at[c, n])
        for part in range(len(PARTS)):
            count = PARTS[part][1]
            drain(sb.at[c, pl.ds(0, 7 * count * SPOT)], ans_send.at[c, part])
        drain(fb.at[c, :, pl.ds(0, PARTS[0][1] * SPOT)], fwd_send.at[c])
    for store in stores:
        store.wait()


def smooth(test_vectors, coef_x, coef_y, coef_z, shift, split, count, owner, local):
    vmem = pl.BlockSpec(memory_space=pltpu.VMEM)
    anywhere = pl.BlockSpec(memory_space=pl.ANY)
    cells = pltpu.VMEM((NX, NY, ROWS), F32)
    rows = pltpu.VMEM((LINE, COARSE, KV, ROWS), BF16)
    dma = pltpu.SemaphoreType.DMA
    return pl.pallas_call(
        smooth_kernel,
        out_shape=(
            jax.ShapeDtypeStruct((VECS, NX, NY, ROWS), F32),
            jax.ShapeDtypeStruct((SLOTS, SITES, ROWS), F32),
        ),
        in_specs=[anywhere] * 9,
        out_specs=(anywhere, vmem),
        scratch_shapes=[
            pltpu.VMEM((NX, 1, NY), jnp.int32),
            pltpu.VMEM((NX, 1, NY), jnp.int32),
            pltpu.VMEM((NX, SLOTS, NY), jnp.int32),
            pltpu.VMEM((NX, SLOTS, NY), jnp.int32),
            pltpu.VMEM((8, ROWS), jnp.int32),
            pltpu.VMEM((8, ROWS), jnp.int32),
            pltpu.SMEM((8, ROWS), jnp.int32),
            pltpu.VMEM((CHUNKS, SITES, KV, ROWS), BF16),
            *([pltpu.VMEM((EMPTY + 8, KV, ROWS), BF16)] * CHUNKS),
            pltpu.VMEM((len(PAIRS), SITES * 8, ROWS), F32),
            pltpu.VMEM((VECS, NX, NY, ROWS), F32),
            pltpu.VMEM((4, NX, NY, ROWS), F32),
            pltpu.VMEM((CHUNKS, EXT, ROWS), F32),
            pltpu.VMEM((CHUNKS, EXT, ROWS), F32),
            cells, cells, cells, cells,
            pltpu.VMEM((SWEEPS, CHUNKS, 2, NY * KV, ROWS), BF16),
            pltpu.VMEM((SWEEPS, CHUNKS, 2, NY * KV, ROWS), BF16),
            pltpu.VMEM((SWEEPS, CHUNKS, 2, NX * KV, ROWS), BF16),
            pltpu.VMEM((SWEEPS, CHUNKS, 2, NX * KV, ROWS), BF16),
            pltpu.VMEM((CORES, 3, 1, ROWS), jnp.int32),
            pltpu.VMEM((len(AXES), LINE, CORES, 3, 1, ROWS), jnp.int32),
            pltpu.VMEM((CHUNKS, LINE, LINE, 1, ROWS), jnp.int32),
            pltpu.VMEM((COARSE, ROWS), jnp.int32),
            pltpu.SMEM((len(AXES), LINE, CORES, 3, 1, ROWS), jnp.int32),
            pltpu.SMEM((CHUNKS, LINE, LINE, 1, ROWS), jnp.int32),
            pltpu.SMEM((COARSE, ROWS), jnp.int32),
            pltpu.SMEM((CHUNKS, LINE * CORES, REPLY), jnp.int32),
            *([rows] * (LINE * CHUNKS)),
            pltpu.VMEM((CHUNKS, EMPTY, KV, ROWS), BF16),
            pltpu.VMEM((CHUNKS, CORES, REPLY, KV, ROWS), BF16),
            dma((CHUNKS,)),
            dma((4,)),
            dma((CHUNKS,)),
            dma((2,)),
            dma((SWEEPS, CHUNKS, 2)),
            dma((2,)),
            dma((2, 2)),
            dma((CHUNKS, 2)),
            dma((CHUNKS, 3)),
            dma((CHUNKS, 4)),
            dma((CHUNKS, len(PARTS))),
            dma((CHUNKS, len(PARTS))),
            dma((CHUNKS, CORES)),
            dma((CHUNKS,)),
            dma((CHUNKS, len(PARTS))),
            dma((4,)),
            dma((4,)),
        ],
        compiler_params=pltpu.CompilerParams(
            collective_id=0, has_side_effects=True, vmem_limit_bytes=60 * 1024 * 1024
        ),
        name="smooth",
    )(test_vectors, coef_x, coef_y, coef_z, shift, split, count, owner, local)


def pass_kernel(w_in, sm_in, w_out, sm_out, w_hold, sm_hold, in_sem, out_sem):
    parts = [(w_in, w_hold, w_out)]
    for c in range(CHUNKS):
        part = pl.ds(c * KV, KV)
        parts.append((sm_in.at[part], sm_hold.at[part], sm_out.at[part]))
    ins = [pltpu.make_async_copy(a, b, in_sem.at[n]) for n, (a, b, _) in enumerate(parts)]
    outs = [pltpu.make_async_copy(b, d, out_sem.at[n]) for n, (_, b, d) in enumerate(parts)]
    for copy in ins:
        copy.start()
    for load, store in zip(ins, outs):
        load.wait()
        store.start()
    for store in outs:
        store.wait()


def pass_on_results(weights, sm):
    anywhere = pl.BlockSpec(memory_space=pl.ANY)
    dma = pltpu.SemaphoreType.DMA
    return pl.pallas_call(
        pass_kernel,
        out_shape=(
            jax.ShapeDtypeStruct(weights.shape, F32),
            jax.ShapeDtypeStruct(sm.shape, F32),
        ),
        in_specs=[anywhere, anywhere],
        out_specs=(anywhere, anywhere),
        scratch_shapes=[
            pltpu.VMEM(weights.shape, F32),
            pltpu.VMEM(sm.shape, F32),
            dma((CHUNKS + 1,)),
            dma((CHUNKS + 1,)),
        ],
        compiler_params=pltpu.CompilerParams(vmem_limit_bytes=60 * 1024 * 1024),
        name="fit",
    )(weights, sm)


def per_device(
    test_vectors, coef_x, coef_y, coef_z, shift, cf_split, nbr_count, nbr_owner, nbr_block
):
    sm, weights = smooth(
        test_vectors, coef_x, coef_y, coef_z, shift,
        jnp.swapaxes(cf_split, 1, 2),
        jnp.swapaxes(nbr_count, 1, 2),
        jnp.transpose(nbr_owner, (0, 2, 3, 1)).reshape(NX, SLOTS, NY),
        jnp.transpose(nbr_block, (0, 2, 3, 1)).reshape(NX, SLOTS, NY),
    )
    weights, smoothed = pass_on_results(weights.reshape(SLOTS, NX, NY, ROWS), sm)
    return (smoothed, weights)


def solution(mesh):
    cells = P("gx", "gy", None)
    lists = P("gx", "gy", None, None)
    vectors = P(None, "gx", "gy", None)
    return jax.shard_map(
        per_device,
        mesh=mesh,
        in_specs=(vectors, cells, cells, cells, cells, cells, cells, lists, lists),
        out_specs=(vectors, vectors),
        check_vma=False,
    )
```

```python
import jax
import jax.numpy as jnp
from jax import lax
from jax.experimental import pallas as pl
from jax.experimental.pallas import tpu as pltpu
from jax.sharding import PartitionSpec as P

SLOTS = 4
SWEEPS = 3
ROWS = 128
OMEGA = 0.8
RIDGE = 0.05
VECS = 48
CHUNKS = 3
KV = VECS // CHUNKS
NX = 4
NY = 16
SITES = NX * NY
XROW = (NY + 2) * KV
EXT = (NX + 2) * XROW
GX = 16
GY = 8
MESH = pl.DeviceIdType.MESH
F32 = jnp.float32
BF16 = jnp.bfloat16


def site_row(x, y):
    return (x + 1) * XROW + (y + 1) * KV


def solve_rows(gram, rhs):
    low = [[None] * SLOTS for _ in range(SLOTS)]
    inv = []
    for r in range(SLOTS):
        scaled = []
        diag = gram[r, r]
        for c in range(r):
            rest = gram[r, c]
            for m in range(c):
                rest = rest - scaled[m] * low[c][m]
            scaled.append(rest)
            low[r][c] = rest * inv[c]
            diag = diag - rest * low[r][c]
        inv.append(1.0 / diag)
    fwd = []
    for r in range(SLOTS):
        rest = rhs[r]
        for m in range(r):
            rest = rest - low[r][m] * fwd[m]
        fwd.append(rest)
    out = [None] * SLOTS
    for r in reversed(range(SLOTS)):
        rest = fwd[r] * inv[r]
        for m in range(r + 1, SLOTS):
            rest = rest - low[m][r] * out[m]
        out[r] = rest
    return out


PAIRS = [(s, t) for s in range(SLOTS) for t in range(s + 1)] + [(s, SLOTS) for s in range(SLOTS)]
AXES = "xyz"
LINE = 4
CORES = 2
COARSE = 16
PLANE = LINE * LINE
ROUTES = (("z", "x", "y"), ("y", "z", "x"), ("x", "y", "z"))
BACKS = (0, 1, 3, 2)
EMPTY = LINE * CORES * PLANE * 2
SPOT = 2 * LINE
GRAM_ORDER = (1, 0, 2)
REPLY = PLANE * 2
PARTS = ((0, 3), (3, 1))


def lists_of(meta, here):
    lane = lax.broadcasted_iota(jnp.int32, (ROWS, ROWS), 1)
    sub = lax.broadcasted_iota(jnp.int32, (ROWS, ROWS), 0)
    diag = lane == sub
    none = 1 << 20

    def column(row):
        return jnp.sum(jnp.where(diag, row, 0), axis=1, keepdims=True)

    def line(col):
        return jnp.sum(jnp.where(diag, col, 0), axis=0, keepdims=True)

    members, keys, owners = [], [], []
    for h in range(2):
        entry = meta[h : h + 1]
        owner = entry >> 6
        key = (lane[:1] + h * ROWS) * SITES + (entry & (SITES - 1))
        owners.append(owner)
        keys.append(key)
        members.append(owner == sub)
    first = jnp.minimum(*[jnp.where(m, k, none) for m, k in zip(members, keys)])
    first = jnp.min(first, axis=1, keepdims=True)
    first = jnp.where(first >= none, 0, first)
    second = jnp.maximum(*[jnp.where(m, k, 0) for m, k in zip(members, keys)])
    second = jnp.max(second, axis=1, keepdims=True)
    wanted = [line(v) & (SITES - 1) for v in (first, second)]
    targets = [[] for _ in ROUTES]
    for h in range(2):
        own = owners[h]
        at_first = jnp.sum(jnp.where(members[h], first, 0), axis=0, keepdims=True)
        place = jnp.where(keys[h] == at_first, 0, 1)
        at = {"x": (own >> 5) & 3, "z": (own >> 3) & 3, "y": (own >> 1) & 3}
        for c, (a, u, v) in enumerate(ROUTES):
            back = (at[v] - here[v]) & 3
            spot = jnp.where(back == 2, 3, jnp.where(back == 3, 2, back))
            slot = ((at[a] * CORES + (own & 1)) * PLANE + spot * LINE + ((at[u] - here[u]) & 3)) * 2 + place
            targets[c].append(jnp.where(own < 0, EMPTY, slot))
    coarse = meta[2:3]
    rank = jnp.sum(jnp.where(sub < lane, column(coarse), 0), axis=0, keepdims=True)
    hit = (rank == sub[:COARSE]) & (coarse > 0)
    ids = jnp.sum(jnp.where(hit, lane[:COARSE], 0), axis=1, keepdims=True)
    ids = jnp.broadcast_to(ids, (COARSE, ROWS))
    rank = jnp.minimum(rank, COARSE - 1)
    return wanted, targets, rank, ids


def smooth_kernel(
    tv, cx, cy, cz, sh, split, count, owner, local, sm_out, w_out,
    split_v, count_v, owner_v, local_v, meta, tgt, tgt_s, blk, rb0, rb1, rb2, part_sums,
    stage, coef, wa, wb, ka, kb, km, kp, fxs, fxr, fys, fyr,
    pair, lines, ranks, idv, line_s, rank_s, id_s, tile_s, p00, p01, p02, p03, p10, p11, p12, p13, p20, p21, p22, p23, sb, fb,
    in_sem, coef_sem, out_sem, send_sem, recv_sem, pair_sem, table_sem,
    near_sem, cast_send, cast_recv, ans_send, ans_recv, hop_recv, fwd_send, own_sem, smem_sem, list_sem,
):
    cells = (split_v, count_v, owner_v, local_v)
    rb = (rb0, rb1, rb2)
    pg = ((p00, p01, p02, p03), (p10, p11, p12, p13), (p20, p21, p22, p23))
    i = lax.axis_index("gx")
    j = lax.axis_index("gy")
    core = lax.rem(j, CORES)
    at = {"x": i // LINE, "z": lax.rem(i, LINE), "y": j // CORES}
    peers = (
        (lax.rem(i + GX - 1, GX), j),
        (lax.rem(i + 1, GX), j),
        (i, lax.rem(j + GY - 1, GY)),
        (i, lax.rem(j + 1, GY)),
    )

    def device(axis, d, e):
        moved = dict(at)
        moved[axis] = lax.rem(at[axis] + d, LINE)
        return (moved["x"] * LINE + moved["z"], moved["y"] * CORES + lax.rem(core + e, CORES))

    def remote(src, dst, send, recv, peer):
        return pltpu.make_async_remote_copy(
            src_ref=src, dst_ref=dst, send_sem=send, recv_sem=recv,
            device_id=peer, device_id_type=MESH,
        )

    loads = []
    for c in range(CHUNKS):
        part = pl.ds(c * KV, KV)
        loads.append(pltpu.make_async_copy(tv.at[part], stage.at[part], in_sem.at[c]))
    loads[0].start()
    barrier = pltpu.get_barrier_semaphore()
    for peer in peers[:2]:
        pl.semaphore_signal(barrier, inc=1, device_id=peer, device_id_type=MESH)
    pl.semaphore_signal(barrier, inc=1, device_id=device("x", 0, 1), device_id_type=MESH)
    for axis in AXES:
        for d in range(1, LINE):
            for e in range(CORES):
                pl.semaphore_signal(
                    barrier, inc=1, device_id=device(axis, d, e), device_id_type=MESH
                )
    greeted = 3 + len(AXES) * (LINE - 1) * CORES
    for load in loads[1:]:
        load.start()
    coef_loads = []
    for n, part in enumerate((cx, cy, cz, sh)):
        load = pltpu.make_async_copy(part, coef.at[n], coef_sem.at[n])
        load.start()
        coef_loads.append(load)
    lists = []
    for n, part in enumerate((split, count, owner, local)):
        load = pltpu.make_async_copy(part, cells[n], list_sem.at[n])
        load.start()
        lists.append(load)

    keep = (
        (i > 0).astype(F32),
        (i < GX - 1).astype(F32),
        (j > 0).astype(F32),
        (j < GY - 1).astype(F32),
    )

    def drain(ref, sem):
        pltpu.make_async_copy(ref, ref, sem).wait()

    def copies(s, c):
        out = []
        for d in range(4):
            src, dst = (fxs, fxr) if d < 2 else (fys, fyr)
            out.append(
                remote(
                    src.at[s, c, d % 2], dst.at[s, c, 1 - d % 2],
                    send_sem.at[d // 2], recv_sem.at[s, c, d // 2], peers[d],
                )
            )
        return out

    def send_faces(s, c, w):
        for side in range(2):
            x = side * (NX - 1)
            fxs[s, c, side] = w[c, pl.ds(site_row(x, 0), NY * KV)].astype(BF16)
            y = side * (NY - 1)
            for x in range(NX):
                fys[s, c, side, pl.ds(x * KV, KV)] = w[c, pl.ds(site_row(x, y), KV)].astype(BF16)
        for copy in copies(s, c):
            copy.start()

    def fill_halo(s, c, w):
        drain(fxr.at[s, c], recv_sem.at[s, c, 0])
        drain(fyr.at[s, c], recv_sem.at[s, c, 1])
        for side in range(2):
            x = -1 if side == 0 else NX
            w[c, pl.ds(site_row(x, 0), NY * KV)] = fxr[s, c, side].astype(F32) * keep[side]
            y = -1 if side == 0 else NY
            for x in range(NX):
                w[c, pl.ds(site_row(x, y), KV)] = (
                    fyr[s, c, side, pl.ds(x * KV, KV)].astype(F32) * keep[2 + side]
                )

    def sweep(c, src, dst, last):
        def plane(x, carry):
            base = pl.multiple_of(x * XROW, 16)

            def cell(dx, y):
                return src[c, pl.ds(base + site_row(dx, y), KV)]

            below, here = cell(0, -1), cell(0, 0)
            for y in range(NY):
                above = cell(0, y + 1)
                row = slice(y, y + 1)
                new = (
                    ka[x, row] * (cell(-1, y) + cell(1, y))
                    + kb[x, row] * (below + above)
                    + km[x, row] * pltpu.roll(here, 1, 1)
                    + kp[x, row] * pltpu.roll(here, ROWS - 1, 1)
                    + (1.0 - OMEGA) * here
                )
                dst[c, pl.ds(base + site_row(0, y), KV)] = new
                if last:
                    blk[c, x * NY + y] = new.astype(BF16)
                below, here = here, above
            return carry

        lax.fori_loop(0, NX, plane, 0)

    def pair_copy():
        slot = pair.at[core]
        return remote(slot, slot, pair_sem.at[0], pair_sem.at[1], device("x", 0, 1))

    def line_copies():
        return [
            remote(
                pair, lines.at[n, at[axis]], table_sem.at[0, 0], table_sem.at[0, 1],
                device(axis, d, 0),
            )
            for n, axis in enumerate(AXES)
            for d in range(1, LINE)
        ]

    def rank_copies():
        out = []
        for c, (a, u, v) in enumerate(ROUTES):
            src = lines.at[AXES.index(u), :, core, 2]
            for d in range(1, LINE):
                out.append(
                    remote(
                        src, ranks.at[c, at[v]], table_sem.at[1, 0], table_sem.at[1, 1],
                        device(v, d, 0),
                    )
                )
        return out

    def spread_copies(c):
        a, u, v = ROUTES[c]
        return [
            remote(
                pg[c][0].at[0], pg[c][0].at[LINE - d],
                near_sem.at[c, 0], near_sem.at[c, 1], device(u, d, 0),
            )
            for d in (2, 1, 3)
        ]

    def cast_copies(c):
        a, u, v = ROUTES[c]
        plan = (
            (0, 0, 1, 3, 1, 0, 0),
            (0, 0, 1, 1, 3, 1, 2),
            (0, 1, 1, 3, 1, 0, 0),
            (0, 2, 2, 1, 3, 1, 1),
            (0, 2, 2, 3, 1, 0, 2),
            (0, 1, 1, 1, 3, 1, 2),
            (3, 0, 2, 2, 1, 2, 3),
            (1, 2, 2, 2, 3, 2, 3),
        )
        return [
            remote(
                pg[c][src].at[pl.ds(first, size)], pg[c][dst].at[pl.ds(first, size)],
                cast_send.at[c, out], cast_recv.at[c, into], device(v, d, 0),
            )
            for src, first, size, dst, d, out, into in plan
        ]

    def piece(slot, part):
        first, count = PARTS[part]
        return pl.ds(slot * REPLY + first * SPOT, count * SPOT)

    def answer(c, part, d, e):
        a = ROUTES[c][0]
        slot = lax.rem(at[a] + d, LINE) * CORES + lax.rem(core + e, CORES)
        here = at[a] * CORES + core
        src = sb.at[c, piece(slot, part)]
        dst, peer = rb[c].at[piece(here, part)], device(a, d, e)
        if d == 0 and e == 0:
            return pltpu.make_async_copy(src, dst, own_sem.at[c, part])
        if d == 2 and part == 0:
            dst, peer = fb.at[c, e, piece(0, part)], device(a, 1 + 2 * e, 0)
            return remote(src, dst, ans_send.at[c, part], hop_recv.at[c, e], peer)
        return remote(src, dst, ans_send.at[c, part], ans_recv.at[c, part], peer)

    def forward(c, part, e):
        a = ROUTES[c][0]
        origin = lax.rem(at[a] + 3 - 2 * e, LINE) * CORES + core
        return remote(
            fb.at[c, e, piece(0, part)], rb[c].at[piece(origin, part)],
            fwd_send.at[c], ans_recv.at[c, part], device(a, 1 + 2 * e, e),
        )

    order = [(d, e) for d in (2, 1, 3, 0) for e in range(CORES)]

    def spread(c):
        a, u, v = ROUTES[c]
        for r in range(COARSE):
            pg[c][0][0, r] = blk[c, id_s[r, 0] & (SITES - 1)]
        for copy in spread_copies(c) + cast_copies(c)[:2]:
            copy.start()

    def cast(c):
        drain(pg[c][1].at[pl.ds(0, 3)], near_sem.at[c, 1])
        for copy in cast_copies(c)[2:6]:
            copy.start()

    def pass_on(c):
        for n in range(2):
            drain(pg[c][0].at[pl.ds(0, 2)], cast_recv.at[c, n])
            cast_copies(c)[6 + n].start()

    def find_tiles(c):
        a, u, v = ROUTES[c]
        n = AXES.index(a)

        def one(slot, carry):
            q, to = slot // CORES, lax.rem(slot, CORES)
            for place, back in enumerate(BACKS):
                vv = lax.rem(at[v] + back, LINE)
                for ahead in range(LINE):
                    uu = lax.rem(at[u] + ahead, LINE)
                    whose = {a: at[a], u: uu, v: vv}
                    owner = whose["x"] * 32 + whose["z"] * 8 + whose["y"] * 2 + core
                    for p in range(2):
                        block = line_s[n, q, to, p, 0, owner] & (SITES - 1)
                        rank = rank_s[c, vv, uu, 0, block] & (COARSE - 1)
                        tile_s[c, slot, place * SPOT + ahead * 2 + p] = rank
            return carry

        lax.fori_loop(0, LINE * CORES, one, 0)

    def reply(c, part):
        a, u, v = ROUTES[c]
        drain(pg[c][0], cast_recv.at[c, 2 + part])
        first, count = PARTS[part]
        for d, e in order:
            slot = lax.rem(at[a] + d, LINE) * CORES + lax.rem(core + e, CORES)
            for place in range(first, first + count):
                tiles = []
                for t in range(SPOT):
                    rank = tile_s[c, slot, place * SPOT + t] & (COARSE - 1)
                    tiles.append(pg[c][BACKS[place]][t // 2, rank])
                for t, tile in enumerate(tiles):
                    sb[c, slot * REPLY + place * SPOT + t] = tile
            answer(c, part, d, e).start()

    def reply_on(c, part):
        for e in range(2):
            answer(c, part, 2, e).wait_recv()
            forward(c, part, e).start()

    def transpose_in(c):
        loads[c].wait()
        for x in range(NX):
            for half in range(NY // 8):
                for k in range(KV):
                    wa[c, pl.ds(site_row(x, half * 8) + k, 8, stride=KV), :] = stage[
                        c * KV + k, x, pl.ds(half * 8, 8), :
                    ]

    def products(c, b):
        column = ((b >> 4) & 1) * (ROWS // 2) + (b & (NY - 1))
        values = []
        for t in range(SLOTS):
            found = tgt_s[2 * c + (b >> 5), column + t * NY]
            values.append(rb[c][found].astype(F32))
        values.append(blk[c, b].astype(F32))
        for n, (p, q) in enumerate(PAIRS):
            product = values[p] * values[q]
            product = product[0:8] + product[8:16]
            row = pl.ds(pl.multiple_of(b * 8, 8), 8)
            if c != GRAM_ORDER[0]:
                product = product + part_sums[n, row, :]
            part_sums[n, row, :] = product

    def add_products(c):
        def step(g, carry):
            for m in range(4):
                products(c, g * 4 + m)
            return carry

        lax.fori_loop(0, SITES // 4, step, 0)

    def finish():
        sub = lax.broadcasted_iota(jnp.int32, (8, ROWS), 0)
        low4, low2, low1 = sub < 4, (sub & 2) == 0, (sub & 1) == 0

        def merge(first, second, keep_first, shift):
            first = first + pltpu.roll(first, 8 - shift, 0)
            second = second + pltpu.roll(second, shift, 0)
            return jnp.where(keep_first, first, second)

        def group(g, carry):
            total = {}
            for n, pair in enumerate(PAIRS):
                rows = [
                    part_sums[n, pl.ds(pl.multiple_of(g * 64, 64) + 8 * m, 8), :]
                    for m in range(8)
                ]
                rows = [
                    jnp.where(low4, rows[m], rows[m + 4])
                    + pltpu.roll(jnp.where(low4, rows[m + 4], rows[m]), 4, 0)
                    for m in range(4)
                ]
                rows = [merge(rows[m], rows[m + 2], low2, 2) for m in range(2)]
                total[pair] = merge(rows[0], rows[1], low1, 1) * (1.0 / VECS)
                if pair[0] == pair[1]:
                    total[pair] = total[pair] + RIDGE
            out = solve_rows(total, [total[s, SLOTS] for s in range(SLOTS)])
            for s in range(SLOTS):
                w_out[s, pl.ds(pl.multiple_of(g * 8, 8), 8), :] = out[s]
            return carry

        lax.fori_loop(0, SITES // 8, group, 0)

    stores = []

    def transpose_out(c, w):
        for x in range(NX):
            for half in range(NY // 8):
                for k in range(KV):
                    stage[c * KV + k, x, pl.ds(half * 8, 8), :] = w[
                        c, pl.ds(site_row(x, half * 8) + k, 8, stride=KV), :
                    ]
        part = pl.ds(c * KV, KV)
        store = pltpu.make_async_copy(stage.at[part], sm_out.at[part], out_sem.at[c])
        store.start()
        stores.append(store)

    for c in range(CHUNKS):
        transpose_in(c)
        if c == 0:
            pl.semaphore_wait(barrier, greeted)
        send_faces(0, c, wa)

    for load in coef_loads:
        load.wait()
    ax, ay, az = coef[0], coef[1], coef[2]
    scale = OMEGA / (2.0 * (ax + ay + az) + coef[3])
    ka[...] = ax * scale
    kb[...] = ay * scale
    az = az * scale
    lane = lax.broadcasted_iota(jnp.int32, az.shape, 2)
    km[...] = jnp.where(lane == 0, 0.0, az)
    kp[...] = jnp.where(lane == ROWS - 1, 0.0, az)

    for load in lists:
        load.wait()
    meta[...] = jnp.zeros_like(meta)
    slots = lax.broadcasted_iota(jnp.int32, (SLOTS, NY), 0)
    for x in range(NX):
        live = (cells[0][x] == 0) & (slots < cells[1][x])
        listed = jnp.where(live, cells[2][x] * SITES + cells[3][x], -1)
        for t in range(SLOTS):
            where = pl.ds((x % 2) * (ROWS // 2) + t * NY, NY)
            meta[x // 2 : x // 2 + 1, where] = listed[t : t + 1]
        meta[2:3, pl.ds(x * NY, NY)] = cells[0][x]
    wanted, targets, rank, ids = lists_of(meta[...], at)
    idv[...] = ids
    id_copy = pltpu.make_async_copy(idv, id_s, smem_sem.at[0])
    id_copy.start()
    for n, row in enumerate((*wanted, rank)):
        pair[core, n] = row
    pair_copy().start()
    tgt[...] = jnp.zeros_like(tgt)
    for c in range(CHUNKS):
        for h in range(2):
            tgt[2 * c + h : 2 * c + h + 1] = targets[c][h]
        rb[c][EMPTY] = jnp.zeros((KV, ROWS), BF16)
    tgt_copy = pltpu.make_async_copy(tgt, tgt_s, smem_sem.at[3])
    tgt_copy.start()

    for c in range(CHUNKS):
        fill_halo(0, c, wa)
        sweep(c, wa, wb, False)
        send_faces(1, c, wb)
    pair_copy().wait_recv()
    for copy in line_copies():
        copy.start()
    for n, axis in enumerate(AXES):
        lines[n, at[axis]] = pair[...]
    for c in range(CHUNKS):
        fill_halo(1, c, wb)
        sweep(c, wb, wa, False)
        send_faces(2, c, wa)
    drain(lines.at[:, pl.ds(0, 3)], table_sem.at[0, 1])
    for copy in rank_copies():
        copy.start()
    for c, (a, u, v) in enumerate(ROUTES):
        ranks[c, at[v]] = lines[AXES.index(u), :, core, 2]
    line_copy = pltpu.make_async_copy(lines, line_s, smem_sem.at[1])
    line_copy.start()
    id_copy.wait()
    for c in range(CHUNKS):
        fill_halo(2, c, wa)
        sweep(c, wa, wb, True)
        spread(c)
    drain(ranks.at[:, pl.ds(0, 3)], table_sem.at[1, 1])
    rank_copy = pltpu.make_async_copy(ranks, rank_s, smem_sem.at[2])
    rank_copy.start()
    cast(0)
    cast(1)
    line_copy.wait()
    rank_copy.wait()
    find_tiles(1)
    cast(2)
    find_tiles(0)
    find_tiles(2)
    for c in range(CHUNKS):
        pass_on(c)
    for c in GRAM_ORDER:
        reply(c, 0)
    for c in (0, 1, 2):
        reply_on(c, 0)
        reply(c, 1)
    for c in range(CHUNKS):
        transpose_out(c, wb)
    tgt_copy.wait()
    for c in GRAM_ORDER:
        for part in range(len(PARTS)):
            answer(c, part, 0, 0).wait()
            drain(sb.at[c, pl.ds(0, 7 * PARTS[part][1] * SPOT)], ans_recv.at[c, part])
        add_products(c)
    finish()

    drain(fxs, send_sem.at[0])
    drain(fys, send_sem.at[1])
    pair_copy().wait_send()
    drain(lines.at[:, pl.ds(0, 3)], table_sem.at[0, 0])
    drain(ranks.at[:, pl.ds(0, 3)], table_sem.at[1, 0])
    for c in range(CHUNKS):
        drain(pg[c][0].at[pl.ds(0, 3)], near_sem.at[c, 0])
        for n in range(3):
            drain(pg[c][0], cast_send.at[c, n])
        for part in range(len(PARTS)):
            count = PARTS[part][1]
            drain(sb.at[c, pl.ds(0, 7 * count * SPOT)], ans_send.at[c, part])
        drain(fb.at[c, :, pl.ds(0, PARTS[0][1] * SPOT)], fwd_send.at[c])
    for store in stores:
        store.wait()


def smooth(test_vectors, coef_x, coef_y, coef_z, shift, split, count, owner, local):
    vmem = pl.BlockSpec(memory_space=pltpu.VMEM)
    anywhere = pl.BlockSpec(memory_space=pl.ANY)
    cells = pltpu.VMEM((NX, NY, ROWS), F32)
    rows = pltpu.VMEM((LINE, COARSE, KV, ROWS), BF16)
    dma = pltpu.SemaphoreType.DMA
    return pl.pallas_call(
        smooth_kernel,
        out_shape=(
            jax.ShapeDtypeStruct((VECS, NX, NY, ROWS), F32),
            jax.ShapeDtypeStruct((SLOTS, SITES, ROWS), F32),
        ),
        in_specs=[anywhere] * 9,
        out_specs=(anywhere, vmem),
        scratch_shapes=[
            pltpu.VMEM((NX, 1, NY), jnp.int32),
            pltpu.VMEM((NX, 1, NY), jnp.int32),
            pltpu.VMEM((NX, SLOTS, NY), jnp.int32),
            pltpu.VMEM((NX, SLOTS, NY), jnp.int32),
            pltpu.VMEM((8, ROWS), jnp.int32),
            pltpu.VMEM((8, ROWS), jnp.int32),
            pltpu.SMEM((8, ROWS), jnp.int32),
            pltpu.VMEM((CHUNKS, SITES, KV, ROWS), BF16),
            *([pltpu.VMEM((EMPTY + 8, KV, ROWS), BF16)] * CHUNKS),
            pltpu.VMEM((len(PAIRS), SITES * 8, ROWS), F32),
            pltpu.VMEM((VECS, NX, NY, ROWS), F32),
            pltpu.VMEM((4, NX, NY, ROWS), F32),
            pltpu.VMEM((CHUNKS, EXT, ROWS), F32),
            pltpu.VMEM((CHUNKS, EXT, ROWS), F32),
            cells, cells, cells, cells,
            pltpu.VMEM((SWEEPS, CHUNKS, 2, NY * KV, ROWS), BF16),
            pltpu.VMEM((SWEEPS, CHUNKS, 2, NY * KV, ROWS), BF16),
            pltpu.VMEM((SWEEPS, CHUNKS, 2, NX * KV, ROWS), BF16),
            pltpu.VMEM((SWEEPS, CHUNKS, 2, NX * KV, ROWS), BF16),
            pltpu.VMEM((CORES, 3, 1, ROWS), jnp.int32),
            pltpu.VMEM((len(AXES), LINE, CORES, 3, 1, ROWS), jnp.int32),
            pltpu.VMEM((CHUNKS, LINE, LINE, 1, ROWS), jnp.int32),
            pltpu.VMEM((COARSE, ROWS), jnp.int32),
            pltpu.SMEM((len(AXES), LINE, CORES, 3, 1, ROWS), jnp.int32),
            pltpu.SMEM((CHUNKS, LINE, LINE, 1, ROWS), jnp.int32),
            pltpu.SMEM((COARSE, ROWS), jnp.int32),
            pltpu.SMEM((CHUNKS, LINE * CORES, REPLY), jnp.int32),
            *([rows] * (LINE * CHUNKS)),
            pltpu.VMEM((CHUNKS, EMPTY, KV, ROWS), BF16),
            pltpu.VMEM((CHUNKS, CORES, REPLY, KV, ROWS), BF16),
            dma((CHUNKS,)),
            dma((4,)),
            dma((CHUNKS,)),
            dma((2,)),
            dma((SWEEPS, CHUNKS, 2)),
            dma((2,)),
            dma((2, 2)),
            dma((CHUNKS, 2)),
            dma((CHUNKS, 3)),
            dma((CHUNKS, 4)),
            dma((CHUNKS, len(PARTS))),
            dma((CHUNKS, len(PARTS))),
            dma((CHUNKS, CORES)),
            dma((CHUNKS,)),
            dma((CHUNKS, len(PARTS))),
            dma((4,)),
            dma((4,)),
        ],
        compiler_params=pltpu.CompilerParams(
            collective_id=0, has_side_effects=True, vmem_limit_bytes=60 * 1024 * 1024
        ),
        name="smooth",
    )(test_vectors, coef_x, coef_y, coef_z, shift, split, count, owner, local)


def pass_kernel(w_in, sm_in, w_out, sm_out, w_hold, sm_hold, in_sem, out_sem):
    parts = [(w_in, w_hold, w_out)]
    for c in range(CHUNKS):
        part = pl.ds(c * KV, KV)
        parts.append((sm_in.at[part], sm_hold.at[part], sm_out.at[part]))
    ins = [pltpu.make_async_copy(a, b, in_sem.at[n]) for n, (a, b, _) in enumerate(parts)]
    outs = [pltpu.make_async_copy(b, d, out_sem.at[n]) for n, (_, b, d) in enumerate(parts)]
    for copy in ins:
        copy.start()
    for load, store in zip(ins, outs):
        load.wait()
        store.start()
    for store in outs:
        store.wait()


def pass_on_results(weights, sm):
    anywhere = pl.BlockSpec(memory_space=pl.ANY)
    dma = pltpu.SemaphoreType.DMA
    return pl.pallas_call(
        pass_kernel,
        out_shape=(
            jax.ShapeDtypeStruct(weights.shape, F32),
            jax.ShapeDtypeStruct(sm.shape, F32),
        ),
        in_specs=[anywhere, anywhere],
        out_specs=(anywhere, anywhere),
        scratch_shapes=[
            pltpu.VMEM(weights.shape, F32),
            pltpu.VMEM(sm.shape, F32),
            dma((CHUNKS + 1,)),
            dma((CHUNKS + 1,)),
        ],
        compiler_params=pltpu.CompilerParams(vmem_limit_bytes=60 * 1024 * 1024),
        name="fit",
    )(weights, sm)


def per_device(
    test_vectors, coef_x, coef_y, coef_z, shift, cf_split, nbr_count, nbr_owner, nbr_block
):
    sm, weights = smooth(
        test_vectors, coef_x, coef_y, coef_z, shift,
        jnp.swapaxes(cf_split, 1, 2),
        jnp.swapaxes(nbr_count, 1, 2),
        jnp.transpose(nbr_owner, (0, 2, 3, 1)).reshape(NX, SLOTS, NY),
        jnp.transpose(nbr_block, (0, 2, 3, 1)).reshape(NX, SLOTS, NY),
    )
    weights, smoothed = pass_on_results(weights.reshape(SLOTS, NX, NY, ROWS), sm)
    return (smoothed, weights)


def solution(mesh):
    cells = P("gx", "gy", None)
    lists = P("gx", "gy", None, None)
    vectors = P(None, "gx", "gy", None)
    return jax.shard_map(
        per_device,
        mesh=mesh,
        in_specs=(vectors, cells, cells, cells, cells, cells, cells, lists, lists),
        out_specs=(vectors, vectors),
        check_vma=False,
    )
```

```python
import jax
import jax.numpy as jnp
from jax import lax
from jax.experimental import pallas as pl
from jax.experimental.pallas import tpu as pltpu
from jax.sharding import PartitionSpec as P

SLOTS = 4
SWEEPS = 3
ROWS = 128
OMEGA = 0.8
RIDGE = 0.05
VECS = 48
CHUNKS = 3
KV = VECS // CHUNKS
NX = 4
NY = 16
SITES = NX * NY
XROW = (NY + 2) * KV
EXT = (NX + 2) * XROW
GX = 16
GY = 8
MESH = pl.DeviceIdType.MESH
F32 = jnp.float32
BF16 = jnp.bfloat16


def site_row(x, y):
    return (x + 1) * XROW + (y + 1) * KV


def solve_rows(gram, rhs):
    low = [[None] * SLOTS for _ in range(SLOTS)]
    inv = []
    for r in range(SLOTS):
        scaled = []
        diag = gram[r, r]
        for c in range(r):
            rest = gram[r, c]
            for m in range(c):
                rest = rest - scaled[m] * low[c][m]
            scaled.append(rest)
            low[r][c] = rest * inv[c]
            diag = diag - rest * low[r][c]
        inv.append(1.0 / diag)
    fwd = []
    for r in range(SLOTS):
        rest = rhs[r]
        for m in range(r):
            rest = rest - low[r][m] * fwd[m]
        fwd.append(rest)
    out = [None] * SLOTS
    for r in reversed(range(SLOTS)):
        rest = fwd[r] * inv[r]
        for m in range(r + 1, SLOTS):
            rest = rest - low[m][r] * out[m]
        out[r] = rest
    return out


PAIRS = [(s, t) for s in range(SLOTS) for t in range(s + 1)] + [(s, SLOTS) for s in range(SLOTS)]
AXES = "xyz"
LINE = 4
CORES = 2
COARSE = 16
FINE = 48
PLANE = LINE * LINE
ROUTES = (("x", "z", "y"), ("y", "x", "z"), ("z", "y", "x"))
BACKS = (0, 1, 3, 2)
EMPTY = LINE * CORES * PLANE * 2
SPOT = 2 * LINE
GRAM_ORDER = (1, 2, 0)
REPLY = PLANE * 2
PARTS = ((0, 3), (3, 1))


def lists_of(meta, here):
    lane = lax.broadcasted_iota(jnp.int32, (ROWS, ROWS), 1)
    sub = lax.broadcasted_iota(jnp.int32, (ROWS, ROWS), 0)
    diag = lane == sub
    none = 1 << 20

    def column(row):
        return jnp.sum(jnp.where(diag, row, 0), axis=1, keepdims=True)

    members, keys, owners = [], [], []
    for h in range(2):
        entry = meta[h : h + 1]
        owner = entry >> 6
        key = (lane[:1] + h * ROWS) * SITES + (entry & (SITES - 1))
        owners.append(owner)
        keys.append(key)
        members.append(owner == sub)
    first = jnp.minimum(*[jnp.where(m, k, none) for m, k in zip(members, keys)])
    first = jnp.min(first, axis=1, keepdims=True)
    first = jnp.where(first >= none, 0, first)
    second = jnp.maximum(*[jnp.where(m, k, 0) for m, k in zip(members, keys)])
    second = jnp.max(second, axis=1, keepdims=True)
    targets = [[] for _ in ROUTES]
    for h in range(2):
        own = owners[h]
        at_first = jnp.sum(jnp.where(members[h], first, 0), axis=0, keepdims=True)
        place = jnp.where(keys[h] == at_first, 0, 1)
        at = {"x": (own >> 5) & 3, "z": (own >> 3) & 3, "y": (own >> 1) & 3}
        for c, (a, u, v) in enumerate(ROUTES):
            back = (at[v] - here[v]) & 3
            spot = jnp.where(back == 2, 3, jnp.where(back == 3, 2, back))
            slot = ((at[a] * CORES + (own & 1)) * PLANE + spot * LINE + ((at[u] - here[u]) & 3)) * 2 + place
            targets[c].append(jnp.where(own < 0, EMPTY, slot))
    coarse = meta[2:3]
    rank = jnp.sum(jnp.where(sub < lane, column(coarse), 0), axis=0, keepdims=True)
    fine_rank = jnp.minimum(lane[:1] - rank, FINE)
    fine_rank = jnp.where(coarse > 0, FINE, fine_rank)

    def numbers(hit):
        found = jnp.sum(jnp.where(hit, lane[: hit.shape[0]], 0), axis=1, keepdims=True)
        return jnp.broadcast_to(found, hit.shape)

    ids = numbers((rank == sub[:COARSE]) & (coarse > 0))
    fine_ids = numbers((fine_rank == sub[:FINE]) & (lane[:1] < SITES))
    rank = jnp.minimum(rank, COARSE - 1)
    return (first, second), targets, rank, ids, fine_ids, fine_rank


def ranks_wanted(blocks, table):
    lane = lax.broadcasted_iota(jnp.int32, (ROWS, ROWS), 1)
    sub = lax.broadcasted_iota(jnp.int32, (ROWS, ROWS), 0)
    found = jnp.sum(
        jnp.where(lane == (blocks & (SITES - 1)), table, 0), axis=1, keepdims=True
    )
    return jnp.sum(jnp.where(lane == sub, found, 0), axis=0, keepdims=True)


def smooth_kernel(
    tv, cx, cy, cz, sh, split, count, owner, local, sm_out, w_out,
    split_v, count_v, owner_v, local_v, meta, tgt, tgt_s, blk, rb0, rb1, rb2, part_sums,
    stage, coef, wa, wb, ka, kb, km, kp, fxs, fxr, fys, fyr,
    pair, lines, near, far, block_cols, idv, line_s, id_s, fine_s, spot_s, p00, p01, p02, p03, p10, p11, p12, p13, p20, p21, p22, p23, sb, fb,
    in_sem, coef_sem, out_sem, send_sem, recv_sem, pair_sem, table_sem, gather_sem,
    near_sem, cast_send, cast_recv, ans_send, ans_recv, hop_recv, fwd_send, own_sem, smem_sem, list_sem,
):
    cells = (split_v, count_v, owner_v, local_v)
    rb = (rb0, rb1, rb2)
    pg = ((p00, p01, p02, p03), (p10, p11, p12, p13), (p20, p21, p22, p23))
    i = lax.axis_index("gx")
    j = lax.axis_index("gy")
    core = lax.rem(j, CORES)
    at = {"x": i // LINE, "z": lax.rem(i, LINE), "y": j // CORES}
    peers = (
        (lax.rem(i + GX - 1, GX), j),
        (lax.rem(i + 1, GX), j),
        (i, lax.rem(j + GY - 1, GY)),
        (i, lax.rem(j + 1, GY)),
    )

    def device(axis, d, e):
        moved = dict(at)
        moved[axis] = lax.rem(at[axis] + d, LINE)
        return (moved["x"] * LINE + moved["z"], moved["y"] * CORES + lax.rem(core + e, CORES))

    def remote(src, dst, send, recv, peer):
        return pltpu.make_async_remote_copy(
            src_ref=src, dst_ref=dst, send_sem=send, recv_sem=recv,
            device_id=peer, device_id_type=MESH,
        )

    loads = []
    for c in range(CHUNKS):
        part = pl.ds(c * KV, KV)
        loads.append(pltpu.make_async_copy(tv.at[part], stage.at[part], in_sem.at[c]))
    loads[0].start()
    barrier = pltpu.get_barrier_semaphore()
    for peer in peers[:2]:
        pl.semaphore_signal(barrier, inc=1, device_id=peer, device_id_type=MESH)
    pl.semaphore_signal(barrier, inc=1, device_id=device("x", 0, 1), device_id_type=MESH)
    for axis in AXES:
        for d in range(1, LINE):
            for e in range(CORES):
                pl.semaphore_signal(
                    barrier, inc=1, device_id=device(axis, d, e), device_id_type=MESH
                )
    greeted = 3 + len(AXES) * (LINE - 1) * CORES
    for load in loads[1:]:
        load.start()
    coef_loads = []
    for n, part in enumerate((cx, cy, cz, sh)):
        load = pltpu.make_async_copy(part, coef.at[n], coef_sem.at[n])
        load.start()
        coef_loads.append(load)
    lists = []
    for n, part in enumerate((split, count, owner, local)):
        load = pltpu.make_async_copy(part, cells[n], list_sem.at[n])
        load.start()
        lists.append(load)

    keep = (
        (i > 0).astype(F32),
        (i < GX - 1).astype(F32),
        (j > 0).astype(F32),
        (j < GY - 1).astype(F32),
    )

    def drain(ref, sem):
        pltpu.make_async_copy(ref, ref, sem).wait()

    def copies(s, c):
        out = []
        for d in range(4):
            src, dst = (fxs, fxr) if d < 2 else (fys, fyr)
            out.append(
                remote(
                    src.at[s, c, d % 2], dst.at[s, c, 1 - d % 2],
                    send_sem.at[d // 2], recv_sem.at[s, c, d // 2], peers[d],
                )
            )
        return out

    def send_faces(s, c, w):
        for side in range(2):
            x = side * (NX - 1)
            fxs[s, c, side] = w[c, pl.ds(site_row(x, 0), NY * KV)].astype(BF16)
            y = side * (NY - 1)
            for x in range(NX):
                fys[s, c, side, pl.ds(x * KV, KV)] = w[c, pl.ds(site_row(x, y), KV)].astype(BF16)
        for copy in copies(s, c):
            copy.start()

    def fill_halo(s, c, w):
        drain(fxr.at[s, c], recv_sem.at[s, c, 0])
        drain(fyr.at[s, c], recv_sem.at[s, c, 1])
        for side in range(2):
            x = -1 if side == 0 else NX
            w[c, pl.ds(site_row(x, 0), NY * KV)] = fxr[s, c, side].astype(F32) * keep[side]
            y = -1 if side == 0 else NY
            for x in range(NX):
                w[c, pl.ds(site_row(x, y), KV)] = (
                    fyr[s, c, side, pl.ds(x * KV, KV)].astype(F32) * keep[2 + side]
                )

    def sweep(c, src, dst, last):
        def plane(x, carry):
            base = pl.multiple_of(x * XROW, 16)

            def cell(dx, y):
                return src[c, pl.ds(base + site_row(dx, y), KV)]

            below, here = cell(0, -1), cell(0, 0)
            for y in range(NY):
                above = cell(0, y + 1)
                row = slice(y, y + 1)
                new = (
                    ka[x, row] * (cell(-1, y) + cell(1, y))
                    + kb[x, row] * (below + above)
                    + km[x, row] * pltpu.roll(here, 1, 1)
                    + kp[x, row] * pltpu.roll(here, ROWS - 1, 1)
                    + (1.0 - OMEGA) * here
                )
                dst[c, pl.ds(base + site_row(0, y), KV)] = new
                if last:
                    blk[c, x * NY + y] = new.astype(BF16)
                below, here = here, above
            return carry

        lax.fori_loop(0, NX, plane, 0)

    def pair_copy():
        slot = pair.at[core]
        return remote(slot, slot, pair_sem.at[0], pair_sem.at[1], device("x", 0, 1))

    def line_copies():
        return [
            remote(
                pair, lines.at[n, at[axis]], table_sem.at[0], table_sem.at[1],
                device(axis, d, 0),
            )
            for n, axis in enumerate(AXES)
            for d in range(1, LINE)
        ]

    def gather_copies(step):
        send, recv = gather_sem.at[step, 0], gather_sem.at[step, 1]
        if step == 0:
            slot = near.at[at["y"] * CORES + core]
            return [
                remote(slot, slot, send, recv, device("y", d, e))
                for d in range(LINE)
                for e in range(CORES)
                if d or e
            ]
        slot = far.at[at["x"], at["z"]] if step == 1 else far.at[at["x"]]
        return [
            remote(slot, slot, send, recv, device("zx"[step - 1], d, 0)) for d in range(1, LINE)
        ]

    def gathered(step):
        if step == 0:
            return near.at[pl.ds(0, 7)]
        return far.at[0, pl.ds(0, 3)] if step == 1 else far.at[pl.ds(0, 3)]

    def gather_step(step):
        drain(gathered(step), gather_sem.at[step, 1])
        if step == 0:
            for n in range(LINE * CORES):
                far[at["x"], at["z"], n : n + 1] = near[n, 0:1]
        for copy in gather_copies(step + 1):
            copy.start()

    def ask():
        drain(gathered(2), gather_sem.at[2, 1])
        table = far[...].reshape(ROWS, ROWS)
        for p in range(2):
            pair[core, p] = ranks_wanted(block_cols[p], table)
        pair_copy().start()

    def ask_lines():
        pair_copy().wait_recv()
        for copy in line_copies():
            copy.start()
        for n, axis in enumerate(AXES):
            lines[n, at[axis]] = pair[...]

    steps = {
        (0, 1): lambda: gather_step(0),
        (1, 0): lambda: gather_step(1),
        (1, 2): ask,
        (2, 1): ask_lines,
    }

    def spread_copies(c):
        a, u, v = ROUTES[c]
        return [
            remote(
                pg[c][0].at[0], pg[c][0].at[LINE - d],
                near_sem.at[c, 0], near_sem.at[c, 1], device(u, d, 0),
            )
            for d in (2, 1, 3)
        ]

    def cast_copies(c):
        a, u, v = ROUTES[c]
        plan = (
            (0, 0, 1, 3, 1, 0, 0),
            (0, 0, 1, 1, 3, 1, 2),
            (0, 1, 1, 3, 1, 0, 0),
            (0, 2, 2, 1, 3, 1, 1),
            (0, 2, 2, 3, 1, 0, 2),
            (0, 1, 1, 1, 3, 1, 2),
            (3, 0, 2, 2, 1, 2, 3),
            (1, 2, 2, 2, 3, 2, 3),
        )
        return [
            remote(
                pg[c][src].at[pl.ds(first, size)], pg[c][dst].at[pl.ds(first, size)],
                cast_send.at[c, out], cast_recv.at[c, into], device(v, d, 0),
            )
            for src, first, size, dst, d, out, into in plan
        ]

    def piece(slot, part):
        first, count = PARTS[part]
        return pl.ds(slot * REPLY + first * SPOT, count * SPOT)

    def answer(c, part, d, e):
        a = ROUTES[c][0]
        slot = lax.rem(at[a] + d, LINE) * CORES + lax.rem(core + e, CORES)
        here = at[a] * CORES + core
        src = sb.at[c, piece(slot, part)]
        dst, peer = rb[c].at[piece(here, part)], device(a, d, e)
        if d == 0 and e == 0:
            return pltpu.make_async_copy(src, dst, own_sem.at[c, part])
        if d == 2 and part == 0:
            dst, peer = fb.at[c, e, piece(0, part)], device(a, 1 + 2 * e, 0)
            return remote(src, dst, ans_send.at[c, part], hop_recv.at[c, e], peer)
        return remote(src, dst, ans_send.at[c, part], ans_recv.at[c, part], peer)

    def forward(c, part, e):
        a = ROUTES[c][0]
        origin = lax.rem(at[a] + 3 - 2 * e, LINE) * CORES + core
        return remote(
            fb.at[c, e, piece(0, part)], rb[c].at[piece(origin, part)],
            fwd_send.at[c], ans_recv.at[c, part], device(a, 1 + 2 * e, e),
        )

    order = [(d, e) for d in (2, 1, 3, 0) for e in range(CORES)]

    def spread(c):
        a, u, v = ROUTES[c]
        for r in range(COARSE):
            pg[c][0][0, r] = blk[c, id_s[r, 0] & (SITES - 1)]
        for copy in spread_copies(c) + cast_copies(c)[:2]:
            copy.start()

    def cast(c):
        drain(pg[c][1].at[pl.ds(0, 3)], near_sem.at[c, 1])
        for copy in cast_copies(c)[2:6]:
            copy.start()

    def pass_on(c):
        for n in range(2):
            drain(pg[c][0].at[pl.ds(0, 2)], cast_recv.at[c, n])
            cast_copies(c)[6 + n].start()

    def reply(c, part):
        a, u, v = ROUTES[c]
        n = AXES.index(a)
        drain(pg[c][0], cast_recv.at[c, 2 + part])
        first, count = PARTS[part]
        for d, e in order:
            q, to = lax.rem(at[a] + d, LINE), lax.rem(core + e, CORES)
            slot = q * CORES + to
            for place in range(first, first + count):
                back = BACKS[place]
                tiles = []
                for ahead in range(LINE):
                    whose = {
                        a: at[a],
                        u: lax.rem(at[u] + ahead, LINE),
                        v: lax.rem(at[v] + back, LINE),
                    }
                    owner = whose["x"] * 32 + whose["z"] * 8 + whose["y"] * 2 + core
                    for p in range(2):
                        rank = line_s[n, q, to, p, 0, owner] & (COARSE - 1)
                        tiles.append(pg[c][back][ahead, rank])
                for t, tile in enumerate(tiles):
                    sb[c, slot * REPLY + place * SPOT + t] = tile
            answer(c, part, d, e).start()

    def reply_on(c, part):
        for e in range(2):
            answer(c, part, 2, e).wait_recv()
            forward(c, part, e).start()

    def transpose_in(c):
        loads[c].wait()
        for x in range(NX):
            for half in range(NY // 8):
                for k in range(KV):
                    wa[c, pl.ds(site_row(x, half * 8) + k, 8, stride=KV), :] = stage[
                        c * KV + k, x, pl.ds(half * 8, 8), :
                    ]

    def products(c, place):
        b = fine_s[place, 0] & (SITES - 1)
        column = ((b >> 4) & 1) * (ROWS // 2) + (b & (NY - 1))
        values = []
        for t in range(SLOTS):
            found = tgt_s[2 * c + (b >> 5), column + t * NY]
            values.append(rb[c][found].astype(F32))
        values.append(blk[c, b].astype(F32))
        for n, (p, q) in enumerate(PAIRS):
            product = values[p] * values[q]
            product = product[0:8] + product[8:16]
            if c != GRAM_ORDER[0]:
                product = product + part_sums[n, place]
            part_sums[n, place] = product

    def add_products(c):
        def step(g, carry):
            for m in range(4):
                products(c, g * 4 + m)
            return carry

        lax.fori_loop(0, FINE // 4, step, 0)

    def finish():
        sub = lax.broadcasted_iota(jnp.int32, (8, ROWS), 0)
        low4, low2, low1 = sub < 4, (sub & 2) == 0, (sub & 1) == 0

        def merge(first, second, keep_first, shift):
            first = first + pltpu.roll(first, 8 - shift, 0)
            second = second + pltpu.roll(second, shift, 0)
            return jnp.where(keep_first, first, second)

        def group(g, carry):
            total = {}
            spots = [spot_s[0, g * 8 + m] & (SITES - 1) for m in range(8)]
            for n, couple in enumerate(PAIRS):
                rows = [part_sums[n, spot] for spot in spots]
                rows = [
                    jnp.where(low4, rows[m], rows[m + 4])
                    + pltpu.roll(jnp.where(low4, rows[m + 4], rows[m]), 4, 0)
                    for m in range(4)
                ]
                rows = [merge(rows[m], rows[m + 2], low2, 2) for m in range(2)]
                total[couple] = merge(rows[0], rows[1], low1, 1) * (1.0 / VECS)
                if couple[0] == couple[1]:
                    total[couple] = total[couple] + RIDGE
            out = solve_rows(total, [total[s, SLOTS] for s in range(SLOTS)])
            for s in range(SLOTS):
                w_out[s, pl.ds(pl.multiple_of(g * 8, 8), 8), :] = out[s]
            return carry

        lax.fori_loop(0, SITES // 8, group, 0)

    stores = []

    def transpose_out(c, w):
        for x in range(NX):
            for half in range(NY // 8):
                for k in range(KV):
                    stage[c * KV + k, x, pl.ds(half * 8, 8), :] = w[
                        c, pl.ds(site_row(x, half * 8) + k, 8, stride=KV), :
                    ]
        part = pl.ds(c * KV, KV)
        store = pltpu.make_async_copy(stage.at[part], sm_out.at[part], out_sem.at[c])
        store.start()
        stores.append(store)

    for c in range(CHUNKS):
        transpose_in(c)
        if c == 0:
            pl.semaphore_wait(barrier, greeted)
        send_faces(0, c, wa)

    for load in coef_loads:
        load.wait()
    ax, ay, az = coef[0], coef[1], coef[2]
    scale = OMEGA / (2.0 * (ax + ay + az) + coef[3])
    ka[...] = ax * scale
    kb[...] = ay * scale
    az = az * scale
    lane = lax.broadcasted_iota(jnp.int32, az.shape, 2)
    km[...] = jnp.where(lane == 0, 0.0, az)
    kp[...] = jnp.where(lane == ROWS - 1, 0.0, az)

    for load in lists:
        load.wait()
    meta[...] = jnp.zeros_like(meta)
    slots = lax.broadcasted_iota(jnp.int32, (SLOTS, NY), 0)
    for x in range(NX):
        live = (cells[0][x] == 0) & (slots < cells[1][x])
        listed = jnp.where(live, cells[2][x] * SITES + cells[3][x], -1)
        for t in range(SLOTS):
            where = pl.ds((x % 2) * (ROWS // 2) + t * NY, NY)
            meta[x // 2 : x // 2 + 1, where] = listed[t : t + 1]
        meta[2:3, pl.ds(x * NY, NY)] = cells[0][x]
    blocks, targets, rank, ids, fine_ids, fine_rank = lists_of(meta[...], at)
    near[at["y"] * CORES + core] = jnp.broadcast_to(rank, (8, ROWS))
    for copy in gather_copies(0):
        copy.start()
    for p in range(2):
        block_cols[p] = jnp.broadcast_to(blocks[p], (ROWS, ROWS))
    idv[:COARSE] = ids
    idv[COARSE : COARSE + FINE] = fine_ids
    idv[COARSE + FINE :] = jnp.broadcast_to(fine_rank, (8, ROWS))
    part_sums[:, FINE] = jnp.zeros((len(PAIRS), 8, ROWS), F32)
    id_copies = [
        pltpu.make_async_copy(idv.at[pl.ds(0, COARSE)], id_s, smem_sem.at[0]),
        pltpu.make_async_copy(idv.at[pl.ds(COARSE, FINE)], fine_s, smem_sem.at[2]),
        pltpu.make_async_copy(idv.at[pl.ds(COARSE + FINE, 8)], spot_s, smem_sem.at[4]),
    ]
    for copy in id_copies:
        copy.start()
    tgt[...] = jnp.zeros_like(tgt)
    for c in range(CHUNKS):
        for h in range(2):
            tgt[2 * c + h : 2 * c + h + 1] = targets[c][h]
        rb[c][EMPTY] = jnp.zeros((KV, ROWS), BF16)
    tgt_copy = pltpu.make_async_copy(tgt, tgt_s, smem_sem.at[3])
    tgt_copy.start()

    for s in range(SWEEPS):
        src, dst = (wb, wa) if s % 2 else (wa, wb)
        for c in range(CHUNKS):
            fill_halo(s, c, src)
            sweep(c, src, dst, s == SWEEPS - 1)
            if s < SWEEPS - 1:
                send_faces(s + 1, c, dst)
            else:
                if c == 0:
                    for copy in id_copies:
                        copy.wait()
                spread(c)
            if (s, c) in steps:
                steps[s, c]()
    drain(lines.at[:, pl.ds(0, 3)], table_sem.at[1])
    line_copy = pltpu.make_async_copy(lines, line_s, smem_sem.at[1])
    line_copy.start()
    cast(0)
    cast(1)
    cast(2)
    line_copy.wait()
    for c in range(CHUNKS):
        pass_on(c)
    for c in (1, 2, 0):
        reply(c, 0)
    for c in (1, 0, 2):
        reply_on(c, 0)
        reply(c, 1)
    for c in range(CHUNKS):
        transpose_out(c, wb)
    tgt_copy.wait()
    for c in GRAM_ORDER:
        for part in range(len(PARTS)):
            answer(c, part, 0, 0).wait()
            drain(sb.at[c, pl.ds(0, 7 * PARTS[part][1] * SPOT)], ans_recv.at[c, part])
        add_products(c)
    finish()

    drain(fxs, send_sem.at[0])
    drain(fys, send_sem.at[1])
    pair_copy().wait_send()
    drain(lines.at[:, pl.ds(0, 3)], table_sem.at[0])
    for step in range(3):
        drain(gathered(step), gather_sem.at[step, 0])
    for c in range(CHUNKS):
        drain(pg[c][0].at[pl.ds(0, 3)], near_sem.at[c, 0])
        for n in range(3):
            drain(pg[c][0], cast_send.at[c, n])
        for part in range(len(PARTS)):
            count = PARTS[part][1]
            drain(sb.at[c, pl.ds(0, 7 * count * SPOT)], ans_send.at[c, part])
        drain(fb.at[c, :, pl.ds(0, PARTS[0][1] * SPOT)], fwd_send.at[c])
    for store in stores:
        store.wait()


def smooth(test_vectors, coef_x, coef_y, coef_z, shift, split, count, owner, local):
    vmem = pl.BlockSpec(memory_space=pltpu.VMEM)
    anywhere = pl.BlockSpec(memory_space=pl.ANY)
    cells = pltpu.VMEM((NX, NY, ROWS), F32)
    rows = pltpu.VMEM((LINE, COARSE, KV, ROWS), BF16)
    dma = pltpu.SemaphoreType.DMA
    return pl.pallas_call(
        smooth_kernel,
        out_shape=(
            jax.ShapeDtypeStruct((VECS, NX, NY, ROWS), F32),
            jax.ShapeDtypeStruct((SLOTS, SITES, ROWS), F32),
        ),
        in_specs=[anywhere] * 9,
        out_specs=(anywhere, vmem),
        scratch_shapes=[
            pltpu.VMEM((NX, 1, NY), jnp.int32),
            pltpu.VMEM((NX, 1, NY), jnp.int32),
            pltpu.VMEM((NX, SLOTS, NY), jnp.int32),
            pltpu.VMEM((NX, SLOTS, NY), jnp.int32),
            pltpu.VMEM((8, ROWS), jnp.int32),
            pltpu.VMEM((8, ROWS), jnp.int32),
            pltpu.SMEM((8, ROWS), jnp.int32),
            pltpu.VMEM((CHUNKS, SITES, KV, ROWS), BF16),
            *([pltpu.VMEM((EMPTY + 8, KV, ROWS), BF16)] * CHUNKS),
            pltpu.VMEM((len(PAIRS), SITES, 8, ROWS), F32),
            pltpu.VMEM((VECS, NX, NY, ROWS), F32),
            pltpu.VMEM((4, NX, NY, ROWS), F32),
            pltpu.VMEM((CHUNKS, EXT, ROWS), F32),
            pltpu.VMEM((CHUNKS, EXT, ROWS), F32),
            cells, cells, cells, cells,
            pltpu.VMEM((SWEEPS, CHUNKS, 2, NY * KV, ROWS), BF16),
            pltpu.VMEM((SWEEPS, CHUNKS, 2, NY * KV, ROWS), BF16),
            pltpu.VMEM((SWEEPS, CHUNKS, 2, NX * KV, ROWS), BF16),
            pltpu.VMEM((SWEEPS, CHUNKS, 2, NX * KV, ROWS), BF16),
            pltpu.VMEM((CORES, 2, 1, ROWS), jnp.int32),
            pltpu.VMEM((len(AXES), LINE, CORES, 2, 1, ROWS), jnp.int32),
            pltpu.VMEM((LINE * CORES, 8, ROWS), jnp.int32),
            pltpu.VMEM((LINE, LINE, LINE * CORES, ROWS), jnp.int32),
            pltpu.VMEM((2, ROWS, ROWS), jnp.int32),
            pltpu.VMEM((COARSE + FINE + 8, ROWS), jnp.int32),
            pltpu.SMEM((len(AXES), LINE, CORES, 2, 1, ROWS), jnp.int32),
            pltpu.SMEM((COARSE, ROWS), jnp.int32),
            pltpu.SMEM((FINE, ROWS), jnp.int32),
            pltpu.SMEM((8, ROWS), jnp.int32),
            *([rows] * (LINE * CHUNKS)),
            pltpu.VMEM((CHUNKS, EMPTY, KV, ROWS), BF16),
            pltpu.VMEM((CHUNKS, CORES, REPLY, KV, ROWS), BF16),
            dma((CHUNKS,)),
            dma((4,)),
            dma((CHUNKS,)),
            dma((2,)),
            dma((SWEEPS, CHUNKS, 2)),
            dma((2,)),
            dma((2,)),
            dma((3, 2)),
            dma((CHUNKS, 2)),
            dma((CHUNKS, 3)),
            dma((CHUNKS, 4)),
            dma((CHUNKS, len(PARTS))),
            dma((CHUNKS, len(PARTS))),
            dma((CHUNKS, CORES)),
            dma((CHUNKS,)),
            dma((CHUNKS, len(PARTS))),
            dma((5,)),
            dma((4,)),
        ],
        compiler_params=pltpu.CompilerParams(
            collective_id=0, has_side_effects=True, vmem_limit_bytes=60 * 1024 * 1024
        ),
        name="smooth",
    )(test_vectors, coef_x, coef_y, coef_z, shift, split, count, owner, local)


def pass_kernel(w_in, sm_in, w_out, sm_out, w_hold, sm_hold, in_sem, out_sem):
    parts = [(w_in, w_hold, w_out)]
    for c in range(CHUNKS):
        part = pl.ds(c * KV, KV)
        parts.append((sm_in.at[part], sm_hold.at[part], sm_out.at[part]))
    ins = [pltpu.make_async_copy(a, b, in_sem.at[n]) for n, (a, b, _) in enumerate(parts)]
    outs = [pltpu.make_async_copy(b, d, out_sem.at[n]) for n, (_, b, d) in enumerate(parts)]
    for copy in ins:
        copy.start()
    for load, store in zip(ins, outs):
        load.wait()
        store.start()
    for store in outs:
        store.wait()


def pass_on_results(weights, sm):
    anywhere = pl.BlockSpec(memory_space=pl.ANY)
    dma = pltpu.SemaphoreType.DMA
    return pl.pallas_call(
        pass_kernel,
        out_shape=(
            jax.ShapeDtypeStruct(weights.shape, F32),
            jax.ShapeDtypeStruct(sm.shape, F32),
        ),
        in_specs=[anywhere, anywhere],
        out_specs=(anywhere, anywhere),
        scratch_shapes=[
            pltpu.VMEM(weights.shape, F32),
            pltpu.VMEM(sm.shape, F32),
            dma((CHUNKS + 1,)),
            dma((CHUNKS + 1,)),
        ],
        compiler_params=pltpu.CompilerParams(vmem_limit_bytes=60 * 1024 * 1024),
        name="fit",
    )(weights, sm)


def per_device(
    test_vectors, coef_x, coef_y, coef_z, shift, cf_split, nbr_count, nbr_owner, nbr_block
):
    sm, weights = smooth(
        test_vectors, coef_x, coef_y, coef_z, shift,
        jnp.swapaxes(cf_split, 1, 2),
        jnp.swapaxes(nbr_count, 1, 2),
        jnp.transpose(nbr_owner, (0, 2, 3, 1)).reshape(NX, SLOTS, NY),
        jnp.transpose(nbr_block, (0, 2, 3, 1)).reshape(NX, SLOTS, NY),
    )
    weights, smoothed = pass_on_results(weights.reshape(SLOTS, NX, NY, ROWS), sm)
    return (smoothed, weights)


def solution(mesh):
    cells = P("gx", "gy", None)
    lists = P("gx", "gy", None, None)
    vectors = P(None, "gx", "gy", None)
    return jax.shard_map(
        per_device,
        mesh=mesh,
        in_specs=(vectors, cells, cells, cells, cells, cells, cells, lists, lists),
        out_specs=(vectors, vectors),
        check_vma=False,
    )
```

```python
import jax
import jax.numpy as jnp
from jax import lax
from jax.experimental import pallas as pl
from jax.experimental.pallas import tpu as pltpu
from jax.sharding import PartitionSpec as P

SLOTS = 4
SWEEPS = 3
ROWS = 128
OMEGA = 0.8
RIDGE = 0.05
VECS = 48
CHUNKS = 3
KV = VECS // CHUNKS
NX = 4
NY = 16
SITES = NX * NY
XROW = (NY + 2) * KV
EXT = (NX + 2) * XROW
GX = 16
GY = 8
MESH = pl.DeviceIdType.MESH
F32 = jnp.float32
BF16 = jnp.bfloat16


def site_row(x, y):
    return (x + 1) * XROW + (y + 1) * KV


def solve_rows(gram, rhs):
    low = [[None] * SLOTS for _ in range(SLOTS)]
    inv = []
    for r in range(SLOTS):
        scaled = []
        diag = gram[r, r]
        for c in range(r):
            rest = gram[r, c]
            for m in range(c):
                rest = rest - scaled[m] * low[c][m]
            scaled.append(rest)
            low[r][c] = rest * inv[c]
            diag = diag - rest * low[r][c]
        inv.append(1.0 / diag)
    fwd = []
    for r in range(SLOTS):
        rest = rhs[r]
        for m in range(r):
            rest = rest - low[r][m] * fwd[m]
        fwd.append(rest)
    out = [None] * SLOTS
    for r in reversed(range(SLOTS)):
        rest = fwd[r] * inv[r]
        for m in range(r + 1, SLOTS):
            rest = rest - low[m][r] * out[m]
        out[r] = rest
    return out


PAIRS = [(s, t) for s in range(SLOTS) for t in range(s + 1)] + [(s, SLOTS) for s in range(SLOTS)]
AXES = "xyz"
LINE = 4
CORES = 2
COARSE = 16
FINE = 48
PIECES = 6
PLANE = LINE * LINE
ROUTES = (("x", "z", "y"), ("y", "x", "z"), ("z", "y", "x"))
BACKS = (0, 1, 3, 2)
EMPTY = LINE * CORES * PLANE * 2
SPOT = 2 * LINE
GRAM_ORDER = (1, 2, 0)
REPLY = PLANE * 2
PARTS = ((0, 3), (3, 1))


def lists_of(meta, here):
    lane = lax.broadcasted_iota(jnp.int32, (ROWS, ROWS), 1)
    sub = lax.broadcasted_iota(jnp.int32, (ROWS, ROWS), 0)
    diag = lane == sub
    none = 1 << 20

    def column(row):
        return jnp.sum(jnp.where(diag, row, 0), axis=1, keepdims=True)

    members, keys, owners = [], [], []
    for h in range(2):
        entry = meta[h : h + 1]
        owner = entry >> 6
        key = (lane[:1] + h * ROWS) * SITES + (entry & (SITES - 1))
        owners.append(owner)
        keys.append(key)
        members.append(owner == sub)
    first = jnp.minimum(*[jnp.where(m, k, none) for m, k in zip(members, keys)])
    first = jnp.min(first, axis=1, keepdims=True)
    first = jnp.where(first >= none, 0, first)
    second = jnp.maximum(*[jnp.where(m, k, 0) for m, k in zip(members, keys)])
    second = jnp.max(second, axis=1, keepdims=True)
    targets = [[] for _ in ROUTES]
    for h in range(2):
        own = owners[h]
        at_first = jnp.sum(jnp.where(members[h], first, 0), axis=0, keepdims=True)
        place = jnp.where(keys[h] == at_first, 0, 1)
        at = {"x": (own >> 5) & 3, "z": (own >> 3) & 3, "y": (own >> 1) & 3}
        for c, (a, u, v) in enumerate(ROUTES):
            back = (at[v] - here[v]) & 3
            spot = jnp.where(back == 2, 3, jnp.where(back == 3, 2, back))
            slot = ((at[a] * CORES + (own & 1)) * PLANE + spot * LINE + ((at[u] - here[u]) & 3)) * 2 + place
            targets[c].append(jnp.where(own < 0, EMPTY, slot))
    coarse = meta[2:3]
    rank = jnp.sum(jnp.where(sub < lane, column(coarse), 0), axis=0, keepdims=True)
    fine_rank = jnp.minimum(lane[:1] - rank, FINE)
    fine_rank = jnp.where(coarse > 0, FINE, fine_rank)

    def numbers(hit):
        found = jnp.sum(jnp.where(hit, lane[: hit.shape[0]], 0), axis=1, keepdims=True)
        return jnp.broadcast_to(found, hit.shape)

    ids = numbers((rank == sub[:COARSE]) & (coarse > 0))
    fine_ids = numbers((fine_rank == sub[:FINE]) & (lane[:1] < SITES))
    rank = jnp.minimum(rank, COARSE - 1)
    return (first, second), targets, rank, ids, fine_ids, fine_rank


def ranks_wanted(blocks, table):
    lane = lax.broadcasted_iota(jnp.int32, (ROWS, ROWS), 1)
    sub = lax.broadcasted_iota(jnp.int32, (ROWS, ROWS), 0)
    found = jnp.sum(
        jnp.where(lane == (blocks & (SITES - 1)), table, 0), axis=1, keepdims=True
    )
    return jnp.sum(jnp.where(lane == sub, found, 0), axis=0, keepdims=True)


def smooth_kernel(
    tv, cx, cy, cz, sh, split, count, owner, local, sm_out, w_out,
    split_v, count_v, owner_v, local_v, meta, tgt, tgt_s, blk, rb0, rb1, rb2, part_sums,
    stage, coef, wa, wb, ka, kb, km, kp, fxs, fxr, fys, fyr,
    pair, lines, near, far, block_cols, idv, line_s, id_s, fine_s, spot_s, p00, p01, p02, p03, p10, p11, p12, p13, p20, p21, p22, p23, sb, fb,
    in_sem, coef_sem, out_sem, send_sem, recv_sem, pair_sem, table_sem, gather_sem,
    near_sem, cast_send, cast_recv, ans_send, ans_recv, hop_recv, fwd_send, own_sem, smem_sem, list_sem,
):
    cells = (split_v, count_v, owner_v, local_v)
    rb = (rb0, rb1, rb2)
    pg = ((p00, p01, p02, p03), (p10, p11, p12, p13), (p20, p21, p22, p23))
    i = lax.axis_index("gx")
    j = lax.axis_index("gy")
    core = lax.rem(j, CORES)
    at = {"x": i // LINE, "z": lax.rem(i, LINE), "y": j // CORES}
    peers = (
        (lax.rem(i + GX - 1, GX), j),
        (lax.rem(i + 1, GX), j),
        (i, lax.rem(j + GY - 1, GY)),
        (i, lax.rem(j + 1, GY)),
    )

    def device(axis, d, e):
        moved = dict(at)
        moved[axis] = lax.rem(at[axis] + d, LINE)
        return (moved["x"] * LINE + moved["z"], moved["y"] * CORES + lax.rem(core + e, CORES))

    def remote(src, dst, send, recv, peer):
        return pltpu.make_async_remote_copy(
            src_ref=src, dst_ref=dst, send_sem=send, recv_sem=recv,
            device_id=peer, device_id_type=MESH,
        )

    loads = []
    for c in range(CHUNKS):
        part = pl.ds(c * KV, KV)
        loads.append(pltpu.make_async_copy(tv.at[part], stage.at[part], in_sem.at[c]))
    loads[0].start()
    barrier = pltpu.get_barrier_semaphore()
    for peer in peers[:2]:
        pl.semaphore_signal(barrier, inc=1, device_id=peer, device_id_type=MESH)
    pl.semaphore_signal(barrier, inc=1, device_id=device("x", 0, 1), device_id_type=MESH)
    for axis in AXES:
        for d in range(1, LINE):
            for e in range(CORES):
                pl.semaphore_signal(
                    barrier, inc=1, device_id=device(axis, d, e), device_id_type=MESH
                )
    greeted = 3 + len(AXES) * (LINE - 1) * CORES
    for load in loads[1:]:
        load.start()
    coef_loads = []
    for n, part in enumerate((cx, cy, cz, sh)):
        load = pltpu.make_async_copy(part, coef.at[n], coef_sem.at[n])
        load.start()
        coef_loads.append(load)
    lists = []
    for n, part in enumerate((split, count, owner, local)):
        load = pltpu.make_async_copy(part, cells[n], list_sem.at[n])
        load.start()
        lists.append(load)

    keep = (
        (i > 0).astype(F32),
        (i < GX - 1).astype(F32),
        (j > 0).astype(F32),
        (j < GY - 1).astype(F32),
    )

    def drain(ref, sem):
        pltpu.make_async_copy(ref, ref, sem).wait()

    def copies(s, c):
        out = []
        for d in range(4):
            src, dst = (fxs, fxr) if d < 2 else (fys, fyr)
            out.append(
                remote(
                    src.at[s, c, d % 2], dst.at[s, c, 1 - d % 2],
                    send_sem.at[d // 2], recv_sem.at[s, c, d // 2], peers[d],
                )
            )
        return out

    def send_faces(s, c, w):
        for side in range(2):
            x = side * (NX - 1)
            fxs[s, c, side] = w[c, pl.ds(site_row(x, 0), NY * KV)].astype(BF16)
            y = side * (NY - 1)
            for x in range(NX):
                fys[s, c, side, pl.ds(x * KV, KV)] = w[c, pl.ds(site_row(x, y), KV)].astype(BF16)
        for copy in copies(s, c):
            copy.start()

    def fill_halo(s, c, w):
        drain(fxr.at[s, c], recv_sem.at[s, c, 0])
        drain(fyr.at[s, c], recv_sem.at[s, c, 1])
        for side in range(2):
            x = -1 if side == 0 else NX
            w[c, pl.ds(site_row(x, 0), NY * KV)] = fxr[s, c, side].astype(F32) * keep[side]
            y = -1 if side == 0 else NY
            for x in range(NX):
                w[c, pl.ds(site_row(x, y), KV)] = (
                    fyr[s, c, side, pl.ds(x * KV, KV)].astype(F32) * keep[2 + side]
                )

    def sweep(c, src, dst, last):
        def plane(x, carry):
            base = pl.multiple_of(x * XROW, 16)

            def cell(dx, y):
                return src[c, pl.ds(base + site_row(dx, y), KV)]

            below, here = cell(0, -1), cell(0, 0)
            for y in range(NY):
                above = cell(0, y + 1)
                row = slice(y, y + 1)
                new = (
                    ka[x, row] * (cell(-1, y) + cell(1, y))
                    + kb[x, row] * (below + above)
                    + km[x, row] * pltpu.roll(here, 1, 1)
                    + kp[x, row] * pltpu.roll(here, ROWS - 1, 1)
                    + (1.0 - OMEGA) * here
                )
                dst[c, pl.ds(base + site_row(0, y), KV)] = new
                if last:
                    blk[c, x * NY + y] = new.astype(BF16)
                below, here = here, above
            return carry

        lax.fori_loop(0, NX, plane, 0)

    def pair_copy():
        slot = pair.at[core]
        return remote(slot, slot, pair_sem.at[0], pair_sem.at[1], device("x", 0, 1))

    def line_copies():
        return [
            remote(
                pair, lines.at[n, at[axis]], table_sem.at[0], table_sem.at[1],
                device(axis, d, 0),
            )
            for n, axis in enumerate(AXES)
            for d in range(1, LINE)
        ]

    def gather_copies(step):
        send, recv = gather_sem.at[step, 0], gather_sem.at[step, 1]
        if step == 0:
            slot = near.at[at["y"] * CORES + core]
            return [
                remote(slot, slot, send, recv, device("y", d, e))
                for d in range(LINE)
                for e in range(CORES)
                if d or e
            ]
        slot = far.at[at["x"], at["z"]] if step == 1 else far.at[at["x"]]
        return [
            remote(slot, slot, send, recv, device("zx"[step - 1], d, 0)) for d in range(1, LINE)
        ]

    def gathered(step):
        if step == 0:
            return near.at[pl.ds(0, 7)]
        return far.at[0, pl.ds(0, 3)] if step == 1 else far.at[pl.ds(0, 3)]

    def gather_step(step):
        drain(gathered(step), gather_sem.at[step, 1])
        if step == 0:
            for n in range(LINE * CORES):
                far[at["x"], at["z"], n : n + 1] = near[n, 0:1]
        for copy in gather_copies(step + 1):
            copy.start()

    def ask():
        drain(gathered(2), gather_sem.at[2, 1])
        table = far[...].reshape(ROWS, ROWS)
        for p in range(2):
            pair[core, p] = ranks_wanted(block_cols[p], table)
        pair_copy().start()

    def ask_lines():
        pair_copy().wait_recv()
        for copy in line_copies():
            copy.start()
        for n, axis in enumerate(AXES):
            lines[n, at[axis]] = pair[...]

    steps = {
        (0, 1): lambda: gather_step(0),
        (1, 0): lambda: gather_step(1),
        (1, 2): ask,
        (2, 1): ask_lines,
    }

    def spread_copies(c):
        a, u, v = ROUTES[c]
        half = COARSE // 2
        plan = ((0, 0, COARSE, 3, 1, 0), (0, 0, COARSE, 1, 3, 1), (3, 0, half, 2, 1, 2), (1, half, half, 2, 3, 2))
        return [
            remote(
                pg[c][0].at[src, pl.ds(first, size)], pg[c][0].at[dst, pl.ds(first, size)],
                near_sem.at[c, 3], near_sem.at[c, into], device(u, d, 0),
            )
            for src, first, size, dst, d, into in plan
        ]

    def cast_copies(c):
        a, u, v = ROUTES[c]
        plan = (
            (0, 0, 1, 3, 1, 0, 0),
            (0, 0, 1, 1, 3, 1, 2),
            (0, 1, 1, 3, 1, 0, 0),
            (0, 2, 2, 1, 3, 1, 1),
            (0, 2, 2, 3, 1, 0, 2),
            (0, 1, 1, 1, 3, 1, 2),
            (3, 0, 2, 2, 1, 2, 3),
            (1, 2, 2, 2, 3, 2, 3),
        )
        return [
            remote(
                pg[c][src].at[pl.ds(first, size)], pg[c][dst].at[pl.ds(first, size)],
                cast_send.at[c, out], cast_recv.at[c, into], device(v, d, 0),
            )
            for src, first, size, dst, d, out, into in plan
        ]

    def piece(slot, part):
        first, count = PARTS[part]
        return pl.ds(slot * REPLY + first * SPOT, count * SPOT)

    def answer(c, part, d, e):
        a = ROUTES[c][0]
        slot = lax.rem(at[a] + d, LINE) * CORES + lax.rem(core + e, CORES)
        here = at[a] * CORES + core
        src = sb.at[c, piece(slot, part)]
        dst, peer = rb[c].at[piece(here, part)], device(a, d, e)
        if d == 0 and e == 0:
            return pltpu.make_async_copy(src, dst, own_sem.at[c, part])
        if d == 2:
            dst, peer = fb.at[c, e, piece(0, part)], device(a, 1 + 2 * e, 0)
            return remote(src, dst, ans_send.at[c, part], hop_recv.at[c, part, e], peer)
        return remote(src, dst, ans_send.at[c, part], ans_recv.at[c, part], peer)

    def forward(c, part, e):
        a = ROUTES[c][0]
        origin = lax.rem(at[a] + 3 - 2 * e, LINE) * CORES + core
        return remote(
            fb.at[c, e, piece(0, part)], rb[c].at[piece(origin, part)],
            fwd_send.at[c, part], ans_recv.at[c, part], device(a, 1 + 2 * e, e),
        )

    order = [(d, e) for d in (2, 1, 3, 0) for e in range(CORES)]

    def spread(c):
        a, u, v = ROUTES[c]
        for r in range(COARSE):
            pg[c][0][0, r] = blk[c, id_s[r, 0] & (SITES - 1)]
        for copy in spread_copies(c)[:2] + cast_copies(c)[:2]:
            copy.start()

    def spread_on(c):
        for n in range(2):
            drain(pg[c][0].at[0], near_sem.at[c, n])
            spread_copies(c)[2 + n].start()

    def cast(c):
        drain(pg[c][0].at[0], near_sem.at[c, 2])
        for copy in cast_copies(c)[2:6]:
            copy.start()

    def pass_on(c):
        for n in range(2):
            drain(pg[c][0].at[pl.ds(0, 2)], cast_recv.at[c, n])
            cast_copies(c)[6 + n].start()

    def reply(c, part):
        a, u, v = ROUTES[c]
        n = AXES.index(a)
        drain(pg[c][0], cast_recv.at[c, 2 + part])
        first, count = PARTS[part]
        for d, e in order:
            q, to = lax.rem(at[a] + d, LINE), lax.rem(core + e, CORES)
            slot = q * CORES + to
            for place in range(first, first + count):
                back = BACKS[place]
                tiles = []
                for ahead in range(LINE):
                    whose = {
                        a: at[a],
                        u: lax.rem(at[u] + ahead, LINE),
                        v: lax.rem(at[v] + back, LINE),
                    }
                    owner = whose["x"] * 32 + whose["z"] * 8 + whose["y"] * 2 + core
                    for p in range(2):
                        rank = line_s[n, q, to, p, 0, owner] & (COARSE - 1)
                        tiles.append(pg[c][back][ahead, rank])
                for t, tile in enumerate(tiles):
                    sb[c, slot * REPLY + place * SPOT + t] = tile
            answer(c, part, d, e).start()

    def reply_on(c, part):
        for e in range(2):
            answer(c, part, 2, e).wait_recv()
            forward(c, part, e).start()

    def transpose_in(c):
        loads[c].wait()
        for x in range(NX):
            for half in range(NY // 8):
                for k in range(KV):
                    wa[c, pl.ds(site_row(x, half * 8) + k, 8, stride=KV), :] = stage[
                        c * KV + k, x, pl.ds(half * 8, 8), :
                    ]

    def products(c, place):
        b = fine_s[place, 0] & (SITES - 1)
        column = ((b >> 4) & 1) * (ROWS // 2) + (b & (NY - 1))
        values = []
        for t in range(SLOTS):
            found = tgt_s[2 * c + (b >> 5), column + t * NY]
            values.append(rb[c][found].astype(F32))
        values.append(blk[c, b].astype(F32))
        for n, (p, q) in enumerate(PAIRS):
            product = values[p] * values[q]
            product = product[0:8] + product[8:16]
            if c != GRAM_ORDER[0]:
                product = product + part_sums[n, place]
            part_sums[n, place] = product

    def add_products(c):
        def step(g, carry):
            for m in range(4):
                products(c, g * 4 + m)
            return carry

        lax.fori_loop(0, FINE // 4, step, 0)

    def finish():
        sub = lax.broadcasted_iota(jnp.int32, (8, ROWS), 0)
        low4, low2, low1 = sub < 4, (sub & 2) == 0, (sub & 1) == 0

        def merge(first, second, keep_first, shift):
            first = first + pltpu.roll(first, 8 - shift, 0)
            second = second + pltpu.roll(second, shift, 0)
            return jnp.where(keep_first, first, second)

        def group(g, carry):
            total = {}
            spots = [spot_s[0, g * 8 + m] & (SITES - 1) for m in range(8)]
            for n, couple in enumerate(PAIRS):
                rows = [part_sums[n, spot] for spot in spots]
                rows = [
                    jnp.where(low4, rows[m], rows[m + 4])
                    + pltpu.roll(jnp.where(low4, rows[m + 4], rows[m]), 4, 0)
                    for m in range(4)
                ]
                rows = [merge(rows[m], rows[m + 2], low2, 2) for m in range(2)]
                total[couple] = merge(rows[0], rows[1], low1, 1) * (1.0 / VECS)
                if couple[0] == couple[1]:
                    total[couple] = total[couple] + RIDGE
            out = solve_rows(total, [total[s, SLOTS] for s in range(SLOTS)])
            for s in range(SLOTS):
                w_out[s, pl.ds(pl.multiple_of(g * 8, 8), 8), :] = out[s]
            return carry

        lax.fori_loop(0, SITES // 8, group, 0)

    stores = []

    def transpose_out(c, w):
        for x in range(NX):
            for half in range(NY // 8):
                for k in range(KV):
                    stage[c * KV + k, x, pl.ds(half * 8, 8), :] = w[
                        c, pl.ds(site_row(x, half * 8) + k, 8, stride=KV), :
                    ]
        part = pl.ds(c * KV, KV)
        store = pltpu.make_async_copy(stage.at[part], sm_out.at[part], out_sem.at[c])
        store.start()
        stores.append(store)

    for c in range(CHUNKS):
        transpose_in(c)
        if c == 0:
            pl.semaphore_wait(barrier, greeted)
        send_faces(0, c, wa)

    for load in coef_loads:
        load.wait()
    ax, ay, az = coef[0], coef[1], coef[2]
    scale = OMEGA / (2.0 * (ax + ay + az) + coef[3])
    ka[...] = ax * scale
    kb[...] = ay * scale
    az = az * scale
    lane = lax.broadcasted_iota(jnp.int32, az.shape, 2)
    km[...] = jnp.where(lane == 0, 0.0, az)
    kp[...] = jnp.where(lane == ROWS - 1, 0.0, az)

    for load in lists:
        load.wait()
    meta[...] = jnp.zeros_like(meta)
    slots = lax.broadcasted_iota(jnp.int32, (SLOTS, NY), 0)
    for x in range(NX):
        live = (cells[0][x] == 0) & (slots < cells[1][x])
        listed = jnp.where(live, cells[2][x] * SITES + cells[3][x], -1)
        for t in range(SLOTS):
            where = pl.ds((x % 2) * (ROWS // 2) + t * NY, NY)
            meta[x // 2 : x // 2 + 1, where] = listed[t : t + 1]
        meta[2:3, pl.ds(x * NY, NY)] = cells[0][x]
    blocks, targets, rank, ids, fine_ids, fine_rank = lists_of(meta[...], at)
    near[at["y"] * CORES + core] = jnp.broadcast_to(rank, (8, ROWS))
    for copy in gather_copies(0):
        copy.start()
    for p in range(2):
        block_cols[p] = jnp.broadcast_to(blocks[p], (ROWS, ROWS))
    idv[:COARSE] = ids
    idv[COARSE : COARSE + FINE] = fine_ids
    idv[COARSE + FINE :] = jnp.broadcast_to(fine_rank, (8, ROWS))
    part_sums[:, FINE] = jnp.zeros((len(PAIRS), 8, ROWS), F32)
    id_copies = [
        pltpu.make_async_copy(idv.at[pl.ds(0, COARSE)], id_s, smem_sem.at[0]),
        pltpu.make_async_copy(idv.at[pl.ds(COARSE, FINE)], fine_s, smem_sem.at[2]),
        pltpu.make_async_copy(idv.at[pl.ds(COARSE + FINE, 8)], spot_s, smem_sem.at[4]),
    ]
    for copy in id_copies:
        copy.start()
    tgt[...] = jnp.zeros_like(tgt)
    for c in range(CHUNKS):
        for h in range(2):
            tgt[2 * c + h : 2 * c + h + 1] = targets[c][h]
        rb[c][EMPTY] = jnp.zeros((KV, ROWS), BF16)
    tgt_copy = pltpu.make_async_copy(tgt, tgt_s, smem_sem.at[3])
    tgt_copy.start()

    for s in range(SWEEPS):
        src, dst = (wb, wa) if s % 2 else (wa, wb)
        for c in range(CHUNKS):
            fill_halo(s, c, src)
            sweep(c, src, dst, s == SWEEPS - 1)
            if s < SWEEPS - 1:
                send_faces(s + 1, c, dst)
            else:
                if c == 0:
                    for copy in id_copies:
                        copy.wait()
                spread(c)
                if c > 0:
                    spread_on(c - 1)
            if (s, c) in steps:
                steps[s, c]()
    drain(lines.at[:, pl.ds(0, 3)], table_sem.at[1])
    line_copy = pltpu.make_async_copy(lines, line_s, smem_sem.at[1])
    line_copy.start()
    cast(0)
    spread_on(2)
    cast(1)
    cast(2)
    line_copy.wait()
    for c in range(CHUNKS):
        pass_on(c)
    for c in (1, 2, 0):
        reply(c, 0)
    for c in (1, 0, 2):
        reply_on(c, 0)
        reply(c, 1)
    transpose_out(0, wb)
    for c in (1, 0, 2):
        reply_on(c, 1)
    transpose_out(1, wb)
    transpose_out(2, wb)
    tgt_copy.wait()
    for c in GRAM_ORDER:
        for part in range(len(PARTS)):
            answer(c, part, 0, 0).wait()
            drain(sb.at[c, pl.ds(0, 7 * PARTS[part][1] * SPOT)], ans_recv.at[c, part])
        add_products(c)
    finish()

    drain(fxs, send_sem.at[0])
    drain(fys, send_sem.at[1])
    pair_copy().wait_send()
    drain(lines.at[:, pl.ds(0, 3)], table_sem.at[0])
    for step in range(3):
        drain(gathered(step), gather_sem.at[step, 0])
    for c in range(CHUNKS):
        drain(pg[c][0].at[pl.ds(0, 3)], near_sem.at[c, 3])
        for n in range(3):
            drain(pg[c][0], cast_send.at[c, n])
        for part in range(len(PARTS)):
            count = PARTS[part][1]
            drain(sb.at[c, pl.ds(0, 7 * count * SPOT)], ans_send.at[c, part])
            drain(fb.at[c, :, pl.ds(0, count * SPOT)], fwd_send.at[c, part])
    for store in stores:
        store.wait()


def smooth(test_vectors, coef_x, coef_y, coef_z, shift, split, count, owner, local):
    vmem = pl.BlockSpec(memory_space=pltpu.VMEM)
    anywhere = pl.BlockSpec(memory_space=pl.ANY)
    cells = pltpu.VMEM((NX, NY, ROWS), F32)
    rows = pltpu.VMEM((LINE, COARSE, KV, ROWS), BF16)
    dma = pltpu.SemaphoreType.DMA
    return pl.pallas_call(
        smooth_kernel,
        out_shape=(
            jax.ShapeDtypeStruct((VECS, NX, NY, ROWS), F32),
            jax.ShapeDtypeStruct((SLOTS, SITES, ROWS), F32),
        ),
        in_specs=[anywhere] * 9,
        out_specs=(anywhere, vmem),
        scratch_shapes=[
            pltpu.VMEM((NX, 1, NY), jnp.int32),
            pltpu.VMEM((NX, 1, NY), jnp.int32),
            pltpu.VMEM((NX, SLOTS, NY), jnp.int32),
            pltpu.VMEM((NX, SLOTS, NY), jnp.int32),
            pltpu.VMEM((8, ROWS), jnp.int32),
            pltpu.VMEM((8, ROWS), jnp.int32),
            pltpu.SMEM((8, ROWS), jnp.int32),
            pltpu.VMEM((CHUNKS, SITES, KV, ROWS), BF16),
            *([pltpu.VMEM((EMPTY + 8, KV, ROWS), BF16)] * CHUNKS),
            pltpu.VMEM((len(PAIRS), SITES, 8, ROWS), F32),
            pltpu.VMEM((VECS, NX, NY, ROWS), F32),
            pltpu.VMEM((4, NX, NY, ROWS), F32),
            pltpu.VMEM((CHUNKS, EXT, ROWS), F32),
            pltpu.VMEM((CHUNKS, EXT, ROWS), F32),
            cells, cells, cells, cells,
            pltpu.VMEM((SWEEPS, CHUNKS, 2, NY * KV, ROWS), BF16),
            pltpu.VMEM((SWEEPS, CHUNKS, 2, NY * KV, ROWS), BF16),
            pltpu.VMEM((SWEEPS, CHUNKS, 2, NX * KV, ROWS), BF16),
            pltpu.VMEM((SWEEPS, CHUNKS, 2, NX * KV, ROWS), BF16),
            pltpu.VMEM((CORES, 2, 1, ROWS), jnp.int32),
            pltpu.VMEM((len(AXES), LINE, CORES, 2, 1, ROWS), jnp.int32),
            pltpu.VMEM((LINE * CORES, 8, ROWS), jnp.int32),
            pltpu.VMEM((LINE, LINE, LINE * CORES, ROWS), jnp.int32),
            pltpu.VMEM((2, ROWS, ROWS), jnp.int32),
            pltpu.VMEM((COARSE + FINE + 8, ROWS), jnp.int32),
            pltpu.SMEM((len(AXES), LINE, CORES, 2, 1, ROWS), jnp.int32),
            pltpu.SMEM((COARSE, ROWS), jnp.int32),
            pltpu.SMEM((FINE, ROWS), jnp.int32),
            pltpu.SMEM((8, ROWS), jnp.int32),
            *([rows] * (LINE * CHUNKS)),
            pltpu.VMEM((CHUNKS, EMPTY, KV, ROWS), BF16),
            pltpu.VMEM((CHUNKS, CORES, REPLY, KV, ROWS), BF16),
            dma((CHUNKS,)),
            dma((4,)),
            dma((CHUNKS,)),
            dma((2,)),
            dma((SWEEPS, CHUNKS, 2)),
            dma((2,)),
            dma((2,)),
            dma((3, 2)),
            dma((CHUNKS, 4)),
            dma((CHUNKS, 3)),
            dma((CHUNKS, 4)),
            dma((CHUNKS, len(PARTS))),
            dma((CHUNKS, len(PARTS))),
            dma((CHUNKS, len(PARTS), CORES)),
            dma((CHUNKS, len(PARTS))),
            dma((CHUNKS, len(PARTS))),
            dma((5,)),
            dma((4,)),
        ],
        compiler_params=pltpu.CompilerParams(
            collective_id=0, has_side_effects=True, vmem_limit_bytes=60 * 1024 * 1024
        ),
        name="smooth",
    )(test_vectors, coef_x, coef_y, coef_z, shift, split, count, owner, local)


def pass_kernel(w_in, sm_in, w_out, sm_out, w_hold, sm_hold, in_sem, out_sem):
    parts = [(w_in, w_hold, w_out)]
    for c in range(PIECES):
        part = pl.ds(c * (VECS // PIECES), VECS // PIECES)
        parts.append((sm_in.at[part], sm_hold.at[part], sm_out.at[part]))
    ins = [pltpu.make_async_copy(a, b, in_sem.at[n]) for n, (a, b, _) in enumerate(parts)]
    outs = [pltpu.make_async_copy(b, d, out_sem.at[n]) for n, (_, b, d) in enumerate(parts)]
    for copy in ins:
        copy.start()
    for load, store in zip(ins, outs):
        load.wait()
        store.start()
    for store in outs:
        store.wait()


def pass_on_results(weights, sm):
    anywhere = pl.BlockSpec(memory_space=pl.ANY)
    dma = pltpu.SemaphoreType.DMA
    return pl.pallas_call(
        pass_kernel,
        out_shape=(
            jax.ShapeDtypeStruct(weights.shape, F32),
            jax.ShapeDtypeStruct(sm.shape, F32),
        ),
        in_specs=[anywhere, anywhere],
        out_specs=(anywhere, anywhere),
        scratch_shapes=[
            pltpu.VMEM(weights.shape, F32),
            pltpu.VMEM(sm.shape, F32),
            dma((PIECES + 1,)),
            dma((PIECES + 1,)),
        ],
        compiler_params=pltpu.CompilerParams(vmem_limit_bytes=60 * 1024 * 1024),
        name="fit",
    )(weights, sm)


def per_device(
    test_vectors, coef_x, coef_y, coef_z, shift, cf_split, nbr_count, nbr_owner, nbr_block
):
    sm, weights = smooth(
        test_vectors, coef_x, coef_y, coef_z, shift,
        jnp.swapaxes(cf_split, 1, 2),
        jnp.swapaxes(nbr_count, 1, 2),
        jnp.transpose(nbr_owner, (0, 2, 3, 1)).reshape(NX, SLOTS, NY),
        jnp.transpose(nbr_block, (0, 2, 3, 1)).reshape(NX, SLOTS, NY),
    )
    weights, smoothed = pass_on_results(weights.reshape(SLOTS, NX, NY, ROWS), sm)
    return (smoothed, weights)


def solution(mesh):
    cells = P("gx", "gy", None)
    lists = P("gx", "gy", None, None)
    vectors = P(None, "gx", "gy", None)
    return jax.shard_map(
        per_device,
        mesh=mesh,
        in_specs=(vectors, cells, cells, cells, cells, cells, cells, lists, lists),
        out_specs=(vectors, vectors),
        check_vma=False,
    )
```

```python
import jax
import jax.numpy as jnp
from jax import lax
from jax.experimental import pallas as pl
from jax.experimental.pallas import tpu as pltpu
from jax.sharding import PartitionSpec as P

SLOTS = 4
SWEEPS = 3
ROWS = 128
OMEGA = 0.8
RIDGE = 0.05
VECS = 48
CHUNKS = 3
KV = VECS // CHUNKS
NX = 4
NY = 16
SITES = NX * NY
XROW = (NY + 2) * KV
EXT = (NX + 2) * XROW
GX = 16
GY = 8
MESH = pl.DeviceIdType.MESH
F32 = jnp.float32
BF16 = jnp.bfloat16


def site_row(x, y):
    return (x + 1) * XROW + (y + 1) * KV


def solve_rows(gram, rhs):
    low = [[None] * SLOTS for _ in range(SLOTS)]
    inv = []
    for r in range(SLOTS):
        scaled = []
        diag = gram[r, r]
        for c in range(r):
            rest = gram[r, c]
            for m in range(c):
                rest = rest - scaled[m] * low[c][m]
            scaled.append(rest)
            low[r][c] = rest * inv[c]
            diag = diag - rest * low[r][c]
        inv.append(1.0 / diag)
    fwd = []
    for r in range(SLOTS):
        rest = rhs[r]
        for m in range(r):
            rest = rest - low[r][m] * fwd[m]
        fwd.append(rest)
    out = [None] * SLOTS
    for r in reversed(range(SLOTS)):
        rest = fwd[r] * inv[r]
        for m in range(r + 1, SLOTS):
            rest = rest - low[m][r] * out[m]
        out[r] = rest
    return out


PAIRS = [(s, t) for s in range(SLOTS) for t in range(s + 1)] + [(s, SLOTS) for s in range(SLOTS)]
AXES = "xyz"
LINE = 4
CORES = 2
COARSE = 16
FINE = 48
PLANE = LINE * LINE
ROUTES = (("x", "z", "y"), ("y", "x", "z"), ("z", "y", "x"))
BACKS = (0, 1, 3, 2)
EMPTY = LINE * CORES * PLANE * 2
SPOT = 2 * LINE
GRAM_ORDER = (1, 2, 0)
REPLY = PLANE * 2
PARTS = ((0, 3), (3, 1))


def lists_of(meta, here):
    lane = lax.broadcasted_iota(jnp.int32, (ROWS, ROWS), 1)
    sub = lax.broadcasted_iota(jnp.int32, (ROWS, ROWS), 0)
    diag = lane == sub
    none = 1 << 20

    def column(row):
        return jnp.sum(jnp.where(diag, row, 0), axis=1, keepdims=True)

    members, keys, owners = [], [], []
    for h in range(2):
        entry = meta[h : h + 1]
        owner = entry >> 6
        key = (lane[:1] + h * ROWS) * SITES + (entry & (SITES - 1))
        owners.append(owner)
        keys.append(key)
        members.append(owner == sub)
    first = jnp.minimum(*[jnp.where(m, k, none) for m, k in zip(members, keys)])
    first = jnp.min(first, axis=1, keepdims=True)
    first = jnp.where(first >= none, 0, first)
    second = jnp.maximum(*[jnp.where(m, k, 0) for m, k in zip(members, keys)])
    second = jnp.max(second, axis=1, keepdims=True)
    targets = [[] for _ in ROUTES]
    for h in range(2):
        own = owners[h]
        at_first = jnp.sum(jnp.where(members[h], first, 0), axis=0, keepdims=True)
        place = jnp.where(keys[h] == at_first, 0, 1)
        at = {"x": (own >> 5) & 3, "z": (own >> 3) & 3, "y": (own >> 1) & 3}
        for c, (a, u, v) in enumerate(ROUTES):
            back = (at[v] - here[v]) & 3
            spot = jnp.where(back == 2, 3, jnp.where(back == 3, 2, back))
            slot = ((at[a] * CORES + (own & 1)) * PLANE + spot * LINE + ((at[u] - here[u]) & 3)) * 2 + place
            targets[c].append(jnp.where(own < 0, EMPTY, slot))
    coarse = meta[2:3]
    rank = jnp.sum(jnp.where(sub < lane, column(coarse), 0), axis=0, keepdims=True)
    fine_rank = jnp.minimum(lane[:1] - rank, FINE)
    fine_rank = jnp.where(coarse > 0, FINE, fine_rank)

    def numbers(hit):
        found = jnp.sum(jnp.where(hit, lane[: hit.shape[0]], 0), axis=1, keepdims=True)
        return jnp.broadcast_to(found, hit.shape)

    ids = numbers((rank == sub[:COARSE]) & (coarse > 0))
    fine_ids = numbers((fine_rank == sub[:FINE]) & (lane[:1] < SITES))
    rank = jnp.minimum(rank, COARSE - 1)
    return (first, second), targets, rank, ids, fine_ids, fine_rank


def ranks_wanted(blocks, table):
    lane = lax.broadcasted_iota(jnp.int32, (ROWS, ROWS), 1)
    sub = lax.broadcasted_iota(jnp.int32, (ROWS, ROWS), 0)
    found = jnp.sum(
        jnp.where(lane == (blocks & (SITES - 1)), table, 0), axis=1, keepdims=True
    )
    return jnp.sum(jnp.where(lane == sub, found, 0), axis=0, keepdims=True)


def smooth_kernel(
    tv, cx, cy, cz, sh, split, count, owner, local, sm_out, w_out,
    split_v, count_v, owner_v, local_v, meta, tgt, tgt_s, blk, rb0, rb1, rb2, part_sums,
    stage, coef, wa, wb, ka, kb, km, kp, fxs, fxr, fys, fyr,
    pair, lines, near, far, block_cols, idv, line_s, id_s, fine_s, spot_s, p00, p01, p02, p03, p10, p11, p12, p13, p20, p21, p22, p23, sb,
    in_sem, coef_sem, out_sem, send_sem, recv_sem, pair_sem, table_sem, gather_sem,
    near_sem, cast_send, cast_recv, ans_send, ans_recv, own_sem, smem_sem, list_sem,
):
    cells = (split_v, count_v, owner_v, local_v)
    rb = (rb0, rb1, rb2)
    pg = ((p00, p01, p02, p03), (p10, p11, p12, p13), (p20, p21, p22, p23))
    i = lax.axis_index("gx")
    j = lax.axis_index("gy")
    core = lax.rem(j, CORES)
    at = {"x": i // LINE, "z": lax.rem(i, LINE), "y": j // CORES}
    peers = (
        (lax.rem(i + GX - 1, GX), j),
        (lax.rem(i + 1, GX), j),
        (i, lax.rem(j + GY - 1, GY)),
        (i, lax.rem(j + 1, GY)),
    )

    def device(axis, d, e):
        moved = dict(at)
        moved[axis] = lax.rem(at[axis] + d, LINE)
        return (moved["x"] * LINE + moved["z"], moved["y"] * CORES + lax.rem(core + e, CORES))

    def remote(src, dst, send, recv, peer):
        return pltpu.make_async_remote_copy(
            src_ref=src, dst_ref=dst, send_sem=send, recv_sem=recv,
            device_id=peer, device_id_type=MESH,
        )

    loads = []
    for c in range(CHUNKS):
        part = pl.ds(c * KV, KV)
        loads.append(pltpu.make_async_copy(tv.at[part], stage.at[part], in_sem.at[c]))
    loads[0].start()
    barrier = pltpu.get_barrier_semaphore()
    for peer in peers[:2]:
        pl.semaphore_signal(barrier, inc=1, device_id=peer, device_id_type=MESH)
    pl.semaphore_signal(barrier, inc=1, device_id=device("x", 0, 1), device_id_type=MESH)
    for axis in AXES:
        for d in range(1, LINE):
            for e in range(CORES):
                pl.semaphore_signal(
                    barrier, inc=1, device_id=device(axis, d, e), device_id_type=MESH
                )
    greeted = 3 + len(AXES) * (LINE - 1) * CORES
    for load in loads[1:]:
        load.start()
    coef_loads = []
    for n, part in enumerate((cx, cy, cz, sh)):
        load = pltpu.make_async_copy(part, coef.at[n], coef_sem.at[n])
        load.start()
        coef_loads.append(load)
    lists = []
    for n, part in enumerate((split, count, owner, local)):
        load = pltpu.make_async_copy(part, cells[n], list_sem.at[n])
        load.start()
        lists.append(load)

    keep = (
        (i > 0).astype(F32),
        (i < GX - 1).astype(F32),
        (j > 0).astype(F32),
        (j < GY - 1).astype(F32),
    )

    def drain(ref, sem):
        pltpu.make_async_copy(ref, ref, sem).wait()

    def copies(s, c):
        out = []
        for d in range(4):
            src, dst = (fxs, fxr) if d < 2 else (fys, fyr)
            out.append(
                remote(
                    src.at[s, c, d % 2], dst.at[s, c, 1 - d % 2],
                    send_sem.at[d // 2], recv_sem.at[s, c, d // 2], peers[d],
                )
            )
        return out

    def send_faces(s, c, w):
        for side in range(2):
            x = side * (NX - 1)
            fxs[s, c, side] = w[c, pl.ds(site_row(x, 0), NY * KV)].astype(BF16)
            y = side * (NY - 1)
            for x in range(NX):
                fys[s, c, side, pl.ds(x * KV, KV)] = w[c, pl.ds(site_row(x, y), KV)].astype(BF16)
        for copy in copies(s, c):
            copy.start()

    def fill_halo(s, c, w):
        drain(fxr.at[s, c], recv_sem.at[s, c, 0])
        drain(fyr.at[s, c], recv_sem.at[s, c, 1])
        for side in range(2):
            x = -1 if side == 0 else NX
            w[c, pl.ds(site_row(x, 0), NY * KV)] = fxr[s, c, side].astype(F32) * keep[side]
            y = -1 if side == 0 else NY
            for x in range(NX):
                w[c, pl.ds(site_row(x, y), KV)] = (
                    fyr[s, c, side, pl.ds(x * KV, KV)].astype(F32) * keep[2 + side]
                )

    def sweep(c, src, dst, last):
        def plane(x, carry):
            base = pl.multiple_of(x * XROW, 16)

            def cell(dx, y):
                return src[c, pl.ds(base + site_row(dx, y), KV)]

            below, here = cell(0, -1), cell(0, 0)
            for y in range(NY):
                above = cell(0, y + 1)
                row = slice(y, y + 1)
                new = (
                    ka[x, row] * (cell(-1, y) + cell(1, y))
                    + kb[x, row] * (below + above)
                    + km[x, row] * pltpu.roll(here, 1, 1)
                    + kp[x, row] * pltpu.roll(here, ROWS - 1, 1)
                    + (1.0 - OMEGA) * here
                )
                dst[c, pl.ds(base + site_row(0, y), KV)] = new
                if last:
                    blk[c, x * NY + y] = new.astype(BF16)
                below, here = here, above
            return carry

        lax.fori_loop(0, NX, plane, 0)

    def pair_copy():
        slot = pair.at[core]
        return remote(slot, slot, pair_sem.at[0], pair_sem.at[1], device("x", 0, 1))

    def line_copies():
        return [
            remote(
                pair, lines.at[n, at[axis]], table_sem.at[0], table_sem.at[1],
                device(axis, d, 0),
            )
            for n, axis in enumerate(AXES)
            for d in range(1, LINE)
        ]

    def gather_copies(step):
        send, recv = gather_sem.at[step, 0], gather_sem.at[step, 1]
        if step == 0:
            slot = near.at[at["y"] * CORES + core]
            return [
                remote(slot, slot, send, recv, device("y", d, e))
                for d in range(LINE)
                for e in range(CORES)
                if d or e
            ]
        slot = far.at[at["x"], at["z"]] if step == 1 else far.at[at["x"]]
        return [
            remote(slot, slot, send, recv, device("zx"[step - 1], d, 0)) for d in range(1, LINE)
        ]

    def gathered(step):
        if step == 0:
            return near.at[pl.ds(0, 7)]
        return far.at[0, pl.ds(0, 3)] if step == 1 else far.at[pl.ds(0, 3)]

    def gather_step(step):
        drain(gathered(step), gather_sem.at[step, 1])
        if step == 0:
            for n in range(LINE * CORES):
                far[at["x"], at["z"], n : n + 1] = near[n, 0:1]
        for copy in gather_copies(step + 1):
            copy.start()

    def ask():
        drain(gathered(2), gather_sem.at[2, 1])
        table = far[...].reshape(ROWS, ROWS)
        for p in range(2):
            pair[core, p] = ranks_wanted(block_cols[p], table)
        pair_copy().start()

    def ask_lines():
        pair_copy().wait_recv()
        for copy in line_copies():
            copy.start()
        for n, axis in enumerate(AXES):
            lines[n, at[axis]] = pair[...]

    steps = {
        (0, 1): lambda: gather_step(0),
        (1, 0): lambda: gather_step(1),
        (1, 2): ask,
        (2, 1): ask_lines,
    }

    def spread_copies(c):
        a, u, v = ROUTES[c]
        return [
            remote(
                pg[c][0].at[0], pg[c][0].at[LINE - d],
                near_sem.at[c, 0], near_sem.at[c, 1], device(u, d, 0),
            )
            for d in (2, 1, 3)
        ]

    def cast_copies(c):
        a, u, v = ROUTES[c]
        plan = (
            (0, 0, 1, 3, 1, 0, 0),
            (0, 0, 1, 1, 3, 1, 2),
            (0, 1, 1, 3, 1, 0, 0),
            (0, 2, 2, 1, 3, 1, 1),
            (0, 2, 2, 3, 1, 0, 2),
            (0, 1, 1, 1, 3, 1, 2),
            (3, 0, 2, 2, 1, 2, 3),
            (1, 2, 2, 2, 3, 2, 3),
        )
        return [
            remote(
                pg[c][src].at[pl.ds(first, size)], pg[c][dst].at[pl.ds(first, size)],
                cast_send.at[c, out], cast_recv.at[c, into], device(v, d, 0),
            )
            for src, first, size, dst, d, out, into in plan
        ]

    def piece(slot, part):
        first, count = PARTS[part]
        return pl.ds(slot * REPLY + first * SPOT, count * SPOT)

    def answer(c, part, d, e):
        a = ROUTES[c][0]
        slot = lax.rem(at[a] + d, LINE) * CORES + lax.rem(core + e, CORES)
        here = at[a] * CORES + core
        src = sb.at[c, piece(slot, part)]
        dst, peer = rb[c].at[piece(here, part)], device(a, d, e)
        if d == 0 and e == 0:
            return pltpu.make_async_copy(src, dst, own_sem.at[c, part])
        return remote(src, dst, ans_send.at[c, part], ans_recv.at[c, part], peer)

    order = [(d, e) for d in (2, 1, 3, 0) for e in range(CORES)]

    def spread(c):
        a, u, v = ROUTES[c]
        for r in range(COARSE):
            pg[c][0][0, r] = blk[c, id_s[r, 0] & (SITES - 1)]
        for copy in spread_copies(c) + cast_copies(c)[:2]:
            copy.start()

    def cast(c):
        drain(pg[c][1].at[pl.ds(0, 3)], near_sem.at[c, 1])
        for copy in cast_copies(c)[2:6]:
            copy.start()

    def pass_on(c):
        for n in range(2):
            drain(pg[c][0].at[pl.ds(0, 2)], cast_recv.at[c, n])
            cast_copies(c)[6 + n].start()

    def reply(c, part):
        a, u, v = ROUTES[c]
        n = AXES.index(a)
        drain(pg[c][0], cast_recv.at[c, 2 + part])
        first, count = PARTS[part]
        for d, e in order:
            q, to = lax.rem(at[a] + d, LINE), lax.rem(core + e, CORES)
            slot = q * CORES + to
            for place in range(first, first + count):
                back = BACKS[place]
                tiles = []
                for ahead in range(LINE):
                    whose = {
                        a: at[a],
                        u: lax.rem(at[u] + ahead, LINE),
                        v: lax.rem(at[v] + back, LINE),
                    }
                    owner = whose["x"] * 32 + whose["z"] * 8 + whose["y"] * 2 + core
                    for p in range(2):
                        rank = line_s[n, q, to, p, 0, owner] & (COARSE - 1)
                        tiles.append(pg[c][back][ahead, rank])
                for t, tile in enumerate(tiles):
                    sb[c, slot * REPLY + place * SPOT + t] = tile
            answer(c, part, d, e).start()

    def transpose_in(c):
        loads[c].wait()
        for x in range(NX):
            for half in range(NY // 8):
                for k in range(KV):
                    wa[c, pl.ds(site_row(x, half * 8) + k, 8, stride=KV), :] = stage[
                        c * KV + k, x, pl.ds(half * 8, 8), :
                    ]

    def products(c, place):
        b = fine_s[place, 0] & (SITES - 1)
        column = ((b >> 4) & 1) * (ROWS // 2) + (b & (NY - 1))
        values = []
        for t in range(SLOTS):
            found = tgt_s[2 * c + (b >> 5), column + t * NY]
            values.append(rb[c][found].astype(F32))
        values.append(blk[c, b].astype(F32))
        for n, (p, q) in enumerate(PAIRS):
            product = values[p] * values[q]
            product = product[0:8] + product[8:16]
            if c != GRAM_ORDER[0]:
                product = product + part_sums[n, place]
            part_sums[n, place] = product

    def add_products(c):
        def step(g, carry):
            for m in range(4):
                products(c, g * 4 + m)
            return carry

        lax.fori_loop(0, FINE // 4, step, 0)

    def finish():
        sub = lax.broadcasted_iota(jnp.int32, (8, ROWS), 0)
        low4, low2, low1 = sub < 4, (sub & 2) == 0, (sub & 1) == 0

        def merge(first, second, keep_first, shift):
            first = first + pltpu.roll(first, 8 - shift, 0)
            second = second + pltpu.roll(second, shift, 0)
            return jnp.where(keep_first, first, second)

        def group(g, carry):
            total = {}
            spots = [spot_s[0, g * 8 + m] & (SITES - 1) for m in range(8)]
            for n, couple in enumerate(PAIRS):
                rows = [part_sums[n, spot] for spot in spots]
                rows = [
                    jnp.where(low4, rows[m], rows[m + 4])
                    + pltpu.roll(jnp.where(low4, rows[m + 4], rows[m]), 4, 0)
                    for m in range(4)
                ]
                rows = [merge(rows[m], rows[m + 2], low2, 2) for m in range(2)]
                total[couple] = merge(rows[0], rows[1], low1, 1) * (1.0 / VECS)
                if couple[0] == couple[1]:
                    total[couple] = total[couple] + RIDGE
            out = solve_rows(total, [total[s, SLOTS] for s in range(SLOTS)])
            for s in range(SLOTS):
                w_out[s, pl.ds(pl.multiple_of(g * 8, 8), 8), :] = out[s]
            return carry

        lax.fori_loop(0, SITES // 8, group, 0)

    stores = []

    def transpose_out(c, w):
        for x in range(NX):
            for half in range(NY // 8):
                for k in range(KV):
                    stage[c * KV + k, x, pl.ds(half * 8, 8), :] = w[
                        c, pl.ds(site_row(x, half * 8) + k, 8, stride=KV), :
                    ]
        part = pl.ds(c * KV, KV)
        store = pltpu.make_async_copy(stage.at[part], sm_out.at[part], out_sem.at[c])
        store.start()
        stores.append(store)

    for c in range(CHUNKS):
        transpose_in(c)
        if c == 0:
            pl.semaphore_wait(barrier, greeted)
        send_faces(0, c, wa)

    for load in coef_loads:
        load.wait()
    ax, ay, az = coef[0], coef[1], coef[2]
    scale = OMEGA / (2.0 * (ax + ay + az) + coef[3])
    ka[...] = ax * scale
    kb[...] = ay * scale
    az = az * scale
    lane = lax.broadcasted_iota(jnp.int32, az.shape, 2)
    km[...] = jnp.where(lane == 0, 0.0, az)
    kp[...] = jnp.where(lane == ROWS - 1, 0.0, az)

    for load in lists:
        load.wait()
    meta[...] = jnp.zeros_like(meta)
    slots = lax.broadcasted_iota(jnp.int32, (SLOTS, NY), 0)
    for x in range(NX):
        live = (cells[0][x] == 0) & (slots < cells[1][x])
        listed = jnp.where(live, cells[2][x] * SITES + cells[3][x], -1)
        for t in range(SLOTS):
            where = pl.ds((x % 2) * (ROWS // 2) + t * NY, NY)
            meta[x // 2 : x // 2 + 1, where] = listed[t : t + 1]
        meta[2:3, pl.ds(x * NY, NY)] = cells[0][x]
    blocks, targets, rank, ids, fine_ids, fine_rank = lists_of(meta[...], at)
    near[at["y"] * CORES + core] = jnp.broadcast_to(rank, (8, ROWS))
    for copy in gather_copies(0):
        copy.start()
    for p in range(2):
        block_cols[p] = jnp.broadcast_to(blocks[p], (ROWS, ROWS))
    idv[:COARSE] = ids
    idv[COARSE : COARSE + FINE] = fine_ids
    idv[COARSE + FINE :] = jnp.broadcast_to(fine_rank, (8, ROWS))
    part_sums[:, FINE] = jnp.zeros((len(PAIRS), 8, ROWS), F32)
    id_copies = [
        pltpu.make_async_copy(idv.at[pl.ds(0, COARSE)], id_s, smem_sem.at[0]),
        pltpu.make_async_copy(idv.at[pl.ds(COARSE, FINE)], fine_s, smem_sem.at[2]),
        pltpu.make_async_copy(idv.at[pl.ds(COARSE + FINE, 8)], spot_s, smem_sem.at[4]),
    ]
    for copy in id_copies:
        copy.start()
    tgt[...] = jnp.zeros_like(tgt)
    for c in range(CHUNKS):
        for h in range(2):
            tgt[2 * c + h : 2 * c + h + 1] = targets[c][h]
        rb[c][EMPTY] = jnp.zeros((KV, ROWS), BF16)
    tgt_copy = pltpu.make_async_copy(tgt, tgt_s, smem_sem.at[3])
    tgt_copy.start()

    for s in range(SWEEPS):
        src, dst = (wb, wa) if s % 2 else (wa, wb)
        for c in range(CHUNKS):
            fill_halo(s, c, src)
            sweep(c, src, dst, s == SWEEPS - 1)
            if s < SWEEPS - 1:
                send_faces(s + 1, c, dst)
            else:
                if c == 0:
                    for copy in id_copies:
                        copy.wait()
                spread(c)
            if (s, c) in steps:
                steps[s, c]()
    drain(lines.at[:, pl.ds(0, 3)], table_sem.at[1])
    line_copy = pltpu.make_async_copy(lines, line_s, smem_sem.at[1])
    line_copy.start()
    cast(0)
    cast(1)
    cast(2)
    line_copy.wait()
    for c in range(CHUNKS):
        pass_on(c)
    for c in (1, 2, 0):
        reply(c, 0)
    for c in (1, 0, 2):
        reply(c, 1)
    for c in range(CHUNKS):
        transpose_out(c, wb)
    tgt_copy.wait()
    for c in GRAM_ORDER:
        for part in range(len(PARTS)):
            answer(c, part, 0, 0).wait()
            drain(sb.at[c, pl.ds(0, 7 * PARTS[part][1] * SPOT)], ans_recv.at[c, part])
        add_products(c)
    finish()

    drain(fxs, send_sem.at[0])
    drain(fys, send_sem.at[1])
    pair_copy().wait_send()
    drain(lines.at[:, pl.ds(0, 3)], table_sem.at[0])
    for step in range(3):
        drain(gathered(step), gather_sem.at[step, 0])
    for c in range(CHUNKS):
        drain(pg[c][0].at[pl.ds(0, 3)], near_sem.at[c, 0])
        for n in range(3):
            drain(pg[c][0], cast_send.at[c, n])
        for part in range(len(PARTS)):
            count = PARTS[part][1]
            drain(sb.at[c, pl.ds(0, 7 * count * SPOT)], ans_send.at[c, part])
    for store in stores:
        store.wait()


def smooth(test_vectors, coef_x, coef_y, coef_z, shift, split, count, owner, local):
    vmem = pl.BlockSpec(memory_space=pltpu.VMEM)
    anywhere = pl.BlockSpec(memory_space=pl.ANY)
    cells = pltpu.VMEM((NX, NY, ROWS), F32)
    rows = pltpu.VMEM((LINE, COARSE, KV, ROWS), BF16)
    dma = pltpu.SemaphoreType.DMA
    return pl.pallas_call(
        smooth_kernel,
        out_shape=(
            jax.ShapeDtypeStruct((VECS, NX, NY, ROWS), F32),
            jax.ShapeDtypeStruct((SLOTS, SITES, ROWS), F32),
        ),
        in_specs=[anywhere] * 9,
        out_specs=(anywhere, vmem),
        scratch_shapes=[
            pltpu.VMEM((NX, 1, NY), jnp.int32),
            pltpu.VMEM((NX, 1, NY), jnp.int32),
            pltpu.VMEM((NX, SLOTS, NY), jnp.int32),
            pltpu.VMEM((NX, SLOTS, NY), jnp.int32),
            pltpu.VMEM((8, ROWS), jnp.int32),
            pltpu.VMEM((8, ROWS), jnp.int32),
            pltpu.SMEM((8, ROWS), jnp.int32),
            pltpu.VMEM((CHUNKS, SITES, KV, ROWS), BF16),
            *([pltpu.VMEM((EMPTY + 8, KV, ROWS), BF16)] * CHUNKS),
            pltpu.VMEM((len(PAIRS), SITES, 8, ROWS), F32),
            pltpu.VMEM((VECS, NX, NY, ROWS), F32),
            pltpu.VMEM((4, NX, NY, ROWS), F32),
            pltpu.VMEM((CHUNKS, EXT, ROWS), F32),
            pltpu.VMEM((CHUNKS, EXT, ROWS), F32),
            cells, cells, cells, cells,
            pltpu.VMEM((SWEEPS, CHUNKS, 2, NY * KV, ROWS), BF16),
            pltpu.VMEM((SWEEPS, CHUNKS, 2, NY * KV, ROWS), BF16),
            pltpu.VMEM((SWEEPS, CHUNKS, 2, NX * KV, ROWS), BF16),
            pltpu.VMEM((SWEEPS, CHUNKS, 2, NX * KV, ROWS), BF16),
            pltpu.VMEM((CORES, 2, 1, ROWS), jnp.int32),
            pltpu.VMEM((len(AXES), LINE, CORES, 2, 1, ROWS), jnp.int32),
            pltpu.VMEM((LINE * CORES, 8, ROWS), jnp.int32),
            pltpu.VMEM((LINE, LINE, LINE * CORES, ROWS), jnp.int32),
            pltpu.VMEM((2, ROWS, ROWS), jnp.int32),
            pltpu.VMEM((COARSE + FINE + 8, ROWS), jnp.int32),
            pltpu.SMEM((len(AXES), LINE, CORES, 2, 1, ROWS), jnp.int32),
            pltpu.SMEM((COARSE, ROWS), jnp.int32),
            pltpu.SMEM((FINE, ROWS), jnp.int32),
            pltpu.SMEM((8, ROWS), jnp.int32),
            *([rows] * (LINE * CHUNKS)),
            pltpu.VMEM((CHUNKS, EMPTY, KV, ROWS), BF16),
            dma((CHUNKS,)),
            dma((4,)),
            dma((CHUNKS,)),
            dma((2,)),
            dma((SWEEPS, CHUNKS, 2)),
            dma((2,)),
            dma((2,)),
            dma((3, 2)),
            dma((CHUNKS, 2)),
            dma((CHUNKS, 3)),
            dma((CHUNKS, 4)),
            dma((CHUNKS, len(PARTS))),
            dma((CHUNKS, len(PARTS))),
            dma((CHUNKS, len(PARTS))),
            dma((5,)),
            dma((4,)),
        ],
        compiler_params=pltpu.CompilerParams(
            collective_id=0, has_side_effects=True, vmem_limit_bytes=60 * 1024 * 1024
        ),
        name="smooth",
    )(test_vectors, coef_x, coef_y, coef_z, shift, split, count, owner, local)


def pass_kernel(w_in, sm_in, w_out, sm_out, w_hold, sm_hold, in_sem, out_sem):
    parts = [(w_in, w_hold, w_out)]
    for c in range(CHUNKS):
        part = pl.ds(c * KV, KV)
        parts.append((sm_in.at[part], sm_hold.at[part], sm_out.at[part]))
    ins = [pltpu.make_async_copy(a, b, in_sem.at[n]) for n, (a, b, _) in enumerate(parts)]
    outs = [pltpu.make_async_copy(b, d, out_sem.at[n]) for n, (_, b, d) in enumerate(parts)]
    for copy in ins:
        copy.start()
    for load, store in zip(ins, outs):
        load.wait()
        store.start()
    for store in outs:
        store.wait()


def pass_on_results(weights, sm):
    anywhere = pl.BlockSpec(memory_space=pl.ANY)
    dma = pltpu.SemaphoreType.DMA
    return pl.pallas_call(
        pass_kernel,
        out_shape=(
            jax.ShapeDtypeStruct(weights.shape, F32),
            jax.ShapeDtypeStruct(sm.shape, F32),
        ),
        in_specs=[anywhere, anywhere],
        out_specs=(anywhere, anywhere),
        scratch_shapes=[
            pltpu.VMEM(weights.shape, F32),
            pltpu.VMEM(sm.shape, F32),
            dma((CHUNKS + 1,)),
            dma((CHUNKS + 1,)),
        ],
        compiler_params=pltpu.CompilerParams(vmem_limit_bytes=60 * 1024 * 1024),
        name="fit",
    )(weights, sm)


def per_device(
    test_vectors, coef_x, coef_y, coef_z, shift, cf_split, nbr_count, nbr_owner, nbr_block
):
    sm, weights = smooth(
        test_vectors, coef_x, coef_y, coef_z, shift,
        jnp.swapaxes(cf_split, 1, 2),
        jnp.swapaxes(nbr_count, 1, 2),
        jnp.transpose(nbr_owner, (0, 2, 3, 1)).reshape(NX, SLOTS, NY),
        jnp.transpose(nbr_block, (0, 2, 3, 1)).reshape(NX, SLOTS, NY),
    )
    weights, smoothed = pass_on_results(weights.reshape(SLOTS, NX, NY, ROWS), sm)
    return (smoothed, weights)


def solution(mesh):
    cells = P("gx", "gy", None)
    lists = P("gx", "gy", None, None)
    vectors = P(None, "gx", "gy", None)
    return jax.shard_map(
        per_device,
        mesh=mesh,
        in_specs=(vectors, cells, cells, cells, cells, cells, cells, lists, lists),
        out_specs=(vectors, vectors),
        check_vma=False,
    )
```

```python
import jax
import jax.numpy as jnp
from jax import lax
from jax.experimental import pallas as pl
from jax.experimental.pallas import tpu as pltpu
from jax.sharding import PartitionSpec as P

SLOTS = 4
SWEEPS = 3
ROWS = 128
OMEGA = 0.8
RIDGE = 0.05
VECS = 48
CHUNKS = 3
KV = VECS // CHUNKS
NX = 4
NY = 16
SITES = NX * NY
XROW = (NY + 2) * KV
EXT = (NX + 2) * XROW
GX = 16
GY = 8
MESH = pl.DeviceIdType.MESH
F32 = jnp.float32
BF16 = jnp.bfloat16


def site_row(x, y):
    return (x + 1) * XROW + (y + 1) * KV


def solve_rows(gram, rhs):
    low = [[None] * SLOTS for _ in range(SLOTS)]
    inv = []
    for r in range(SLOTS):
        scaled = []
        diag = gram[r, r]
        for c in range(r):
            rest = gram[r, c]
            for m in range(c):
                rest = rest - scaled[m] * low[c][m]
            scaled.append(rest)
            low[r][c] = rest * inv[c]
            diag = diag - rest * low[r][c]
        inv.append(1.0 / diag)
    fwd = []
    for r in range(SLOTS):
        rest = rhs[r]
        for m in range(r):
            rest = rest - low[r][m] * fwd[m]
        fwd.append(rest)
    out = [None] * SLOTS
    for r in reversed(range(SLOTS)):
        rest = fwd[r] * inv[r]
        for m in range(r + 1, SLOTS):
            rest = rest - low[m][r] * out[m]
        out[r] = rest
    return out


PAIRS = [(s, t) for s in range(SLOTS) for t in range(s + 1)] + [(s, SLOTS) for s in range(SLOTS)]
AXES = "xyz"
LINE = 4
CORES = 2
COARSE = 16
FINE = 48
PLANE = LINE * LINE
ROUTES = (("x", "z", "y"), ("y", "x", "z"), ("z", "y", "x"))
BACKS = (0, 1, 3, 2)
EMPTY = LINE * CORES * PLANE * 2
SPOT = 2 * LINE
GRAM_ORDER = (1, 2, 0)
REPLY = PLANE * 2
PARTS = ((0, 3), (3, 1))


def lists_of(meta, here):
    lane = lax.broadcasted_iota(jnp.int32, (ROWS, ROWS), 1)
    sub = lax.broadcasted_iota(jnp.int32, (ROWS, ROWS), 0)
    diag = lane == sub
    none = 1 << 20

    def column(row):
        return jnp.sum(jnp.where(diag, row, 0), axis=1, keepdims=True)

    members, keys, owners = [], [], []
    for h in range(2):
        entry = meta[h : h + 1]
        owner = entry >> 6
        key = (lane[:1] + h * ROWS) * SITES + (entry & (SITES - 1))
        owners.append(owner)
        keys.append(key)
        members.append(owner == sub)
    first = jnp.minimum(*[jnp.where(m, k, none) for m, k in zip(members, keys)])
    first = jnp.min(first, axis=1, keepdims=True)
    first = jnp.where(first >= none, 0, first)
    second = jnp.maximum(*[jnp.where(m, k, 0) for m, k in zip(members, keys)])
    second = jnp.max(second, axis=1, keepdims=True)
    targets = [[] for _ in ROUTES]
    for h in range(2):
        own = owners[h]
        at_first = jnp.sum(jnp.where(members[h], first, 0), axis=0, keepdims=True)
        place = jnp.where(keys[h] == at_first, 0, 1)
        at = {"x": (own >> 5) & 3, "z": (own >> 3) & 3, "y": (own >> 1) & 3}
        for c, (a, u, v) in enumerate(ROUTES):
            back = (at[v] - here[v]) & 3
            spot = jnp.where(back == 2, 3, jnp.where(back == 3, 2, back))
            slot = ((at[a] * CORES + (own & 1)) * PLANE + spot * LINE + ((at[u] - here[u]) & 3)) * 2 + place
            targets[c].append(jnp.where(own < 0, EMPTY, slot))
    coarse = meta[2:3]
    rank = jnp.sum(jnp.where(sub < lane, column(coarse), 0), axis=0, keepdims=True)
    fine_rank = jnp.minimum(lane[:1] - rank, FINE)
    fine_rank = jnp.where(coarse > 0, FINE, fine_rank)

    def numbers(hit):
        found = jnp.sum(jnp.where(hit, lane[: hit.shape[0]], 0), axis=1, keepdims=True)
        return jnp.broadcast_to(found, hit.shape)

    ids = numbers((rank == sub[:COARSE]) & (coarse > 0))
    fine_ids = numbers((fine_rank == sub[:FINE]) & (lane[:1] < SITES))
    rank = jnp.minimum(rank, COARSE - 1)
    return (first, second), targets, rank, ids, fine_ids, fine_rank


def ranks_wanted(blocks, table):
    lane = lax.broadcasted_iota(jnp.int32, (ROWS, ROWS), 1)
    sub = lax.broadcasted_iota(jnp.int32, (ROWS, ROWS), 0)
    found = jnp.sum(
        jnp.where(lane == (blocks & (SITES - 1)), table, 0), axis=1, keepdims=True
    )
    return jnp.sum(jnp.where(lane == sub, found, 0), axis=0, keepdims=True)


def smooth_kernel(
    tv, cx, cy, cz, sh, split, count, owner, local, sm_out, w_out,
    split_v, count_v, owner_v, local_v, meta, tgt, tgt_s, blk, rb0, rb1, rb2, part_sums,
    stage, coef, wa, wb, ka, kb, km, kp, fxs, fxr, fys, fyr,
    pair, lines, near, far, block_cols, idv, line_s, id_s, fine_s, spot_s, p00, p01, p02, p03, p10, p11, p12, p13, p20, p21, p22, p23, sb,
    in_sem, coef_sem, out_sem, send_sem, recv_sem, pair_sem, table_sem, gather_sem,
    near_sem, cast_send, cast_recv, ans_send, ans_recv, own_sem, smem_sem, list_sem,
):
    cells = (split_v, count_v, owner_v, local_v)
    rb = (rb0, rb1, rb2)
    pg = ((p00, p01, p02, p03), (p10, p11, p12, p13), (p20, p21, p22, p23))
    i = lax.axis_index("gx")
    j = lax.axis_index("gy")
    core = lax.rem(j, CORES)
    at = {"x": i // LINE, "z": lax.rem(i, LINE), "y": j // CORES}
    peers = (
        (lax.rem(i + GX - 1, GX), j),
        (lax.rem(i + 1, GX), j),
        (i, lax.rem(j + GY - 1, GY)),
        (i, lax.rem(j + 1, GY)),
    )

    def device(axis, d, e):
        moved = dict(at)
        moved[axis] = lax.rem(at[axis] + d, LINE)
        return (moved["x"] * LINE + moved["z"], moved["y"] * CORES + lax.rem(core + e, CORES))

    def remote(src, dst, send, recv, peer):
        return pltpu.make_async_remote_copy(
            src_ref=src, dst_ref=dst, send_sem=send, recv_sem=recv,
            device_id=peer, device_id_type=MESH,
        )

    loads = []
    for c in range(CHUNKS):
        part = pl.ds(c * KV, KV)
        loads.append(pltpu.make_async_copy(tv.at[part], stage.at[part], in_sem.at[c]))
    loads[0].start()
    barrier = pltpu.get_barrier_semaphore()
    for peer in peers[:2]:
        pl.semaphore_signal(barrier, inc=1, device_id=peer, device_id_type=MESH)
    pl.semaphore_signal(barrier, inc=1, device_id=device("x", 0, 1), device_id_type=MESH)
    for axis in AXES:
        for d in range(1, LINE):
            for e in range(CORES):
                pl.semaphore_signal(
                    barrier, inc=1, device_id=device(axis, d, e), device_id_type=MESH
                )
    greeted = 3 + len(AXES) * (LINE - 1) * CORES
    for load in loads[1:]:
        load.start()
    coef_loads = []
    for n, part in enumerate((cx, cy, cz, sh)):
        load = pltpu.make_async_copy(part, coef.at[n], coef_sem.at[n])
        load.start()
        coef_loads.append(load)
    lists = []
    for n, part in enumerate((split, count, owner, local)):
        load = pltpu.make_async_copy(part, cells[n], list_sem.at[n])
        load.start()
        lists.append(load)

    keep = (
        (i > 0).astype(F32),
        (i < GX - 1).astype(F32),
        (j > 0).astype(F32),
        (j < GY - 1).astype(F32),
    )

    def drain(ref, sem):
        pltpu.make_async_copy(ref, ref, sem).wait()

    def copies(s, c):
        out = []
        for d in range(4):
            src, dst = (fxs, fxr) if d < 2 else (fys, fyr)
            out.append(
                remote(
                    src.at[s, c, d % 2], dst.at[s, c, 1 - d % 2],
                    send_sem.at[d // 2], recv_sem.at[s, c, d // 2], peers[d],
                )
            )
        return out

    def send_faces(s, c, w):
        for side in range(2):
            x = side * (NX - 1)
            fxs[s, c, side] = w[c, pl.ds(site_row(x, 0), NY * KV)].astype(BF16)
            y = side * (NY - 1)
            for x in range(NX):
                fys[s, c, side, pl.ds(x * KV, KV)] = w[c, pl.ds(site_row(x, y), KV)].astype(BF16)
        for copy in copies(s, c):
            copy.start()

    def fill_halo(s, c, w):
        drain(fxr.at[s, c], recv_sem.at[s, c, 0])
        drain(fyr.at[s, c], recv_sem.at[s, c, 1])
        for side in range(2):
            x = -1 if side == 0 else NX
            w[c, pl.ds(site_row(x, 0), NY * KV)] = fxr[s, c, side].astype(F32) * keep[side]
            y = -1 if side == 0 else NY
            for x in range(NX):
                w[c, pl.ds(site_row(x, y), KV)] = (
                    fyr[s, c, side, pl.ds(x * KV, KV)].astype(F32) * keep[2 + side]
                )

    def sweep(c, src, dst, last):
        def plane(x, carry):
            base = pl.multiple_of(x * XROW, 16)

            def cell(dx, y):
                return src[c, pl.ds(base + site_row(dx, y), KV)]

            below, here = cell(0, -1), cell(0, 0)
            for y in range(NY):
                above = cell(0, y + 1)
                row = slice(y, y + 1)
                new = (
                    ka[x, row] * (cell(-1, y) + cell(1, y))
                    + kb[x, row] * (below + above)
                    + km[x, row] * pltpu.roll(here, 1, 1)
                    + kp[x, row] * pltpu.roll(here, ROWS - 1, 1)
                    + (1.0 - OMEGA) * here
                )
                dst[c, pl.ds(base + site_row(0, y), KV)] = new
                if last:
                    blk[c, x * NY + y] = new.astype(BF16)
                below, here = here, above
            return carry

        lax.fori_loop(0, NX, plane, 0)

    def pair_copy():
        slot = pair.at[core]
        return remote(slot, slot, pair_sem.at[0], pair_sem.at[1], device("x", 0, 1))

    def line_copies():
        return [
            remote(
                pair, lines.at[n, at[axis]], table_sem.at[0], table_sem.at[1],
                device(axis, d, 0),
            )
            for n, axis in enumerate(AXES)
            for d in range(1, LINE)
        ]

    def gather_copies(step):
        send, recv = gather_sem.at[step, 0], gather_sem.at[step, 1]
        if step == 0:
            slot = near.at[at["y"] * CORES + core]
            return [
                remote(slot, slot, send, recv, device("y", d, e))
                for d in range(LINE)
                for e in range(CORES)
                if d or e
            ]
        slot = far.at[at["x"], at["z"]] if step == 1 else far.at[at["x"]]
        return [
            remote(slot, slot, send, recv, device("zx"[step - 1], d, 0)) for d in range(1, LINE)
        ]

    def gathered(step):
        if step == 0:
            return near.at[pl.ds(0, 7)]
        return far.at[0, pl.ds(0, 3)] if step == 1 else far.at[pl.ds(0, 3)]

    def gather_step(step):
        drain(gathered(step), gather_sem.at[step, 1])
        if step == 0:
            for n in range(LINE * CORES):
                far[at["x"], at["z"], n : n + 1] = near[n, 0:1]
        for copy in gather_copies(step + 1):
            copy.start()

    def ask():
        drain(gathered(2), gather_sem.at[2, 1])
        table = far[...].reshape(ROWS, ROWS)
        for p in range(2):
            pair[core, p] = ranks_wanted(block_cols[p], table)
        pair_copy().start()

    def ask_lines():
        pair_copy().wait_recv()
        for copy in line_copies():
            copy.start()
        for n, axis in enumerate(AXES):
            lines[n, at[axis]] = pair[...]

    steps = {
        (0, 1): lambda: gather_step(0),
        (1, 0): lambda: gather_step(1),
        (1, 2): ask,
        (2, 1): ask_lines,
    }

    def spread_copies(c):
        a, u, v = ROUTES[c]
        return [
            remote(
                pg[c][0].at[0], pg[c][0].at[LINE - d],
                near_sem.at[c, 0], near_sem.at[c, 1], device(u, d, 0),
            )
            for d in (2, 1, 3)
        ]

    def cast_copies(c, first, size):
        a, u, v = ROUTES[c]
        shards = pl.ds(first, size)
        return [
            remote(
                pg[c][0].at[shards], pg[c][LINE - d].at[shards],
                cast_send.at[c, d - 1], cast_recv.at[c, LINE - d], device(v, d, 0),
            )
            for d in (2, 1, 3)
        ]

    def piece(slot, part):
        first, count = PARTS[part]
        return pl.ds(slot * REPLY + first * SPOT, count * SPOT)

    def answer(c, part, d, e):
        a = ROUTES[c][0]
        slot = lax.rem(at[a] + d, LINE) * CORES + lax.rem(core + e, CORES)
        here = at[a] * CORES + core
        src = sb.at[c, piece(slot, part)]
        dst, peer = rb[c].at[piece(here, part)], device(a, d, e)
        if d == 0 and e == 0:
            return pltpu.make_async_copy(src, dst, own_sem.at[c, part])
        return remote(src, dst, ans_send.at[c, part], ans_recv.at[c, part], peer)

    order = [(d, e) for d in (2, 1, 3, 0) for e in range(CORES)]

    def spread(c):
        a, u, v = ROUTES[c]
        for r in range(COARSE):
            pg[c][0][0, r] = blk[c, id_s[r, 0] & (SITES - 1)]
        for copy in spread_copies(c) + cast_copies(c, 0, 1):
            copy.start()

    def cast(c):
        drain(pg[c][1].at[pl.ds(0, 3)], near_sem.at[c, 1])
        for copy in cast_copies(c, 1, LINE - 1):
            copy.start()

    def reply(c, part):
        a, u, v = ROUTES[c]
        n = AXES.index(a)
        for back in ((1, 3), (2,))[part]:
            drain(pg[c][0], cast_recv.at[c, back])
        first, count = PARTS[part]
        for d, e in order:
            q, to = lax.rem(at[a] + d, LINE), lax.rem(core + e, CORES)
            slot = q * CORES + to
            for place in range(first, first + count):
                back = BACKS[place]
                tiles = []
                for ahead in range(LINE):
                    whose = {
                        a: at[a],
                        u: lax.rem(at[u] + ahead, LINE),
                        v: lax.rem(at[v] + back, LINE),
                    }
                    owner = whose["x"] * 32 + whose["z"] * 8 + whose["y"] * 2 + core
                    for p in range(2):
                        rank = line_s[n, q, to, p, 0, owner] & (COARSE - 1)
                        tiles.append(pg[c][back][ahead, rank])
                for t, tile in enumerate(tiles):
                    sb[c, slot * REPLY + place * SPOT + t] = tile
            answer(c, part, d, e).start()

    def transpose_in(c):
        loads[c].wait()
        for x in range(NX):
            for half in range(NY // 8):
                for k in range(KV):
                    wa[c, pl.ds(site_row(x, half * 8) + k, 8, stride=KV), :] = stage[
                        c * KV + k, x, pl.ds(half * 8, 8), :
                    ]

    def products(c, place):
        b = fine_s[place, 0] & (SITES - 1)
        column = ((b >> 4) & 1) * (ROWS // 2) + (b & (NY - 1))
        values = []
        for t in range(SLOTS):
            found = tgt_s[2 * c + (b >> 5), column + t * NY]
            values.append(rb[c][found].astype(F32))
        values.append(blk[c, b].astype(F32))
        for n, (p, q) in enumerate(PAIRS):
            product = values[p] * values[q]
            product = product[0:8] + product[8:16]
            if c != GRAM_ORDER[0]:
                product = product + part_sums[n, place]
            part_sums[n, place] = product

    def add_products(c):
        def step(g, carry):
            for m in range(4):
                products(c, g * 4 + m)
            return carry

        lax.fori_loop(0, FINE // 4, step, 0)

    def finish():
        sub = lax.broadcasted_iota(jnp.int32, (8, ROWS), 0)
        low4, low2, low1 = sub < 4, (sub & 2) == 0, (sub & 1) == 0

        def merge(first, second, keep_first, shift):
            first = first + pltpu.roll(first, 8 - shift, 0)
            second = second + pltpu.roll(second, shift, 0)
            return jnp.where(keep_first, first, second)

        def group(g, carry):
            total = {}
            spots = [spot_s[0, g * 8 + m] & (SITES - 1) for m in range(8)]
            for n, couple in enumerate(PAIRS):
                rows = [part_sums[n, spot] for spot in spots]
                rows = [
                    jnp.where(low4, rows[m], rows[m + 4])
                    + pltpu.roll(jnp.where(low4, rows[m + 4], rows[m]), 4, 0)
                    for m in range(4)
                ]
                rows = [merge(rows[m], rows[m + 2], low2, 2) for m in range(2)]
                total[couple] = merge(rows[0], rows[1], low1, 1) * (1.0 / VECS)
                if couple[0] == couple[1]:
                    total[couple] = total[couple] + RIDGE
            out = solve_rows(total, [total[s, SLOTS] for s in range(SLOTS)])
            for s in range(SLOTS):
                w_out[s, pl.ds(pl.multiple_of(g * 8, 8), 8), :] = out[s]
            return carry

        lax.fori_loop(0, SITES // 8, group, 0)

    stores = []

    def transpose_out(c, w):
        for x in range(NX):
            for half in range(NY // 8):
                for k in range(KV):
                    stage[c * KV + k, x, pl.ds(half * 8, 8), :] = w[
                        c, pl.ds(site_row(x, half * 8) + k, 8, stride=KV), :
                    ]
        part = pl.ds(c * KV, KV)
        store = pltpu.make_async_copy(stage.at[part], sm_out.at[part], out_sem.at[c])
        store.start()
        stores.append(store)

    for c in range(CHUNKS):
        transpose_in(c)
        if c == 0:
            pl.semaphore_wait(barrier, greeted)
        send_faces(0, c, wa)

    for load in coef_loads:
        load.wait()
    ax, ay, az = coef[0], coef[1], coef[2]
    scale = OMEGA / (2.0 * (ax + ay + az) + coef[3])
    ka[...] = ax * scale
    kb[...] = ay * scale
    az = az * scale
    lane = lax.broadcasted_iota(jnp.int32, az.shape, 2)
    km[...] = jnp.where(lane == 0, 0.0, az)
    kp[...] = jnp.where(lane == ROWS - 1, 0.0, az)

    for load in lists:
        load.wait()
    meta[...] = jnp.zeros_like(meta)
    slots = lax.broadcasted_iota(jnp.int32, (SLOTS, NY), 0)
    for x in range(NX):
        live = (cells[0][x] == 0) & (slots < cells[1][x])
        listed = jnp.where(live, cells[2][x] * SITES + cells[3][x], -1)
        for t in range(SLOTS):
            where = pl.ds((x % 2) * (ROWS // 2) + t * NY, NY)
            meta[x // 2 : x // 2 + 1, where] = listed[t : t + 1]
        meta[2:3, pl.ds(x * NY, NY)] = cells[0][x]
    blocks, targets, rank, ids, fine_ids, fine_rank = lists_of(meta[...], at)
    near[at["y"] * CORES + core] = jnp.broadcast_to(rank, (8, ROWS))
    for copy in gather_copies(0):
        copy.start()
    for p in range(2):
        block_cols[p] = jnp.broadcast_to(blocks[p], (ROWS, ROWS))
    idv[:COARSE] = ids
    idv[COARSE : COARSE + FINE] = fine_ids
    idv[COARSE + FINE :] = jnp.broadcast_to(fine_rank, (8, ROWS))
    part_sums[:, FINE] = jnp.zeros((len(PAIRS), 8, ROWS), F32)
    id_copies = [
        pltpu.make_async_copy(idv.at[pl.ds(0, COARSE)], id_s, smem_sem.at[0]),
        pltpu.make_async_copy(idv.at[pl.ds(COARSE, FINE)], fine_s, smem_sem.at[2]),
        pltpu.make_async_copy(idv.at[pl.ds(COARSE + FINE, 8)], spot_s, smem_sem.at[4]),
    ]
    for copy in id_copies:
        copy.start()
    tgt[...] = jnp.zeros_like(tgt)
    for c in range(CHUNKS):
        for h in range(2):
            tgt[2 * c + h : 2 * c + h + 1] = targets[c][h]
        rb[c][EMPTY] = jnp.zeros((KV, ROWS), BF16)
    tgt_copy = pltpu.make_async_copy(tgt, tgt_s, smem_sem.at[3])
    tgt_copy.start()

    for s in range(SWEEPS):
        src, dst = (wb, wa) if s % 2 else (wa, wb)
        for c in range(CHUNKS):
            fill_halo(s, c, src)
            sweep(c, src, dst, s == SWEEPS - 1)
            if s < SWEEPS - 1:
                send_faces(s + 1, c, dst)
            else:
                if c == 0:
                    for copy in id_copies:
                        copy.wait()
                spread(c)
            if (s, c) in steps:
                steps[s, c]()
    drain(lines.at[:, pl.ds(0, 3)], table_sem.at[1])
    line_copy = pltpu.make_async_copy(lines, line_s, smem_sem.at[1])
    line_copy.start()
    cast(0)
    cast(1)
    cast(2)
    line_copy.wait()
    for c in (1, 2, 0):
        reply(c, 0)
    for c in (1, 0, 2):
        reply(c, 1)
    for c in range(CHUNKS):
        transpose_out(c, wb)
    tgt_copy.wait()
    for c in GRAM_ORDER:
        for part in range(len(PARTS)):
            answer(c, part, 0, 0).wait()
            drain(sb.at[c, pl.ds(0, 7 * PARTS[part][1] * SPOT)], ans_recv.at[c, part])
        add_products(c)
    finish()

    drain(fxs, send_sem.at[0])
    drain(fys, send_sem.at[1])
    pair_copy().wait_send()
    drain(lines.at[:, pl.ds(0, 3)], table_sem.at[0])
    for step in range(3):
        drain(gathered(step), gather_sem.at[step, 0])
    for c in range(CHUNKS):
        drain(pg[c][0].at[pl.ds(0, 3)], near_sem.at[c, 0])
        for n in range(3):
            drain(pg[c][0], cast_send.at[c, n])
        for part in range(len(PARTS)):
            count = PARTS[part][1]
            drain(sb.at[c, pl.ds(0, 7 * count * SPOT)], ans_send.at[c, part])
    for store in stores:
        store.wait()


def smooth(test_vectors, coef_x, coef_y, coef_z, shift, split, count, owner, local):
    vmem = pl.BlockSpec(memory_space=pltpu.VMEM)
    anywhere = pl.BlockSpec(memory_space=pl.ANY)
    cells = pltpu.VMEM((NX, NY, ROWS), F32)
    rows = pltpu.VMEM((LINE, COARSE, KV, ROWS), BF16)
    dma = pltpu.SemaphoreType.DMA
    return pl.pallas_call(
        smooth_kernel,
        out_shape=(
            jax.ShapeDtypeStruct((VECS, NX, NY, ROWS), F32),
            jax.ShapeDtypeStruct((SLOTS, SITES, ROWS), F32),
        ),
        in_specs=[anywhere] * 9,
        out_specs=(anywhere, vmem),
        scratch_shapes=[
            pltpu.VMEM((NX, 1, NY), jnp.int32),
            pltpu.VMEM((NX, 1, NY), jnp.int32),
            pltpu.VMEM((NX, SLOTS, NY), jnp.int32),
            pltpu.VMEM((NX, SLOTS, NY), jnp.int32),
            pltpu.VMEM((8, ROWS), jnp.int32),
            pltpu.VMEM((8, ROWS), jnp.int32),
            pltpu.SMEM((8, ROWS), jnp.int32),
            pltpu.VMEM((CHUNKS, SITES, KV, ROWS), BF16),
            *([pltpu.VMEM((EMPTY + 8, KV, ROWS), BF16)] * CHUNKS),
            pltpu.VMEM((len(PAIRS), SITES, 8, ROWS), F32),
            pltpu.VMEM((VECS, NX, NY, ROWS), F32),
            pltpu.VMEM((4, NX, NY, ROWS), F32),
            pltpu.VMEM((CHUNKS, EXT, ROWS), F32),
            pltpu.VMEM((CHUNKS, EXT, ROWS), F32),
            cells, cells, cells, cells,
            pltpu.VMEM((SWEEPS, CHUNKS, 2, NY * KV, ROWS), BF16),
            pltpu.VMEM((SWEEPS, CHUNKS, 2, NY * KV, ROWS), BF16),
            pltpu.VMEM((SWEEPS, CHUNKS, 2, NX * KV, ROWS), BF16),
            pltpu.VMEM((SWEEPS, CHUNKS, 2, NX * KV, ROWS), BF16),
            pltpu.VMEM((CORES, 2, 1, ROWS), jnp.int32),
            pltpu.VMEM((len(AXES), LINE, CORES, 2, 1, ROWS), jnp.int32),
            pltpu.VMEM((LINE * CORES, 8, ROWS), jnp.int32),
            pltpu.VMEM((LINE, LINE, LINE * CORES, ROWS), jnp.int32),
            pltpu.VMEM((2, ROWS, ROWS), jnp.int32),
            pltpu.VMEM((COARSE + FINE + 8, ROWS), jnp.int32),
            pltpu.SMEM((len(AXES), LINE, CORES, 2, 1, ROWS), jnp.int32),
            pltpu.SMEM((COARSE, ROWS), jnp.int32),
            pltpu.SMEM((FINE, ROWS), jnp.int32),
            pltpu.SMEM((8, ROWS), jnp.int32),
            *([rows] * (LINE * CHUNKS)),
            pltpu.VMEM((CHUNKS, EMPTY, KV, ROWS), BF16),
            dma((CHUNKS,)),
            dma((4,)),
            dma((CHUNKS,)),
            dma((2,)),
            dma((SWEEPS, CHUNKS, 2)),
            dma((2,)),
            dma((2,)),
            dma((3, 2)),
            dma((CHUNKS, 2)),
            dma((CHUNKS, 3)),
            dma((CHUNKS, LINE)),
            dma((CHUNKS, len(PARTS))),
            dma((CHUNKS, len(PARTS))),
            dma((CHUNKS, len(PARTS))),
            dma((5,)),
            dma((4,)),
        ],
        compiler_params=pltpu.CompilerParams(
            collective_id=0, has_side_effects=True, vmem_limit_bytes=60 * 1024 * 1024
        ),
        name="smooth",
    )(test_vectors, coef_x, coef_y, coef_z, shift, split, count, owner, local)


def pass_kernel(w_in, sm_in, w_out, sm_out, w_hold, sm_hold, in_sem, out_sem):
    parts = [(w_in, w_hold, w_out)]
    for c in range(CHUNKS):
        part = pl.ds(c * KV, KV)
        parts.append((sm_in.at[part], sm_hold.at[part], sm_out.at[part]))
    ins = [pltpu.make_async_copy(a, b, in_sem.at[n]) for n, (a, b, _) in enumerate(parts)]
    outs = [pltpu.make_async_copy(b, d, out_sem.at[n]) for n, (_, b, d) in enumerate(parts)]
    for copy in ins:
        copy.start()
    for load, store in zip(ins, outs):
        load.wait()
        store.start()
    for store in outs:
        store.wait()


def pass_on_results(weights, sm):
    anywhere = pl.BlockSpec(memory_space=pl.ANY)
    dma = pltpu.SemaphoreType.DMA
    return pl.pallas_call(
        pass_kernel,
        out_shape=(
            jax.ShapeDtypeStruct(weights.shape, F32),
            jax.ShapeDtypeStruct(sm.shape, F32),
        ),
        in_specs=[anywhere, anywhere],
        out_specs=(anywhere, anywhere),
        scratch_shapes=[
            pltpu.VMEM(weights.shape, F32),
            pltpu.VMEM(sm.shape, F32),
            dma((CHUNKS + 1,)),
            dma((CHUNKS + 1,)),
        ],
        compiler_params=pltpu.CompilerParams(vmem_limit_bytes=60 * 1024 * 1024),
        name="fit",
    )(weights, sm)


def per_device(
    test_vectors, coef_x, coef_y, coef_z, shift, cf_split, nbr_count, nbr_owner, nbr_block
):
    sm, weights = smooth(
        test_vectors, coef_x, coef_y, coef_z, shift,
        jnp.swapaxes(cf_split, 1, 2),
        jnp.swapaxes(nbr_count, 1, 2),
        jnp.transpose(nbr_owner, (0, 2, 3, 1)).reshape(NX, SLOTS, NY),
        jnp.transpose(nbr_block, (0, 2, 3, 1)).reshape(NX, SLOTS, NY),
    )
    weights, smoothed = pass_on_results(weights.reshape(SLOTS, NX, NY, ROWS), sm)
    return (smoothed, weights)


def solution(mesh):
    cells = P("gx", "gy", None)
    lists = P("gx", "gy", None, None)
    vectors = P(None, "gx", "gy", None)
    return jax.shard_map(
        per_device,
        mesh=mesh,
        in_specs=(vectors, cells, cells, cells, cells, cells, cells, lists, lists),
        out_specs=(vectors, vectors),
        check_vma=False,
    )
```

```python
import jax
import jax.numpy as jnp
from jax import lax
from jax.experimental import pallas as pl
from jax.experimental.pallas import tpu as pltpu
from jax.sharding import PartitionSpec as P

SLOTS = 4
SWEEPS = 3
ROWS = 128
OMEGA = 0.8
RIDGE = 0.05
VECS = 48
CHUNKS = 3
KV = VECS // CHUNKS
NX = 4
NY = 16
SITES = NX * NY
XROW = (NY + 2) * KV
EXT = (NX + 2) * XROW
GX = 16
GY = 8
MESH = pl.DeviceIdType.MESH
F32 = jnp.float32
BF16 = jnp.bfloat16


def site_row(x, y):
    return (x + 1) * XROW + (y + 1) * KV


def solve_rows(gram, rhs):
    low = [[None] * SLOTS for _ in range(SLOTS)]
    inv = []
    for r in range(SLOTS):
        scaled = []
        diag = gram[r, r]
        for c in range(r):
            rest = gram[r, c]
            for m in range(c):
                rest = rest - scaled[m] * low[c][m]
            scaled.append(rest)
            low[r][c] = rest * inv[c]
            diag = diag - rest * low[r][c]
        inv.append(1.0 / diag)
    fwd = []
    for r in range(SLOTS):
        rest = rhs[r]
        for m in range(r):
            rest = rest - low[r][m] * fwd[m]
        fwd.append(rest)
    out = [None] * SLOTS
    for r in reversed(range(SLOTS)):
        rest = fwd[r] * inv[r]
        for m in range(r + 1, SLOTS):
            rest = rest - low[m][r] * out[m]
        out[r] = rest
    return out


PAIRS = [(s, t) for s in range(SLOTS) for t in range(s + 1)] + [(s, SLOTS) for s in range(SLOTS)]
AXES = "xyz"
LINE = 4
CORES = 2
COARSE = 16
FINE = 48
PLANE = LINE * LINE
ROUTES = (("x", "z", "y"), ("y", "x", "z"), ("z", "y", "x"))
BACKS = (0, 1, 3, 2)
EMPTY = LINE * CORES * PLANE * 2
SPOT = 2 * LINE
GRAM_ORDER = (1, 2, 0)
REPLY = PLANE * 2
PARTS = ((0, 3), (3, 1))


def lists_of(meta, here):
    lane = lax.broadcasted_iota(jnp.int32, (ROWS, ROWS), 1)
    sub = lax.broadcasted_iota(jnp.int32, (ROWS, ROWS), 0)
    diag = lane == sub
    none = 1 << 20

    def column(row):
        return jnp.sum(jnp.where(diag, row, 0), axis=1, keepdims=True)

    members, keys, owners = [], [], []
    for h in range(2):
        entry = meta[h : h + 1]
        owner = entry >> 6
        key = (lane[:1] + h * ROWS) * SITES + (entry & (SITES - 1))
        owners.append(owner)
        keys.append(key)
        members.append(owner == sub)
    first = jnp.minimum(*[jnp.where(m, k, none) for m, k in zip(members, keys)])
    first = jnp.min(first, axis=1, keepdims=True)
    first = jnp.where(first >= none, 0, first)
    second = jnp.maximum(*[jnp.where(m, k, 0) for m, k in zip(members, keys)])
    second = jnp.max(second, axis=1, keepdims=True)
    targets = [[] for _ in ROUTES]
    for h in range(2):
        own = owners[h]
        at_first = jnp.sum(jnp.where(members[h], first, 0), axis=0, keepdims=True)
        place = jnp.where(keys[h] == at_first, 0, 1)
        at = {"x": (own >> 5) & 3, "z": (own >> 3) & 3, "y": (own >> 1) & 3}
        for c, (a, u, v) in enumerate(ROUTES):
            back = (at[v] - here[v]) & 3
            spot = jnp.where(back == 2, 3, jnp.where(back == 3, 2, back))
            slot = ((at[a] * CORES + (own & 1)) * PLANE + spot * LINE + ((at[u] - here[u]) & 3)) * 2 + place
            targets[c].append(jnp.where(own < 0, EMPTY, slot))
    coarse = meta[2:3]
    rank = jnp.sum(jnp.where(sub < lane, column(coarse), 0), axis=0, keepdims=True)
    fine_rank = jnp.minimum(lane[:1] - rank, FINE)
    fine_rank = jnp.where(coarse > 0, FINE, fine_rank)

    def numbers(hit):
        found = jnp.sum(jnp.where(hit, lane[: hit.shape[0]], 0), axis=1, keepdims=True)
        return jnp.broadcast_to(found, hit.shape)

    ids = numbers((rank == sub[:COARSE]) & (coarse > 0))
    fine_ids = numbers((fine_rank == sub[:FINE]) & (lane[:1] < SITES))
    rank = jnp.minimum(rank, COARSE - 1)
    return (first, second), targets, rank, ids, fine_ids, fine_rank


def ranks_wanted(blocks, table):
    lane = lax.broadcasted_iota(jnp.int32, (ROWS, ROWS), 1)
    sub = lax.broadcasted_iota(jnp.int32, (ROWS, ROWS), 0)
    found = jnp.sum(
        jnp.where(lane == (blocks & (SITES - 1)), table, 0), axis=1, keepdims=True
    )
    return jnp.sum(jnp.where(lane == sub, found, 0), axis=0, keepdims=True)


def smooth_kernel(
    tv, cx, cy, cz, sh, split, count, owner, local, sm_out, w_out,
    split_v, count_v, owner_v, local_v, meta, tgt, tgt_s, blk, rb0, rb1, rb2, part_sums,
    stage, coef, wa, wb, ka, kb, km, kp, fxs, fxr, fys, fyr,
    pair, lines, near, far, block_cols, idv, line_s, id_s, fine_s, spot_s, p00, p01, p02, p03, p10, p11, p12, p13, p20, p21, p22, p23, sb, fb,
    in_sem, coef_sem, out_sem, send_sem, recv_sem, pair_sem, table_sem, gather_sem,
    near_sem, cast_send, cast_recv, ans_send, ans_recv, hop_recv, fwd_send, own_sem, smem_sem, list_sem,
):
    cells = (split_v, count_v, owner_v, local_v)
    rb = (rb0, rb1, rb2)
    pg = ((p00, p01, p02, p03), (p10, p11, p12, p13), (p20, p21, p22, p23))
    i = lax.axis_index("gx")
    j = lax.axis_index("gy")
    core = lax.rem(j, CORES)
    at = {"x": i // LINE, "z": lax.rem(i, LINE), "y": j // CORES}
    peers = (
        (lax.rem(i + GX - 1, GX), j),
        (lax.rem(i + 1, GX), j),
        (i, lax.rem(j + GY - 1, GY)),
        (i, lax.rem(j + 1, GY)),
    )

    def device(axis, d, e):
        moved = dict(at)
        moved[axis] = lax.rem(at[axis] + d, LINE)
        return (moved["x"] * LINE + moved["z"], moved["y"] * CORES + lax.rem(core + e, CORES))

    def remote(src, dst, send, recv, peer):
        return pltpu.make_async_remote_copy(
            src_ref=src, dst_ref=dst, send_sem=send, recv_sem=recv,
            device_id=peer, device_id_type=MESH,
        )

    loads = []
    for c in range(CHUNKS):
        part = pl.ds(c * KV, KV)
        loads.append(pltpu.make_async_copy(tv.at[part], stage.at[part], in_sem.at[c]))
    loads[0].start()
    barrier = pltpu.get_barrier_semaphore()
    for peer in peers[:2]:
        pl.semaphore_signal(barrier, inc=1, device_id=peer, device_id_type=MESH)
    pl.semaphore_signal(barrier, inc=1, device_id=device("x", 0, 1), device_id_type=MESH)
    for axis in AXES:
        for d in range(1, LINE):
            for e in range(CORES):
                pl.semaphore_signal(
                    barrier, inc=1, device_id=device(axis, d, e), device_id_type=MESH
                )
    greeted = 3 + len(AXES) * (LINE - 1) * CORES
    for load in loads[1:]:
        load.start()
    coef_loads = []
    for n, part in enumerate((cx, cy, cz, sh)):
        load = pltpu.make_async_copy(part, coef.at[n], coef_sem.at[n])
        load.start()
        coef_loads.append(load)
    lists = []
    for n, part in enumerate((split, count, owner, local)):
        load = pltpu.make_async_copy(part, cells[n], list_sem.at[n])
        load.start()
        lists.append(load)

    keep = (
        (i > 0).astype(F32),
        (i < GX - 1).astype(F32),
        (j > 0).astype(F32),
        (j < GY - 1).astype(F32),
    )

    def drain(ref, sem):
        pltpu.make_async_copy(ref, ref, sem).wait()

    def copies(s, c):
        out = []
        for d in range(4):
            src, dst = (fxs, fxr) if d < 2 else (fys, fyr)
            out.append(
                remote(
                    src.at[s, c, d % 2], dst.at[s, c, 1 - d % 2],
                    send_sem.at[d // 2], recv_sem.at[s, c, d // 2], peers[d],
                )
            )
        return out

    def send_faces(s, c, w):
        for side in range(2):
            x = side * (NX - 1)
            fxs[s, c, side] = w[c, pl.ds(site_row(x, 0), NY * KV)].astype(BF16)
            y = side * (NY - 1)
            for x in range(NX):
                fys[s, c, side, pl.ds(x * KV, KV)] = w[c, pl.ds(site_row(x, y), KV)].astype(BF16)
        for copy in copies(s, c):
            copy.start()

    def fill_halo(s, c, w):
        drain(fxr.at[s, c], recv_sem.at[s, c, 0])
        drain(fyr.at[s, c], recv_sem.at[s, c, 1])
        for side in range(2):
            x = -1 if side == 0 else NX
            w[c, pl.ds(site_row(x, 0), NY * KV)] = fxr[s, c, side].astype(F32) * keep[side]
            y = -1 if side == 0 else NY
            for x in range(NX):
                w[c, pl.ds(site_row(x, y), KV)] = (
                    fyr[s, c, side, pl.ds(x * KV, KV)].astype(F32) * keep[2 + side]
                )

    def sweep(c, src, dst, last):
        def plane(x, carry):
            base = pl.multiple_of(x * XROW, 16)

            def cell(dx, y):
                return src[c, pl.ds(base + site_row(dx, y), KV)]

            below, here = cell(0, -1), cell(0, 0)
            for y in range(NY):
                above = cell(0, y + 1)
                row = slice(y, y + 1)
                new = (
                    ka[x, row] * (cell(-1, y) + cell(1, y))
                    + kb[x, row] * (below + above)
                    + km[x, row] * pltpu.roll(here, 1, 1)
                    + kp[x, row] * pltpu.roll(here, ROWS - 1, 1)
                    + (1.0 - OMEGA) * here
                )
                dst[c, pl.ds(base + site_row(0, y), KV)] = new
                if last:
                    blk[c, x * NY + y] = new.astype(BF16)
                below, here = here, above
            return carry

        lax.fori_loop(0, NX, plane, 0)

    def pair_copy():
        slot = pair.at[core]
        return remote(slot, slot, pair_sem.at[0], pair_sem.at[1], device("x", 0, 1))

    def line_copies():
        return [
            remote(
                pair, lines.at[n, at[axis]], table_sem.at[0], table_sem.at[1],
                device(axis, d, 0),
            )
            for n, axis in enumerate(AXES)
            for d in range(1, LINE)
        ]

    def gather_copies(step):
        send, recv = gather_sem.at[step, 0], gather_sem.at[step, 1]
        if step == 0:
            slot = near.at[at["y"] * CORES + core]
            return [
                remote(slot, slot, send, recv, device("y", d, e))
                for d in range(LINE)
                for e in range(CORES)
                if d or e
            ]
        slot = far.at[at["x"], at["z"]] if step == 1 else far.at[at["x"]]
        return [
            remote(slot, slot, send, recv, device("zx"[step - 1], d, 0)) for d in range(1, LINE)
        ]

    def gathered(step):
        if step == 0:
            return near.at[pl.ds(0, 7)]
        return far.at[0, pl.ds(0, 3)] if step == 1 else far.at[pl.ds(0, 3)]

    def gather_step(step):
        drain(gathered(step), gather_sem.at[step, 1])
        if step == 0:
            for n in range(LINE * CORES):
                far[at["x"], at["z"], n : n + 1] = near[n, 0:1]
        for copy in gather_copies(step + 1):
            copy.start()

    def ask():
        drain(gathered(2), gather_sem.at[2, 1])
        table = far[...].reshape(ROWS, ROWS)
        for p in range(2):
            pair[core, p] = ranks_wanted(block_cols[p], table)
        pair_copy().start()

    def ask_lines():
        pair_copy().wait_recv()
        for copy in line_copies():
            copy.start()
        for n, axis in enumerate(AXES):
            lines[n, at[axis]] = pair[...]

    steps = {
        (0, 1): lambda: gather_step(0),
        (1, 0): lambda: gather_step(1),
        (1, 2): ask,
        (2, 1): ask_lines,
    }

    def spread_copies(c):
        a, u, v = ROUTES[c]
        return [
            remote(
                pg[c][0].at[0], pg[c][0].at[LINE - d],
                near_sem.at[c, 0], near_sem.at[c, 1], device(u, d, 0),
            )
            for d in (2, 1, 3)
        ]

    def cast_copies(c):
        a, u, v = ROUTES[c]
        plan = (
            (0, 0, 1, 3, 1, 0, 0),
            (0, 0, 1, 1, 3, 1, 2),
            (0, 1, 1, 3, 1, 0, 0),
            (0, 2, 2, 1, 3, 1, 1),
            (0, 2, 2, 3, 1, 0, 2),
            (0, 1, 1, 1, 3, 1, 2),
            (3, 0, 2, 2, 1, 2, 3),
            (1, 2, 2, 2, 3, 2, 3),
        )
        return [
            remote(
                pg[c][src].at[pl.ds(first, size)], pg[c][dst].at[pl.ds(first, size)],
                cast_send.at[c, out], cast_recv.at[c, into], device(v, d, 0),
            )
            for src, first, size, dst, d, out, into in plan
        ]

    def piece(slot, part):
        first, count = PARTS[part]
        return pl.ds(slot * REPLY + first * SPOT, count * SPOT)

    def answer(c, part, d, e):
        a = ROUTES[c][0]
        slot = lax.rem(at[a] + d, LINE) * CORES + lax.rem(core + e, CORES)
        here = at[a] * CORES + core
        src = sb.at[c, piece(slot, part)]
        dst, peer = rb[c].at[piece(here, part)], device(a, d, e)
        if d == 0 and e == 0:
            return pltpu.make_async_copy(src, dst, own_sem.at[c, part])
        if d == 2 and part == 0:
            dst, peer = fb.at[c, e, piece(0, part)], device(a, 1 + 2 * e, 0)
            return remote(src, dst, ans_send.at[c, part], hop_recv.at[c, e], peer)
        return remote(src, dst, ans_send.at[c, part], ans_recv.at[c, part], peer)

    def forward(c, part, e):
        a = ROUTES[c][0]
        origin = lax.rem(at[a] + 3 - 2 * e, LINE) * CORES + core
        return remote(
            fb.at[c, e, piece(0, part)], rb[c].at[piece(origin, part)],
            fwd_send.at[c], ans_recv.at[c, part], device(a, 1 + 2 * e, e),
        )

    order = [(d, e) for d in (2, 1, 3, 0) for e in range(CORES)]

    def spread(c):
        a, u, v = ROUTES[c]
        for r in range(COARSE):
            pg[c][0][0, r] = blk[c, id_s[r, 0] & (SITES - 1)]
        for copy in spread_copies(c) + cast_copies(c)[:2]:
            copy.start()

    def cast(c):
        drain(pg[c][1].at[pl.ds(0, 3)], near_sem.at[c, 1])
        for copy in cast_copies(c)[2:6]:
            copy.start()

    def pass_on(c):
        for n in range(2):
            drain(pg[c][0].at[pl.ds(0, 2)], cast_recv.at[c, n])
            cast_copies(c)[6 + n].start()

    def pack(c, d, e, places):
        a, u, v = ROUTES[c]
        n = AXES.index(a)
        q, to = lax.rem(at[a] + d, LINE), lax.rem(core + e, CORES)
        slot = q * CORES + to
        for place in places:
            back = BACKS[place]
            tiles = []
            for ahead in range(LINE):
                whose = {
                    a: at[a],
                    u: lax.rem(at[u] + ahead, LINE),
                    v: lax.rem(at[v] + back, LINE),
                }
                owner = whose["x"] * 32 + whose["z"] * 8 + whose["y"] * 2 + core
                for p in range(2):
                    rank = line_s[n, q, to, p, 0, owner] & (COARSE - 1)
                    tiles.append(pg[c][back][ahead, rank])
            for t, tile in enumerate(tiles):
                sb[c, slot * REPLY + place * SPOT + t] = tile

    def pack_own(c):
        for d, e in order:
            pack(c, d, e, (0,))

    def reply(part):
        for n, group in enumerate(((2,), (1, 3), (0,))):
            for c in GRAM_ORDER:
                if n == 0:
                    drain(pg[c][0], cast_recv.at[c, 2 + part])
                for d in group:
                    for e in range(CORES):
                        pack(c, d, e, (3,) if part else (1, 2))
                        answer(c, part, d, e).start()
            if part == 0 and n == 1:
                for c in GRAM_ORDER:
                    reply_on(c, 0)

    def reply_on(c, part):
        for e in range(2):
            answer(c, part, 2, e).wait_recv()
            forward(c, part, e).start()

    def transpose_in(c):
        loads[c].wait()
        for x in range(NX):
            for half in range(NY // 8):
                for k in range(KV):
                    wa[c, pl.ds(site_row(x, half * 8) + k, 8, stride=KV), :] = stage[
                        c * KV + k, x, pl.ds(half * 8, 8), :
                    ]

    def products(c, place):
        b = fine_s[place, 0] & (SITES - 1)
        column = ((b >> 4) & 1) * (ROWS // 2) + (b & (NY - 1))
        values = []
        for t in range(SLOTS):
            found = tgt_s[2 * c + (b >> 5), column + t * NY]
            values.append(rb[c][found].astype(F32))
        values.append(blk[c, b].astype(F32))
        for n, (p, q) in enumerate(PAIRS):
            product = values[p] * values[q]
            product = product[0:8] + product[8:16]
            if c != GRAM_ORDER[0]:
                product = product + part_sums[n, place]
            part_sums[n, place] = product

    def add_products(c):
        def step(g, carry):
            for m in range(4):
                products(c, g * 4 + m)
            return carry

        lax.fori_loop(0, FINE // 4, step, 0)

    def finish():
        sub = lax.broadcasted_iota(jnp.int32, (8, ROWS), 0)
        low4, low2, low1 = sub < 4, (sub & 2) == 0, (sub & 1) == 0

        def merge(first, second, keep_first, shift):
            first = first + pltpu.roll(first, 8 - shift, 0)
            second = second + pltpu.roll(second, shift, 0)
            return jnp.where(keep_first, first, second)

        def group(g, carry):
            total = {}
            spots = [spot_s[0, g * 8 + m] & (SITES - 1) for m in range(8)]
            for n, couple in enumerate(PAIRS):
                rows = [part_sums[n, spot] for spot in spots]
                rows = [
                    jnp.where(low4, rows[m], rows[m + 4])
                    + pltpu.roll(jnp.where(low4, rows[m + 4], rows[m]), 4, 0)
                    for m in range(4)
                ]
                rows = [merge(rows[m], rows[m + 2], low2, 2) for m in range(2)]
                total[couple] = merge(rows[0], rows[1], low1, 1) * (1.0 / VECS)
                if couple[0] == couple[1]:
                    total[couple] = total[couple] + RIDGE
            out = solve_rows(total, [total[s, SLOTS] for s in range(SLOTS)])
            for s in range(SLOTS):
                w_out[s, pl.ds(pl.multiple_of(g * 8, 8), 8), :] = out[s]
            return carry

        lax.fori_loop(0, SITES // 8, group, 0)

    stores = []

    def transpose_out(c, w):
        for x in range(NX):
            for half in range(NY // 8):
                for k in range(KV):
                    stage[c * KV + k, x, pl.ds(half * 8, 8), :] = w[
                        c, pl.ds(site_row(x, half * 8) + k, 8, stride=KV), :
                    ]
        part = pl.ds(c * KV, KV)
        store = pltpu.make_async_copy(stage.at[part], sm_out.at[part], out_sem.at[c])
        store.start()
        stores.append(store)

    for c in range(CHUNKS):
        transpose_in(c)
        if c == 0:
            pl.semaphore_wait(barrier, greeted)
        send_faces(0, c, wa)

    for load in coef_loads:
        load.wait()
    ax, ay, az = coef[0], coef[1], coef[2]
    scale = OMEGA / (2.0 * (ax + ay + az) + coef[3])
    ka[...] = ax * scale
    kb[...] = ay * scale
    az = az * scale
    lane = lax.broadcasted_iota(jnp.int32, az.shape, 2)
    km[...] = jnp.where(lane == 0, 0.0, az)
    kp[...] = jnp.where(lane == ROWS - 1, 0.0, az)

    for load in lists:
        load.wait()
    meta[...] = jnp.zeros_like(meta)
    slots = lax.broadcasted_iota(jnp.int32, (SLOTS, NY), 0)
    for x in range(NX):
        live = (cells[0][x] == 0) & (slots < cells[1][x])
        listed = jnp.where(live, cells[2][x] * SITES + cells[3][x], -1)
        for t in range(SLOTS):
            where = pl.ds((x % 2) * (ROWS // 2) + t * NY, NY)
            meta[x // 2 : x // 2 + 1, where] = listed[t : t + 1]
        meta[2:3, pl.ds(x * NY, NY)] = cells[0][x]
    blocks, targets, rank, ids, fine_ids, fine_rank = lists_of(meta[...], at)
    near[at["y"] * CORES + core] = jnp.broadcast_to(rank, (8, ROWS))
    for copy in gather_copies(0):
        copy.start()
    for p in range(2):
        block_cols[p] = jnp.broadcast_to(blocks[p], (ROWS, ROWS))
    idv[:COARSE] = ids
    idv[COARSE : COARSE + FINE] = fine_ids
    idv[COARSE + FINE :] = jnp.broadcast_to(fine_rank, (8, ROWS))
    part_sums[:, FINE] = jnp.zeros((len(PAIRS), 8, ROWS), F32)
    id_copies = [
        pltpu.make_async_copy(idv.at[pl.ds(0, COARSE)], id_s, smem_sem.at[0]),
        pltpu.make_async_copy(idv.at[pl.ds(COARSE, FINE)], fine_s, smem_sem.at[2]),
        pltpu.make_async_copy(idv.at[pl.ds(COARSE + FINE, 8)], spot_s, smem_sem.at[4]),
    ]
    for copy in id_copies:
        copy.start()
    tgt[...] = jnp.zeros_like(tgt)
    for c in range(CHUNKS):
        for h in range(2):
            tgt[2 * c + h : 2 * c + h + 1] = targets[c][h]
        rb[c][EMPTY] = jnp.zeros((KV, ROWS), BF16)
    tgt_copy = pltpu.make_async_copy(tgt, tgt_s, smem_sem.at[3])
    tgt_copy.start()

    for s in range(SWEEPS):
        src, dst = (wb, wa) if s % 2 else (wa, wb)
        for c in range(CHUNKS):
            fill_halo(s, c, src)
            sweep(c, src, dst, s == SWEEPS - 1)
            if s < SWEEPS - 1:
                send_faces(s + 1, c, dst)
            else:
                if c == 0:
                    for copy in id_copies:
                        copy.wait()
                spread(c)
            if (s, c) in steps:
                steps[s, c]()
    drain(lines.at[:, pl.ds(0, 3)], table_sem.at[1])
    line_copy = pltpu.make_async_copy(lines, line_s, smem_sem.at[1])
    line_copy.start()
    cast(0)
    cast(1)
    cast(2)
    line_copy.wait()
    for c in range(CHUNKS):
        pack_own(c)
    for c in range(CHUNKS):
        pass_on(c)
    reply(0)
    reply(1)
    for c in range(CHUNKS):
        transpose_out(c, wb)
    tgt_copy.wait()
    for c in GRAM_ORDER:
        for part in range(len(PARTS)):
            answer(c, part, 0, 0).wait()
            drain(sb.at[c, pl.ds(0, 7 * PARTS[part][1] * SPOT)], ans_recv.at[c, part])
        add_products(c)
    finish()

    drain(fxs, send_sem.at[0])
    drain(fys, send_sem.at[1])
    pair_copy().wait_send()
    drain(lines.at[:, pl.ds(0, 3)], table_sem.at[0])
    for step in range(3):
        drain(gathered(step), gather_sem.at[step, 0])
    for c in range(CHUNKS):
        drain(pg[c][0].at[pl.ds(0, 3)], near_sem.at[c, 0])
        for n in range(3):
            drain(pg[c][0], cast_send.at[c, n])
        for part in range(len(PARTS)):
            count = PARTS[part][1]
            drain(sb.at[c, pl.ds(0, 7 * count * SPOT)], ans_send.at[c, part])
        drain(fb.at[c, :, pl.ds(0, PARTS[0][1] * SPOT)], fwd_send.at[c])
    for store in stores:
        store.wait()


def smooth(test_vectors, coef_x, coef_y, coef_z, shift, split, count, owner, local):
    vmem = pl.BlockSpec(memory_space=pltpu.VMEM)
    anywhere = pl.BlockSpec(memory_space=pl.ANY)
    cells = pltpu.VMEM((NX, NY, ROWS), F32)
    rows = pltpu.VMEM((LINE, COARSE, KV, ROWS), BF16)
    dma = pltpu.SemaphoreType.DMA
    return pl.pallas_call(
        smooth_kernel,
        out_shape=(
            jax.ShapeDtypeStruct((VECS, NX, NY, ROWS), F32),
            jax.ShapeDtypeStruct((SLOTS, SITES, ROWS), F32),
        ),
        in_specs=[anywhere] * 9,
        out_specs=(anywhere, vmem),
        scratch_shapes=[
            pltpu.VMEM((NX, 1, NY), jnp.int32),
            pltpu.VMEM((NX, 1, NY), jnp.int32),
            pltpu.VMEM((NX, SLOTS, NY), jnp.int32),
            pltpu.VMEM((NX, SLOTS, NY), jnp.int32),
            pltpu.VMEM((8, ROWS), jnp.int32),
            pltpu.VMEM((8, ROWS), jnp.int32),
            pltpu.SMEM((8, ROWS), jnp.int32),
            pltpu.VMEM((CHUNKS, SITES, KV, ROWS), BF16),
            *([pltpu.VMEM((EMPTY + 8, KV, ROWS), BF16)] * CHUNKS),
            pltpu.VMEM((len(PAIRS), SITES, 8, ROWS), F32),
            pltpu.VMEM((VECS, NX, NY, ROWS), F32),
            pltpu.VMEM((4, NX, NY, ROWS), F32),
            pltpu.VMEM((CHUNKS, EXT, ROWS), F32),
            pltpu.VMEM((CHUNKS, EXT, ROWS), F32),
            cells, cells, cells, cells,
            pltpu.VMEM((SWEEPS, CHUNKS, 2, NY * KV, ROWS), BF16),
            pltpu.VMEM((SWEEPS, CHUNKS, 2, NY * KV, ROWS), BF16),
            pltpu.VMEM((SWEEPS, CHUNKS, 2, NX * KV, ROWS), BF16),
            pltpu.VMEM((SWEEPS, CHUNKS, 2, NX * KV, ROWS), BF16),
            pltpu.VMEM((CORES, 2, 1, ROWS), jnp.int32),
            pltpu.VMEM((len(AXES), LINE, CORES, 2, 1, ROWS), jnp.int32),
            pltpu.VMEM((LINE * CORES, 8, ROWS), jnp.int32),
            pltpu.VMEM((LINE, LINE, LINE * CORES, ROWS), jnp.int32),
            pltpu.VMEM((2, ROWS, ROWS), jnp.int32),
            pltpu.VMEM((COARSE + FINE + 8, ROWS), jnp.int32),
            pltpu.SMEM((len(AXES), LINE, CORES, 2, 1, ROWS), jnp.int32),
            pltpu.SMEM((COARSE, ROWS), jnp.int32),
            pltpu.SMEM((FINE, ROWS), jnp.int32),
            pltpu.SMEM((8, ROWS), jnp.int32),
            *([rows] * (LINE * CHUNKS)),
            pltpu.VMEM((CHUNKS, EMPTY, KV, ROWS), BF16),
            pltpu.VMEM((CHUNKS, CORES, REPLY, KV, ROWS), BF16),
            dma((CHUNKS,)),
            dma((4,)),
            dma((CHUNKS,)),
            dma((2,)),
            dma((SWEEPS, CHUNKS, 2)),
            dma((2,)),
            dma((2,)),
            dma((3, 2)),
            dma((CHUNKS, 2)),
            dma((CHUNKS, 3)),
            dma((CHUNKS, 4)),
            dma((CHUNKS, len(PARTS))),
            dma((CHUNKS, len(PARTS))),
            dma((CHUNKS, CORES)),
            dma((CHUNKS,)),
            dma((CHUNKS, len(PARTS))),
            dma((5,)),
            dma((4,)),
        ],
        compiler_params=pltpu.CompilerParams(
            collective_id=0, has_side_effects=True, vmem_limit_bytes=60 * 1024 * 1024
        ),
        name="smooth",
    )(test_vectors, coef_x, coef_y, coef_z, shift, split, count, owner, local)


def pass_kernel(w_in, sm_in, w_out, sm_out, w_hold, sm_hold, in_sem, out_sem):
    parts = [(w_in, w_hold, w_out)]
    for c in range(CHUNKS):
        part = pl.ds(c * KV, KV)
        parts.append((sm_in.at[part], sm_hold.at[part], sm_out.at[part]))
    ins = [pltpu.make_async_copy(a, b, in_sem.at[n]) for n, (a, b, _) in enumerate(parts)]
    outs = [pltpu.make_async_copy(b, d, out_sem.at[n]) for n, (_, b, d) in enumerate(parts)]
    for copy in ins:
        copy.start()
    for load, store in zip(ins, outs):
        load.wait()
        store.start()
    for store in outs:
        store.wait()


def pass_on_results(weights, sm):
    anywhere = pl.BlockSpec(memory_space=pl.ANY)
    dma = pltpu.SemaphoreType.DMA
    return pl.pallas_call(
        pass_kernel,
        out_shape=(
            jax.ShapeDtypeStruct(weights.shape, F32),
            jax.ShapeDtypeStruct(sm.shape, F32),
        ),
        in_specs=[anywhere, anywhere],
        out_specs=(anywhere, anywhere),
        scratch_shapes=[
            pltpu.VMEM(weights.shape, F32),
            pltpu.VMEM(sm.shape, F32),
            dma((CHUNKS + 1,)),
            dma((CHUNKS + 1,)),
        ],
        compiler_params=pltpu.CompilerParams(vmem_limit_bytes=60 * 1024 * 1024),
        name="fit",
    )(weights, sm)


def per_device(
    test_vectors, coef_x, coef_y, coef_z, shift, cf_split, nbr_count, nbr_owner, nbr_block
):
    sm, weights = smooth(
        test_vectors, coef_x, coef_y, coef_z, shift,
        jnp.swapaxes(cf_split, 1, 2),
        jnp.swapaxes(nbr_count, 1, 2),
        jnp.transpose(nbr_owner, (0, 2, 3, 1)).reshape(NX, SLOTS, NY),
        jnp.transpose(nbr_block, (0, 2, 3, 1)).reshape(NX, SLOTS, NY),
    )
    weights, smoothed = pass_on_results(weights.reshape(SLOTS, NX, NY, ROWS), sm)
    return (smoothed, weights)


def solution(mesh):
    cells = P("gx", "gy", None)
    lists = P("gx", "gy", None, None)
    vectors = P(None, "gx", "gy", None)
    return jax.shard_map(
        per_device,
        mesh=mesh,
        in_specs=(vectors, cells, cells, cells, cells, cells, cells, lists, lists),
        out_specs=(vectors, vectors),
        check_vma=False,
    )
```

```python
import jax
import jax.numpy as jnp
from jax import lax
from jax.experimental import pallas as pl
from jax.experimental.pallas import tpu as pltpu
from jax.sharding import PartitionSpec as P

SLOTS = 4
SWEEPS = 3
ROWS = 128
OMEGA = 0.8
RIDGE = 0.05
VECS = 48
CHUNKS = 3
KV = VECS // CHUNKS
NX = 4
NY = 16
SITES = NX * NY
XROW = (NY + 2) * KV
EXT = (NX + 2) * XROW
GX = 16
GY = 8
MESH = pl.DeviceIdType.MESH
F32 = jnp.float32
BF16 = jnp.bfloat16


def site_row(x, y):
    return (x + 1) * XROW + (y + 1) * KV


def solve_rows(gram, rhs):
    low = [[None] * SLOTS for _ in range(SLOTS)]
    inv = []
    for r in range(SLOTS):
        scaled = []
        diag = gram[r, r]
        for c in range(r):
            rest = gram[r, c]
            for m in range(c):
                rest = rest - scaled[m] * low[c][m]
            scaled.append(rest)
            low[r][c] = rest * inv[c]
            diag = diag - rest * low[r][c]
        inv.append(1.0 / diag)
    fwd = []
    for r in range(SLOTS):
        rest = rhs[r]
        for m in range(r):
            rest = rest - low[r][m] * fwd[m]
        fwd.append(rest)
    out = [None] * SLOTS
    for r in reversed(range(SLOTS)):
        rest = fwd[r] * inv[r]
        for m in range(r + 1, SLOTS):
            rest = rest - low[m][r] * out[m]
        out[r] = rest
    return out


PAIRS = [(s, t) for s in range(SLOTS) for t in range(s + 1)] + [(s, SLOTS) for s in range(SLOTS)]
AXES = "xyz"
LINE = 4
CORES = 2
COARSE = 16
FINE = 48
PLANE = LINE * LINE
ROUTES = (("x", "z", "y"), ("y", "x", "z"), ("z", "y", "x"))
BACKS = (0, 1, 3, 2)
EMPTY = LINE * CORES * PLANE * 2
SPOT = 2 * LINE
GRAM_ORDER = (1, 2, 0)
REPLY = PLANE * 2
PARTS = ((0, 3), (3, 1))


def lists_of(meta, here):
    lane = lax.broadcasted_iota(jnp.int32, (ROWS, ROWS), 1)
    sub = lax.broadcasted_iota(jnp.int32, (ROWS, ROWS), 0)
    diag = lane == sub
    none = 1 << 20

    def column(row):
        return jnp.sum(jnp.where(diag, row, 0), axis=1, keepdims=True)

    members, keys, owners = [], [], []
    for h in range(2):
        entry = meta[h : h + 1]
        owner = entry >> 6
        key = (lane[:1] + h * ROWS) * SITES + (entry & (SITES - 1))
        owners.append(owner)
        keys.append(key)
        members.append(owner == sub)
    first = jnp.minimum(*[jnp.where(m, k, none) for m, k in zip(members, keys)])
    first = jnp.min(first, axis=1, keepdims=True)
    first = jnp.where(first >= none, 0, first)
    second = jnp.maximum(*[jnp.where(m, k, 0) for m, k in zip(members, keys)])
    second = jnp.max(second, axis=1, keepdims=True)
    targets = [[] for _ in ROUTES]
    for h in range(2):
        own = owners[h]
        at_first = jnp.sum(jnp.where(members[h], first, 0), axis=0, keepdims=True)
        place = jnp.where(keys[h] == at_first, 0, 1)
        at = {"x": (own >> 5) & 3, "z": (own >> 3) & 3, "y": (own >> 1) & 3}
        for c, (a, u, v) in enumerate(ROUTES):
            back = (at[v] - here[v]) & 3
            spot = jnp.where(back == 2, 3, jnp.where(back == 3, 2, back))
            slot = ((at[a] * CORES + (own & 1)) * PLANE + spot * LINE + ((at[u] - here[u]) & 3)) * 2 + place
            targets[c].append(jnp.where(own < 0, EMPTY, slot))
    coarse = meta[2:3]
    rank = jnp.sum(jnp.where(sub < lane, column(coarse), 0), axis=0, keepdims=True)
    fine_rank = jnp.minimum(lane[:1] - rank, FINE)
    fine_rank = jnp.where(coarse > 0, FINE, fine_rank)

    def numbers(hit):
        found = jnp.sum(jnp.where(hit, lane[: hit.shape[0]], 0), axis=1, keepdims=True)
        return jnp.broadcast_to(found, hit.shape)

    ids = numbers((rank == sub[:COARSE]) & (coarse > 0))
    fine_ids = numbers((fine_rank == sub[:FINE]) & (lane[:1] < SITES))
    rank = jnp.minimum(rank, COARSE - 1)
    return (first, second), targets, rank, ids, fine_ids, fine_rank


def ranks_wanted(blocks, table):
    lane = lax.broadcasted_iota(jnp.int32, (ROWS, ROWS), 1)
    sub = lax.broadcasted_iota(jnp.int32, (ROWS, ROWS), 0)
    found = jnp.sum(
        jnp.where(lane == (blocks & (SITES - 1)), table, 0), axis=1, keepdims=True
    )
    return jnp.sum(jnp.where(lane == sub, found, 0), axis=0, keepdims=True)


def smooth_kernel(
    tv, cx, cy, cz, sh, split, count, owner, local, sm_out, w_out,
    split_v, count_v, owner_v, local_v, meta, tgt, tgt_s, blk, rb0, rb1, rb2, part_sums,
    stage, coef, wa, wb, ka, kb, km, kp, fxs, fxr, fys, fyr,
    pair, lines, near, far, block_cols, idv, line_s, id_s, fine_s, spot_s, p00, p01, p02, p03, p10, p11, p12, p13, p20, p21, p22, p23, sb, fb,
    in_sem, coef_sem, out_sem, send_sem, recv_sem, pair_sem, table_sem, gather_sem,
    near_sem, cast_send, cast_recv, ans_send, ans_recv, hop_recv, fwd_send, own_sem, smem_sem, list_sem,
):
    cells = (split_v, count_v, owner_v, local_v)
    rb = (rb0, rb1, rb2)
    pg = ((p00, p01, p02, p03), (p10, p11, p12, p13), (p20, p21, p22, p23))
    i = lax.axis_index("gx")
    j = lax.axis_index("gy")
    core = lax.rem(j, CORES)
    at = {"x": i // LINE, "z": lax.rem(i, LINE), "y": j // CORES}
    peers = (
        (lax.rem(i + GX - 1, GX), j),
        (lax.rem(i + 1, GX), j),
        (i, lax.rem(j + GY - 1, GY)),
        (i, lax.rem(j + 1, GY)),
    )

    def device(axis, d, e):
        moved = dict(at)
        moved[axis] = lax.rem(at[axis] + d, LINE)
        return (moved["x"] * LINE + moved["z"], moved["y"] * CORES + lax.rem(core + e, CORES))

    def remote(src, dst, send, recv, peer):
        return pltpu.make_async_remote_copy(
            src_ref=src, dst_ref=dst, send_sem=send, recv_sem=recv,
            device_id=peer, device_id_type=MESH,
        )

    loads = []
    for c in range(CHUNKS):
        part = pl.ds(c * KV, KV)
        loads.append(pltpu.make_async_copy(tv.at[part], stage.at[part], in_sem.at[c]))
    loads[0].start()
    barrier = pltpu.get_barrier_semaphore()
    for peer in peers[:2]:
        pl.semaphore_signal(barrier, inc=1, device_id=peer, device_id_type=MESH)
    pl.semaphore_signal(barrier, inc=1, device_id=device("x", 0, 1), device_id_type=MESH)
    for axis in AXES:
        for d in range(1, LINE):
            for e in range(CORES):
                pl.semaphore_signal(
                    barrier, inc=1, device_id=device(axis, d, e), device_id_type=MESH
                )
    greeted = 3 + len(AXES) * (LINE - 1) * CORES
    for load in loads[1:]:
        load.start()
    coef_loads = []
    for n, part in enumerate((cx, cy, cz, sh)):
        load = pltpu.make_async_copy(part, coef.at[n], coef_sem.at[n])
        load.start()
        coef_loads.append(load)
    lists = []
    for n, part in enumerate((split, count, owner, local)):
        load = pltpu.make_async_copy(part, cells[n], list_sem.at[n])
        load.start()
        lists.append(load)

    keep = (
        (i > 0).astype(F32),
        (i < GX - 1).astype(F32),
        (j > 0).astype(F32),
        (j < GY - 1).astype(F32),
    )

    def drain(ref, sem):
        pltpu.make_async_copy(ref, ref, sem).wait()

    def copies(s, c):
        out = []
        for d in range(4):
            src, dst = (fxs, fxr) if d < 2 else (fys, fyr)
            out.append(
                remote(
                    src.at[s, c, d % 2], dst.at[s, c, 1 - d % 2],
                    send_sem.at[d // 2], recv_sem.at[s, c, d // 2], peers[d],
                )
            )
        return out

    def send_faces(s, c, w):
        for side in range(2):
            x = side * (NX - 1)
            fxs[s, c, side] = w[c, pl.ds(site_row(x, 0), NY * KV)].astype(BF16)
            y = side * (NY - 1)
            for x in range(NX):
                fys[s, c, side, pl.ds(x * KV, KV)] = w[c, pl.ds(site_row(x, y), KV)].astype(BF16)
        for copy in copies(s, c):
            copy.start()

    def fill_halo(s, c, w):
        drain(fxr.at[s, c], recv_sem.at[s, c, 0])
        drain(fyr.at[s, c], recv_sem.at[s, c, 1])
        for side in range(2):
            x = -1 if side == 0 else NX
            w[c, pl.ds(site_row(x, 0), NY * KV)] = fxr[s, c, side].astype(F32) * keep[side]
            y = -1 if side == 0 else NY
            for x in range(NX):
                w[c, pl.ds(site_row(x, y), KV)] = (
                    fyr[s, c, side, pl.ds(x * KV, KV)].astype(F32) * keep[2 + side]
                )

    def sweep(c, src, dst, last):
        def plane(x, carry):
            base = pl.multiple_of(x * XROW, 16)

            def cell(dx, y):
                return src[c, pl.ds(base + site_row(dx, y), KV)]

            below, here = cell(0, -1), cell(0, 0)
            for y in range(NY):
                above = cell(0, y + 1)
                row = slice(y, y + 1)
                new = (
                    ka[x, row] * (cell(-1, y) + cell(1, y))
                    + kb[x, row] * (below + above)
                    + km[x, row] * pltpu.roll(here, 1, 1)
                    + kp[x, row] * pltpu.roll(here, ROWS - 1, 1)
                    + (1.0 - OMEGA) * here
                )
                dst[c, pl.ds(base + site_row(0, y), KV)] = new
                if last:
                    blk[c, x * NY + y] = new.astype(BF16)
                below, here = here, above
            return carry

        lax.fori_loop(0, NX, plane, 0)

    def pair_copy():
        slot = pair.at[core]
        return remote(slot, slot, pair_sem.at[0], pair_sem.at[1], device("x", 0, 1))

    def line_copies():
        return [
            remote(
                pair, lines.at[n, at[axis]], table_sem.at[0], table_sem.at[1],
                device(axis, d, 0),
            )
            for n, axis in enumerate(AXES)
            for d in range(1, LINE)
        ]

    def gather_copies(step):
        send, recv = gather_sem.at[step, 0], gather_sem.at[step, 1]
        if step == 0:
            slot = near.at[at["y"] * CORES + core]
            return [
                remote(slot, slot, send, recv, device("y", d, e))
                for d in range(LINE)
                for e in range(CORES)
                if d or e
            ]
        slot = far.at[at["x"], at["z"]] if step == 1 else far.at[at["x"]]
        return [
            remote(slot, slot, send, recv, device("zx"[step - 1], d, 0)) for d in range(1, LINE)
        ]

    def gathered(step):
        if step == 0:
            return near.at[pl.ds(0, 7)]
        return far.at[0, pl.ds(0, 3)] if step == 1 else far.at[pl.ds(0, 3)]

    def gather_step(step):
        drain(gathered(step), gather_sem.at[step, 1])
        if step == 0:
            for n in range(LINE * CORES):
                far[at["x"], at["z"], n : n + 1] = near[n, 0:1]
        for copy in gather_copies(step + 1):
            copy.start()

    def ask():
        drain(gathered(2), gather_sem.at[2, 1])
        table = far[...].reshape(ROWS, ROWS)
        for p in range(2):
            pair[core, p] = ranks_wanted(block_cols[p], table)
        pair_copy().start()

    def ask_lines():
        pair_copy().wait_recv()
        for copy in line_copies():
            copy.start()
        for n, axis in enumerate(AXES):
            lines[n, at[axis]] = pair[...]

    steps = {
        (0, 1): lambda: gather_step(0),
        (1, 0): lambda: gather_step(1),
        (1, 2): ask,
        (2, 1): ask_lines,
    }

    def spread_copies(c):
        a, u, v = ROUTES[c]
        return [
            remote(
                pg[c][0].at[0], pg[c][0].at[LINE - d],
                near_sem.at[c, 2], near_sem.at[c, into], device(u, d, 0),
            )
            for d, into in ((1, 0), (3, 0), (2, 1))
        ]

    def cast_copies(c):
        a, u, v = ROUTES[c]
        plan = (
            (0, 0, 1, 3, 1, 0, 0),
            (0, 0, 1, 1, 3, 1, 2),
            (0, 1, 1, 3, 1, 0, 0),
            (0, 3, 1, 1, 3, 1, 1),
            (0, 3, 1, 3, 1, 0, 2),
            (0, 1, 1, 1, 3, 1, 2),
            (0, 2, 1, 1, 3, 1, 1),
            (0, 2, 1, 3, 1, 0, 2),
            (3, 0, 2, 2, 1, 2, 3),
            (1, 2, 2, 2, 3, 2, 3),
        )
        return [
            remote(
                pg[c][src].at[pl.ds(first, size)], pg[c][dst].at[pl.ds(first, size)],
                cast_send.at[c, out], cast_recv.at[c, into], device(v, d, 0),
            )
            for src, first, size, dst, d, out, into in plan
        ]

    def piece(slot, part):
        first, count = PARTS[part]
        return pl.ds(slot * REPLY + first * SPOT, count * SPOT)

    def answer(c, part, d, e):
        a = ROUTES[c][0]
        slot = lax.rem(at[a] + d, LINE) * CORES + lax.rem(core + e, CORES)
        here = at[a] * CORES + core
        src = sb.at[c, piece(slot, part)]
        dst, peer = rb[c].at[piece(here, part)], device(a, d, e)
        if d == 0 and e == 0:
            return pltpu.make_async_copy(src, dst, own_sem.at[c, part])
        if d == 2 and part == 0:
            dst, peer = fb.at[c, e, piece(0, part)], device(a, 1 + 2 * e, 0)
            return remote(src, dst, ans_send.at[c, part], hop_recv.at[c, e], peer)
        return remote(src, dst, ans_send.at[c, part], ans_recv.at[c, part], peer)

    def forward(c, part, e):
        a = ROUTES[c][0]
        origin = lax.rem(at[a] + 3 - 2 * e, LINE) * CORES + core
        return remote(
            fb.at[c, e, piece(0, part)], rb[c].at[piece(origin, part)],
            fwd_send.at[c], ans_recv.at[c, part], device(a, 1 + 2 * e, e),
        )

    order = [(d, e) for d in (2, 1, 3, 0) for e in range(CORES)]

    def spread(c):
        a, u, v = ROUTES[c]
        for r in range(COARSE):
            pg[c][0][0, r] = blk[c, id_s[r, 0] & (SITES - 1)]
        for copy in spread_copies(c) + cast_copies(c)[:2]:
            copy.start()

    def cast(c, late):
        drain(pg[c][0].at[pl.ds(0, 2 - late)], near_sem.at[c, late])
        for copy in cast_copies(c)[6:8] if late else cast_copies(c)[2:6]:
            copy.start()

    def pass_on(c, n):
        drain(pg[c][0].at[pl.ds(0, 2)], cast_recv.at[c, n])
        cast_copies(c)[8 + n].start()

    def pack(c, d, e, places):
        a, u, v = ROUTES[c]
        n = AXES.index(a)
        q, to = lax.rem(at[a] + d, LINE), lax.rem(core + e, CORES)
        slot = q * CORES + to
        for place in places:
            back = BACKS[place]
            tiles = []
            for ahead in range(LINE):
                whose = {
                    a: at[a],
                    u: lax.rem(at[u] + ahead, LINE),
                    v: lax.rem(at[v] + back, LINE),
                }
                owner = whose["x"] * 32 + whose["z"] * 8 + whose["y"] * 2 + core
                for p in range(2):
                    rank = line_s[n, q, to, p, 0, owner] & (COARSE - 1)
                    tiles.append(pg[c][back][ahead, rank])
            for t, tile in enumerate(tiles):
                sb[c, slot * REPLY + place * SPOT + t] = tile

    def pack_own(c):
        for d, e in order:
            pack(c, d, e, (0,))

    def reply(part):
        for n, group in enumerate(((2,), (1, 3), (0,))):
            for c in GRAM_ORDER:
                if n == 0:
                    drain(pg[c][0], cast_recv.at[c, 2 + part])
                for d in group:
                    for e in range(CORES):
                        pack(c, d, e, (3,) if part else (1, 2))
                        answer(c, part, d, e).start()
            if part == 0 and n == 1:
                for c in GRAM_ORDER:
                    reply_on(c, 0)

    def reply_on(c, part):
        for e in range(2):
            answer(c, part, 2, e).wait_recv()
            forward(c, part, e).start()

    def transpose_in(c):
        loads[c].wait()
        for x in range(NX):
            for half in range(NY // 8):
                for k in range(KV):
                    wa[c, pl.ds(site_row(x, half * 8) + k, 8, stride=KV), :] = stage[
                        c * KV + k, x, pl.ds(half * 8, 8), :
                    ]

    def products(c, place):
        b = fine_s[place, 0] & (SITES - 1)
        column = ((b >> 4) & 1) * (ROWS // 2) + (b & (NY - 1))
        values = []
        for t in range(SLOTS):
            found = tgt_s[2 * c + (b >> 5), column + t * NY]
            values.append(rb[c][found].astype(F32))
        values.append(blk[c, b].astype(F32))
        for n, (p, q) in enumerate(PAIRS):
            product = values[p] * values[q]
            product = product[0:8] + product[8:16]
            if c != GRAM_ORDER[0]:
                product = product + part_sums[n, place]
            part_sums[n, place] = product

    def add_products(c):
        def step(g, carry):
            for m in range(4):
                products(c, g * 4 + m)
            return carry

        lax.fori_loop(0, FINE // 4, step, 0)

    def finish():
        sub = lax.broadcasted_iota(jnp.int32, (8, ROWS), 0)
        low4, low2, low1 = sub < 4, (sub & 2) == 0, (sub & 1) == 0

        def merge(first, second, keep_first, shift):
            first = first + pltpu.roll(first, 8 - shift, 0)
            second = second + pltpu.roll(second, shift, 0)
            return jnp.where(keep_first, first, second)

        def group(g, carry):
            total = {}
            spots = [spot_s[0, g * 8 + m] & (SITES - 1) for m in range(8)]
            for n, couple in enumerate(PAIRS):
                rows = [part_sums[n, spot] for spot in spots]
                rows = [
                    jnp.where(low4, rows[m], rows[m + 4])
                    + pltpu.roll(jnp.where(low4, rows[m + 4], rows[m]), 4, 0)
                    for m in range(4)
                ]
                rows = [merge(rows[m], rows[m + 2], low2, 2) for m in range(2)]
                total[couple] = merge(rows[0], rows[1], low1, 1) * (1.0 / VECS)
                if couple[0] == couple[1]:
                    total[couple] = total[couple] + RIDGE
            out = solve_rows(total, [total[s, SLOTS] for s in range(SLOTS)])
            for s in range(SLOTS):
                w_out[s, pl.ds(pl.multiple_of(g * 8, 8), 8), :] = out[s]
            return carry

        lax.fori_loop(0, SITES // 8, group, 0)

    stores = []

    def transpose_out(c, w):
        for x in range(NX):
            for half in range(NY // 8):
                for k in range(KV):
                    stage[c * KV + k, x, pl.ds(half * 8, 8), :] = w[
                        c, pl.ds(site_row(x, half * 8) + k, 8, stride=KV), :
                    ]
        part = pl.ds(c * KV, KV)
        store = pltpu.make_async_copy(stage.at[part], sm_out.at[part], out_sem.at[c])
        store.start()
        stores.append(store)

    for c in range(CHUNKS):
        transpose_in(c)
        if c == 0:
            pl.semaphore_wait(barrier, greeted)
        send_faces(0, c, wa)

    for load in coef_loads:
        load.wait()
    ax, ay, az = coef[0], coef[1], coef[2]
    scale = OMEGA / (2.0 * (ax + ay + az) + coef[3])
    ka[...] = ax * scale
    kb[...] = ay * scale
    az = az * scale
    lane = lax.broadcasted_iota(jnp.int32, az.shape, 2)
    km[...] = jnp.where(lane == 0, 0.0, az)
    kp[...] = jnp.where(lane == ROWS - 1, 0.0, az)

    for load in lists:
        load.wait()
    meta[...] = jnp.zeros_like(meta)
    slots = lax.broadcasted_iota(jnp.int32, (SLOTS, NY), 0)
    for x in range(NX):
        live = (cells[0][x] == 0) & (slots < cells[1][x])
        listed = jnp.where(live, cells[2][x] * SITES + cells[3][x], -1)
        for t in range(SLOTS):
            where = pl.ds((x % 2) * (ROWS // 2) + t * NY, NY)
            meta[x // 2 : x // 2 + 1, where] = listed[t : t + 1]
        meta[2:3, pl.ds(x * NY, NY)] = cells[0][x]
    blocks, targets, rank, ids, fine_ids, fine_rank = lists_of(meta[...], at)
    near[at["y"] * CORES + core] = jnp.broadcast_to(rank, (8, ROWS))
    for copy in gather_copies(0):
        copy.start()
    for p in range(2):
        block_cols[p] = jnp.broadcast_to(blocks[p], (ROWS, ROWS))
    idv[:COARSE] = ids
    idv[COARSE : COARSE + FINE] = fine_ids
    idv[COARSE + FINE :] = jnp.broadcast_to(fine_rank, (8, ROWS))
    part_sums[:, FINE] = jnp.zeros((len(PAIRS), 8, ROWS), F32)
    id_copies = [
        pltpu.make_async_copy(idv.at[pl.ds(0, COARSE)], id_s, smem_sem.at[0]),
        pltpu.make_async_copy(idv.at[pl.ds(COARSE, FINE)], fine_s, smem_sem.at[2]),
        pltpu.make_async_copy(idv.at[pl.ds(COARSE + FINE, 8)], spot_s, smem_sem.at[4]),
    ]
    for copy in id_copies:
        copy.start()
    tgt[...] = jnp.zeros_like(tgt)
    for c in range(CHUNKS):
        for h in range(2):
            tgt[2 * c + h : 2 * c + h + 1] = targets[c][h]
        rb[c][EMPTY] = jnp.zeros((KV, ROWS), BF16)
    tgt_copy = pltpu.make_async_copy(tgt, tgt_s, smem_sem.at[3])
    tgt_copy.start()

    for s in range(SWEEPS):
        src, dst = (wb, wa) if s % 2 else (wa, wb)
        for c in range(CHUNKS):
            fill_halo(s, c, src)
            sweep(c, src, dst, s == SWEEPS - 1)
            if s < SWEEPS - 1:
                send_faces(s + 1, c, dst)
            else:
                if c == 0:
                    for copy in id_copies:
                        copy.wait()
                spread(c)
            if (s, c) in steps:
                steps[s, c]()
    drain(lines.at[:, pl.ds(0, 3)], table_sem.at[1])
    line_copy = pltpu.make_async_copy(lines, line_s, smem_sem.at[1])
    line_copy.start()
    cast(0, 0)
    cast(1, 0)
    cast(0, 1)
    cast(2, 0)
    pass_on(0, 0)
    cast(1, 1)
    pass_on(1, 0)
    cast(2, 1)
    line_copy.wait()
    pack_own(0)
    pass_on(0, 1)
    pass_on(2, 0)
    pack_own(1)
    pass_on(1, 1)
    pack_own(2)
    pass_on(2, 1)
    reply(0)
    reply(1)
    for c in range(CHUNKS):
        transpose_out(c, wb)
    tgt_copy.wait()
    for c in GRAM_ORDER:
        for part in range(len(PARTS)):
            answer(c, part, 0, 0).wait()
            drain(sb.at[c, pl.ds(0, 7 * PARTS[part][1] * SPOT)], ans_recv.at[c, part])
        add_products(c)
    finish()

    drain(fxs, send_sem.at[0])
    drain(fys, send_sem.at[1])
    pair_copy().wait_send()
    drain(lines.at[:, pl.ds(0, 3)], table_sem.at[0])
    for step in range(3):
        drain(gathered(step), gather_sem.at[step, 0])
    for c in range(CHUNKS):
        drain(pg[c][0].at[pl.ds(0, 3)], near_sem.at[c, 2])
        for n in range(3):
            drain(pg[c][0], cast_send.at[c, n])
        for part in range(len(PARTS)):
            count = PARTS[part][1]
            drain(sb.at[c, pl.ds(0, 7 * count * SPOT)], ans_send.at[c, part])
        drain(fb.at[c, :, pl.ds(0, PARTS[0][1] * SPOT)], fwd_send.at[c])
    for store in stores:
        store.wait()


def smooth(test_vectors, coef_x, coef_y, coef_z, shift, split, count, owner, local):
    vmem = pl.BlockSpec(memory_space=pltpu.VMEM)
    anywhere = pl.BlockSpec(memory_space=pl.ANY)
    cells = pltpu.VMEM((NX, NY, ROWS), F32)
    rows = pltpu.VMEM((LINE, COARSE, KV, ROWS), BF16)
    dma = pltpu.SemaphoreType.DMA
    return pl.pallas_call(
        smooth_kernel,
        out_shape=(
            jax.ShapeDtypeStruct((VECS, NX, NY, ROWS), F32),
            jax.ShapeDtypeStruct((SLOTS, SITES, ROWS), F32),
        ),
        in_specs=[anywhere] * 9,
        out_specs=(anywhere, vmem),
        scratch_shapes=[
            pltpu.VMEM((NX, 1, NY), jnp.int32),
            pltpu.VMEM((NX, 1, NY), jnp.int32),
            pltpu.VMEM((NX, SLOTS, NY), jnp.int32),
            pltpu.VMEM((NX, SLOTS, NY), jnp.int32),
            pltpu.VMEM((8, ROWS), jnp.int32),
            pltpu.VMEM((8, ROWS), jnp.int32),
            pltpu.SMEM((8, ROWS), jnp.int32),
            pltpu.VMEM((CHUNKS, SITES, KV, ROWS), BF16),
            *([pltpu.VMEM((EMPTY + 8, KV, ROWS), BF16)] * CHUNKS),
            pltpu.VMEM((len(PAIRS), SITES, 8, ROWS), F32),
            pltpu.VMEM((VECS, NX, NY, ROWS), F32),
            pltpu.VMEM((4, NX, NY, ROWS), F32),
            pltpu.VMEM((CHUNKS, EXT, ROWS), F32),
            pltpu.VMEM((CHUNKS, EXT, ROWS), F32),
            cells, cells, cells, cells,
            pltpu.VMEM((SWEEPS, CHUNKS, 2, NY * KV, ROWS), BF16),
            pltpu.VMEM((SWEEPS, CHUNKS, 2, NY * KV, ROWS), BF16),
            pltpu.VMEM((SWEEPS, CHUNKS, 2, NX * KV, ROWS), BF16),
            pltpu.VMEM((SWEEPS, CHUNKS, 2, NX * KV, ROWS), BF16),
            pltpu.VMEM((CORES, 2, 1, ROWS), jnp.int32),
            pltpu.VMEM((len(AXES), LINE, CORES, 2, 1, ROWS), jnp.int32),
            pltpu.VMEM((LINE * CORES, 8, ROWS), jnp.int32),
            pltpu.VMEM((LINE, LINE, LINE * CORES, ROWS), jnp.int32),
            pltpu.VMEM((2, ROWS, ROWS), jnp.int32),
            pltpu.VMEM((COARSE + FINE + 8, ROWS), jnp.int32),
            pltpu.SMEM((len(AXES), LINE, CORES, 2, 1, ROWS), jnp.int32),
            pltpu.SMEM((COARSE, ROWS), jnp.int32),
            pltpu.SMEM((FINE, ROWS), jnp.int32),
            pltpu.SMEM((8, ROWS), jnp.int32),
            *([rows] * (LINE * CHUNKS)),
            pltpu.VMEM((CHUNKS, EMPTY, KV, ROWS), BF16),
            pltpu.VMEM((CHUNKS, CORES, REPLY, KV, ROWS), BF16),
            dma((CHUNKS,)),
            dma((4,)),
            dma((CHUNKS,)),
            dma((2,)),
            dma((SWEEPS, CHUNKS, 2)),
            dma((2,)),
            dma((2,)),
            dma((3, 2)),
            dma((CHUNKS, 3)),
            dma((CHUNKS, 3)),
            dma((CHUNKS, 4)),
            dma((CHUNKS, len(PARTS))),
            dma((CHUNKS, len(PARTS))),
            dma((CHUNKS, CORES)),
            dma((CHUNKS,)),
            dma((CHUNKS, len(PARTS))),
            dma((5,)),
            dma((4,)),
        ],
        compiler_params=pltpu.CompilerParams(
            collective_id=0, has_side_effects=True, vmem_limit_bytes=60 * 1024 * 1024
        ),
        name="smooth",
    )(test_vectors, coef_x, coef_y, coef_z, shift, split, count, owner, local)


def pass_kernel(w_in, sm_in, w_out, sm_out, w_hold, sm_hold, in_sem, out_sem):
    parts = [(w_in, w_hold, w_out)]
    for c in range(CHUNKS):
        part = pl.ds(c * KV, KV)
        parts.append((sm_in.at[part], sm_hold.at[part], sm_out.at[part]))
    ins = [pltpu.make_async_copy(a, b, in_sem.at[n]) for n, (a, b, _) in enumerate(parts)]
    outs = [pltpu.make_async_copy(b, d, out_sem.at[n]) for n, (_, b, d) in enumerate(parts)]
    for copy in ins:
        copy.start()
    for load, store in zip(ins, outs):
        load.wait()
        store.start()
    for store in outs:
        store.wait()


def pass_on_results(weights, sm):
    anywhere = pl.BlockSpec(memory_space=pl.ANY)
    dma = pltpu.SemaphoreType.DMA
    return pl.pallas_call(
        pass_kernel,
        out_shape=(
            jax.ShapeDtypeStruct(weights.shape, F32),
            jax.ShapeDtypeStruct(sm.shape, F32),
        ),
        in_specs=[anywhere, anywhere],
        out_specs=(anywhere, anywhere),
        scratch_shapes=[
            pltpu.VMEM(weights.shape, F32),
            pltpu.VMEM(sm.shape, F32),
            dma((CHUNKS + 1,)),
            dma((CHUNKS + 1,)),
        ],
        compiler_params=pltpu.CompilerParams(vmem_limit_bytes=60 * 1024 * 1024),
        name="fit",
    )(weights, sm)


def per_device(
    test_vectors, coef_x, coef_y, coef_z, shift, cf_split, nbr_count, nbr_owner, nbr_block
):
    sm, weights = smooth(
        test_vectors, coef_x, coef_y, coef_z, shift,
        jnp.swapaxes(cf_split, 1, 2),
        jnp.swapaxes(nbr_count, 1, 2),
        jnp.transpose(nbr_owner, (0, 2, 3, 1)).reshape(NX, SLOTS, NY),
        jnp.transpose(nbr_block, (0, 2, 3, 1)).reshape(NX, SLOTS, NY),
    )
    weights, smoothed = pass_on_results(weights.reshape(SLOTS, NX, NY, ROWS), sm)
    return (smoothed, weights)


def solution(mesh):
    cells = P("gx", "gy", None)
    lists = P("gx", "gy", None, None)
    vectors = P(None, "gx", "gy", None)
    return jax.shard_map(
        per_device,
        mesh=mesh,
        in_specs=(vectors, cells, cells, cells, cells, cells, cells, lists, lists),
        out_specs=(vectors, vectors),
        check_vma=False,
    )
```

```python
import jax
import jax.numpy as jnp
from jax import lax
from jax.experimental import pallas as pl
from jax.experimental.pallas import tpu as pltpu
from jax.sharding import PartitionSpec as P

SLOTS = 4
SWEEPS = 3
ROWS = 128
OMEGA = 0.8
RIDGE = 0.05
VECS = 48
CHUNKS = 3
KV = VECS // CHUNKS
NX = 4
NY = 16
SITES = NX * NY
XROW = (NY + 2) * KV
EXT = (NX + 2) * XROW
GX = 16
GY = 8
MESH = pl.DeviceIdType.MESH
F32 = jnp.float32
BF16 = jnp.bfloat16


def site_row(x, y):
    return (x + 1) * XROW + (y + 1) * KV


def solve_rows(gram, rhs):
    low = [[None] * SLOTS for _ in range(SLOTS)]
    inv = []
    for r in range(SLOTS):
        scaled = []
        diag = gram[r, r]
        for c in range(r):
            rest = gram[r, c]
            for m in range(c):
                rest = rest - scaled[m] * low[c][m]
            scaled.append(rest)
            low[r][c] = rest * inv[c]
            diag = diag - rest * low[r][c]
        inv.append(1.0 / diag)
    fwd = []
    for r in range(SLOTS):
        rest = rhs[r]
        for m in range(r):
            rest = rest - low[r][m] * fwd[m]
        fwd.append(rest)
    out = [None] * SLOTS
    for r in reversed(range(SLOTS)):
        rest = fwd[r] * inv[r]
        for m in range(r + 1, SLOTS):
            rest = rest - low[m][r] * out[m]
        out[r] = rest
    return out


PAIRS = [(s, t) for s in range(SLOTS) for t in range(s + 1)] + [(s, SLOTS) for s in range(SLOTS)]
AXES = "xyz"
LINE = 4
CORES = 2
COARSE = 16
FINE = 48
PLANE = LINE * LINE
ROUTES = (("x", "z", "y"), ("y", "x", "z"), ("z", "y", "x"))
BACKS = (0, 1, 3, 2)
EMPTY = LINE * CORES * PLANE * 2
SPOT = 2 * LINE
GRAM_ORDER = (0, 1, 2)
REPLY = PLANE * 2
PARTS = ((0, 4),)


def lists_of(meta, here):
    lane = lax.broadcasted_iota(jnp.int32, (ROWS, ROWS), 1)
    sub = lax.broadcasted_iota(jnp.int32, (ROWS, ROWS), 0)
    diag = lane == sub
    none = 1 << 20

    def column(row):
        return jnp.sum(jnp.where(diag, row, 0), axis=1, keepdims=True)

    members, keys, owners = [], [], []
    for h in range(2):
        entry = meta[h : h + 1]
        owner = entry >> 6
        key = (lane[:1] + h * ROWS) * SITES + (entry & (SITES - 1))
        owners.append(owner)
        keys.append(key)
        members.append(owner == sub)
    first = jnp.minimum(*[jnp.where(m, k, none) for m, k in zip(members, keys)])
    first = jnp.min(first, axis=1, keepdims=True)
    first = jnp.where(first >= none, 0, first)
    second = jnp.maximum(*[jnp.where(m, k, 0) for m, k in zip(members, keys)])
    second = jnp.max(second, axis=1, keepdims=True)
    targets = [[] for _ in ROUTES]
    for h in range(2):
        own = owners[h]
        at_first = jnp.sum(jnp.where(members[h], first, 0), axis=0, keepdims=True)
        place = jnp.where(keys[h] == at_first, 0, 1)
        at = {"x": (own >> 5) & 3, "z": (own >> 3) & 3, "y": (own >> 1) & 3}
        for c, (a, u, v) in enumerate(ROUTES):
            back = (at[v] - here[v]) & 3
            spot = jnp.where(back == 2, 3, jnp.where(back == 3, 2, back))
            slot = ((at[a] * CORES + (own & 1)) * PLANE + spot * LINE + ((at[u] - here[u]) & 3)) * 2 + place
            targets[c].append(jnp.where(own < 0, EMPTY, slot))
    coarse = meta[2:3]
    rank = jnp.sum(jnp.where(sub < lane, column(coarse), 0), axis=0, keepdims=True)
    fine_rank = jnp.minimum(lane[:1] - rank, FINE)
    fine_rank = jnp.where(coarse > 0, FINE, fine_rank)

    def numbers(hit):
        found = jnp.sum(jnp.where(hit, lane[: hit.shape[0]], 0), axis=1, keepdims=True)
        return jnp.broadcast_to(found, hit.shape)

    ids = numbers((rank == sub[:COARSE]) & (coarse > 0))
    fine_ids = numbers((fine_rank == sub[:FINE]) & (lane[:1] < SITES))
    rank = jnp.minimum(rank, COARSE - 1)
    return (first, second), targets, rank, ids, fine_ids, fine_rank


def ranks_wanted(blocks, table):
    lane = lax.broadcasted_iota(jnp.int32, (ROWS, ROWS), 1)
    sub = lax.broadcasted_iota(jnp.int32, (ROWS, ROWS), 0)
    found = jnp.sum(
        jnp.where(lane == (blocks & (SITES - 1)), table, 0), axis=1, keepdims=True
    )
    return jnp.sum(jnp.where(lane == sub, found, 0), axis=0, keepdims=True)


def smooth_kernel(
    tv, cx, cy, cz, sh, split, count, owner, local, sm_out, w_out,
    split_v, count_v, owner_v, local_v, meta, tgt, tgt_s, blk, rb0, rb1, rb2, part_sums,
    stage, coef, wa, wb, ka, kb, km, kp, fxs, fxr, fys, fyr,
    pair, lines, near, far, block_cols, idv, line_s, id_s, fine_s, spot_s, p00, p01, p02, p03, p10, p11, p12, p13, p20, p21, p22, p23, sb,
    in_sem, coef_sem, out_sem, send_sem, recv_sem, pair_sem, table_sem, gather_sem,
    near_sem, cast_send, cast_recv, ans_send, ans_recv, own_sem, smem_sem, list_sem,
):
    cells = (split_v, count_v, owner_v, local_v)
    rb = (rb0, rb1, rb2)
    pg = ((p00, p01, p02, p03), (p10, p11, p12, p13), (p20, p21, p22, p23))
    i = lax.axis_index("gx")
    j = lax.axis_index("gy")
    core = lax.rem(j, CORES)
    at = {"x": i // LINE, "z": lax.rem(i, LINE), "y": j // CORES}
    peers = (
        (lax.rem(i + GX - 1, GX), j),
        (lax.rem(i + 1, GX), j),
        (i, lax.rem(j + GY - 1, GY)),
        (i, lax.rem(j + 1, GY)),
    )

    def device(axis, d, e):
        moved = dict(at)
        moved[axis] = lax.rem(at[axis] + d, LINE)
        return (moved["x"] * LINE + moved["z"], moved["y"] * CORES + lax.rem(core + e, CORES))

    def remote(src, dst, send, recv, peer):
        return pltpu.make_async_remote_copy(
            src_ref=src, dst_ref=dst, send_sem=send, recv_sem=recv,
            device_id=peer, device_id_type=MESH,
        )

    loads = []
    for c in range(CHUNKS):
        part = pl.ds(c * KV, KV)
        loads.append(pltpu.make_async_copy(tv.at[part], stage.at[part], in_sem.at[c]))
    loads[0].start()
    barrier = pltpu.get_barrier_semaphore()
    for peer in peers[:2]:
        pl.semaphore_signal(barrier, inc=1, device_id=peer, device_id_type=MESH)
    pl.semaphore_signal(barrier, inc=1, device_id=device("x", 0, 1), device_id_type=MESH)
    for axis in AXES:
        for d in range(1, LINE):
            for e in range(CORES):
                pl.semaphore_signal(
                    barrier, inc=1, device_id=device(axis, d, e), device_id_type=MESH
                )
    greeted = 3 + len(AXES) * (LINE - 1) * CORES
    for load in loads[1:]:
        load.start()
    coef_loads = []
    for n, part in enumerate((cx, cy, cz, sh)):
        load = pltpu.make_async_copy(part, coef.at[n], coef_sem.at[n])
        load.start()
        coef_loads.append(load)
    lists = []
    for n, part in enumerate((split, count, owner, local)):
        load = pltpu.make_async_copy(part, cells[n], list_sem.at[n])
        load.start()
        lists.append(load)

    keep = (
        (i > 0).astype(F32),
        (i < GX - 1).astype(F32),
        (j > 0).astype(F32),
        (j < GY - 1).astype(F32),
    )

    def drain(ref, sem):
        pltpu.make_async_copy(ref, ref, sem).wait()

    def copies(s, c):
        out = []
        for d in range(4):
            src, dst = (fxs, fxr) if d < 2 else (fys, fyr)
            out.append(
                remote(
                    src.at[s, c, d % 2], dst.at[s, c, 1 - d % 2],
                    send_sem.at[d // 2], recv_sem.at[s, c, d // 2], peers[d],
                )
            )
        return out

    def send_faces(s, c, w):
        for side in range(2):
            x = side * (NX - 1)
            fxs[s, c, side] = w[c, pl.ds(site_row(x, 0), NY * KV)].astype(BF16)
            y = side * (NY - 1)
            for x in range(NX):
                fys[s, c, side, pl.ds(x * KV, KV)] = w[c, pl.ds(site_row(x, y), KV)].astype(BF16)
        for copy in copies(s, c):
            copy.start()

    def fill_halo(s, c, w):
        drain(fxr.at[s, c], recv_sem.at[s, c, 0])
        drain(fyr.at[s, c], recv_sem.at[s, c, 1])
        for side in range(2):
            x = -1 if side == 0 else NX
            w[c, pl.ds(site_row(x, 0), NY * KV)] = fxr[s, c, side].astype(F32) * keep[side]
            y = -1 if side == 0 else NY
            for x in range(NX):
                w[c, pl.ds(site_row(x, y), KV)] = (
                    fyr[s, c, side, pl.ds(x * KV, KV)].astype(F32) * keep[2 + side]
                )

    def sweep(c, src, dst, last):
        def plane(x, carry):
            base = pl.multiple_of(x * XROW, 16)

            def cell(dx, y):
                return src[c, pl.ds(base + site_row(dx, y), KV)]

            below, here = cell(0, -1), cell(0, 0)
            for y in range(NY):
                above = cell(0, y + 1)
                row = slice(y, y + 1)
                new = (
                    ka[x, row] * (cell(-1, y) + cell(1, y))
                    + kb[x, row] * (below + above)
                    + km[x, row] * pltpu.roll(here, 1, 1)
                    + kp[x, row] * pltpu.roll(here, ROWS - 1, 1)
                    + (1.0 - OMEGA) * here
                )
                dst[c, pl.ds(base + site_row(0, y), KV)] = new
                if last:
                    blk[c, x * NY + y] = new.astype(BF16)
                below, here = here, above
            return carry

        lax.fori_loop(0, NX, plane, 0)

    def pair_copy():
        slot = pair.at[core]
        return remote(slot, slot, pair_sem.at[0], pair_sem.at[1], device("x", 0, 1))

    def line_copies():
        return [
            remote(
                pair, lines.at[n, at[axis]], table_sem.at[0], table_sem.at[1],
                device(axis, d, 0),
            )
            for n, axis in enumerate(AXES)
            for d in range(1, LINE)
        ]

    def gather_copies(step):
        send, recv = gather_sem.at[step, 0], gather_sem.at[step, 1]
        if step == 0:
            slot = near.at[at["y"] * CORES + core]
            return [
                remote(slot, slot, send, recv, device("y", d, e))
                for d in range(LINE)
                for e in range(CORES)
                if d or e
            ]
        slot = far.at[at["x"], at["z"]] if step == 1 else far.at[at["x"]]
        return [
            remote(slot, slot, send, recv, device("zx"[step - 1], d, 0)) for d in range(1, LINE)
        ]

    def gathered(step):
        if step == 0:
            return near.at[pl.ds(0, 7)]
        return far.at[0, pl.ds(0, 3)] if step == 1 else far.at[pl.ds(0, 3)]

    def gather_step(step):
        drain(gathered(step), gather_sem.at[step, 1])
        if step == 0:
            for n in range(LINE * CORES):
                far[at["x"], at["z"], n : n + 1] = near[n, 0:1]
        for copy in gather_copies(step + 1):
            copy.start()

    def ask():
        drain(gathered(2), gather_sem.at[2, 1])
        table = far[...].reshape(ROWS, ROWS)
        for p in range(2):
            pair[core, p] = ranks_wanted(block_cols[p], table)
        pair_copy().start()

    def ask_lines():
        pair_copy().wait_recv()
        for copy in line_copies():
            copy.start()
        for n, axis in enumerate(AXES):
            lines[n, at[axis]] = pair[...]

    steps = {
        (0, 1): lambda: gather_step(0),
        (1, 0): lambda: gather_step(1),
        (1, 2): ask,
        (2, 1): ask_lines,
    }

    def spread_copies(c):
        a, u, v = ROUTES[c]
        return [
            remote(
                pg[c][0].at[0], pg[c][0].at[LINE - d],
                near_sem.at[c, 0], near_sem.at[c, 1], device(u, d, 0),
            )
            for d in (2, 1, 3)
        ]

    def cast_copies(c):
        a, u, v = ROUTES[c]
        plan = (
            (0, 0, 1, 3, 1, 0, 0),
            (0, 0, 1, 1, 3, 1, 2),
            (0, 1, 1, 3, 1, 0, 0),
            (0, 2, 2, 1, 3, 1, 1),
            (0, 2, 2, 3, 1, 0, 2),
            (0, 1, 1, 1, 3, 1, 2),
            (3, 0, 2, 2, 1, 2, 3),
            (1, 2, 2, 2, 3, 2, 3),
        )
        return [
            remote(
                pg[c][src].at[pl.ds(first, size)], pg[c][dst].at[pl.ds(first, size)],
                cast_send.at[c, out], cast_recv.at[c, into], device(v, d, 0),
            )
            for src, first, size, dst, d, out, into in plan
        ]

    def piece(slot, part):
        first, count = PARTS[part]
        return pl.ds(slot * REPLY + first * SPOT, count * SPOT)

    def answer(c, part, d, e):
        a = ROUTES[c][0]
        slot = lax.rem(at[a] + d, LINE) * CORES + lax.rem(core + e, CORES)
        here = at[a] * CORES + core
        src = sb.at[c, piece(slot, part)]
        dst, peer = rb[c].at[piece(here, part)], device(a, d, e)
        if d == 0 and e == 0:
            return pltpu.make_async_copy(src, dst, own_sem.at[c, part])
        return remote(src, dst, ans_send.at[c, part], ans_recv.at[c, part], peer)

    order = [(d, e) for d in (2, 1, 3, 0) for e in range(CORES)]

    def spread(c):
        a, u, v = ROUTES[c]
        for r in range(COARSE):
            pg[c][0][0, r] = blk[c, id_s[r, 0] & (SITES - 1)]
        for copy in spread_copies(c) + cast_copies(c)[:2]:
            copy.start()

    def cast(c):
        drain(pg[c][1].at[pl.ds(0, 3)], near_sem.at[c, 1])
        for copy in cast_copies(c)[2:6]:
            copy.start()

    def pass_on(c):
        for n in range(2):
            drain(pg[c][0].at[pl.ds(0, 2)], cast_recv.at[c, n])
            cast_copies(c)[6 + n].start()

    def pack(c, d, e, places):
        a, u, v = ROUTES[c]
        n = AXES.index(a)
        q, to = lax.rem(at[a] + d, LINE), lax.rem(core + e, CORES)
        slot = q * CORES + to
        for place in places:
            back = BACKS[place]
            tiles = []
            for ahead in range(LINE):
                whose = {
                    a: at[a],
                    u: lax.rem(at[u] + ahead, LINE),
                    v: lax.rem(at[v] + back, LINE),
                }
                owner = whose["x"] * 32 + whose["z"] * 8 + whose["y"] * 2 + core
                for p in range(2):
                    rank = line_s[n, q, to, p, 0, owner] & (COARSE - 1)
                    tiles.append(pg[c][back][ahead, rank])
            for t, tile in enumerate(tiles):
                sb[c, slot * REPLY + place * SPOT + t] = tile

    def pack_rows(c, places):
        for d, e in order:
            pack(c, d, e, places)

    def reply(c):
        drain(pg[c][0], cast_recv.at[c, 3])
        for d, e in order:
            pack(c, d, e, (3,))
            answer(c, 0, d, e).start()

    def transpose_in(c):
        loads[c].wait()
        for x in range(NX):
            for half in range(NY // 8):
                for k in range(KV):
                    wa[c, pl.ds(site_row(x, half * 8) + k, 8, stride=KV), :] = stage[
                        c * KV + k, x, pl.ds(half * 8, 8), :
                    ]

    def products(c, place):
        b = fine_s[place, 0] & (SITES - 1)
        column = ((b >> 4) & 1) * (ROWS // 2) + (b & (NY - 1))
        values = []
        for t in range(SLOTS):
            found = tgt_s[2 * c + (b >> 5), column + t * NY]
            values.append(rb[c][found].astype(F32))
        values.append(blk[c, b].astype(F32))
        for n, (p, q) in enumerate(PAIRS):
            product = values[p] * values[q]
            product = product[0:8] + product[8:16]
            if c != GRAM_ORDER[0]:
                product = product + part_sums[n, place]
            part_sums[n, place] = product

    def add_products(c):
        def step(g, carry):
            for m in range(4):
                products(c, g * 4 + m)
            return carry

        lax.fori_loop(0, FINE // 4, step, 0)

    def finish():
        sub = lax.broadcasted_iota(jnp.int32, (8, ROWS), 0)
        low4, low2, low1 = sub < 4, (sub & 2) == 0, (sub & 1) == 0

        def merge(first, second, keep_first, shift):
            first = first + pltpu.roll(first, 8 - shift, 0)
            second = second + pltpu.roll(second, shift, 0)
            return jnp.where(keep_first, first, second)

        def group(g, carry):
            total = {}
            spots = [spot_s[0, g * 8 + m] & (SITES - 1) for m in range(8)]
            for n, couple in enumerate(PAIRS):
                rows = [part_sums[n, spot] for spot in spots]
                rows = [
                    jnp.where(low4, rows[m], rows[m + 4])
                    + pltpu.roll(jnp.where(low4, rows[m + 4], rows[m]), 4, 0)
                    for m in range(4)
                ]
                rows = [merge(rows[m], rows[m + 2], low2, 2) for m in range(2)]
                total[couple] = merge(rows[0], rows[1], low1, 1) * (1.0 / VECS)
                if couple[0] == couple[1]:
                    total[couple] = total[couple] + RIDGE
            out = solve_rows(total, [total[s, SLOTS] for s in range(SLOTS)])
            for s in range(SLOTS):
                w_out[s, pl.ds(pl.multiple_of(g * 8, 8), 8), :] = out[s]
            return carry

        lax.fori_loop(0, SITES // 8, group, 0)

    stores = []

    def transpose_out(c, w):
        for x in range(NX):
            for half in range(NY // 8):
                for k in range(KV):
                    stage[c * KV + k, x, pl.ds(half * 8, 8), :] = w[
                        c, pl.ds(site_row(x, half * 8) + k, 8, stride=KV), :
                    ]
        part = pl.ds(c * KV, KV)
        store = pltpu.make_async_copy(stage.at[part], sm_out.at[part], out_sem.at[c])
        store.start()
        stores.append(store)

    for c in range(CHUNKS):
        transpose_in(c)
        if c == 0:
            pl.semaphore_wait(barrier, greeted)
        send_faces(0, c, wa)

    for load in coef_loads:
        load.wait()
    ax, ay, az = coef[0], coef[1], coef[2]
    scale = OMEGA / (2.0 * (ax + ay + az) + coef[3])
    ka[...] = ax * scale
    kb[...] = ay * scale
    az = az * scale
    lane = lax.broadcasted_iota(jnp.int32, az.shape, 2)
    km[...] = jnp.where(lane == 0, 0.0, az)
    kp[...] = jnp.where(lane == ROWS - 1, 0.0, az)

    for load in lists:
        load.wait()
    meta[...] = jnp.zeros_like(meta)
    slots = lax.broadcasted_iota(jnp.int32, (SLOTS, NY), 0)
    for x in range(NX):
        live = (cells[0][x] == 0) & (slots < cells[1][x])
        listed = jnp.where(live, cells[2][x] * SITES + cells[3][x], -1)
        for t in range(SLOTS):
            where = pl.ds((x % 2) * (ROWS // 2) + t * NY, NY)
            meta[x // 2 : x // 2 + 1, where] = listed[t : t + 1]
        meta[2:3, pl.ds(x * NY, NY)] = cells[0][x]
    blocks, targets, rank, ids, fine_ids, fine_rank = lists_of(meta[...], at)
    near[at["y"] * CORES + core] = jnp.broadcast_to(rank, (8, ROWS))
    for copy in gather_copies(0):
        copy.start()
    for p in range(2):
        block_cols[p] = jnp.broadcast_to(blocks[p], (ROWS, ROWS))
    idv[:COARSE] = ids
    idv[COARSE : COARSE + FINE] = fine_ids
    idv[COARSE + FINE :] = jnp.broadcast_to(fine_rank, (8, ROWS))
    part_sums[:, FINE] = jnp.zeros((len(PAIRS), 8, ROWS), F32)
    id_copies = [
        pltpu.make_async_copy(idv.at[pl.ds(0, COARSE)], id_s, smem_sem.at[0]),
        pltpu.make_async_copy(idv.at[pl.ds(COARSE, FINE)], fine_s, smem_sem.at[2]),
        pltpu.make_async_copy(idv.at[pl.ds(COARSE + FINE, 8)], spot_s, smem_sem.at[4]),
    ]
    for copy in id_copies:
        copy.start()
    tgt[...] = jnp.zeros_like(tgt)
    for c in range(CHUNKS):
        for h in range(2):
            tgt[2 * c + h : 2 * c + h + 1] = targets[c][h]
        rb[c][EMPTY] = jnp.zeros((KV, ROWS), BF16)
    tgt_copy = pltpu.make_async_copy(tgt, tgt_s, smem_sem.at[3])
    tgt_copy.start()

    for s in range(SWEEPS):
        src, dst = (wb, wa) if s % 2 else (wa, wb)
        for c in range(CHUNKS):
            fill_halo(s, c, src)
            sweep(c, src, dst, s == SWEEPS - 1)
            if s < SWEEPS - 1:
                send_faces(s + 1, c, dst)
            else:
                if c == 0:
                    for copy in id_copies:
                        copy.wait()
                spread(c)
            if (s, c) in steps:
                steps[s, c]()
    drain(lines.at[:, pl.ds(0, 3)], table_sem.at[1])
    line_copy = pltpu.make_async_copy(lines, line_s, smem_sem.at[1])
    line_copy.start()
    cast(0)
    cast(1)
    cast(2)
    line_copy.wait()
    for c in range(CHUNKS):
        pack_rows(c, (0,))
    for c in range(CHUNKS):
        pass_on(c)
    for c in GRAM_ORDER:
        drain(pg[c][0], cast_recv.at[c, 2])
        pack_rows(c, (1, 2))
    for c in GRAM_ORDER:
        reply(c)
    for c in range(CHUNKS):
        transpose_out(c, wb)
    tgt_copy.wait()
    for c in GRAM_ORDER:
        for part in range(len(PARTS)):
            answer(c, part, 0, 0).wait()
            drain(sb.at[c, pl.ds(0, 7 * PARTS[part][1] * SPOT)], ans_recv.at[c, part])
        add_products(c)
    finish()

    drain(fxs, send_sem.at[0])
    drain(fys, send_sem.at[1])
    pair_copy().wait_send()
    drain(lines.at[:, pl.ds(0, 3)], table_sem.at[0])
    for step in range(3):
        drain(gathered(step), gather_sem.at[step, 0])
    for c in range(CHUNKS):
        drain(pg[c][0].at[pl.ds(0, 3)], near_sem.at[c, 0])
        for n in range(3):
            drain(pg[c][0], cast_send.at[c, n])
        for part in range(len(PARTS)):
            count = PARTS[part][1]
            drain(sb.at[c, pl.ds(0, 7 * count * SPOT)], ans_send.at[c, part])
    for store in stores:
        store.wait()


def smooth(test_vectors, coef_x, coef_y, coef_z, shift, split, count, owner, local):
    vmem = pl.BlockSpec(memory_space=pltpu.VMEM)
    anywhere = pl.BlockSpec(memory_space=pl.ANY)
    cells = pltpu.VMEM((NX, NY, ROWS), F32)
    rows = pltpu.VMEM((LINE, COARSE, KV, ROWS), BF16)
    dma = pltpu.SemaphoreType.DMA
    return pl.pallas_call(
        smooth_kernel,
        out_shape=(
            jax.ShapeDtypeStruct((VECS, NX, NY, ROWS), F32),
            jax.ShapeDtypeStruct((SLOTS, SITES, ROWS), F32),
        ),
        in_specs=[anywhere] * 9,
        out_specs=(anywhere, vmem),
        scratch_shapes=[
            pltpu.VMEM((NX, 1, NY), jnp.int32),
            pltpu.VMEM((NX, 1, NY), jnp.int32),
            pltpu.VMEM((NX, SLOTS, NY), jnp.int32),
            pltpu.VMEM((NX, SLOTS, NY), jnp.int32),
            pltpu.VMEM((8, ROWS), jnp.int32),
            pltpu.VMEM((8, ROWS), jnp.int32),
            pltpu.SMEM((8, ROWS), jnp.int32),
            pltpu.VMEM((CHUNKS, SITES, KV, ROWS), BF16),
            *([pltpu.VMEM((EMPTY + 8, KV, ROWS), BF16)] * CHUNKS),
            pltpu.VMEM((len(PAIRS), SITES, 8, ROWS), F32),
            pltpu.VMEM((VECS, NX, NY, ROWS), F32),
            pltpu.VMEM((4, NX, NY, ROWS), F32),
            pltpu.VMEM((CHUNKS, EXT, ROWS), F32),
            pltpu.VMEM((CHUNKS, EXT, ROWS), F32),
            cells, cells, cells, cells,
            pltpu.VMEM((SWEEPS, CHUNKS, 2, NY * KV, ROWS), BF16),
            pltpu.VMEM((SWEEPS, CHUNKS, 2, NY * KV, ROWS), BF16),
            pltpu.VMEM((SWEEPS, CHUNKS, 2, NX * KV, ROWS), BF16),
            pltpu.VMEM((SWEEPS, CHUNKS, 2, NX * KV, ROWS), BF16),
            pltpu.VMEM((CORES, 2, 1, ROWS), jnp.int32),
            pltpu.VMEM((len(AXES), LINE, CORES, 2, 1, ROWS), jnp.int32),
            pltpu.VMEM((LINE * CORES, 8, ROWS), jnp.int32),
            pltpu.VMEM((LINE, LINE, LINE * CORES, ROWS), jnp.int32),
            pltpu.VMEM((2, ROWS, ROWS), jnp.int32),
            pltpu.VMEM((COARSE + FINE + 8, ROWS), jnp.int32),
            pltpu.SMEM((len(AXES), LINE, CORES, 2, 1, ROWS), jnp.int32),
            pltpu.SMEM((COARSE, ROWS), jnp.int32),
            pltpu.SMEM((FINE, ROWS), jnp.int32),
            pltpu.SMEM((8, ROWS), jnp.int32),
            *([rows] * (LINE * CHUNKS)),
            pltpu.VMEM((CHUNKS, EMPTY, KV, ROWS), BF16),
            dma((CHUNKS,)),
            dma((4,)),
            dma((CHUNKS,)),
            dma((2,)),
            dma((SWEEPS, CHUNKS, 2)),
            dma((2,)),
            dma((2,)),
            dma((3, 2)),
            dma((CHUNKS, 2)),
            dma((CHUNKS, 3)),
            dma((CHUNKS, 4)),
            dma((CHUNKS, len(PARTS))),
            dma((CHUNKS, len(PARTS))),
            dma((CHUNKS, len(PARTS))),
            dma((5,)),
            dma((4,)),
        ],
        compiler_params=pltpu.CompilerParams(
            collective_id=0, has_side_effects=True, vmem_limit_bytes=60 * 1024 * 1024
        ),
        name="smooth",
    )(test_vectors, coef_x, coef_y, coef_z, shift, split, count, owner, local)


def pass_kernel(w_in, sm_in, w_out, sm_out, w_hold, sm_hold, in_sem, out_sem):
    parts = [(w_in, w_hold, w_out)]
    for c in range(CHUNKS):
        part = pl.ds(c * KV, KV)
        parts.append((sm_in.at[part], sm_hold.at[part], sm_out.at[part]))
    ins = [pltpu.make_async_copy(a, b, in_sem.at[n]) for n, (a, b, _) in enumerate(parts)]
    outs = [pltpu.make_async_copy(b, d, out_sem.at[n]) for n, (_, b, d) in enumerate(parts)]
    for copy in ins:
        copy.start()
    for load, store in zip(ins, outs):
        load.wait()
        store.start()
    for store in outs:
        store.wait()


def pass_on_results(weights, sm):
    anywhere = pl.BlockSpec(memory_space=pl.ANY)
    dma = pltpu.SemaphoreType.DMA
    return pl.pallas_call(
        pass_kernel,
        out_shape=(
            jax.ShapeDtypeStruct(weights.shape, F32),
            jax.ShapeDtypeStruct(sm.shape, F32),
        ),
        in_specs=[anywhere, anywhere],
        out_specs=(anywhere, anywhere),
        scratch_shapes=[
            pltpu.VMEM(weights.shape, F32),
            pltpu.VMEM(sm.shape, F32),
            dma((CHUNKS + 1,)),
            dma((CHUNKS + 1,)),
        ],
        compiler_params=pltpu.CompilerParams(vmem_limit_bytes=60 * 1024 * 1024),
        name="fit",
    )(weights, sm)


def per_device(
    test_vectors, coef_x, coef_y, coef_z, shift, cf_split, nbr_count, nbr_owner, nbr_block
):
    sm, weights = smooth(
        test_vectors, coef_x, coef_y, coef_z, shift,
        jnp.swapaxes(cf_split, 1, 2),
        jnp.swapaxes(nbr_count, 1, 2),
        jnp.transpose(nbr_owner, (0, 2, 3, 1)).reshape(NX, SLOTS, NY),
        jnp.transpose(nbr_block, (0, 2, 3, 1)).reshape(NX, SLOTS, NY),
    )
    weights, smoothed = pass_on_results(weights.reshape(SLOTS, NX, NY, ROWS), sm)
    return (smoothed, weights)


def solution(mesh):
    cells = P("gx", "gy", None)
    lists = P("gx", "gy", None, None)
    vectors = P(None, "gx", "gy", None)
    return jax.shard_map(
        per_device,
        mesh=mesh,
        in_specs=(vectors, cells, cells, cells, cells, cells, cells, lists, lists),
        out_specs=(vectors, vectors),
        check_vma=False,
    )
```

```python
import jax
import jax.numpy as jnp
from jax import lax
from jax.experimental import pallas as pl
from jax.experimental.pallas import tpu as pltpu
from jax.sharding import PartitionSpec as P

SLOTS = 4
SWEEPS = 3
ROWS = 128
OMEGA = 0.8
RIDGE = 0.05
VECS = 48
CHUNKS = 3
KV = VECS // CHUNKS
NX = 4
NY = 16
SITES = NX * NY
XROW = (NY + 2) * KV
EXT = (NX + 2) * XROW
GX = 16
GY = 8
MESH = pl.DeviceIdType.MESH
F32 = jnp.float32
BF16 = jnp.bfloat16


def site_row(x, y):
    return (x + 1) * XROW + (y + 1) * KV


def solve_rows(gram, rhs):
    low = [[None] * SLOTS for _ in range(SLOTS)]
    inv = []
    for r in range(SLOTS):
        scaled = []
        diag = gram[r, r]
        for c in range(r):
            rest = gram[r, c]
            for m in range(c):
                rest = rest - scaled[m] * low[c][m]
            scaled.append(rest)
            low[r][c] = rest * inv[c]
            diag = diag - rest * low[r][c]
        inv.append(1.0 / diag)
    fwd = []
    for r in range(SLOTS):
        rest = rhs[r]
        for m in range(r):
            rest = rest - low[r][m] * fwd[m]
        fwd.append(rest)
    out = [None] * SLOTS
    for r in reversed(range(SLOTS)):
        rest = fwd[r] * inv[r]
        for m in range(r + 1, SLOTS):
            rest = rest - low[m][r] * out[m]
        out[r] = rest
    return out


PAIRS = [(s, t) for s in range(SLOTS) for t in range(s + 1)] + [(s, SLOTS) for s in range(SLOTS)]
AXES = "xyz"
LINE = 4
CORES = 2
COARSE = 16
FINE = 48
PLANE = LINE * LINE
ROUTES = (("x", "z", "y"), ("y", "x", "z"), ("z", "y", "x"))
BACKS = (0, 1, 3, 2)
EMPTY = LINE * CORES * PLANE * 2
SPOT = 2 * LINE
GRAM_ORDER = (1, 2, 0)
REPLY = PLANE * 2
PARTS = ((0, 3), (3, 1))


def lists_of(meta, here):
    lane = lax.broadcasted_iota(jnp.int32, (ROWS, ROWS), 1)
    sub = lax.broadcasted_iota(jnp.int32, (ROWS, ROWS), 0)
    diag = lane == sub
    none = 1 << 20

    def column(row):
        return jnp.sum(jnp.where(diag, row, 0), axis=1, keepdims=True)

    members, keys, owners = [], [], []
    for h in range(2):
        entry = meta[h : h + 1]
        owner = entry >> 6
        key = (lane[:1] + h * ROWS) * SITES + (entry & (SITES - 1))
        owners.append(owner)
        keys.append(key)
        members.append(owner == sub)
    first = jnp.minimum(*[jnp.where(m, k, none) for m, k in zip(members, keys)])
    first = jnp.min(first, axis=1, keepdims=True)
    first = jnp.where(first >= none, 0, first)
    second = jnp.maximum(*[jnp.where(m, k, 0) for m, k in zip(members, keys)])
    second = jnp.max(second, axis=1, keepdims=True)
    targets = [[] for _ in ROUTES]
    for h in range(2):
        own = owners[h]
        at_first = jnp.sum(jnp.where(members[h], first, 0), axis=0, keepdims=True)
        place = jnp.where(keys[h] == at_first, 0, 1)
        at = {"x": (own >> 5) & 3, "z": (own >> 3) & 3, "y": (own >> 1) & 3}
        for c, (a, u, v) in enumerate(ROUTES):
            back = (at[v] - here[v]) & 3
            spot = jnp.where(back == 2, 3, jnp.where(back == 3, 2, back))
            slot = ((at[a] * CORES + (own & 1)) * PLANE + spot * LINE + ((at[u] - here[u]) & 3)) * 2 + place
            targets[c].append(jnp.where(own < 0, EMPTY, slot))
    coarse = meta[2:3]
    rank = jnp.sum(jnp.where(sub < lane, column(coarse), 0), axis=0, keepdims=True)
    fine_rank = jnp.minimum(lane[:1] - rank, FINE)
    fine_rank = jnp.where(coarse > 0, FINE, fine_rank)

    def numbers(hit):
        found = jnp.sum(jnp.where(hit, lane[: hit.shape[0]], 0), axis=1, keepdims=True)
        return jnp.broadcast_to(found, hit.shape)

    ids = numbers((rank == sub[:COARSE]) & (coarse > 0))
    fine_ids = numbers((fine_rank == sub[:FINE]) & (lane[:1] < SITES))
    rank = jnp.minimum(rank, COARSE - 1)
    return (first, second), targets, rank, ids, fine_ids, fine_rank


def ranks_wanted(blocks, table):
    lane = lax.broadcasted_iota(jnp.int32, (ROWS, ROWS), 1)
    sub = lax.broadcasted_iota(jnp.int32, (ROWS, ROWS), 0)
    found = jnp.sum(
        jnp.where(lane == (blocks & (SITES - 1)), table, 0), axis=1, keepdims=True
    )
    return jnp.sum(jnp.where(lane == sub, found, 0), axis=0, keepdims=True)


def smooth_kernel(
    tv, cx, cy, cz, sh, split, count, owner, local, sm_out, w_out,
    split_v, count_v, owner_v, local_v, meta, tgt, tgt_s, blk, rb0, rb1, rb2, part_sums,
    stage, coef, wa, wb, ka, kb, km, kp, fxs, fxr, fys, fyr,
    pair, lines, near, far, block_cols, idv, line_s, id_s, fine_s, spot_s, p00, p01, p02, p03, p10, p11, p12, p13, p20, p21, p22, p23, sb,
    in_sem, coef_sem, out_sem, send_sem, recv_sem, pair_sem, table_sem, gather_sem,
    near_sem, cast_send, cast_recv, ans_send, ans_recv, own_sem, smem_sem, list_sem,
):
    cells = (split_v, count_v, owner_v, local_v)
    rb = (rb0, rb1, rb2)
    pg = ((p00, p01, p02, p03), (p10, p11, p12, p13), (p20, p21, p22, p23))
    i = lax.axis_index("gx")
    j = lax.axis_index("gy")
    core = lax.rem(j, CORES)
    at = {"x": i // LINE, "z": lax.rem(i, LINE), "y": j // CORES}
    peers = (
        (lax.rem(i + GX - 1, GX), j),
        (lax.rem(i + 1, GX), j),
        (i, lax.rem(j + GY - 1, GY)),
        (i, lax.rem(j + 1, GY)),
    )

    def device(axis, d, e):
        moved = dict(at)
        moved[axis] = lax.rem(at[axis] + d, LINE)
        return (moved["x"] * LINE + moved["z"], moved["y"] * CORES + lax.rem(core + e, CORES))

    def remote(src, dst, send, recv, peer):
        return pltpu.make_async_remote_copy(
            src_ref=src, dst_ref=dst, send_sem=send, recv_sem=recv,
            device_id=peer, device_id_type=MESH,
        )

    loads = []
    for c in range(CHUNKS):
        part = pl.ds(c * KV, KV)
        loads.append(pltpu.make_async_copy(tv.at[part], stage.at[part], in_sem.at[c]))
    loads[0].start()
    barrier = pltpu.get_barrier_semaphore()
    for peer in peers[:2]:
        pl.semaphore_signal(barrier, inc=1, device_id=peer, device_id_type=MESH)
    pl.semaphore_signal(barrier, inc=1, device_id=device("x", 0, 1), device_id_type=MESH)
    for axis in AXES:
        for d in range(1, LINE):
            for e in range(CORES):
                pl.semaphore_signal(
                    barrier, inc=1, device_id=device(axis, d, e), device_id_type=MESH
                )
    greeted = 3 + len(AXES) * (LINE - 1) * CORES
    for load in loads[1:]:
        load.start()
    coef_loads = []
    for n, part in enumerate((cx, cy, cz, sh)):
        load = pltpu.make_async_copy(part, coef.at[n], coef_sem.at[n])
        load.start()
        coef_loads.append(load)
    lists = []
    for n, part in enumerate((split, count, owner, local)):
        load = pltpu.make_async_copy(part, cells[n], list_sem.at[n])
        load.start()
        lists.append(load)

    keep = (
        (i > 0).astype(F32),
        (i < GX - 1).astype(F32),
        (j > 0).astype(F32),
        (j < GY - 1).astype(F32),
    )

    def drain(ref, sem):
        pltpu.make_async_copy(ref, ref, sem).wait()

    def copies(s, c):
        out = []
        for d in range(4):
            src, dst = (fxs, fxr) if d < 2 else (fys, fyr)
            out.append(
                remote(
                    src.at[s, c, d % 2], dst.at[s, c, 1 - d % 2],
                    send_sem.at[d // 2], recv_sem.at[s, c, d // 2], peers[d],
                )
            )
        return out

    def send_faces(s, c, w):
        for side in range(2):
            x = side * (NX - 1)
            fxs[s, c, side] = w[c, pl.ds(site_row(x, 0), NY * KV)].astype(BF16)
            y = side * (NY - 1)
            for x in range(NX):
                fys[s, c, side, pl.ds(x * KV, KV)] = w[c, pl.ds(site_row(x, y), KV)].astype(BF16)
        for copy in copies(s, c):
            copy.start()

    def fill_halo(s, c, w):
        drain(fxr.at[s, c], recv_sem.at[s, c, 0])
        drain(fyr.at[s, c], recv_sem.at[s, c, 1])
        for side in range(2):
            x = -1 if side == 0 else NX
            w[c, pl.ds(site_row(x, 0), NY * KV)] = fxr[s, c, side].astype(F32) * keep[side]
            y = -1 if side == 0 else NY
            for x in range(NX):
                w[c, pl.ds(site_row(x, y), KV)] = (
                    fyr[s, c, side, pl.ds(x * KV, KV)].astype(F32) * keep[2 + side]
                )

    def sweep(c, src, dst, last):
        def plane(x, carry):
            base = pl.multiple_of(x * XROW, 16)

            def cell(dx, y):
                return src[c, pl.ds(base + site_row(dx, y), KV)]

            below, here = cell(0, -1), cell(0, 0)
            for y in range(NY):
                above = cell(0, y + 1)
                row = slice(y, y + 1)
                new = (
                    ka[x, row] * (cell(-1, y) + cell(1, y))
                    + kb[x, row] * (below + above)
                    + km[x, row] * pltpu.roll(here, 1, 1)
                    + kp[x, row] * pltpu.roll(here, ROWS - 1, 1)
                    + (1.0 - OMEGA) * here
                )
                dst[c, pl.ds(base + site_row(0, y), KV)] = new
                if last:
                    blk[c, x * NY + y] = new.astype(BF16)
                below, here = here, above
            return carry

        lax.fori_loop(0, NX, plane, 0)

    def pair_copy():
        slot = pair.at[core]
        return remote(slot, slot, pair_sem.at[0], pair_sem.at[1], device("x", 0, 1))

    def line_copies():
        return [
            remote(
                pair, lines.at[n, at[axis]], table_sem.at[0], table_sem.at[1],
                device(axis, d, 0),
            )
            for n, axis in enumerate(AXES)
            for d in range(1, LINE)
        ]

    def gather_copies(step):
        send, recv = gather_sem.at[step, 0], gather_sem.at[step, 1]
        if step == 0:
            slot = near.at[at["y"] * CORES + core]
            return [
                remote(slot, slot, send, recv, device("y", d, e))
                for d in range(LINE)
                for e in range(CORES)
                if d or e
            ]
        slot = far.at[at["x"], at["z"]] if step == 1 else far.at[at["x"]]
        return [
            remote(slot, slot, send, recv, device("zx"[step - 1], d, 0)) for d in range(1, LINE)
        ]

    def gathered(step):
        if step == 0:
            return near.at[pl.ds(0, 7)]
        return far.at[0, pl.ds(0, 3)] if step == 1 else far.at[pl.ds(0, 3)]

    def gather_step(step):
        drain(gathered(step), gather_sem.at[step, 1])
        if step == 0:
            for n in range(LINE * CORES):
                far[at["x"], at["z"], n : n + 1] = near[n, 0:1]
        for copy in gather_copies(step + 1):
            copy.start()

    def ask():
        drain(gathered(2), gather_sem.at[2, 1])
        table = far[...].reshape(ROWS, ROWS)
        for p in range(2):
            pair[core, p] = ranks_wanted(block_cols[p], table)
        pair_copy().start()

    def ask_lines():
        pair_copy().wait_recv()
        for copy in line_copies():
            copy.start()
        for n, axis in enumerate(AXES):
            lines[n, at[axis]] = pair[...]

    steps = {
        (0, 1): lambda: gather_step(0),
        (1, 0): lambda: gather_step(1),
        (1, 2): ask,
        (2, 1): ask_lines,
    }

    def spread_copies(c):
        a, u, v = ROUTES[c]
        return [
            remote(
                pg[c][0].at[0], pg[c][0].at[LINE - d],
                near_sem.at[c, 0], near_sem.at[c, 1], device(u, d, 0),
            )
            for d in (2, 1, 3)
        ]

    def cast_copies(c):
        a, u, v = ROUTES[c]
        plan = (
            (0, 0, 1, 3, 1, 0, 0),
            (0, 0, 1, 1, 3, 1, 2),
            (0, 1, 1, 3, 1, 0, 0),
            (0, 2, 2, 1, 3, 1, 1),
            (0, 2, 2, 3, 1, 0, 2),
            (0, 1, 1, 1, 3, 1, 2),
            (3, 0, 2, 2, 1, 2, 3),
            (1, 2, 2, 2, 3, 2, 3),
        )
        return [
            remote(
                pg[c][src].at[pl.ds(first, size)], pg[c][dst].at[pl.ds(first, size)],
                cast_send.at[c, out], cast_recv.at[c, into], device(v, d, 0),
            )
            for src, first, size, dst, d, out, into in plan
        ]

    def piece(slot, part):
        first, count = PARTS[part]
        return pl.ds(slot * REPLY + first * SPOT, count * SPOT)

    def answer(c, part, d, e):
        a = ROUTES[c][0]
        slot = lax.rem(at[a] + d, LINE) * CORES + lax.rem(core + e, CORES)
        here = at[a] * CORES + core
        src = sb.at[c, piece(slot, part)]
        dst, peer = rb[c].at[piece(here, part)], device(a, d, e)
        if isinstance(d, int) and d == 0 and e == 0:
            return pltpu.make_async_copy(src, dst, own_sem.at[c, part])
        return remote(src, dst, ans_send.at[c, part], ans_recv.at[c, part], peer)

    order = [(d, e) for d in (2, 1, 3, 0) for e in range(CORES)]

    def spread(c):
        a, u, v = ROUTES[c]
        for r in range(COARSE):
            pg[c][0][0, r] = blk[c, id_s[r, 0] & (SITES - 1)]
        for copy in spread_copies(c) + cast_copies(c)[:2]:
            copy.start()

    def cast(c):
        drain(pg[c][1].at[pl.ds(0, 3)], near_sem.at[c, 1])
        for copy in cast_copies(c)[2:6]:
            copy.start()

    def pass_on(c):
        for n in range(2):
            drain(pg[c][0].at[pl.ds(0, 2)], cast_recv.at[c, n])
            cast_copies(c)[6 + n].start()

    def pack(c, d, e, places):
        a, u, v = ROUTES[c]
        n = AXES.index(a)
        q, to = lax.rem(at[a] + d, LINE), lax.rem(core + e, CORES)
        slot = q * CORES + to
        for place in places:
            back = BACKS[place]
            tiles = []
            for ahead in range(LINE):
                whose = {
                    a: at[a],
                    u: lax.rem(at[u] + ahead, LINE),
                    v: lax.rem(at[v] + back, LINE),
                }
                owner = whose["x"] * 32 + whose["z"] * 8 + whose["y"] * 2 + core
                for p in range(2):
                    rank = line_s[n, q, to, p, 0, owner] & (COARSE - 1)
                    tiles.append(pg[c][back][ahead, rank])
            for t, tile in enumerate(tiles):
                sb[c, slot * REPLY + place * SPOT + t] = tile

    def reply(c, part):
        drain(pg[c][0], cast_recv.at[c, 2 + part])
        first, count = PARTS[part]
        places = range(first, first + count)

        def to_other_chip(n, carry):
            k, e = n // CORES, lax.rem(n, CORES)
            d = 2 - k + 3 * (k // 2)
            pack(c, d, e, places)
            answer(c, part, d, e).start()
            return carry

        lax.fori_loop(0, (LINE - 1) * CORES, to_other_chip, 0)
        for e in (1, 0):
            pack(c, 0, e, places)
            answer(c, part, 0, e).start()

    def transpose_in(c):
        loads[c].wait()

        def one(k, carry):
            for x in range(NX):
                for half in range(NY // 8):
                    wa[c, pl.ds(site_row(x, half * 8) + k, 8, stride=KV), :] = stage[
                        c * KV + k, x, pl.ds(half * 8, 8), :
                    ]
            return carry

        lax.fori_loop(0, KV, one, 0)

    def products(c, place):
        b = fine_s[place, 0] & (SITES - 1)
        column = ((b >> 4) & 1) * (ROWS // 2) + (b & (NY - 1))
        values = []
        for t in range(SLOTS):
            found = tgt_s[2 * c + (b >> 5), column + t * NY]
            values.append(rb[c][found].astype(F32))
        values.append(blk[c, b].astype(F32))
        for n, (p, q) in enumerate(PAIRS):
            product = values[p] * values[q]
            product = product[0:8] + product[8:16]
            if c != GRAM_ORDER[0]:
                product = product + part_sums[n, place]
            part_sums[n, place] = product

    def add_products(c):
        def step(g, carry):
            for m in range(4):
                products(c, g * 4 + m)
            return carry

        lax.fori_loop(0, FINE // 4, step, 0)

    def finish():
        sub = lax.broadcasted_iota(jnp.int32, (8, ROWS), 0)
        low4, low2, low1 = sub < 4, (sub & 2) == 0, (sub & 1) == 0

        def merge(first, second, keep_first, shift):
            first = first + pltpu.roll(first, 8 - shift, 0)
            second = second + pltpu.roll(second, shift, 0)
            return jnp.where(keep_first, first, second)

        def group(g, carry):
            total = {}
            spots = [spot_s[0, g * 8 + m] & (SITES - 1) for m in range(8)]
            for n, couple in enumerate(PAIRS):
                rows = [part_sums[n, spot] for spot in spots]
                rows = [
                    jnp.where(low4, rows[m], rows[m + 4])
                    + pltpu.roll(jnp.where(low4, rows[m + 4], rows[m]), 4, 0)
                    for m in range(4)
                ]
                rows = [merge(rows[m], rows[m + 2], low2, 2) for m in range(2)]
                total[couple] = merge(rows[0], rows[1], low1, 1) * (1.0 / VECS)
                if couple[0] == couple[1]:
                    total[couple] = total[couple] + RIDGE
            out = solve_rows(total, [total[s, SLOTS] for s in range(SLOTS)])
            for s in range(SLOTS):
                w_out[s, pl.ds(pl.multiple_of(g * 8, 8), 8), :] = out[s]
            return carry

        lax.fori_loop(0, SITES // 8, group, 0)

    stores = []

    def transpose_out(c, w):

        def one(k, carry):
            for x in range(NX):
                for half in range(NY // 8):
                    stage[c * KV + k, x, pl.ds(half * 8, 8), :] = w[
                        c, pl.ds(site_row(x, half * 8) + k, 8, stride=KV), :
                    ]
            return carry

        lax.fori_loop(0, KV, one, 0)
        part = pl.ds(c * KV, KV)
        store = pltpu.make_async_copy(stage.at[part], sm_out.at[part], out_sem.at[c])
        store.start()
        stores.append(store)

    for c in range(CHUNKS):
        transpose_in(c)
        if c == 0:
            pl.semaphore_wait(barrier, greeted)
        send_faces(0, c, wa)

    for load in coef_loads:
        load.wait()
    ax, ay, az = coef[0], coef[1], coef[2]
    scale = OMEGA / (2.0 * (ax + ay + az) + coef[3])
    ka[...] = ax * scale
    kb[...] = ay * scale
    az = az * scale
    lane = lax.broadcasted_iota(jnp.int32, az.shape, 2)
    km[...] = jnp.where(lane == 0, 0.0, az)
    kp[...] = jnp.where(lane == ROWS - 1, 0.0, az)

    for load in lists:
        load.wait()
    meta[...] = jnp.zeros_like(meta)
    slots = lax.broadcasted_iota(jnp.int32, (SLOTS, NY), 0)
    for x in range(NX):
        live = (cells[0][x] == 0) & (slots < cells[1][x])
        listed = jnp.where(live, cells[2][x] * SITES + cells[3][x], -1)
        for t in range(SLOTS):
            where = pl.ds((x % 2) * (ROWS // 2) + t * NY, NY)
            meta[x // 2 : x // 2 + 1, where] = listed[t : t + 1]
        meta[2:3, pl.ds(x * NY, NY)] = cells[0][x]
    blocks, targets, rank, ids, fine_ids, fine_rank = lists_of(meta[...], at)
    near[at["y"] * CORES + core] = jnp.broadcast_to(rank, (8, ROWS))
    for copy in gather_copies(0):
        copy.start()
    for p in range(2):
        block_cols[p] = jnp.broadcast_to(blocks[p], (ROWS, ROWS))
    idv[:COARSE] = ids
    idv[COARSE : COARSE + FINE] = fine_ids
    idv[COARSE + FINE :] = jnp.broadcast_to(fine_rank, (8, ROWS))
    part_sums[:, FINE] = jnp.zeros((len(PAIRS), 8, ROWS), F32)
    id_copies = [
        pltpu.make_async_copy(idv.at[pl.ds(0, COARSE)], id_s, smem_sem.at[0]),
        pltpu.make_async_copy(idv.at[pl.ds(COARSE, FINE)], fine_s, smem_sem.at[2]),
        pltpu.make_async_copy(idv.at[pl.ds(COARSE + FINE, 8)], spot_s, smem_sem.at[4]),
    ]
    for copy in id_copies:
        copy.start()
    tgt[...] = jnp.zeros_like(tgt)
    for c in range(CHUNKS):
        for h in range(2):
            tgt[2 * c + h : 2 * c + h + 1] = targets[c][h]
        rb[c][EMPTY] = jnp.zeros((KV, ROWS), BF16)
    tgt_copy = pltpu.make_async_copy(tgt, tgt_s, smem_sem.at[3])
    tgt_copy.start()

    for s in range(SWEEPS):
        src, dst = (wb, wa) if s % 2 else (wa, wb)
        for c in range(CHUNKS):
            fill_halo(s, c, src)
            sweep(c, src, dst, s == SWEEPS - 1)
            if s < SWEEPS - 1:
                send_faces(s + 1, c, dst)
            else:
                if c == 0:
                    for copy in id_copies:
                        copy.wait()
                spread(c)
            if (s, c) in steps:
                steps[s, c]()
    drain(lines.at[:, pl.ds(0, 3)], table_sem.at[1])
    line_copy = pltpu.make_async_copy(lines, line_s, smem_sem.at[1])
    line_copy.start()
    cast(0)
    cast(1)
    cast(2)
    line_copy.wait()
    for c in range(CHUNKS):
        pass_on(c)
    for c in (1, 2, 0):
        reply(c, 0)
    for c in (1, 0, 2):
        reply(c, 1)
    for c in range(CHUNKS):
        transpose_out(c, wb)
    tgt_copy.wait()
    for c in GRAM_ORDER:
        for part in range(len(PARTS)):
            answer(c, part, 0, 0).wait()
            drain(sb.at[c, pl.ds(0, 7 * PARTS[part][1] * SPOT)], ans_recv.at[c, part])
        add_products(c)
    finish()

    drain(fxs, send_sem.at[0])
    drain(fys, send_sem.at[1])
    pair_copy().wait_send()
    drain(lines.at[:, pl.ds(0, 3)], table_sem.at[0])
    for step in range(3):
        drain(gathered(step), gather_sem.at[step, 0])
    for c in range(CHUNKS):
        drain(pg[c][0].at[pl.ds(0, 3)], near_sem.at[c, 0])
        for n in range(3):
            drain(pg[c][0], cast_send.at[c, n])
        for part in range(len(PARTS)):
            count = PARTS[part][1]
            drain(sb.at[c, pl.ds(0, 7 * count * SPOT)], ans_send.at[c, part])
    for store in stores:
        store.wait()


def smooth(test_vectors, coef_x, coef_y, coef_z, shift, split, count, owner, local):
    vmem = pl.BlockSpec(memory_space=pltpu.VMEM)
    anywhere = pl.BlockSpec(memory_space=pl.ANY)
    cells = pltpu.VMEM((NX, NY, ROWS), F32)
    rows = pltpu.VMEM((LINE, COARSE, KV, ROWS), BF16)
    dma = pltpu.SemaphoreType.DMA
    return pl.pallas_call(
        smooth_kernel,
        out_shape=(
            jax.ShapeDtypeStruct((VECS, NX, NY, ROWS), F32),
            jax.ShapeDtypeStruct((SLOTS, SITES, ROWS), F32),
        ),
        in_specs=[anywhere] * 9,
        out_specs=(anywhere, vmem),
        scratch_shapes=[
            pltpu.VMEM((NX, 1, NY), jnp.int32),
            pltpu.VMEM((NX, 1, NY), jnp.int32),
            pltpu.VMEM((NX, SLOTS, NY), jnp.int32),
            pltpu.VMEM((NX, SLOTS, NY), jnp.int32),
            pltpu.VMEM((8, ROWS), jnp.int32),
            pltpu.VMEM((8, ROWS), jnp.int32),
            pltpu.SMEM((8, ROWS), jnp.int32),
            pltpu.VMEM((CHUNKS, SITES, KV, ROWS), BF16),
            *([pltpu.VMEM((EMPTY + 8, KV, ROWS), BF16)] * CHUNKS),
            pltpu.VMEM((len(PAIRS), SITES, 8, ROWS), F32),
            pltpu.VMEM((VECS, NX, NY, ROWS), F32),
            pltpu.VMEM((4, NX, NY, ROWS), F32),
            pltpu.VMEM((CHUNKS, EXT, ROWS), F32),
            pltpu.VMEM((CHUNKS, EXT, ROWS), F32),
            cells, cells, cells, cells,
            pltpu.VMEM((SWEEPS, CHUNKS, 2, NY * KV, ROWS), BF16),
            pltpu.VMEM((SWEEPS, CHUNKS, 2, NY * KV, ROWS), BF16),
            pltpu.VMEM((SWEEPS, CHUNKS, 2, NX * KV, ROWS), BF16),
            pltpu.VMEM((SWEEPS, CHUNKS, 2, NX * KV, ROWS), BF16),
            pltpu.VMEM((CORES, 2, 1, ROWS), jnp.int32),
            pltpu.VMEM((len(AXES), LINE, CORES, 2, 1, ROWS), jnp.int32),
            pltpu.VMEM((LINE * CORES, 8, ROWS), jnp.int32),
            pltpu.VMEM((LINE, LINE, LINE * CORES, ROWS), jnp.int32),
            pltpu.VMEM((2, ROWS, ROWS), jnp.int32),
            pltpu.VMEM((COARSE + FINE + 8, ROWS), jnp.int32),
            pltpu.SMEM((len(AXES), LINE, CORES, 2, 1, ROWS), jnp.int32),
            pltpu.SMEM((COARSE, ROWS), jnp.int32),
            pltpu.SMEM((FINE, ROWS), jnp.int32),
            pltpu.SMEM((8, ROWS), jnp.int32),
            *([rows] * (LINE * CHUNKS)),
            pltpu.VMEM((CHUNKS, EMPTY, KV, ROWS), BF16),
            dma((CHUNKS,)),
            dma((4,)),
            dma((CHUNKS,)),
            dma((2,)),
            dma((SWEEPS, CHUNKS, 2)),
            dma((2,)),
            dma((2,)),
            dma((3, 2)),
            dma((CHUNKS, 2)),
            dma((CHUNKS, 3)),
            dma((CHUNKS, 4)),
            dma((CHUNKS, len(PARTS))),
            dma((CHUNKS, len(PARTS))),
            dma((CHUNKS, len(PARTS))),
            dma((5,)),
            dma((4,)),
        ],
        compiler_params=pltpu.CompilerParams(
            collective_id=0, has_side_effects=True, vmem_limit_bytes=60 * 1024 * 1024
        ),
        name="smooth",
    )(test_vectors, coef_x, coef_y, coef_z, shift, split, count, owner, local)


def pass_kernel(w_in, sm_in, w_out, sm_out, w_hold, sm_hold, in_sem, out_sem):
    parts = [(w_in, w_hold, w_out)]
    for c in range(CHUNKS):
        part = pl.ds(c * KV, KV)
        parts.append((sm_in.at[part], sm_hold.at[part], sm_out.at[part]))
    ins = [pltpu.make_async_copy(a, b, in_sem.at[n]) for n, (a, b, _) in enumerate(parts)]
    outs = [pltpu.make_async_copy(b, d, out_sem.at[n]) for n, (_, b, d) in enumerate(parts)]
    for copy in ins:
        copy.start()
    for load, store in zip(ins, outs):
        load.wait()
        store.start()
    for store in outs:
        store.wait()


def pass_on_results(weights, sm):
    anywhere = pl.BlockSpec(memory_space=pl.ANY)
    dma = pltpu.SemaphoreType.DMA
    return pl.pallas_call(
        pass_kernel,
        out_shape=(
            jax.ShapeDtypeStruct(weights.shape, F32),
            jax.ShapeDtypeStruct(sm.shape, F32),
        ),
        in_specs=[anywhere, anywhere],
        out_specs=(anywhere, anywhere),
        scratch_shapes=[
            pltpu.VMEM(weights.shape, F32),
            pltpu.VMEM(sm.shape, F32),
            dma((CHUNKS + 1,)),
            dma((CHUNKS + 1,)),
        ],
        compiler_params=pltpu.CompilerParams(vmem_limit_bytes=60 * 1024 * 1024),
        name="fit",
    )(weights, sm)


def per_device(
    test_vectors, coef_x, coef_y, coef_z, shift, cf_split, nbr_count, nbr_owner, nbr_block
):
    sm, weights = smooth(
        test_vectors, coef_x, coef_y, coef_z, shift,
        jnp.swapaxes(cf_split, 1, 2),
        jnp.swapaxes(nbr_count, 1, 2),
        jnp.transpose(nbr_owner, (0, 2, 3, 1)).reshape(NX, SLOTS, NY),
        jnp.transpose(nbr_block, (0, 2, 3, 1)).reshape(NX, SLOTS, NY),
    )
    weights, smoothed = pass_on_results(weights.reshape(SLOTS, NX, NY, ROWS), sm)
    return (smoothed, weights)


def solution(mesh):
    cells = P("gx", "gy", None)
    lists = P("gx", "gy", None, None)
    vectors = P(None, "gx", "gy", None)
    return jax.shard_map(
        per_device,
        mesh=mesh,
        in_specs=(vectors, cells, cells, cells, cells, cells, cells, lists, lists),
        out_specs=(vectors, vectors),
        check_vma=False,
    )
```

```python
import jax
import jax.numpy as jnp
from jax import lax
from jax.experimental import pallas as pl
from jax.experimental.pallas import tpu as pltpu
from jax.sharding import PartitionSpec as P

SLOTS = 4
SWEEPS = 3
ROWS = 128
OMEGA = 0.8
RIDGE = 0.05
VECS = 48
CHUNKS = 3
KV = VECS // CHUNKS
NX = 4
NY = 16
SITES = NX * NY
XROW = (NY + 2) * KV
EXT = (NX + 2) * XROW
GX = 16
GY = 8
MESH = pl.DeviceIdType.MESH
F32 = jnp.float32
BF16 = jnp.bfloat16


def site_row(x, y):
    return (x + 1) * XROW + (y + 1) * KV


def solve_rows(gram, rhs):
    low = [[None] * SLOTS for _ in range(SLOTS)]
    inv = []
    for r in range(SLOTS):
        scaled = []
        diag = gram[r, r]
        for c in range(r):
            rest = gram[r, c]
            for m in range(c):
                rest = rest - scaled[m] * low[c][m]
            scaled.append(rest)
            low[r][c] = rest * inv[c]
            diag = diag - rest * low[r][c]
        inv.append(1.0 / diag)
    fwd = []
    for r in range(SLOTS):
        rest = rhs[r]
        for m in range(r):
            rest = rest - low[r][m] * fwd[m]
        fwd.append(rest)
    out = [None] * SLOTS
    for r in reversed(range(SLOTS)):
        rest = fwd[r] * inv[r]
        for m in range(r + 1, SLOTS):
            rest = rest - low[m][r] * out[m]
        out[r] = rest
    return out


PAIRS = [(s, t) for s in range(SLOTS) for t in range(s + 1)] + [(s, SLOTS) for s in range(SLOTS)]
AXES = "xyz"
LINE = 4
CORES = 2
COARSE = 16
FINE = 48
PLANE = LINE * LINE
ROUTES = (("x", "z", "y"), ("y", "x", "z"), ("z", "y", "x"))
BACKS = (0, 1, 3, 2)
EMPTY = LINE * CORES * PLANE * 2
SPOT = 2 * LINE
GRAM_ORDER = (1, 2, 0)
REPLY = PLANE * 2
PARTS = ((0, 3), (3, 1))


def lists_of(meta, here):
    lane = lax.broadcasted_iota(jnp.int32, (ROWS, ROWS), 1)
    sub = lax.broadcasted_iota(jnp.int32, (ROWS, ROWS), 0)
    diag = lane == sub
    none = 1 << 20

    def column(row):
        return jnp.sum(jnp.where(diag, row, 0), axis=1, keepdims=True)

    members, keys, owners = [], [], []
    for h in range(2):
        entry = meta[h : h + 1]
        owner = entry >> 6
        key = (lane[:1] + h * ROWS) * SITES + (entry & (SITES - 1))
        owners.append(owner)
        keys.append(key)
        members.append(owner == sub)
    first = jnp.minimum(*[jnp.where(m, k, none) for m, k in zip(members, keys)])
    first = jnp.min(first, axis=1, keepdims=True)
    first = jnp.where(first >= none, 0, first)
    second = jnp.maximum(*[jnp.where(m, k, 0) for m, k in zip(members, keys)])
    second = jnp.max(second, axis=1, keepdims=True)
    targets = [[] for _ in ROUTES]
    for h in range(2):
        own = owners[h]
        at_first = jnp.sum(jnp.where(members[h], first, 0), axis=0, keepdims=True)
        place = jnp.where(keys[h] == at_first, 0, 1)
        at = {"x": (own >> 5) & 3, "z": (own >> 3) & 3, "y": (own >> 1) & 3}
        for c, (a, u, v) in enumerate(ROUTES):
            back = (at[v] - here[v]) & 3
            spot = jnp.where(back == 2, 3, jnp.where(back == 3, 2, back))
            slot = ((at[a] * CORES + (own & 1)) * PLANE + spot * LINE + ((at[u] - here[u]) & 3)) * 2 + place
            targets[c].append(jnp.where(own < 0, EMPTY, slot))
    coarse = meta[2:3]
    rank = jnp.sum(jnp.where(sub < lane, column(coarse), 0), axis=0, keepdims=True)
    fine_rank = jnp.minimum(lane[:1] - rank, FINE)
    fine_rank = jnp.where(coarse > 0, FINE, fine_rank)

    def numbers(hit):
        found = jnp.sum(jnp.where(hit, lane[: hit.shape[0]], 0), axis=1, keepdims=True)
        return jnp.broadcast_to(found, hit.shape)

    ids = numbers((rank == sub[:COARSE]) & (coarse > 0))
    fine_ids = numbers((fine_rank == sub[:FINE]) & (lane[:1] < SITES))
    rank = jnp.minimum(rank, COARSE - 1)
    return (first, second), targets, rank, ids, fine_ids, fine_rank


def ranks_wanted(blocks, table):
    lane = lax.broadcasted_iota(jnp.int32, (ROWS, ROWS), 1)
    sub = lax.broadcasted_iota(jnp.int32, (ROWS, ROWS), 0)
    found = jnp.sum(
        jnp.where(lane == (blocks & (SITES - 1)), table, 0), axis=1, keepdims=True
    )
    return jnp.sum(jnp.where(lane == sub, found, 0), axis=0, keepdims=True)


def smooth_kernel(
    tv, cx, cy, cz, sh, split, count, owner, local, sm_out, w_out,
    split_v, count_v, owner_v, local_v, meta, tgt, tgt_s, blk, rb0, rb1, rb2, part_sums,
    stage, coef, wa, wb, ka, kb, km, kp, fxs, fxr, fys, fyr,
    pair, lines, near, far, block_cols, idv, line_s, id_s, fine_s, spot_s, p00, p01, p02, p03, p10, p11, p12, p13, p20, p21, p22, p23, sb,
    in_sem, coef_sem, out_sem, send_sem, recv_sem, pair_sem, table_sem, gather_sem,
    near_sem, cast_send, cast_recv, ans_send, ans_recv, own_sem, smem_sem, list_sem,
):
    cells = (split_v, count_v, owner_v, local_v)
    rb = (rb0, rb1, rb2)
    pg = ((p00, p01, p02, p03), (p10, p11, p12, p13), (p20, p21, p22, p23))
    i = lax.axis_index("gx")
    j = lax.axis_index("gy")
    core = lax.rem(j, CORES)
    at = {"x": i // LINE, "z": lax.rem(i, LINE), "y": j // CORES}
    peers = (
        (lax.rem(i + GX - 1, GX), j),
        (lax.rem(i + 1, GX), j),
        (i, lax.rem(j + GY - 1, GY)),
        (i, lax.rem(j + 1, GY)),
    )

    def device(axis, d, e):
        moved = dict(at)
        moved[axis] = lax.rem(at[axis] + d, LINE)
        return (moved["x"] * LINE + moved["z"], moved["y"] * CORES + lax.rem(core + e, CORES))

    def remote(src, dst, send, recv, peer):
        return pltpu.make_async_remote_copy(
            src_ref=src, dst_ref=dst, send_sem=send, recv_sem=recv,
            device_id=peer, device_id_type=MESH,
        )

    loads = []
    for c in range(CHUNKS):
        part = pl.ds(c * KV, KV)
        loads.append(pltpu.make_async_copy(tv.at[part], stage.at[part], in_sem.at[c]))
    loads[0].start()
    barrier = pltpu.get_barrier_semaphore()
    for peer in peers[:2]:
        pl.semaphore_signal(barrier, inc=1, device_id=peer, device_id_type=MESH)
    pl.semaphore_signal(barrier, inc=1, device_id=device("x", 0, 1), device_id_type=MESH)
    for axis in AXES:
        for d in range(1, LINE):
            for e in range(CORES):
                pl.semaphore_signal(
                    barrier, inc=1, device_id=device(axis, d, e), device_id_type=MESH
                )
    greeted = 3 + len(AXES) * (LINE - 1) * CORES
    for load in loads[1:]:
        load.start()
    coef_loads = []
    for n, part in enumerate((cx, cy, cz, sh)):
        load = pltpu.make_async_copy(part, coef.at[n], coef_sem.at[n])
        load.start()
        coef_loads.append(load)
    lists = []
    for n, part in enumerate((split, count, owner, local)):
        load = pltpu.make_async_copy(part, cells[n], list_sem.at[n])
        load.start()
        lists.append(load)

    keep = (
        (i > 0).astype(F32),
        (i < GX - 1).astype(F32),
        (j > 0).astype(F32),
        (j < GY - 1).astype(F32),
    )

    def drain(ref, sem):
        pltpu.make_async_copy(ref, ref, sem).wait()

    def copies(s, c):
        out = []
        for d in range(4):
            src, dst = (fxs, fxr) if d < 2 else (fys, fyr)
            out.append(
                remote(
                    src.at[s, c, d % 2], dst.at[s, c, 1 - d % 2],
                    send_sem.at[d // 2], recv_sem.at[s, c, d // 2], peers[d],
                )
            )
        return out

    def send_faces(s, c, w):
        for side in range(2):
            x = side * (NX - 1)
            fxs[s, c, side] = w[c, pl.ds(site_row(x, 0), NY * KV)].astype(BF16)
            y = side * (NY - 1)
            for x in range(NX):
                fys[s, c, side, pl.ds(x * KV, KV)] = w[c, pl.ds(site_row(x, y), KV)].astype(BF16)
        for copy in copies(s, c):
            copy.start()

    def fill_halo(s, c, w):
        drain(fxr.at[s, c], recv_sem.at[s, c, 0])
        drain(fyr.at[s, c], recv_sem.at[s, c, 1])
        for side in range(2):
            x = -1 if side == 0 else NX
            w[c, pl.ds(site_row(x, 0), NY * KV)] = fxr[s, c, side].astype(F32) * keep[side]
            y = -1 if side == 0 else NY
            for x in range(NX):
                w[c, pl.ds(site_row(x, y), KV)] = (
                    fyr[s, c, side, pl.ds(x * KV, KV)].astype(F32) * keep[2 + side]
                )

    def sweep(s, c, src, dst):
        last = s == SWEEPS - 1

        def plane(x, side):
            base = pl.multiple_of(x * XROW, 16)

            def cell(dx, y):
                return src[c, pl.ds(base + site_row(dx, y), KV)].reshape(2, 8, ROWS)

            below, here = cell(0, -1), cell(0, 0)
            for y in range(NY):
                above = cell(0, y + 1)
                new = (
                    ka[x, y] * (cell(-1, y) + cell(1, y))
                    + kb[x, y] * (below + above)
                    + km[x, y] * pltpu.roll(here, 1, 2)
                    + kp[x, y] * pltpu.roll(here, ROWS - 1, 2)
                    + (1.0 - OMEGA) * here
                ).reshape(KV, ROWS)
                dst[c, pl.ds(base + site_row(0, y), KV)] = new
                if last:
                    blk[c, x * NY + y] = new.astype(BF16)
                else:
                    if side is not None:
                        fxs[s + 1, c, side, pl.ds(y * KV, KV)] = new.astype(BF16)
                    if y in (0, NY - 1):
                        rows = pl.ds(pl.multiple_of(x * KV, KV), KV)
                        fys[s + 1, c, y // (NY - 1), rows] = new.astype(BF16)
                below, here = here, above

        def outer(n, carry):
            plane(n * (NX - 1), n)
            return carry

        def inner(n, carry):
            plane(n, None)
            return carry

        lax.fori_loop(0, 2, outer, 0)
        if not last:
            for copy in copies(s + 1, c)[:2]:
                copy.start()
        lax.fori_loop(1, NX - 1, inner, 0)
        if not last:
            for copy in copies(s + 1, c)[2:]:
                copy.start()

    def pair_copy():
        slot = pair.at[core]
        return remote(slot, slot, pair_sem.at[0], pair_sem.at[1], device("x", 0, 1))

    def line_copies():
        return [
            remote(
                pair, lines.at[n, at[axis]], table_sem.at[0], table_sem.at[1],
                device(axis, d, 0),
            )
            for n, axis in enumerate(AXES)
            for d in range(1, LINE)
        ]

    def gather_copies(step):
        send, recv = gather_sem.at[step, 0], gather_sem.at[step, 1]
        if step == 0:
            slot = near.at[at["y"] * CORES + core]
            return [
                remote(slot, slot, send, recv, device("y", d, e))
                for d in range(LINE)
                for e in range(CORES)
                if d or e
            ]
        slot = far.at[at["x"], at["z"]] if step == 1 else far.at[at["x"]]
        return [
            remote(slot, slot, send, recv, device("zx"[step - 1], d, 0)) for d in range(1, LINE)
        ]

    def gathered(step):
        if step == 0:
            return near.at[pl.ds(0, 7)]
        return far.at[0, pl.ds(0, 3)] if step == 1 else far.at[pl.ds(0, 3)]

    def gather_step(step):
        drain(gathered(step), gather_sem.at[step, 1])
        if step == 0:
            for n in range(LINE * CORES):
                far[at["x"], at["z"], n : n + 1] = near[n, 0:1]
        for copy in gather_copies(step + 1):
            copy.start()

    def ask():
        drain(gathered(2), gather_sem.at[2, 1])
        table = far[...].reshape(ROWS, ROWS)
        for p in range(2):
            pair[core, p] = ranks_wanted(block_cols[p], table)
        pair_copy().start()

    def ask_lines():
        pair_copy().wait_recv()
        for copy in line_copies():
            copy.start()
        for n, axis in enumerate(AXES):
            lines[n, at[axis]] = pair[...]

    steps = {
        (0, 1): lambda: gather_step(0),
        (1, 0): lambda: gather_step(1),
        (1, 2): ask,
        (2, 1): ask_lines,
    }

    def spread_copies(c):
        a, u, v = ROUTES[c]
        return [
            remote(
                pg[c][0].at[0], pg[c][0].at[LINE - d],
                near_sem.at[c, 0], near_sem.at[c, 1], device(u, d, 0),
            )
            for d in (2, 1, 3)
        ]

    def cast_copies(c):
        a, u, v = ROUTES[c]
        plan = (
            (0, 0, 1, 3, 1, 0, 0),
            (0, 0, 1, 1, 3, 1, 2),
            (0, 1, 1, 3, 1, 0, 0),
            (0, 2, 2, 1, 3, 1, 1),
            (0, 2, 2, 3, 1, 0, 2),
            (0, 1, 1, 1, 3, 1, 2),
            (3, 0, 2, 2, 1, 2, 3),
            (1, 2, 2, 2, 3, 2, 3),
        )
        return [
            remote(
                pg[c][src].at[pl.ds(first, size)], pg[c][dst].at[pl.ds(first, size)],
                cast_send.at[c, out], cast_recv.at[c, into], device(v, d, 0),
            )
            for src, first, size, dst, d, out, into in plan
        ]

    def piece(slot, part):
        first, count = PARTS[part]
        return pl.ds(slot * REPLY + first * SPOT, count * SPOT)

    def answer(c, part, d, e):
        a = ROUTES[c][0]
        slot = lax.rem(at[a] + d, LINE) * CORES + lax.rem(core + e, CORES)
        here = at[a] * CORES + core
        src = sb.at[c, piece(slot, part)]
        dst, peer = rb[c].at[piece(here, part)], device(a, d, e)
        if isinstance(d, int) and d == 0 and e == 0:
            return pltpu.make_async_copy(src, dst, own_sem.at[c, part])
        return remote(src, dst, ans_send.at[c, part], ans_recv.at[c, part], peer)

    order = [(d, e) for d in (2, 1, 3, 0) for e in range(CORES)]

    def spread(c):
        a, u, v = ROUTES[c]
        for r in range(COARSE):
            pg[c][0][0, r] = blk[c, id_s[r, 0] & (SITES - 1)]
        for copy in spread_copies(c) + cast_copies(c)[:2]:
            copy.start()

    def cast(c):
        drain(pg[c][1].at[pl.ds(0, 3)], near_sem.at[c, 1])
        for copy in cast_copies(c)[2:6]:
            copy.start()

    def pass_on(c):
        for n in range(2):
            drain(pg[c][0].at[pl.ds(0, 2)], cast_recv.at[c, n])
            cast_copies(c)[6 + n].start()

    def pack(c, d, e, places):
        a, u, v = ROUTES[c]
        n = AXES.index(a)
        q, to = lax.rem(at[a] + d, LINE), lax.rem(core + e, CORES)
        slot = q * CORES + to
        for place in places:
            back = BACKS[place]
            tiles = []
            for ahead in range(LINE):
                whose = {
                    a: at[a],
                    u: lax.rem(at[u] + ahead, LINE),
                    v: lax.rem(at[v] + back, LINE),
                }
                owner = whose["x"] * 32 + whose["z"] * 8 + whose["y"] * 2 + core
                for p in range(2):
                    rank = line_s[n, q, to, p, 0, owner] & (COARSE - 1)
                    tiles.append(pg[c][back][ahead, rank])
            for t, tile in enumerate(tiles):
                sb[c, slot * REPLY + place * SPOT + t] = tile

    def reply(c, part):
        drain(pg[c][0], cast_recv.at[c, 2 + part])
        first, count = PARTS[part]
        places = range(first, first + count)

        def to_other_chip(n, carry):
            k, e = n // CORES, lax.rem(n, CORES)
            d = 2 - k + 3 * (k // 2)
            pack(c, d, e, places)
            answer(c, part, d, e).start()
            return carry

        lax.fori_loop(0, (LINE - 1) * CORES, to_other_chip, 0)
        for e in (1, 0):
            pack(c, 0, e, places)
            answer(c, part, 0, e).start()

    def transpose_in(c):
        loads[c].wait()

        def one(k, carry):
            for x in range(NX):
                for half in range(NY // 8):
                    wa[c, pl.ds(site_row(x, half * 8) + k, 8, stride=KV), :] = stage[
                        c * KV + k, x, pl.ds(half * 8, 8), :
                    ]
            return carry

        lax.fori_loop(0, KV, one, 0)

    def products(c, place):
        b = fine_s[place, 0] & (SITES - 1)
        column = ((b >> 4) & 1) * (ROWS // 2) + (b & (NY - 1))
        values = []
        for t in range(SLOTS):
            found = tgt_s[2 * c + (b >> 5), column + t * NY]
            values.append(rb[c][found].astype(F32))
        values.append(blk[c, b].astype(F32))
        for n, (p, q) in enumerate(PAIRS):
            product = values[p] * values[q]
            product = product[0:8] + product[8:16]
            if c != GRAM_ORDER[0]:
                product = product + part_sums[n, place]
            part_sums[n, place] = product

    def add_products(c):
        def step(g, carry):
            for m in range(4):
                products(c, g * 4 + m)
            return carry

        lax.fori_loop(0, FINE // 4, step, 0)

    def finish():
        sub = lax.broadcasted_iota(jnp.int32, (8, ROWS), 0)
        low4, low2, low1 = sub < 4, (sub & 2) == 0, (sub & 1) == 0

        def merge(first, second, keep_first, shift):
            first = first + pltpu.roll(first, 8 - shift, 0)
            second = second + pltpu.roll(second, shift, 0)
            return jnp.where(keep_first, first, second)

        def group(g, carry):
            total = {}
            spots = [spot_s[0, g * 8 + m] & (SITES - 1) for m in range(8)]
            for n, couple in enumerate(PAIRS):
                rows = [part_sums[n, spot] for spot in spots]
                rows = [
                    jnp.where(low4, rows[m], rows[m + 4])
                    + pltpu.roll(jnp.where(low4, rows[m + 4], rows[m]), 4, 0)
                    for m in range(4)
                ]
                rows = [merge(rows[m], rows[m + 2], low2, 2) for m in range(2)]
                total[couple] = merge(rows[0], rows[1], low1, 1) * (1.0 / VECS)
                if couple[0] == couple[1]:
                    total[couple] = total[couple] + RIDGE
            out = solve_rows(total, [total[s, SLOTS] for s in range(SLOTS)])
            for s in range(SLOTS):
                w_out[s, pl.ds(pl.multiple_of(g * 8, 8), 8), :] = out[s]
            return carry

        lax.fori_loop(0, SITES // 8, group, 0)

    stores = []

    def transpose_out(c, w):

        def one(k, carry):
            for x in range(NX):
                for half in range(NY // 8):
                    stage[c * KV + k, x, pl.ds(half * 8, 8), :] = w[
                        c, pl.ds(site_row(x, half * 8) + k, 8, stride=KV), :
                    ]
            return carry

        lax.fori_loop(0, KV, one, 0)
        part = pl.ds(c * KV, KV)
        store = pltpu.make_async_copy(stage.at[part], sm_out.at[part], out_sem.at[c])
        store.start()
        stores.append(store)

    for c in range(CHUNKS):
        transpose_in(c)
        if c == 0:
            pl.semaphore_wait(barrier, greeted)
        send_faces(0, c, wa)

    for load in coef_loads:
        load.wait()
    ax, ay, az = coef[0], coef[1], coef[2]
    scale = OMEGA / (2.0 * (ax + ay + az) + coef[3])
    ax, ay, az = ax * scale, ay * scale, az * scale
    lane = lax.broadcasted_iota(jnp.int32, az.shape, 2)
    before = jnp.where(lane == 0, 0.0, az)
    after = jnp.where(lane == ROWS - 1, 0.0, az)
    for x in range(NX):
        for y in range(NY):
            for held, value in ((ka, ax), (kb, ay), (km, before), (kp, after)):
                held[x, y] = jnp.broadcast_to(value[x, y : y + 1], (8, ROWS))

    for load in lists:
        load.wait()
    meta[...] = jnp.zeros_like(meta)
    slots = lax.broadcasted_iota(jnp.int32, (SLOTS, NY), 0)
    for x in range(NX):
        live = (cells[0][x] == 0) & (slots < cells[1][x])
        listed = jnp.where(live, cells[2][x] * SITES + cells[3][x], -1)
        for t in range(SLOTS):
            where = pl.ds((x % 2) * (ROWS // 2) + t * NY, NY)
            meta[x // 2 : x // 2 + 1, where] = listed[t : t + 1]
        meta[2:3, pl.ds(x * NY, NY)] = cells[0][x]
    blocks, targets, rank, ids, fine_ids, fine_rank = lists_of(meta[...], at)
    near[at["y"] * CORES + core] = jnp.broadcast_to(rank, (8, ROWS))
    for copy in gather_copies(0):
        copy.start()
    for p in range(2):
        block_cols[p] = jnp.broadcast_to(blocks[p], (ROWS, ROWS))
    idv[:COARSE] = ids
    idv[COARSE : COARSE + FINE] = fine_ids
    idv[COARSE + FINE :] = jnp.broadcast_to(fine_rank, (8, ROWS))
    part_sums[:, FINE] = jnp.zeros((len(PAIRS), 8, ROWS), F32)
    id_copies = [
        pltpu.make_async_copy(idv.at[pl.ds(0, COARSE)], id_s, smem_sem.at[0]),
        pltpu.make_async_copy(idv.at[pl.ds(COARSE, FINE)], fine_s, smem_sem.at[2]),
        pltpu.make_async_copy(idv.at[pl.ds(COARSE + FINE, 8)], spot_s, smem_sem.at[4]),
    ]
    for copy in id_copies:
        copy.start()
    tgt[...] = jnp.zeros_like(tgt)
    for c in range(CHUNKS):
        for h in range(2):
            tgt[2 * c + h : 2 * c + h + 1] = targets[c][h]
        rb[c][EMPTY] = jnp.zeros((KV, ROWS), BF16)
    tgt_copy = pltpu.make_async_copy(tgt, tgt_s, smem_sem.at[3])
    tgt_copy.start()

    for s in range(SWEEPS):
        src, dst = (wb, wa) if s % 2 else (wa, wb)
        for c in range(CHUNKS):
            fill_halo(s, c, src)
            sweep(s, c, src, dst)
            if s == SWEEPS - 1:
                if c == 0:
                    for copy in id_copies:
                        copy.wait()
                spread(c)
            if (s, c) in steps:
                steps[s, c]()
    drain(lines.at[:, pl.ds(0, 3)], table_sem.at[1])
    line_copy = pltpu.make_async_copy(lines, line_s, smem_sem.at[1])
    line_copy.start()
    cast(0)
    cast(1)
    cast(2)
    line_copy.wait()
    for c in range(CHUNKS):
        pass_on(c)
    for c in (1, 2, 0):
        reply(c, 0)
    for c in (1, 0, 2):
        reply(c, 1)
    for c in range(CHUNKS):
        transpose_out(c, wb)
    tgt_copy.wait()
    for c in GRAM_ORDER:
        for part in range(len(PARTS)):
            answer(c, part, 0, 0).wait()
            drain(sb.at[c, pl.ds(0, 7 * PARTS[part][1] * SPOT)], ans_recv.at[c, part])
        add_products(c)
    finish()

    drain(fxs, send_sem.at[0])
    drain(fys, send_sem.at[1])
    pair_copy().wait_send()
    drain(lines.at[:, pl.ds(0, 3)], table_sem.at[0])
    for step in range(3):
        drain(gathered(step), gather_sem.at[step, 0])
    for c in range(CHUNKS):
        drain(pg[c][0].at[pl.ds(0, 3)], near_sem.at[c, 0])
        for n in range(3):
            drain(pg[c][0], cast_send.at[c, n])
        for part in range(len(PARTS)):
            count = PARTS[part][1]
            drain(sb.at[c, pl.ds(0, 7 * count * SPOT)], ans_send.at[c, part])
    for store in stores:
        store.wait()


def smooth(test_vectors, coef_x, coef_y, coef_z, shift, split, count, owner, local):
    vmem = pl.BlockSpec(memory_space=pltpu.VMEM)
    anywhere = pl.BlockSpec(memory_space=pl.ANY)
    cells = pltpu.VMEM((NX, NY, 8, ROWS), F32)
    rows = pltpu.VMEM((LINE, COARSE, KV, ROWS), BF16)
    dma = pltpu.SemaphoreType.DMA
    return pl.pallas_call(
        smooth_kernel,
        out_shape=(
            jax.ShapeDtypeStruct((VECS, NX, NY, ROWS), F32),
            jax.ShapeDtypeStruct((SLOTS, SITES, ROWS), F32),
        ),
        in_specs=[anywhere] * 9,
        out_specs=(anywhere, vmem),
        scratch_shapes=[
            pltpu.VMEM((NX, 1, NY), jnp.int32),
            pltpu.VMEM((NX, 1, NY), jnp.int32),
            pltpu.VMEM((NX, SLOTS, NY), jnp.int32),
            pltpu.VMEM((NX, SLOTS, NY), jnp.int32),
            pltpu.VMEM((8, ROWS), jnp.int32),
            pltpu.VMEM((8, ROWS), jnp.int32),
            pltpu.SMEM((8, ROWS), jnp.int32),
            pltpu.VMEM((CHUNKS, SITES, KV, ROWS), BF16),
            *([pltpu.VMEM((EMPTY + 8, KV, ROWS), BF16)] * CHUNKS),
            pltpu.VMEM((len(PAIRS), SITES, 8, ROWS), F32),
            pltpu.VMEM((VECS, NX, NY, ROWS), F32),
            pltpu.VMEM((4, NX, NY, ROWS), F32),
            pltpu.VMEM((CHUNKS, EXT, ROWS), F32),
            pltpu.VMEM((CHUNKS, EXT, ROWS), F32),
            cells, cells, cells, cells,
            pltpu.VMEM((SWEEPS, CHUNKS, 2, NY * KV, ROWS), BF16),
            pltpu.VMEM((SWEEPS, CHUNKS, 2, NY * KV, ROWS), BF16),
            pltpu.VMEM((SWEEPS, CHUNKS, 2, NX * KV, ROWS), BF16),
            pltpu.VMEM((SWEEPS, CHUNKS, 2, NX * KV, ROWS), BF16),
            pltpu.VMEM((CORES, 2, 1, ROWS), jnp.int32),
            pltpu.VMEM((len(AXES), LINE, CORES, 2, 1, ROWS), jnp.int32),
            pltpu.VMEM((LINE * CORES, 8, ROWS), jnp.int32),
            pltpu.VMEM((LINE, LINE, LINE * CORES, ROWS), jnp.int32),
            pltpu.VMEM((2, ROWS, ROWS), jnp.int32),
            pltpu.VMEM((COARSE + FINE + 8, ROWS), jnp.int32),
            pltpu.SMEM((len(AXES), LINE, CORES, 2, 1, ROWS), jnp.int32),
            pltpu.SMEM((COARSE, ROWS), jnp.int32),
            pltpu.SMEM((FINE, ROWS), jnp.int32),
            pltpu.SMEM((8, ROWS), jnp.int32),
            *([rows] * (LINE * CHUNKS)),
            pltpu.VMEM((CHUNKS, EMPTY, KV, ROWS), BF16),
            dma((CHUNKS,)),
            dma((4,)),
            dma((CHUNKS,)),
            dma((2,)),
            dma((SWEEPS, CHUNKS, 2)),
            dma((2,)),
            dma((2,)),
            dma((3, 2)),
            dma((CHUNKS, 2)),
            dma((CHUNKS, 3)),
            dma((CHUNKS, 4)),
            dma((CHUNKS, len(PARTS))),
            dma((CHUNKS, len(PARTS))),
            dma((CHUNKS, len(PARTS))),
            dma((5,)),
            dma((4,)),
        ],
        compiler_params=pltpu.CompilerParams(
            collective_id=0, has_side_effects=True, vmem_limit_bytes=60 * 1024 * 1024
        ),
        name="smooth",
    )(test_vectors, coef_x, coef_y, coef_z, shift, split, count, owner, local)


def pass_kernel(w_in, sm_in, w_out, sm_out, w_hold, sm_hold, in_sem, out_sem):
    parts = [(w_in, w_hold, w_out)]
    for c in range(CHUNKS):
        part = pl.ds(c * KV, KV)
        parts.append((sm_in.at[part], sm_hold.at[part], sm_out.at[part]))
    ins = [pltpu.make_async_copy(a, b, in_sem.at[n]) for n, (a, b, _) in enumerate(parts)]
    outs = [pltpu.make_async_copy(b, d, out_sem.at[n]) for n, (_, b, d) in enumerate(parts)]
    for copy in ins:
        copy.start()
    for load, store in zip(ins, outs):
        load.wait()
        store.start()
    for store in outs:
        store.wait()


def pass_on_results(weights, sm):
    anywhere = pl.BlockSpec(memory_space=pl.ANY)
    dma = pltpu.SemaphoreType.DMA
    return pl.pallas_call(
        pass_kernel,
        out_shape=(
            jax.ShapeDtypeStruct(weights.shape, F32),
            jax.ShapeDtypeStruct(sm.shape, F32),
        ),
        in_specs=[anywhere, anywhere],
        out_specs=(anywhere, anywhere),
        scratch_shapes=[
            pltpu.VMEM(weights.shape, F32),
            pltpu.VMEM(sm.shape, F32),
            dma((CHUNKS + 1,)),
            dma((CHUNKS + 1,)),
        ],
        compiler_params=pltpu.CompilerParams(vmem_limit_bytes=60 * 1024 * 1024),
        name="fit",
    )(weights, sm)


def per_device(
    test_vectors, coef_x, coef_y, coef_z, shift, cf_split, nbr_count, nbr_owner, nbr_block
):
    sm, weights = smooth(
        test_vectors, coef_x, coef_y, coef_z, shift,
        jnp.swapaxes(cf_split, 1, 2),
        jnp.swapaxes(nbr_count, 1, 2),
        jnp.transpose(nbr_owner, (0, 2, 3, 1)).reshape(NX, SLOTS, NY),
        jnp.transpose(nbr_block, (0, 2, 3, 1)).reshape(NX, SLOTS, NY),
    )
    weights, smoothed = pass_on_results(weights.reshape(SLOTS, NX, NY, ROWS), sm)
    return (smoothed, weights)


def solution(mesh):
    cells = P("gx", "gy", None)
    lists = P("gx", "gy", None, None)
    vectors = P(None, "gx", "gy", None)
    return jax.shard_map(
        per_device,
        mesh=mesh,
        in_specs=(vectors, cells, cells, cells, cells, cells, cells, lists, lists),
        out_specs=(vectors, vectors),
        check_vma=False,
    )
```

```python
import jax
import jax.numpy as jnp
from jax import lax
from jax.experimental import pallas as pl
from jax.experimental.pallas import tpu as pltpu
from jax.sharding import PartitionSpec as P

SLOTS = 4
SWEEPS = 3
ROWS = 128
OMEGA = 0.8
RIDGE = 0.05
VECS = 48
CHUNKS = 3
KV = VECS // CHUNKS
NX = 4
NY = 16
SITES = NX * NY
XROW = (NY + 2) * KV
EXT = (NX + 2) * XROW
GX = 16
GY = 8
MESH = pl.DeviceIdType.MESH
F32 = jnp.float32
BF16 = jnp.bfloat16


def site_row(x, y):
    return (x + 1) * XROW + (y + 1) * KV


def solve_rows(gram, rhs):
    low = [[None] * SLOTS for _ in range(SLOTS)]
    inv = []
    for r in range(SLOTS):
        scaled = []
        diag = gram[r, r]
        for c in range(r):
            rest = gram[r, c]
            for m in range(c):
                rest = rest - scaled[m] * low[c][m]
            scaled.append(rest)
            low[r][c] = rest * inv[c]
            diag = diag - rest * low[r][c]
        inv.append(1.0 / diag)
    fwd = []
    for r in range(SLOTS):
        rest = rhs[r]
        for m in range(r):
            rest = rest - low[r][m] * fwd[m]
        fwd.append(rest)
    out = [None] * SLOTS
    for r in reversed(range(SLOTS)):
        rest = fwd[r] * inv[r]
        for m in range(r + 1, SLOTS):
            rest = rest - low[m][r] * out[m]
        out[r] = rest
    return out


PAIRS = [(s, t) for s in range(SLOTS) for t in range(s + 1)] + [(s, SLOTS) for s in range(SLOTS)]
AXES = "xyz"
LINE = 4
CORES = 2
COARSE = 16
FINE = 48
PLANE = LINE * LINE
ROUTES = (("x", "z", "y"), ("y", "x", "z"), ("z", "y", "x"))
BACKS = (0, 1, 3, 2)
EMPTY = LINE * CORES * PLANE * 2
SPOT = 2 * LINE
GRAM_ORDER = (1, 2, 0)
REPLY = PLANE * 2
PARTS = ((0, 3), (3, 1))


def lists_of(meta, here):
    lane = lax.broadcasted_iota(jnp.int32, (ROWS, ROWS), 1)
    sub = lax.broadcasted_iota(jnp.int32, (ROWS, ROWS), 0)
    diag = lane == sub
    none = 1 << 20

    def column(row):
        return jnp.sum(jnp.where(diag, row, 0), axis=1, keepdims=True)

    members, keys, owners = [], [], []
    for h in range(2):
        entry = meta[h : h + 1]
        owner = entry >> 6
        key = (lane[:1] + h * ROWS) * SITES + (entry & (SITES - 1))
        owners.append(owner)
        keys.append(key)
        members.append(owner == sub)
    first = jnp.minimum(*[jnp.where(m, k, none) for m, k in zip(members, keys)])
    first = jnp.min(first, axis=1, keepdims=True)
    first = jnp.where(first >= none, 0, first)
    second = jnp.maximum(*[jnp.where(m, k, 0) for m, k in zip(members, keys)])
    second = jnp.max(second, axis=1, keepdims=True)
    targets = [[] for _ in ROUTES]
    for h in range(2):
        own = owners[h]
        at_first = jnp.sum(jnp.where(members[h], first, 0), axis=0, keepdims=True)
        place = jnp.where(keys[h] == at_first, 0, 1)
        at = {"x": (own >> 5) & 3, "z": (own >> 3) & 3, "y": (own >> 1) & 3}
        for c, (a, u, v) in enumerate(ROUTES):
            back = (at[v] - here[v]) & 3
            spot = jnp.where(back == 2, 3, jnp.where(back == 3, 2, back))
            slot = ((at[a] * CORES + (own & 1)) * PLANE + spot * LINE + ((at[u] - here[u]) & 3)) * 2 + place
            targets[c].append(jnp.where(own < 0, EMPTY, slot))
    coarse = meta[2:3]
    rank = jnp.sum(jnp.where(sub < lane, column(coarse), 0), axis=0, keepdims=True)
    fine_rank = jnp.minimum(lane[:1] - rank, FINE)
    fine_rank = jnp.where(coarse > 0, FINE, fine_rank)

    def numbers(hit):
        found = jnp.sum(jnp.where(hit, lane[: hit.shape[0]], 0), axis=1, keepdims=True)
        return jnp.broadcast_to(found, hit.shape)

    ids = numbers((rank == sub[:COARSE]) & (coarse > 0))
    fine_ids = numbers((fine_rank == sub[:FINE]) & (lane[:1] < SITES))
    rank = jnp.minimum(rank, COARSE - 1)
    return (first, second), targets, rank, ids, fine_ids, fine_rank


def ranks_wanted(blocks, table):
    lane = lax.broadcasted_iota(jnp.int32, (ROWS, ROWS), 1)
    sub = lax.broadcasted_iota(jnp.int32, (ROWS, ROWS), 0)
    found = jnp.sum(
        jnp.where(lane == (blocks & (SITES - 1)), table, 0), axis=1, keepdims=True
    )
    return jnp.sum(jnp.where(lane == sub, found, 0), axis=0, keepdims=True)


def smooth_kernel(
    tv, cx, cy, cz, sh, split, count, owner, local, sm_out, w_out,
    split_v, count_v, owner_v, local_v, meta, tgt, tgt_s, blk, rb0, rb1, rb2, part_sums, w_hold,
    stage, coef, wa, wb, ka, kb, km, kp, fxs, fxr, fys, fyr,
    pair, lines, near, far, block_cols, idv, line_s, id_s, fine_s, spot_s, p00, p01, p02, p03, p10, p11, p12, p13, p20, p21, p22, p23, sb,
    in_sem, coef_sem, out_sem, send_sem, recv_sem, pair_sem, table_sem, gather_sem,
    near_sem, cast_send, cast_recv, ans_send, ans_recv, own_sem, smem_sem, list_sem, w_sem,
):
    cells = (split_v, count_v, owner_v, local_v)
    rb = (rb0, rb1, rb2)
    pg = ((p00, p01, p02, p03), (p10, p11, p12, p13), (p20, p21, p22, p23))
    i = lax.axis_index("gx")
    j = lax.axis_index("gy")
    core = lax.rem(j, CORES)
    at = {"x": i // LINE, "z": lax.rem(i, LINE), "y": j // CORES}
    peers = (
        (lax.rem(i + GX - 1, GX), j),
        (lax.rem(i + 1, GX), j),
        (i, lax.rem(j + GY - 1, GY)),
        (i, lax.rem(j + 1, GY)),
    )

    def device(axis, d, e):
        moved = dict(at)
        moved[axis] = lax.rem(at[axis] + d, LINE)
        return (moved["x"] * LINE + moved["z"], moved["y"] * CORES + lax.rem(core + e, CORES))

    def remote(src, dst, send, recv, peer):
        return pltpu.make_async_remote_copy(
            src_ref=src, dst_ref=dst, send_sem=send, recv_sem=recv,
            device_id=peer, device_id_type=MESH,
        )

    loads = []
    for c in range(CHUNKS):
        part = pl.ds(c * KV, KV)
        loads.append(pltpu.make_async_copy(tv.at[part], stage.at[part], in_sem.at[c]))
    loads[0].start()
    barrier = pltpu.get_barrier_semaphore()
    for peer in peers[:2]:
        pl.semaphore_signal(barrier, inc=1, device_id=peer, device_id_type=MESH)
    pl.semaphore_signal(barrier, inc=1, device_id=device("x", 0, 1), device_id_type=MESH)
    for axis in AXES:
        for d in range(1, LINE):
            for e in range(CORES):
                pl.semaphore_signal(
                    barrier, inc=1, device_id=device(axis, d, e), device_id_type=MESH
                )
    greeted = 3 + len(AXES) * (LINE - 1) * CORES
    for load in loads[1:]:
        load.start()
    coef_loads = []
    for n, part in enumerate((cx, cy, cz, sh)):
        load = pltpu.make_async_copy(part, coef.at[n], coef_sem.at[n])
        load.start()
        coef_loads.append(load)
    lists = []
    for n, part in enumerate((split, count, owner, local)):
        load = pltpu.make_async_copy(part, cells[n], list_sem.at[n])
        load.start()
        lists.append(load)

    keep = (
        (i > 0).astype(F32),
        (i < GX - 1).astype(F32),
        (j > 0).astype(F32),
        (j < GY - 1).astype(F32),
    )

    def drain(ref, sem):
        pltpu.make_async_copy(ref, ref, sem).wait()

    def copies(s, c):
        out = []
        for d in range(4):
            src, dst = (fxs, fxr) if d < 2 else (fys, fyr)
            out.append(
                remote(
                    src.at[s, c, d % 2], dst.at[s, c, 1 - d % 2],
                    send_sem.at[d // 2], recv_sem.at[s, c, d // 2], peers[d],
                )
            )
        return out

    def send_faces(s, c, w):
        for side in range(2):
            x = side * (NX - 1)
            fxs[s, c, side] = w[c, pl.ds(site_row(x, 0), NY * KV)].astype(BF16)
            y = side * (NY - 1)
            for x in range(NX):
                fys[s, c, side, pl.ds(x * KV, KV)] = w[c, pl.ds(site_row(x, y), KV)].astype(BF16)
        for copy in copies(s, c):
            copy.start()

    def fill_halo(s, c, w):
        drain(fxr.at[s, c], recv_sem.at[s, c, 0])
        drain(fyr.at[s, c], recv_sem.at[s, c, 1])
        for side in range(2):
            x = -1 if side == 0 else NX
            w[c, pl.ds(site_row(x, 0), NY * KV)] = fxr[s, c, side].astype(F32) * keep[side]
            y = -1 if side == 0 else NY
            for x in range(NX):
                w[c, pl.ds(site_row(x, y), KV)] = (
                    fyr[s, c, side, pl.ds(x * KV, KV)].astype(F32) * keep[2 + side]
                )

    def sweep(s, c, src, dst):
        last = s == SWEEPS - 1

        def plane(x, side):
            base = pl.multiple_of(x * XROW, 16)

            def cell(dx, y):
                return src[c, pl.ds(base + site_row(dx, y), KV)].reshape(2, 8, ROWS)

            below, here = cell(0, -1), cell(0, 0)
            for y in range(NY):
                above = cell(0, y + 1)
                new = (
                    ka[x, y] * (cell(-1, y) + cell(1, y))
                    + kb[x, y] * (below + above)
                    + km[x, y] * pltpu.roll(here, 1, 2)
                    + kp[x, y] * pltpu.roll(here, ROWS - 1, 2)
                    + (1.0 - OMEGA) * here
                ).reshape(KV, ROWS)
                dst[c, pl.ds(base + site_row(0, y), KV)] = new
                if last:
                    blk[c, x * NY + y] = new.astype(BF16)
                else:
                    if side is not None:
                        fxs[s + 1, c, side, pl.ds(y * KV, KV)] = new.astype(BF16)
                    if y in (0, NY - 1):
                        rows = pl.ds(pl.multiple_of(x * KV, KV), KV)
                        fys[s + 1, c, y // (NY - 1), rows] = new.astype(BF16)
                below, here = here, above

        def outer(n, carry):
            plane(n * (NX - 1), n)
            return carry

        def inner(n, carry):
            plane(n, None)
            return carry

        lax.fori_loop(0, 2, outer, 0)
        if not last:
            for copy in copies(s + 1, c)[:2]:
                copy.start()
        lax.fori_loop(1, NX - 1, inner, 0)
        if not last:
            for copy in copies(s + 1, c)[2:]:
                copy.start()

    def pair_copy():
        slot = pair.at[core]
        return remote(slot, slot, pair_sem.at[0], pair_sem.at[1], device("x", 0, 1))

    def line_copies():
        return [
            remote(
                pair, lines.at[n, at[axis]], table_sem.at[0], table_sem.at[1],
                device(axis, d, 0),
            )
            for n, axis in enumerate(AXES)
            for d in range(1, LINE)
        ]

    def gather_copies(step):
        send, recv = gather_sem.at[step, 0], gather_sem.at[step, 1]
        if step == 0:
            slot = near.at[at["y"] * CORES + core]
            return [
                remote(slot, slot, send, recv, device("y", d, e))
                for d in range(LINE)
                for e in range(CORES)
                if d or e
            ]
        slot = far.at[at["x"], at["z"]] if step == 1 else far.at[at["x"]]
        return [
            remote(slot, slot, send, recv, device("zx"[step - 1], d, 0)) for d in range(1, LINE)
        ]

    def gathered(step):
        if step == 0:
            return near.at[pl.ds(0, 7)]
        return far.at[0, pl.ds(0, 3)] if step == 1 else far.at[pl.ds(0, 3)]

    def gather_step(step):
        drain(gathered(step), gather_sem.at[step, 1])
        if step == 0:
            for n in range(LINE * CORES):
                far[at["x"], at["z"], n : n + 1] = near[n, 0:1]
        for copy in gather_copies(step + 1):
            copy.start()

    def ask():
        drain(gathered(2), gather_sem.at[2, 1])
        table = far[...].reshape(ROWS, ROWS)
        for p in range(2):
            pair[core, p] = ranks_wanted(block_cols[p], table)
        pair_copy().start()

    def ask_lines():
        pair_copy().wait_recv()
        for copy in line_copies():
            copy.start()
        for n, axis in enumerate(AXES):
            lines[n, at[axis]] = pair[...]

    steps = {
        (0, 1): lambda: gather_step(0),
        (1, 0): lambda: gather_step(1),
        (1, 2): ask,
        (2, 1): ask_lines,
    }

    def spread_copies(c):
        a, u, v = ROUTES[c]
        return [
            remote(
                pg[c][0].at[0], pg[c][0].at[LINE - d],
                near_sem.at[c, 0], near_sem.at[c, 1], device(u, d, 0),
            )
            for d in (2, 1, 3)
        ]

    def cast_copies(c):
        a, u, v = ROUTES[c]
        plan = (
            (0, 0, 1, 3, 1, 0, 0),
            (0, 0, 1, 1, 3, 1, 2),
            (0, 1, 1, 3, 1, 0, 0),
            (0, 2, 2, 1, 3, 1, 1),
            (0, 2, 2, 3, 1, 0, 2),
            (0, 1, 1, 1, 3, 1, 2),
            (3, 0, 2, 2, 1, 2, 3),
            (1, 2, 2, 2, 3, 2, 3),
        )
        return [
            remote(
                pg[c][src].at[pl.ds(first, size)], pg[c][dst].at[pl.ds(first, size)],
                cast_send.at[c, out], cast_recv.at[c, into], device(v, d, 0),
            )
            for src, first, size, dst, d, out, into in plan
        ]

    def piece(slot, part):
        first, count = PARTS[part]
        return pl.ds(slot * REPLY + first * SPOT, count * SPOT)

    def answer(c, part, d, e):
        a = ROUTES[c][0]
        slot = lax.rem(at[a] + d, LINE) * CORES + lax.rem(core + e, CORES)
        here = at[a] * CORES + core
        src = sb.at[c, piece(slot, part)]
        dst, peer = rb[c].at[piece(here, part)], device(a, d, e)
        if isinstance(d, int) and d == 0 and e == 0:
            return pltpu.make_async_copy(src, dst, own_sem.at[c, part])
        return remote(src, dst, ans_send.at[c, part], ans_recv.at[c, part], peer)

    order = [(d, e) for d in (2, 1, 3, 0) for e in range(CORES)]

    def spread(c):
        a, u, v = ROUTES[c]
        for r in range(COARSE):
            pg[c][0][0, r] = blk[c, id_s[r, 0] & (SITES - 1)]
        for copy in spread_copies(c) + cast_copies(c)[:2]:
            copy.start()

    def cast(c):
        drain(pg[c][1].at[pl.ds(0, 3)], near_sem.at[c, 1])
        for copy in cast_copies(c)[2:6]:
            copy.start()

    def pass_on(c):
        for n in range(2):
            drain(pg[c][0].at[pl.ds(0, 2)], cast_recv.at[c, n])
            cast_copies(c)[6 + n].start()

    def pack(c, d, e, places):
        a, u, v = ROUTES[c]
        n = AXES.index(a)
        q, to = lax.rem(at[a] + d, LINE), lax.rem(core + e, CORES)
        slot = q * CORES + to
        for place in places:
            back = BACKS[place]
            tiles = []
            for ahead in range(LINE):
                whose = {
                    a: at[a],
                    u: lax.rem(at[u] + ahead, LINE),
                    v: lax.rem(at[v] + back, LINE),
                }
                owner = whose["x"] * 32 + whose["z"] * 8 + whose["y"] * 2 + core
                for p in range(2):
                    rank = line_s[n, q, to, p, 0, owner] & (COARSE - 1)
                    tiles.append(pg[c][back][ahead, rank])
            for t, tile in enumerate(tiles):
                sb[c, slot * REPLY + place * SPOT + t] = tile

    def reply(c, part):
        drain(pg[c][0], cast_recv.at[c, 2 + part])
        first, count = PARTS[part]
        places = range(first, first + count)

        def to_other_chip(n, carry):
            k, e = n // CORES, lax.rem(n, CORES)
            d = 2 - k + 3 * (k // 2)
            pack(c, d, e, places)
            answer(c, part, d, e).start()
            return carry

        lax.fori_loop(0, (LINE - 1) * CORES, to_other_chip, 0)
        for e in (1, 0):
            pack(c, 0, e, places)
            answer(c, part, 0, e).start()

    def transpose_in(c):
        loads[c].wait()

        def one(k, carry):
            for x in range(NX):
                for half in range(NY // 8):
                    wa[c, pl.ds(site_row(x, half * 8) + k, 8, stride=KV), :] = stage[
                        c * KV + k, x, pl.ds(half * 8, 8), :
                    ]
            return carry

        lax.fori_loop(0, KV, one, 0)

    def products(c, place):
        b = fine_s[place, 0] & (SITES - 1)
        column = ((b >> 4) & 1) * (ROWS // 2) + (b & (NY - 1))
        values = []
        for t in range(SLOTS):
            found = tgt_s[2 * c + (b >> 5), column + t * NY]
            values.append(rb[c][found].astype(F32))
        values.append(blk[c, b].astype(F32))
        for n, (p, q) in enumerate(PAIRS):
            product = values[p] * values[q]
            product = product[0:8] + product[8:16]
            if c != GRAM_ORDER[0]:
                product = product + part_sums[n, place]
            part_sums[n, place] = product

    def add_products(c):
        def step(g, carry):
            for m in range(4):
                products(c, g * 4 + m)
            return carry

        lax.fori_loop(0, FINE // 4, step, 0)

    def w_copy(g):
        rows = pl.ds(pl.multiple_of(g * 8, 8), 8)
        return pltpu.make_async_copy(w_hold.at[:, rows], w_out.at[:, rows], w_sem.at[g])

    def finish():
        sub = lax.broadcasted_iota(jnp.int32, (8, ROWS), 0)
        low4, low2, low1 = sub < 4, (sub & 2) == 0, (sub & 1) == 0

        def merge(first, second, keep_first, shift):
            first = first + pltpu.roll(first, 8 - shift, 0)
            second = second + pltpu.roll(second, shift, 0)
            return jnp.where(keep_first, first, second)

        def group(g, carry):
            total = {}
            spots = [spot_s[0, g * 8 + m] & (SITES - 1) for m in range(8)]
            for n, couple in enumerate(PAIRS):
                rows = [part_sums[n, spot] for spot in spots]
                rows = [
                    jnp.where(low4, rows[m], rows[m + 4])
                    + pltpu.roll(jnp.where(low4, rows[m + 4], rows[m]), 4, 0)
                    for m in range(4)
                ]
                rows = [merge(rows[m], rows[m + 2], low2, 2) for m in range(2)]
                total[couple] = merge(rows[0], rows[1], low1, 1) * (1.0 / VECS)
                if couple[0] == couple[1]:
                    total[couple] = total[couple] + RIDGE
            out = solve_rows(total, [total[s, SLOTS] for s in range(SLOTS)])
            for s in range(SLOTS):
                w_hold[s, pl.ds(pl.multiple_of(g * 8, 8), 8), :] = out[s]
            w_copy(g).start()
            return carry

        lax.fori_loop(0, SITES // 8, group, 0)
        for g in range(SITES // 8):
            w_copy(g).wait()

    stores = []

    def transpose_out(c, w):

        def one(k, carry):
            for x in range(NX):
                for half in range(NY // 8):
                    stage[c * KV + k, x, pl.ds(half * 8, 8), :] = w[
                        c, pl.ds(site_row(x, half * 8) + k, 8, stride=KV), :
                    ]
            return carry

        lax.fori_loop(0, KV, one, 0)
        part = pl.ds(c * KV, KV)
        store = pltpu.make_async_copy(stage.at[part], sm_out.at[part], out_sem.at[c])
        store.start()
        stores.append(store)

    for c in range(CHUNKS):
        transpose_in(c)
        if c == 0:
            pl.semaphore_wait(barrier, greeted)
        send_faces(0, c, wa)

    for load in coef_loads:
        load.wait()
    ax, ay, az = coef[0], coef[1], coef[2]
    scale = OMEGA / (2.0 * (ax + ay + az) + coef[3])
    ax, ay, az = ax * scale, ay * scale, az * scale
    lane = lax.broadcasted_iota(jnp.int32, az.shape, 2)
    before = jnp.where(lane == 0, 0.0, az)
    after = jnp.where(lane == ROWS - 1, 0.0, az)
    for x in range(NX):
        for y in range(NY):
            for held, value in ((ka, ax), (kb, ay), (km, before), (kp, after)):
                held[x, y] = jnp.broadcast_to(value[x, y : y + 1], (8, ROWS))

    for load in lists:
        load.wait()
    meta[...] = jnp.zeros_like(meta)
    slots = lax.broadcasted_iota(jnp.int32, (SLOTS, NY), 0)
    for x in range(NX):
        live = (cells[0][x] == 0) & (slots < cells[1][x])
        listed = jnp.where(live, cells[2][x] * SITES + cells[3][x], -1)
        for t in range(SLOTS):
            where = pl.ds((x % 2) * (ROWS // 2) + t * NY, NY)
            meta[x // 2 : x // 2 + 1, where] = listed[t : t + 1]
        meta[2:3, pl.ds(x * NY, NY)] = cells[0][x]
    blocks, targets, rank, ids, fine_ids, fine_rank = lists_of(meta[...], at)
    near[at["y"] * CORES + core] = jnp.broadcast_to(rank, (8, ROWS))
    for copy in gather_copies(0):
        copy.start()
    for p in range(2):
        block_cols[p] = jnp.broadcast_to(blocks[p], (ROWS, ROWS))
    idv[:COARSE] = ids
    idv[COARSE : COARSE + FINE] = fine_ids
    idv[COARSE + FINE :] = jnp.broadcast_to(fine_rank, (8, ROWS))
    part_sums[:, FINE] = jnp.zeros((len(PAIRS), 8, ROWS), F32)
    id_copies = [
        pltpu.make_async_copy(idv.at[pl.ds(0, COARSE)], id_s, smem_sem.at[0]),
        pltpu.make_async_copy(idv.at[pl.ds(COARSE, FINE)], fine_s, smem_sem.at[2]),
        pltpu.make_async_copy(idv.at[pl.ds(COARSE + FINE, 8)], spot_s, smem_sem.at[4]),
    ]
    for copy in id_copies:
        copy.start()
    tgt[...] = jnp.zeros_like(tgt)
    for c in range(CHUNKS):
        for h in range(2):
            tgt[2 * c + h : 2 * c + h + 1] = targets[c][h]
        rb[c][EMPTY] = jnp.zeros((KV, ROWS), BF16)
    tgt_copy = pltpu.make_async_copy(tgt, tgt_s, smem_sem.at[3])
    tgt_copy.start()

    for s in range(SWEEPS):
        src, dst = (wb, wa) if s % 2 else (wa, wb)
        for c in range(CHUNKS):
            fill_halo(s, c, src)
            sweep(s, c, src, dst)
            if s == SWEEPS - 1:
                if c == 0:
                    for copy in id_copies:
                        copy.wait()
                spread(c)
            if (s, c) in steps:
                steps[s, c]()
    drain(lines.at[:, pl.ds(0, 3)], table_sem.at[1])
    line_copy = pltpu.make_async_copy(lines, line_s, smem_sem.at[1])
    line_copy.start()
    cast(0)
    cast(1)
    cast(2)
    line_copy.wait()
    for c in range(CHUNKS):
        pass_on(c)
    for c in (1, 2, 0):
        reply(c, 0)
    for c in GRAM_ORDER:
        reply(c, 1)
    for c in range(CHUNKS):
        transpose_out(c, wb)
    drain(fxs, send_sem.at[0])
    drain(fys, send_sem.at[1])
    pair_copy().wait_send()
    drain(lines.at[:, pl.ds(0, 3)], table_sem.at[0])
    for step in range(3):
        drain(gathered(step), gather_sem.at[step, 0])
    for c in range(CHUNKS):
        drain(pg[c][0].at[pl.ds(0, 3)], near_sem.at[c, 0])
        for n in range(3):
            drain(pg[c][0], cast_send.at[c, n])
    tgt_copy.wait()
    for c in GRAM_ORDER:
        for part in range(len(PARTS)):
            answer(c, part, 0, 0).wait()
            drain(sb.at[c, pl.ds(0, 7 * PARTS[part][1] * SPOT)], ans_recv.at[c, part])
        add_products(c)
        for part in range(len(PARTS)):
            count = PARTS[part][1]
            drain(sb.at[c, pl.ds(0, 7 * count * SPOT)], ans_send.at[c, part])
    for store in stores:
        store.wait()
    finish()


def smooth(test_vectors, coef_x, coef_y, coef_z, shift, split, count, owner, local):
    vmem = pl.BlockSpec(memory_space=pltpu.VMEM)
    anywhere = pl.BlockSpec(memory_space=pl.ANY)
    cells = pltpu.VMEM((NX, NY, 8, ROWS), F32)
    rows = pltpu.VMEM((LINE, COARSE, KV, ROWS), BF16)
    dma = pltpu.SemaphoreType.DMA
    return pl.pallas_call(
        smooth_kernel,
        out_shape=(
            jax.ShapeDtypeStruct((VECS, NX, NY, ROWS), F32),
            jax.ShapeDtypeStruct((SLOTS, SITES, ROWS), F32),
        ),
        in_specs=[anywhere] * 9,
        out_specs=(anywhere, anywhere),
        scratch_shapes=[
            pltpu.VMEM((NX, 1, NY), jnp.int32),
            pltpu.VMEM((NX, 1, NY), jnp.int32),
            pltpu.VMEM((NX, SLOTS, NY), jnp.int32),
            pltpu.VMEM((NX, SLOTS, NY), jnp.int32),
            pltpu.VMEM((8, ROWS), jnp.int32),
            pltpu.VMEM((8, ROWS), jnp.int32),
            pltpu.SMEM((8, ROWS), jnp.int32),
            pltpu.VMEM((CHUNKS, SITES, KV, ROWS), BF16),
            *([pltpu.VMEM((EMPTY + 8, KV, ROWS), BF16)] * CHUNKS),
            pltpu.VMEM((len(PAIRS), SITES, 8, ROWS), F32),
            pltpu.VMEM((SLOTS, SITES, ROWS), F32),
            pltpu.VMEM((VECS, NX, NY, ROWS), F32),
            pltpu.VMEM((4, NX, NY, ROWS), F32),
            pltpu.VMEM((CHUNKS, EXT, ROWS), F32),
            pltpu.VMEM((CHUNKS, EXT, ROWS), F32),
            cells, cells, cells, cells,
            pltpu.VMEM((SWEEPS, CHUNKS, 2, NY * KV, ROWS), BF16),
            pltpu.VMEM((SWEEPS, CHUNKS, 2, NY * KV, ROWS), BF16),
            pltpu.VMEM((SWEEPS, CHUNKS, 2, NX * KV, ROWS), BF16),
            pltpu.VMEM((SWEEPS, CHUNKS, 2, NX * KV, ROWS), BF16),
            pltpu.VMEM((CORES, 2, 1, ROWS), jnp.int32),
            pltpu.VMEM((len(AXES), LINE, CORES, 2, 1, ROWS), jnp.int32),
            pltpu.VMEM((LINE * CORES, 8, ROWS), jnp.int32),
            pltpu.VMEM((LINE, LINE, LINE * CORES, ROWS), jnp.int32),
            pltpu.VMEM((2, ROWS, ROWS), jnp.int32),
            pltpu.VMEM((COARSE + FINE + 8, ROWS), jnp.int32),
            pltpu.SMEM((len(AXES), LINE, CORES, 2, 1, ROWS), jnp.int32),
            pltpu.SMEM((COARSE, ROWS), jnp.int32),
            pltpu.SMEM((FINE, ROWS), jnp.int32),
            pltpu.SMEM((8, ROWS), jnp.int32),
            *([rows] * (LINE * CHUNKS)),
            pltpu.VMEM((CHUNKS, EMPTY, KV, ROWS), BF16),
            dma((CHUNKS,)),
            dma((4,)),
            dma((CHUNKS,)),
            dma((2,)),
            dma((SWEEPS, CHUNKS, 2)),
            dma((2,)),
            dma((2,)),
            dma((3, 2)),
            dma((CHUNKS, 2)),
            dma((CHUNKS, 3)),
            dma((CHUNKS, 4)),
            dma((CHUNKS, len(PARTS))),
            dma((CHUNKS, len(PARTS))),
            dma((CHUNKS, len(PARTS))),
            dma((5,)),
            dma((4,)),
            dma((SITES // 8,)),
        ],
        compiler_params=pltpu.CompilerParams(
            collective_id=0, has_side_effects=True, vmem_limit_bytes=60 * 1024 * 1024
        ),
        name="smooth",
    )(test_vectors, coef_x, coef_y, coef_z, shift, split, count, owner, local)


def pass_kernel(w_in, sm_in, w_out, sm_out, w_hold, sm_hold, in_sem, out_sem):
    parts = [(w_in, w_hold, w_out)]
    for c in range(CHUNKS):
        part = pl.ds(c * KV, KV)
        parts.append((sm_in.at[part], sm_hold.at[part], sm_out.at[part]))
    ins = [pltpu.make_async_copy(a, b, in_sem.at[n]) for n, (a, b, _) in enumerate(parts)]
    outs = [pltpu.make_async_copy(b, d, out_sem.at[n]) for n, (_, b, d) in enumerate(parts)]
    for copy in ins:
        copy.start()
    for load, store in zip(ins, outs):
        load.wait()
        store.start()
    for store in outs:
        store.wait()


def pass_on_results(weights, sm):
    anywhere = pl.BlockSpec(memory_space=pl.ANY)
    dma = pltpu.SemaphoreType.DMA
    return pl.pallas_call(
        pass_kernel,
        out_shape=(
            jax.ShapeDtypeStruct(weights.shape, F32),
            jax.ShapeDtypeStruct(sm.shape, F32),
        ),
        in_specs=[anywhere, anywhere],
        out_specs=(anywhere, anywhere),
        scratch_shapes=[
            pltpu.VMEM(weights.shape, F32),
            pltpu.VMEM(sm.shape, F32),
            dma((CHUNKS + 1,)),
            dma((CHUNKS + 1,)),
        ],
        compiler_params=pltpu.CompilerParams(vmem_limit_bytes=60 * 1024 * 1024),
        name="fit",
    )(weights, sm)


def per_device(
    test_vectors, coef_x, coef_y, coef_z, shift, cf_split, nbr_count, nbr_owner, nbr_block
):
    sm, weights = smooth(
        test_vectors, coef_x, coef_y, coef_z, shift,
        jnp.swapaxes(cf_split, 1, 2),
        jnp.swapaxes(nbr_count, 1, 2),
        jnp.transpose(nbr_owner, (0, 2, 3, 1)).reshape(NX, SLOTS, NY),
        jnp.transpose(nbr_block, (0, 2, 3, 1)).reshape(NX, SLOTS, NY),
    )
    weights, smoothed = pass_on_results(weights.reshape(SLOTS, NX, NY, ROWS), sm)
    return (smoothed, weights)


def solution(mesh):
    cells = P("gx", "gy", None)
    lists = P("gx", "gy", None, None)
    vectors = P(None, "gx", "gy", None)
    return jax.shard_map(
        per_device,
        mesh=mesh,
        in_specs=(vectors, cells, cells, cells, cells, cells, cells, lists, lists),
        out_specs=(vectors, vectors),
        check_vma=False,
    )
```

```python
import jax
import jax.numpy as jnp
from jax import lax
from jax.experimental import pallas as pl
from jax.experimental.pallas import tpu as pltpu
from jax.sharding import PartitionSpec as P

SLOTS = 4
SWEEPS = 3
ROWS = 128
OMEGA = 0.8
RIDGE = 0.05
VECS = 48
CHUNKS = 3
KV = VECS // CHUNKS
NX = 4
NY = 16
SITES = NX * NY
XROW = (NY + 2) * KV
EXT = (NX + 2) * XROW
GX = 16
GY = 8
MESH = pl.DeviceIdType.MESH
F32 = jnp.float32
BF16 = jnp.bfloat16


def site_row(x, y):
    return (x + 1) * XROW + (y + 1) * KV


def solve_rows(gram, rhs):
    low = [[None] * SLOTS for _ in range(SLOTS)]
    inv = []
    for r in range(SLOTS):
        scaled = []
        diag = gram[r, r]
        for c in range(r):
            rest = gram[r, c]
            for m in range(c):
                rest = rest - scaled[m] * low[c][m]
            scaled.append(rest)
            low[r][c] = rest * inv[c]
            diag = diag - rest * low[r][c]
        inv.append(1.0 / diag)
    fwd = []
    for r in range(SLOTS):
        rest = rhs[r]
        for m in range(r):
            rest = rest - low[r][m] * fwd[m]
        fwd.append(rest)
    out = [None] * SLOTS
    for r in reversed(range(SLOTS)):
        rest = fwd[r] * inv[r]
        for m in range(r + 1, SLOTS):
            rest = rest - low[m][r] * out[m]
        out[r] = rest
    return out


PAIRS = [(s, t) for s in range(SLOTS) for t in range(s + 1)] + [(s, SLOTS) for s in range(SLOTS)]
AXES = "xyz"
LINE = 4
CORES = 2
COARSE = 16
FINE = 48
PLANE = LINE * LINE
ROUTES = (("x", "z", "y"), ("y", "x", "z"), ("z", "y", "x"))
BACKS = (0, 1, 3, 2)
EMPTY = LINE * CORES * PLANE * 2
SPOT = 2 * LINE
GRAM_ORDER = (1, 2, 0)
REPLY = PLANE * 2
PARTS = ((0, 3), (3, 1))


def lists_of(meta, here):
    lane = lax.broadcasted_iota(jnp.int32, (ROWS, ROWS), 1)
    sub = lax.broadcasted_iota(jnp.int32, (ROWS, ROWS), 0)
    diag = lane == sub
    none = 1 << 20

    def column(row):
        return jnp.sum(jnp.where(diag, row, 0), axis=1, keepdims=True)

    members, keys, owners = [], [], []
    for h in range(2):
        entry = meta[h : h + 1]
        owner = entry >> 6
        key = (lane[:1] + h * ROWS) * SITES + (entry & (SITES - 1))
        owners.append(owner)
        keys.append(key)
        members.append(owner == sub)
    first = jnp.minimum(*[jnp.where(m, k, none) for m, k in zip(members, keys)])
    first = jnp.min(first, axis=1, keepdims=True)
    first = jnp.where(first >= none, 0, first)
    second = jnp.maximum(*[jnp.where(m, k, 0) for m, k in zip(members, keys)])
    second = jnp.max(second, axis=1, keepdims=True)
    targets = [[] for _ in ROUTES]
    for h in range(2):
        own = owners[h]
        at_first = jnp.sum(jnp.where(members[h], first, 0), axis=0, keepdims=True)
        place = jnp.where(keys[h] == at_first, 0, 1)
        at = {"x": (own >> 5) & 3, "z": (own >> 3) & 3, "y": (own >> 1) & 3}
        for c, (a, u, v) in enumerate(ROUTES):
            back = (at[v] - here[v]) & 3
            spot = jnp.where(back == 2, 3, jnp.where(back == 3, 2, back))
            slot = ((at[a] * CORES + (own & 1)) * PLANE + spot * LINE + ((at[u] - here[u]) & 3)) * 2 + place
            targets[c].append(jnp.where(own < 0, EMPTY, slot))
    coarse = meta[2:3]
    rank = jnp.sum(jnp.where(sub < lane, column(coarse), 0), axis=0, keepdims=True)
    fine_rank = jnp.minimum(lane[:1] - rank, FINE)
    fine_rank = jnp.where(coarse > 0, FINE, fine_rank)

    def numbers(hit):
        found = jnp.sum(jnp.where(hit, lane[: hit.shape[0]], 0), axis=1, keepdims=True)
        return jnp.broadcast_to(found, hit.shape)

    ids = numbers((rank == sub[:COARSE]) & (coarse > 0))
    fine_ids = numbers((fine_rank == sub[:FINE]) & (lane[:1] < SITES))
    rank = jnp.minimum(rank, COARSE - 1)
    return (first, second), targets, rank, ids, fine_ids, fine_rank


def ranks_wanted(blocks, table):
    lane = lax.broadcasted_iota(jnp.int32, (ROWS, ROWS), 1)
    sub = lax.broadcasted_iota(jnp.int32, (ROWS, ROWS), 0)
    found = jnp.sum(
        jnp.where(lane == (blocks & (SITES - 1)), table, 0), axis=1, keepdims=True
    )
    return jnp.sum(jnp.where(lane == sub, found, 0), axis=0, keepdims=True)


def smooth_kernel(
    tv, cx, cy, cz, sh, split, count, owner, local, sm_out, w_out,
    split_v, count_v, owner_v, local_v, meta, tgt, tgt_s, blk, rb0, rb1, rb2, part_sums, w_hold,
    stage, coef, wa, wb, ka, kb, km, kp, fxs, fxr, fys, fyr,
    pair, lines, near, far, block_cols, idv, line_s, id_s, fine_s, spot_s, p00, p01, p02, p03, p10, p11, p12, p13, p20, p21, p22, p23, sb,
    in_sem, coef_sem, out_sem, send_sem, recv_sem, pair_sem, table_sem, gather_sem,
    near_sem, cast_send, cast_recv, ans_send, ans_recv, own_sem, smem_sem, list_sem, w_sem,
):
    cells = (split_v, count_v, owner_v, local_v)
    rb = (rb0, rb1, rb2)
    pg = ((p00, p01, p02, p03), (p10, p11, p12, p13), (p20, p21, p22, p23))
    i = lax.axis_index("gx")
    j = lax.axis_index("gy")
    core = lax.rem(j, CORES)
    at = {"x": i // LINE, "z": lax.rem(i, LINE), "y": j // CORES}
    peers = (
        (lax.rem(i + GX - 1, GX), j),
        (lax.rem(i + 1, GX), j),
        (i, lax.rem(j + GY - 1, GY)),
        (i, lax.rem(j + 1, GY)),
    )

    def device(axis, d, e):
        moved = dict(at)
        moved[axis] = lax.rem(at[axis] + d, LINE)
        return (moved["x"] * LINE + moved["z"], moved["y"] * CORES + lax.rem(core + e, CORES))

    def remote(src, dst, send, recv, peer):
        return pltpu.make_async_remote_copy(
            src_ref=src, dst_ref=dst, send_sem=send, recv_sem=recv,
            device_id=peer, device_id_type=MESH,
        )

    loads = []
    for c in range(CHUNKS):
        part = pl.ds(c * KV, KV)
        loads.append(pltpu.make_async_copy(tv.at[part], stage.at[part], in_sem.at[c]))
    loads[0].start()
    barrier = pltpu.get_barrier_semaphore()
    for peer in peers[:2]:
        pl.semaphore_signal(barrier, inc=1, device_id=peer, device_id_type=MESH)
    pl.semaphore_signal(barrier, inc=1, device_id=device("x", 0, 1), device_id_type=MESH)
    for axis in AXES:
        for d in range(1, LINE):
            for e in range(CORES):
                pl.semaphore_signal(
                    barrier, inc=1, device_id=device(axis, d, e), device_id_type=MESH
                )
    greeted = 3 + len(AXES) * (LINE - 1) * CORES
    for load in loads[1:]:
        load.start()
    coef_loads = []
    for n, part in enumerate((cx, cy, cz, sh)):
        load = pltpu.make_async_copy(part, coef.at[n], coef_sem.at[n])
        load.start()
        coef_loads.append(load)
    lists = []
    for n, part in enumerate((split, count, owner, local)):
        load = pltpu.make_async_copy(part, cells[n], list_sem.at[n])
        load.start()
        lists.append(load)

    keep = (
        (i > 0).astype(F32),
        (i < GX - 1).astype(F32),
        (j > 0).astype(F32),
        (j < GY - 1).astype(F32),
    )

    def drain(ref, sem):
        pltpu.make_async_copy(ref, ref, sem).wait()

    def copies(s, c):
        out = []
        for d in range(4):
            src, dst = (fxs, fxr) if d < 2 else (fys, fyr)
            out.append(
                remote(
                    src.at[s, c, d % 2], dst.at[s, c, 1 - d % 2],
                    send_sem.at[d // 2], recv_sem.at[s, c, d // 2], peers[d],
                )
            )
        return out

    def send_faces(s, c, w):
        for side in range(2):
            x = side * (NX - 1)
            fxs[s, c, side] = w[c, pl.ds(site_row(x, 0), NY * KV)].astype(BF16)
            y = side * (NY - 1)
            for x in range(NX):
                fys[s, c, side, pl.ds(x * KV, KV)] = w[c, pl.ds(site_row(x, y), KV)].astype(BF16)
        for copy in copies(s, c):
            copy.start()

    def fill_halo(s, c, w):
        drain(fxr.at[s, c], recv_sem.at[s, c, 0])
        drain(fyr.at[s, c], recv_sem.at[s, c, 1])
        for side in range(2):
            x = -1 if side == 0 else NX
            w[c, pl.ds(site_row(x, 0), NY * KV)] = fxr[s, c, side].astype(F32) * keep[side]
            y = -1 if side == 0 else NY
            for x in range(NX):
                w[c, pl.ds(site_row(x, y), KV)] = (
                    fyr[s, c, side, pl.ds(x * KV, KV)].astype(F32) * keep[2 + side]
                )

    def sweep(s, c, src, dst):
        last = s == SWEEPS - 1

        def plane(x, side):
            base = pl.multiple_of(x * XROW, 16)

            def cell(dx, y):
                return src[c, pl.ds(base + site_row(dx, y), KV)].reshape(2, 8, ROWS)

            below, here = cell(0, -1), cell(0, 0)
            for y in range(NY):
                above = cell(0, y + 1)
                new = (
                    ka[x, y] * (cell(-1, y) + cell(1, y))
                    + kb[x, y] * (below + above)
                    + km[x, y] * pltpu.roll(here, 1, 2)
                    + kp[x, y] * pltpu.roll(here, ROWS - 1, 2)
                    + (1.0 - OMEGA) * here
                ).reshape(KV, ROWS)
                dst[c, pl.ds(base + site_row(0, y), KV)] = new
                if last:
                    blk[c, x * NY + y] = new.astype(BF16)
                else:
                    if side is not None:
                        fxs[s + 1, c, side, pl.ds(y * KV, KV)] = new.astype(BF16)
                    if y in (0, NY - 1):
                        rows = pl.ds(pl.multiple_of(x * KV, KV), KV)
                        fys[s + 1, c, y // (NY - 1), rows] = new.astype(BF16)
                below, here = here, above

        def outer(n, carry):
            plane(n * (NX - 1), n)
            return carry

        def inner(n, carry):
            plane(n, None)
            return carry

        lax.fori_loop(0, 2, outer, 0)
        if not last:
            for copy in copies(s + 1, c)[:2]:
                copy.start()
        lax.fori_loop(1, NX - 1, inner, 0)
        if not last:
            for copy in copies(s + 1, c)[2:]:
                copy.start()

    def pair_copy():
        slot = pair.at[core]
        return remote(slot, slot, pair_sem.at[0], pair_sem.at[1], device("x", 0, 1))

    def line_copies():
        return [
            remote(
                pair, lines.at[n, at[axis]], table_sem.at[0], table_sem.at[1],
                device(axis, d, 0),
            )
            for n, axis in enumerate(AXES)
            for d in range(1, LINE)
        ]

    def gather_copies(step):
        send, recv = gather_sem.at[step, 0], gather_sem.at[step, 1]
        if step == 0:
            slot = near.at[at["y"] * CORES + core]
            return [
                remote(slot, slot, send, recv, device("y", d, e))
                for d in range(LINE)
                for e in range(CORES)
                if d or e
            ]
        slot = far.at[at["x"], at["z"]] if step == 1 else far.at[at["x"]]
        return [
            remote(slot, slot, send, recv, device("zx"[step - 1], d, 0)) for d in range(1, LINE)
        ]

    def gathered(step):
        if step == 0:
            return near.at[pl.ds(0, 7)]
        return far.at[0, pl.ds(0, 3)] if step == 1 else far.at[pl.ds(0, 3)]

    def gather_step(step):
        drain(gathered(step), gather_sem.at[step, 1])
        if step == 0:
            for n in range(LINE * CORES):
                far[at["x"], at["z"], n : n + 1] = near[n, 0:1]
        for copy in gather_copies(step + 1):
            copy.start()

    def ask():
        drain(gathered(2), gather_sem.at[2, 1])
        table = far[...].reshape(ROWS, ROWS)
        for p in range(2):
            pair[core, p] = ranks_wanted(block_cols[p], table)
        pair_copy().start()

    def ask_lines():
        pair_copy().wait_recv()
        for copy in line_copies():
            copy.start()
        for n, axis in enumerate(AXES):
            lines[n, at[axis]] = pair[...]

    steps = {
        (0, 1): lambda: gather_step(0),
        (1, 0): lambda: gather_step(1),
        (1, 2): ask,
        (2, 1): ask_lines,
    }

    def spread_copies(c):
        a, u, v = ROUTES[c]
        return [
            remote(
                pg[c][0].at[0], pg[c][0].at[LINE - d],
                near_sem.at[c, 0], near_sem.at[c, 1], device(u, d, 0),
            )
            for d in (2, 1, 3)
        ]

    def cast_copies(c):
        a, u, v = ROUTES[c]
        plan = (
            (0, 0, 1, 3, 1, 0, 0),
            (0, 0, 1, 1, 3, 1, 2),
            (0, 1, 1, 3, 1, 0, 0),
            (0, 2, 2, 1, 3, 1, 1),
            (0, 2, 2, 3, 1, 0, 2),
            (0, 1, 1, 1, 3, 1, 2),
            (3, 0, 2, 2, 1, 2, 3),
            (1, 2, 2, 2, 3, 2, 3),
        )
        return [
            remote(
                pg[c][src].at[pl.ds(first, size)], pg[c][dst].at[pl.ds(first, size)],
                cast_send.at[c, out], cast_recv.at[c, into], device(v, d, 0),
            )
            for src, first, size, dst, d, out, into in plan
        ]

    def piece(slot, part):
        first, count = PARTS[part]
        return pl.ds(slot * REPLY + first * SPOT, count * SPOT)

    def answer(c, part, d, e):
        a = ROUTES[c][0]
        slot = lax.rem(at[a] + d, LINE) * CORES + lax.rem(core + e, CORES)
        here = at[a] * CORES + core
        src = sb.at[c, piece(slot, part)]
        dst, peer = rb[c].at[piece(here, part)], device(a, d, e)
        if isinstance(d, int) and d == 0 and e == 0:
            return pltpu.make_async_copy(src, dst, own_sem.at[c, part])
        return remote(src, dst, ans_send.at[c, part], ans_recv.at[c, part], peer)

    order = [(d, e) for d in (2, 1, 3, 0) for e in range(CORES)]

    def spread(c):
        a, u, v = ROUTES[c]
        for r in range(COARSE):
            pg[c][0][0, r] = blk[c, id_s[r, 0] & (SITES - 1)]
        for copy in spread_copies(c) + cast_copies(c)[:2]:
            copy.start()

    def cast(c):
        drain(pg[c][1].at[pl.ds(0, 3)], near_sem.at[c, 1])
        for copy in cast_copies(c)[2:6]:
            copy.start()

    def pass_on(c):
        for n in range(2):
            drain(pg[c][0].at[pl.ds(0, 2)], cast_recv.at[c, n])
            cast_copies(c)[6 + n].start()

    def pack(c, d, e, places):
        a, u, v = ROUTES[c]
        n = AXES.index(a)
        q, to = lax.rem(at[a] + d, LINE), lax.rem(core + e, CORES)
        slot = q * CORES + to
        for place in places:
            back = BACKS[place]
            tiles = []
            for ahead in range(LINE):
                whose = {
                    a: at[a],
                    u: lax.rem(at[u] + ahead, LINE),
                    v: lax.rem(at[v] + back, LINE),
                }
                owner = whose["x"] * 32 + whose["z"] * 8 + whose["y"] * 2 + core
                for p in range(2):
                    rank = line_s[n, q, to, p, 0, owner] & (COARSE - 1)
                    tiles.append(pg[c][back][ahead, rank])
            for t, tile in enumerate(tiles):
                sb[c, slot * REPLY + place * SPOT + t] = tile

    def pack_own(c):
        def one(n, carry):
            pack(c, n // CORES, lax.rem(n, CORES), (0,))
            return carry

        lax.fori_loop(0, LINE * CORES, one, 0)

    def reply(c, part):
        drain(pg[c][0], cast_recv.at[c, 2 + part])
        first, count = PARTS[part]
        places = range(max(first, 1), first + count)

        def to_other_chip(n, carry):
            k, e = n // CORES, lax.rem(n, CORES)
            d = 2 - k + 3 * (k // 2)
            pack(c, d, e, places)
            answer(c, part, d, e).start()
            return carry

        lax.fori_loop(0, (LINE - 1) * CORES, to_other_chip, 0)
        for e in (1, 0):
            pack(c, 0, e, places)
            answer(c, part, 0, e).start()

    def transpose_in(c):
        loads[c].wait()

        def one(k, carry):
            for x in range(NX):
                for half in range(NY // 8):
                    wa[c, pl.ds(site_row(x, half * 8) + k, 8, stride=KV), :] = stage[
                        c * KV + k, x, pl.ds(half * 8, 8), :
                    ]
            return carry

        lax.fori_loop(0, KV, one, 0)

    def products(c, place):
        b = fine_s[place, 0] & (SITES - 1)
        column = ((b >> 4) & 1) * (ROWS // 2) + (b & (NY - 1))
        values = []
        for t in range(SLOTS):
            found = tgt_s[2 * c + (b >> 5), column + t * NY]
            values.append(rb[c][found].astype(F32))
        values.append(blk[c, b].astype(F32))
        for n, (p, q) in enumerate(PAIRS):
            product = values[p] * values[q]
            product = product[0:8] + product[8:16]
            if c != GRAM_ORDER[0]:
                product = product + part_sums[n, place]
            part_sums[n, place] = product

    def add_products(c):
        def step(g, carry):
            for m in range(4):
                products(c, g * 4 + m)
            return carry

        lax.fori_loop(0, FINE // 4, step, 0)

    def w_copy(g):
        rows = pl.ds(pl.multiple_of(g * 8, 8), 8)
        return pltpu.make_async_copy(w_hold.at[:, rows], w_out.at[:, rows], w_sem.at[g])

    def finish():
        sub = lax.broadcasted_iota(jnp.int32, (8, ROWS), 0)
        low4, low2, low1 = sub < 4, (sub & 2) == 0, (sub & 1) == 0

        def merge(first, second, keep_first, shift):
            first = first + pltpu.roll(first, 8 - shift, 0)
            second = second + pltpu.roll(second, shift, 0)
            return jnp.where(keep_first, first, second)

        def group(g, carry):
            total = {}
            spots = [spot_s[0, g * 8 + m] & (SITES - 1) for m in range(8)]
            for n, couple in enumerate(PAIRS):
                rows = [part_sums[n, spot] for spot in spots]
                rows = [
                    jnp.where(low4, rows[m], rows[m + 4])
                    + pltpu.roll(jnp.where(low4, rows[m + 4], rows[m]), 4, 0)
                    for m in range(4)
                ]
                rows = [merge(rows[m], rows[m + 2], low2, 2) for m in range(2)]
                total[couple] = merge(rows[0], rows[1], low1, 1) * (1.0 / VECS)
                if couple[0] == couple[1]:
                    total[couple] = total[couple] + RIDGE
            out = solve_rows(total, [total[s, SLOTS] for s in range(SLOTS)])
            for s in range(SLOTS):
                w_hold[s, pl.ds(pl.multiple_of(g * 8, 8), 8), :] = out[s]
            w_copy(g).start()
            return carry

        lax.fori_loop(0, SITES // 8, group, 0)
        for g in range(SITES // 8):
            w_copy(g).wait()

    stores = []

    def transpose_out(c, w):

        def one(k, carry):
            for x in range(NX):
                for half in range(NY // 8):
                    stage[c * KV + k, x, pl.ds(half * 8, 8), :] = w[
                        c, pl.ds(site_row(x, half * 8) + k, 8, stride=KV), :
                    ]
            return carry

        lax.fori_loop(0, KV, one, 0)
        part = pl.ds(c * KV, KV)
        store = pltpu.make_async_copy(stage.at[part], sm_out.at[part], out_sem.at[c])
        store.start()
        stores.append(store)

    for c in range(CHUNKS):
        transpose_in(c)
        if c == 0:
            pl.semaphore_wait(barrier, greeted)
        send_faces(0, c, wa)

    for load in coef_loads:
        load.wait()
    ax, ay, az = coef[0], coef[1], coef[2]
    scale = OMEGA / (2.0 * (ax + ay + az) + coef[3])
    ax, ay, az = ax * scale, ay * scale, az * scale
    lane = lax.broadcasted_iota(jnp.int32, az.shape, 2)
    before = jnp.where(lane == 0, 0.0, az)
    after = jnp.where(lane == ROWS - 1, 0.0, az)
    for x in range(NX):
        for y in range(NY):
            for held, value in ((ka, ax), (kb, ay), (km, before), (kp, after)):
                held[x, y] = jnp.broadcast_to(value[x, y : y + 1], (8, ROWS))

    for load in lists:
        load.wait()
    meta[...] = jnp.zeros_like(meta)
    slots = lax.broadcasted_iota(jnp.int32, (SLOTS, NY), 0)
    for x in range(NX):
        live = (cells[0][x] == 0) & (slots < cells[1][x])
        listed = jnp.where(live, cells[2][x] * SITES + cells[3][x], -1)
        for t in range(SLOTS):
            where = pl.ds((x % 2) * (ROWS // 2) + t * NY, NY)
            meta[x // 2 : x // 2 + 1, where] = listed[t : t + 1]
        meta[2:3, pl.ds(x * NY, NY)] = cells[0][x]
    blocks, targets, rank, ids, fine_ids, fine_rank = lists_of(meta[...], at)
    near[at["y"] * CORES + core] = jnp.broadcast_to(rank, (8, ROWS))
    for copy in gather_copies(0):
        copy.start()
    for p in range(2):
        block_cols[p] = jnp.broadcast_to(blocks[p], (ROWS, ROWS))
    idv[:COARSE] = ids
    idv[COARSE : COARSE + FINE] = fine_ids
    idv[COARSE + FINE :] = jnp.broadcast_to(fine_rank, (8, ROWS))
    part_sums[:, FINE] = jnp.zeros((len(PAIRS), 8, ROWS), F32)
    id_copies = [
        pltpu.make_async_copy(idv.at[pl.ds(0, COARSE)], id_s, smem_sem.at[0]),
        pltpu.make_async_copy(idv.at[pl.ds(COARSE, FINE)], fine_s, smem_sem.at[2]),
        pltpu.make_async_copy(idv.at[pl.ds(COARSE + FINE, 8)], spot_s, smem_sem.at[4]),
    ]
    for copy in id_copies:
        copy.start()
    tgt[...] = jnp.zeros_like(tgt)
    for c in range(CHUNKS):
        for h in range(2):
            tgt[2 * c + h : 2 * c + h + 1] = targets[c][h]
        rb[c][EMPTY] = jnp.zeros((KV, ROWS), BF16)
    tgt_copy = pltpu.make_async_copy(tgt, tgt_s, smem_sem.at[3])
    tgt_copy.start()

    for s in range(SWEEPS):
        src, dst = (wb, wa) if s % 2 else (wa, wb)
        for c in range(CHUNKS):
            fill_halo(s, c, src)
            sweep(s, c, src, dst)
            if s == SWEEPS - 1:
                if c == 0:
                    for copy in id_copies:
                        copy.wait()
                spread(c)
            if (s, c) in steps:
                steps[s, c]()
    drain(lines.at[:, pl.ds(0, 3)], table_sem.at[1])
    line_copy = pltpu.make_async_copy(lines, line_s, smem_sem.at[1])
    line_copy.start()
    cast(0)
    cast(1)
    cast(2)
    line_copy.wait()
    for c in range(CHUNKS):
        pack_own(c)
    for c in range(CHUNKS):
        pass_on(c)
    for c in (1, 2, 0):
        reply(c, 0)
    for c in GRAM_ORDER:
        reply(c, 1)
    for c in range(CHUNKS):
        transpose_out(c, wb)
    drain(fxs, send_sem.at[0])
    drain(fys, send_sem.at[1])
    pair_copy().wait_send()
    drain(lines.at[:, pl.ds(0, 3)], table_sem.at[0])
    for step in range(3):
        drain(gathered(step), gather_sem.at[step, 0])
    for c in range(CHUNKS):
        drain(pg[c][0].at[pl.ds(0, 3)], near_sem.at[c, 0])
        for n in range(3):
            drain(pg[c][0], cast_send.at[c, n])
    tgt_copy.wait()
    for c in GRAM_ORDER:
        for part in range(len(PARTS)):
            answer(c, part, 0, 0).wait()
            drain(sb.at[c, pl.ds(0, 7 * PARTS[part][1] * SPOT)], ans_recv.at[c, part])
        add_products(c)
        for part in range(len(PARTS)):
            count = PARTS[part][1]
            drain(sb.at[c, pl.ds(0, 7 * count * SPOT)], ans_send.at[c, part])
    for store in stores:
        store.wait()
    finish()


def smooth(test_vectors, coef_x, coef_y, coef_z, shift, split, count, owner, local):
    vmem = pl.BlockSpec(memory_space=pltpu.VMEM)
    anywhere = pl.BlockSpec(memory_space=pl.ANY)
    cells = pltpu.VMEM((NX, NY, 8, ROWS), F32)
    rows = pltpu.VMEM((LINE, COARSE, KV, ROWS), BF16)
    dma = pltpu.SemaphoreType.DMA
    return pl.pallas_call(
        smooth_kernel,
        out_shape=(
            jax.ShapeDtypeStruct((VECS, NX, NY, ROWS), F32),
            jax.ShapeDtypeStruct((SLOTS, SITES, ROWS), F32),
        ),
        in_specs=[anywhere] * 9,
        out_specs=(anywhere, anywhere),
        scratch_shapes=[
            pltpu.VMEM((NX, 1, NY), jnp.int32),
            pltpu.VMEM((NX, 1, NY), jnp.int32),
            pltpu.VMEM((NX, SLOTS, NY), jnp.int32),
            pltpu.VMEM((NX, SLOTS, NY), jnp.int32),
            pltpu.VMEM((8, ROWS), jnp.int32),
            pltpu.VMEM((8, ROWS), jnp.int32),
            pltpu.SMEM((8, ROWS), jnp.int32),
            pltpu.VMEM((CHUNKS, SITES, KV, ROWS), BF16),
            *([pltpu.VMEM((EMPTY + 8, KV, ROWS), BF16)] * CHUNKS),
            pltpu.VMEM((len(PAIRS), SITES, 8, ROWS), F32),
            pltpu.VMEM((SLOTS, SITES, ROWS), F32),
            pltpu.VMEM((VECS, NX, NY, ROWS), F32),
            pltpu.VMEM((4, NX, NY, ROWS), F32),
            pltpu.VMEM((CHUNKS, EXT, ROWS), F32),
            pltpu.VMEM((CHUNKS, EXT, ROWS), F32),
            cells, cells, cells, cells,
            pltpu.VMEM((SWEEPS, CHUNKS, 2, NY * KV, ROWS), BF16),
            pltpu.VMEM((SWEEPS, CHUNKS, 2, NY * KV, ROWS), BF16),
            pltpu.VMEM((SWEEPS, CHUNKS, 2, NX * KV, ROWS), BF16),
            pltpu.VMEM((SWEEPS, CHUNKS, 2, NX * KV, ROWS), BF16),
            pltpu.VMEM((CORES, 2, 1, ROWS), jnp.int32),
            pltpu.VMEM((len(AXES), LINE, CORES, 2, 1, ROWS), jnp.int32),
            pltpu.VMEM((LINE * CORES, 8, ROWS), jnp.int32),
            pltpu.VMEM((LINE, LINE, LINE * CORES, ROWS), jnp.int32),
            pltpu.VMEM((2, ROWS, ROWS), jnp.int32),
            pltpu.VMEM((COARSE + FINE + 8, ROWS), jnp.int32),
            pltpu.SMEM((len(AXES), LINE, CORES, 2, 1, ROWS), jnp.int32),
            pltpu.SMEM((COARSE, ROWS), jnp.int32),
            pltpu.SMEM((FINE, ROWS), jnp.int32),
            pltpu.SMEM((8, ROWS), jnp.int32),
            *([rows] * (LINE * CHUNKS)),
            pltpu.VMEM((CHUNKS, EMPTY, KV, ROWS), BF16),
            dma((CHUNKS,)),
            dma((4,)),
            dma((CHUNKS,)),
            dma((2,)),
            dma((SWEEPS, CHUNKS, 2)),
            dma((2,)),
            dma((2,)),
            dma((3, 2)),
            dma((CHUNKS, 2)),
            dma((CHUNKS, 3)),
            dma((CHUNKS, 4)),
            dma((CHUNKS, len(PARTS))),
            dma((CHUNKS, len(PARTS))),
            dma((CHUNKS, len(PARTS))),
            dma((5,)),
            dma((4,)),
            dma((SITES // 8,)),
        ],
        compiler_params=pltpu.CompilerParams(
            collective_id=0, has_side_effects=True, vmem_limit_bytes=60 * 1024 * 1024
        ),
        name="smooth",
    )(test_vectors, coef_x, coef_y, coef_z, shift, split, count, owner, local)


def pass_kernel(w_in, sm_in, w_out, sm_out, w_hold, sm_hold, in_sem, out_sem):
    parts = [(w_in, w_hold, w_out)]
    for c in range(CHUNKS):
        part = pl.ds(c * KV, KV)
        parts.append((sm_in.at[part], sm_hold.at[part], sm_out.at[part]))
    ins = [pltpu.make_async_copy(a, b, in_sem.at[n]) for n, (a, b, _) in enumerate(parts)]
    outs = [pltpu.make_async_copy(b, d, out_sem.at[n]) for n, (_, b, d) in enumerate(parts)]
    for copy in ins:
        copy.start()
    for load, store in zip(ins, outs):
        load.wait()
        store.start()
    for store in outs:
        store.wait()


def pass_on_results(weights, sm):
    anywhere = pl.BlockSpec(memory_space=pl.ANY)
    dma = pltpu.SemaphoreType.DMA
    return pl.pallas_call(
        pass_kernel,
        out_shape=(
            jax.ShapeDtypeStruct(weights.shape, F32),
            jax.ShapeDtypeStruct(sm.shape, F32),
        ),
        in_specs=[anywhere, anywhere],
        out_specs=(anywhere, anywhere),
        scratch_shapes=[
            pltpu.VMEM(weights.shape, F32),
            pltpu.VMEM(sm.shape, F32),
            dma((CHUNKS + 1,)),
            dma((CHUNKS + 1,)),
        ],
        compiler_params=pltpu.CompilerParams(vmem_limit_bytes=60 * 1024 * 1024),
        name="fit",
    )(weights, sm)


def per_device(
    test_vectors, coef_x, coef_y, coef_z, shift, cf_split, nbr_count, nbr_owner, nbr_block
):
    sm, weights = smooth(
        test_vectors, coef_x, coef_y, coef_z, shift,
        jnp.swapaxes(cf_split, 1, 2),
        jnp.swapaxes(nbr_count, 1, 2),
        jnp.transpose(nbr_owner, (0, 2, 3, 1)).reshape(NX, SLOTS, NY),
        jnp.transpose(nbr_block, (0, 2, 3, 1)).reshape(NX, SLOTS, NY),
    )
    weights, smoothed = pass_on_results(weights.reshape(SLOTS, NX, NY, ROWS), sm)
    return (smoothed, weights)


def solution(mesh):
    cells = P("gx", "gy", None)
    lists = P("gx", "gy", None, None)
    vectors = P(None, "gx", "gy", None)
    return jax.shard_map(
        per_device,
        mesh=mesh,
        in_specs=(vectors, cells, cells, cells, cells, cells, cells, lists, lists),
        out_specs=(vectors, vectors),
        check_vma=False,
    )
```

```python
import jax
import jax.numpy as jnp
from jax import lax
from jax.experimental import pallas as pl
from jax.experimental.pallas import tpu as pltpu
from jax.sharding import PartitionSpec as P

SLOTS = 4
SWEEPS = 3
ROWS = 128
OMEGA = 0.8
RIDGE = 0.05
VECS = 48
CHUNKS = 3
KV = VECS // CHUNKS
NX = 4
NY = 16
SITES = NX * NY
XROW = (NY + 2) * KV
EXT = (NX + 2) * XROW
GX = 16
GY = 8
MESH = pl.DeviceIdType.MESH
F32 = jnp.float32
BF16 = jnp.bfloat16


def site_row(x, y):
    return (x + 1) * XROW + (y + 1) * KV


def solve_rows(gram, rhs):
    low = [[None] * SLOTS for _ in range(SLOTS)]
    inv = []
    for r in range(SLOTS):
        scaled = []
        diag = gram[r, r]
        for c in range(r):
            rest = gram[r, c]
            for m in range(c):
                rest = rest - scaled[m] * low[c][m]
            scaled.append(rest)
            low[r][c] = rest * inv[c]
            diag = diag - rest * low[r][c]
        inv.append(1.0 / diag)
    fwd = []
    for r in range(SLOTS):
        rest = rhs[r]
        for m in range(r):
            rest = rest - low[r][m] * fwd[m]
        fwd.append(rest)
    out = [None] * SLOTS
    for r in reversed(range(SLOTS)):
        rest = fwd[r] * inv[r]
        for m in range(r + 1, SLOTS):
            rest = rest - low[m][r] * out[m]
        out[r] = rest
    return out


PAIRS = [(s, t) for s in range(SLOTS) for t in range(s + 1)] + [(s, SLOTS) for s in range(SLOTS)]
AXES = "xyz"
LINE = 4
CORES = 2
COARSE = 16
FINE = 48
PLANE = LINE * LINE
ROUTES = (("x", "z", "y"), ("y", "x", "z"), ("z", "y", "x"))
BACKS = (0, 1, 3, 2)
EMPTY = LINE * CORES * PLANE * 2
SPOT = 2 * LINE
GRAM_ORDER = (1, 2, 0)
REPLY = PLANE * 2
PARTS = ((0, 3), (3, 1))


def lists_of(meta, here):
    lane = lax.broadcasted_iota(jnp.int32, (ROWS, ROWS), 1)
    sub = lax.broadcasted_iota(jnp.int32, (ROWS, ROWS), 0)
    diag = lane == sub
    none = 1 << 20

    def column(row):
        return jnp.sum(jnp.where(diag, row, 0), axis=1, keepdims=True)

    members, keys, owners = [], [], []
    for h in range(2):
        entry = meta[h : h + 1]
        owner = entry >> 6
        key = (lane[:1] + h * ROWS) * SITES + (entry & (SITES - 1))
        owners.append(owner)
        keys.append(key)
        members.append(owner == sub)
    first = jnp.minimum(*[jnp.where(m, k, none) for m, k in zip(members, keys)])
    first = jnp.min(first, axis=1, keepdims=True)
    first = jnp.where(first >= none, 0, first)
    second = jnp.maximum(*[jnp.where(m, k, 0) for m, k in zip(members, keys)])
    second = jnp.max(second, axis=1, keepdims=True)
    targets = [[] for _ in ROUTES]
    for h in range(2):
        own = owners[h]
        at_first = jnp.sum(jnp.where(members[h], first, 0), axis=0, keepdims=True)
        place = jnp.where(keys[h] == at_first, 0, 1)
        at = {"x": (own >> 5) & 3, "z": (own >> 3) & 3, "y": (own >> 1) & 3}
        for c, (a, u, v) in enumerate(ROUTES):
            back = (at[v] - here[v]) & 3
            spot = jnp.where(back == 2, 3, jnp.where(back == 3, 2, back))
            slot = ((at[a] * CORES + (own & 1)) * PLANE + spot * LINE + ((at[u] - here[u]) & 3)) * 2 + place
            targets[c].append(jnp.where(own < 0, EMPTY, slot))
    coarse = meta[2:3]
    rank = jnp.sum(jnp.where(sub < lane, column(coarse), 0), axis=0, keepdims=True)
    fine_rank = jnp.minimum(lane[:1] - rank, FINE)
    fine_rank = jnp.where(coarse > 0, FINE, fine_rank)

    def numbers(hit):
        found = jnp.sum(jnp.where(hit, lane[: hit.shape[0]], 0), axis=1, keepdims=True)
        return jnp.broadcast_to(found, hit.shape)

    ids = numbers((rank == sub[:COARSE]) & (coarse > 0))
    fine_ids = numbers((fine_rank == sub[:FINE]) & (lane[:1] < SITES))
    rank = jnp.minimum(rank, COARSE - 1)
    return (first, second), targets, rank, ids, fine_ids, fine_rank


def ranks_wanted(blocks, table):
    lane = lax.broadcasted_iota(jnp.int32, (ROWS, ROWS), 1)
    sub = lax.broadcasted_iota(jnp.int32, (ROWS, ROWS), 0)
    found = jnp.sum(
        jnp.where(lane == (blocks & (SITES - 1)), table, 0), axis=1, keepdims=True
    )
    return jnp.sum(jnp.where(lane == sub, found, 0), axis=0, keepdims=True)


def smooth_kernel(
    tv, cx, cy, cz, sh, split, count, owner, local, sm_out, w_out,
    split_v, count_v, owner_v, local_v, meta, tgt, tgt_s, blk, rb0, rb1, rb2, part_sums, w_hold,
    stage, coef, wa, wb, ka, kb, km, kp, fxs, fxr, fys, fyr,
    pair, lines, near, far, block_cols, idv, line_s, id_s, fine_s, spot_s, p00, p01, p02, p03, p10, p11, p12, p13, p20, p21, p22, p23, sb,
    in_sem, coef_sem, out_sem, send_sem, recv_sem, pair_sem, table_sem, gather_sem,
    near_sem, cast_send, cast_recv, ans_send, ans_recv, own_sem, smem_sem, list_sem, w_sem,
):
    cells = (split_v, count_v, owner_v, local_v)
    rb = (rb0, rb1, rb2)
    pg = ((p00, p01, p02, p03), (p10, p11, p12, p13), (p20, p21, p22, p23))
    i = lax.axis_index("gx")
    j = lax.axis_index("gy")
    core = lax.rem(j, CORES)
    at = {"x": i // LINE, "z": lax.rem(i, LINE), "y": j // CORES}
    peers = (
        (lax.rem(i + GX - 1, GX), j),
        (lax.rem(i + 1, GX), j),
        (i, lax.rem(j + GY - 1, GY)),
        (i, lax.rem(j + 1, GY)),
    )

    def device(axis, d, e):
        moved = dict(at)
        moved[axis] = lax.rem(at[axis] + d, LINE)
        return (moved["x"] * LINE + moved["z"], moved["y"] * CORES + lax.rem(core + e, CORES))

    def remote(src, dst, send, recv, peer):
        return pltpu.make_async_remote_copy(
            src_ref=src, dst_ref=dst, send_sem=send, recv_sem=recv,
            device_id=peer, device_id_type=MESH,
        )

    loads = []
    for c in range(CHUNKS):
        part = pl.ds(c * KV, KV)
        loads.append(pltpu.make_async_copy(tv.at[part], stage.at[part], in_sem.at[c]))
    loads[0].start()
    barrier = pltpu.get_barrier_semaphore()
    for peer in peers[:2]:
        pl.semaphore_signal(barrier, inc=1, device_id=peer, device_id_type=MESH)
    pl.semaphore_signal(barrier, inc=1, device_id=device("x", 0, 1), device_id_type=MESH)
    for axis in AXES:
        for d in range(1, LINE):
            for e in range(CORES):
                pl.semaphore_signal(
                    barrier, inc=1, device_id=device(axis, d, e), device_id_type=MESH
                )
    greeted = 3 + len(AXES) * (LINE - 1) * CORES
    for load in loads[1:]:
        load.start()
    keep = (
        (i > 0).astype(F32),
        (i < GX - 1).astype(F32),
        (j > 0).astype(F32),
        (j < GY - 1).astype(F32),
    )

    def drain(ref, sem):
        pltpu.make_async_copy(ref, ref, sem).wait()

    def copies(s, c):
        out = []
        for d in range(4):
            src, dst = (fxs, fxr) if d < 2 else (fys, fyr)
            out.append(
                remote(
                    src.at[s, c, d % 2], dst.at[s, c, 1 - d % 2],
                    send_sem.at[d // 2], recv_sem.at[s, c, d // 2], peers[d],
                )
            )
        return out

    def send_x_faces(c, w):
        for side in range(2):
            x = side * (NX - 1)
            fxs[0, c, side] = w[c, pl.ds(site_row(x, 0), NY * KV)].astype(BF16)
        for copy in copies(0, c)[:2]:
            copy.start()

    def send_y_faces(c, w):
        for side in range(2):
            y = side * (NY - 1)
            for x in range(NX):
                fys[0, c, side, pl.ds(x * KV, KV)] = w[c, pl.ds(site_row(x, y), KV)].astype(BF16)
        for copy in copies(0, c)[2:]:
            copy.start()

    def fill_halo(s, c, w):
        drain(fxr.at[s, c], recv_sem.at[s, c, 0])
        drain(fyr.at[s, c], recv_sem.at[s, c, 1])
        for side in range(2):
            x = -1 if side == 0 else NX
            w[c, pl.ds(site_row(x, 0), NY * KV)] = fxr[s, c, side].astype(F32) * keep[side]
            y = -1 if side == 0 else NY
            for x in range(NX):
                w[c, pl.ds(site_row(x, y), KV)] = (
                    fyr[s, c, side, pl.ds(x * KV, KV)].astype(F32) * keep[2 + side]
                )

    def sweep(s, c, src, dst):
        last = s == SWEEPS - 1

        def plane(x, side):
            base = pl.multiple_of(x * XROW, 16)

            def cell(dx, y):
                return src[c, pl.ds(base + site_row(dx, y), KV)].reshape(2, 8, ROWS)

            below, here = cell(0, -1), cell(0, 0)
            for y in range(NY):
                above = cell(0, y + 1)
                new = (
                    ka[x, y] * (cell(-1, y) + cell(1, y))
                    + kb[x, y] * (below + above)
                    + km[x, y] * pltpu.roll(here, 1, 2)
                    + kp[x, y] * pltpu.roll(here, ROWS - 1, 2)
                    + (1.0 - OMEGA) * here
                ).reshape(KV, ROWS)
                dst[c, pl.ds(base + site_row(0, y), KV)] = new
                if last:
                    blk[c, x * NY + y] = new.astype(BF16)
                else:
                    if side is not None:
                        fxs[s + 1, c, side, pl.ds(y * KV, KV)] = new.astype(BF16)
                    if y in (0, NY - 1):
                        rows = pl.ds(pl.multiple_of(x * KV, KV), KV)
                        fys[s + 1, c, y // (NY - 1), rows] = new.astype(BF16)
                below, here = here, above

        def outer(n, carry):
            plane(n * (NX - 1), n)
            return carry

        def inner(n, carry):
            plane(n, None)
            return carry

        lax.fori_loop(0, 2, outer, 0)
        if not last:
            for copy in copies(s + 1, c)[:2]:
                copy.start()
        lax.fori_loop(1, NX - 1, inner, 0)
        if not last:
            for copy in copies(s + 1, c)[2:]:
                copy.start()

    def pair_copy():
        slot = pair.at[core]
        return remote(slot, slot, pair_sem.at[0], pair_sem.at[1], device("x", 0, 1))

    def line_copies():
        return [
            remote(
                pair, lines.at[n, at[axis]], table_sem.at[0], table_sem.at[1],
                device(axis, d, 0),
            )
            for n, axis in enumerate(AXES)
            for d in range(1, LINE)
        ]

    def gather_copies(step):
        send, recv = gather_sem.at[step, 0], gather_sem.at[step, 1]
        if step == 0:
            slot = near.at[at["y"] * CORES + core]
            return [
                remote(slot, slot, send, recv, device("y", d, e))
                for d in range(LINE)
                for e in range(CORES)
                if d or e
            ]
        slot = far.at[at["x"], at["z"]] if step == 1 else far.at[at["x"]]
        return [
            remote(slot, slot, send, recv, device("zx"[step - 1], d, 0)) for d in range(1, LINE)
        ]

    def gathered(step):
        if step == 0:
            return near.at[pl.ds(0, 7)]
        return far.at[0, pl.ds(0, 3)] if step == 1 else far.at[pl.ds(0, 3)]

    def gather_step(step):
        drain(gathered(step), gather_sem.at[step, 1])
        if step == 0:
            for n in range(LINE * CORES):
                far[at["x"], at["z"], n : n + 1] = near[n, 0:1]
        for copy in gather_copies(step + 1):
            copy.start()

    def ask():
        drain(gathered(2), gather_sem.at[2, 1])
        table = far[...].reshape(ROWS, ROWS)
        for p in range(2):
            pair[core, p] = ranks_wanted(block_cols[p], table)
        pair_copy().start()

    def ask_lines():
        pair_copy().wait_recv()
        for copy in line_copies():
            copy.start()
        for n, axis in enumerate(AXES):
            lines[n, at[axis]] = pair[...]

    steps = {
        (0, 1): lambda: gather_step(0),
        (1, 0): lambda: gather_step(1),
        (1, 2): ask,
        (2, 1): ask_lines,
    }

    def spread_copies(c):
        a, u, v = ROUTES[c]
        return [
            remote(
                pg[c][0].at[0], pg[c][0].at[LINE - d],
                near_sem.at[c, 0], near_sem.at[c, 1], device(u, d, 0),
            )
            for d in (2, 1, 3)
        ]

    def cast_copies(c):
        a, u, v = ROUTES[c]
        plan = (
            (0, 0, 1, 3, 1, 0, 0),
            (0, 0, 1, 1, 3, 1, 2),
            (0, 1, 1, 3, 1, 0, 0),
            (0, 2, 2, 1, 3, 1, 1),
            (0, 2, 2, 3, 1, 0, 2),
            (0, 1, 1, 1, 3, 1, 2),
            (3, 0, 2, 2, 1, 2, 3),
            (1, 2, 2, 2, 3, 2, 3),
        )
        return [
            remote(
                pg[c][src].at[pl.ds(first, size)], pg[c][dst].at[pl.ds(first, size)],
                cast_send.at[c, out], cast_recv.at[c, into], device(v, d, 0),
            )
            for src, first, size, dst, d, out, into in plan
        ]

    def piece(slot, part):
        first, count = PARTS[part]
        return pl.ds(slot * REPLY + first * SPOT, count * SPOT)

    def answer(c, part, d, e):
        a = ROUTES[c][0]
        slot = lax.rem(at[a] + d, LINE) * CORES + lax.rem(core + e, CORES)
        here = at[a] * CORES + core
        src = sb.at[c, piece(slot, part)]
        dst, peer = rb[c].at[piece(here, part)], device(a, d, e)
        if isinstance(d, int) and d == 0 and e == 0:
            return pltpu.make_async_copy(src, dst, own_sem.at[c, part])
        return remote(src, dst, ans_send.at[c, part], ans_recv.at[c, part], peer)

    order = [(d, e) for d in (2, 1, 3, 0) for e in range(CORES)]

    def spread(c):
        a, u, v = ROUTES[c]
        for r in range(COARSE):
            pg[c][0][0, r] = blk[c, id_s[r, 0] & (SITES - 1)]
        for copy in spread_copies(c) + cast_copies(c)[:2]:
            copy.start()

    def cast(c):
        drain(pg[c][1].at[pl.ds(0, 3)], near_sem.at[c, 1])
        for copy in cast_copies(c)[2:6]:
            copy.start()

    def pass_on(c):
        for n in range(2):
            drain(pg[c][0].at[pl.ds(0, 2)], cast_recv.at[c, n])
            cast_copies(c)[6 + n].start()

    def pack(c, d, e, places):
        a, u, v = ROUTES[c]
        n = AXES.index(a)
        q, to = lax.rem(at[a] + d, LINE), lax.rem(core + e, CORES)
        slot = q * CORES + to
        for place in places:
            back = BACKS[place]
            tiles = []
            for ahead in range(LINE):
                whose = {
                    a: at[a],
                    u: lax.rem(at[u] + ahead, LINE),
                    v: lax.rem(at[v] + back, LINE),
                }
                owner = whose["x"] * 32 + whose["z"] * 8 + whose["y"] * 2 + core
                for p in range(2):
                    rank = line_s[n, q, to, p, 0, owner] & (COARSE - 1)
                    tiles.append(pg[c][back][ahead, rank])
            for t, tile in enumerate(tiles):
                sb[c, slot * REPLY + place * SPOT + t] = tile

    def reply(c, part):
        drain(pg[c][0], cast_recv.at[c, 2 + part])
        first, count = PARTS[part]
        places = range(first, first + count)

        def to_other_chip(n, carry):
            k, e = n // CORES, lax.rem(n, CORES)
            d = 2 - k + 3 * (k // 2)
            pack(c, d, e, places)
            answer(c, part, d, e).start()
            return carry

        lax.fori_loop(0, (LINE - 1) * CORES, to_other_chip, 0)
        for e in (1, 0):
            pack(c, 0, e, places)
            answer(c, part, 0, e).start()

    def transpose_in(c, planes):

        def one(k, carry):
            for x in planes:
                for half in range(NY // 8):
                    wa[c, pl.ds(site_row(x, half * 8) + k, 8, stride=KV), :] = stage[
                        c * KV + k, x, pl.ds(half * 8, 8), :
                    ]
            return carry

        lax.fori_loop(0, KV, one, 0)

    def products(c, place):
        b = fine_s[place, 0] & (SITES - 1)
        column = ((b >> 4) & 1) * (ROWS // 2) + (b & (NY - 1))
        values = []
        for t in range(SLOTS):
            found = tgt_s[2 * c + (b >> 5), column + t * NY]
            values.append(rb[c][found].astype(F32))
        values.append(blk[c, b].astype(F32))
        for n, (p, q) in enumerate(PAIRS):
            product = values[p] * values[q]
            product = product[0:8] + product[8:16]
            if c != GRAM_ORDER[0]:
                product = product + part_sums[n, place]
            part_sums[n, place] = product

    def add_products(c):
        def step(g, carry):
            for m in range(4):
                products(c, g * 4 + m)
            return carry

        lax.fori_loop(0, FINE // 4, step, 0)

    def w_copy(g):
        rows = pl.ds(pl.multiple_of(g * 8, 8), 8)
        return pltpu.make_async_copy(w_hold.at[:, rows], w_out.at[:, rows], w_sem.at[g])

    def finish():
        sub = lax.broadcasted_iota(jnp.int32, (8, ROWS), 0)
        low4, low2, low1 = sub < 4, (sub & 2) == 0, (sub & 1) == 0

        def merge(first, second, keep_first, shift):
            first = first + pltpu.roll(first, 8 - shift, 0)
            second = second + pltpu.roll(second, shift, 0)
            return jnp.where(keep_first, first, second)

        def group(g, carry):
            total = {}
            spots = [spot_s[0, g * 8 + m] & (SITES - 1) for m in range(8)]
            for n, couple in enumerate(PAIRS):
                rows = [part_sums[n, spot] for spot in spots]
                rows = [
                    jnp.where(low4, rows[m], rows[m + 4])
                    + pltpu.roll(jnp.where(low4, rows[m + 4], rows[m]), 4, 0)
                    for m in range(4)
                ]
                rows = [merge(rows[m], rows[m + 2], low2, 2) for m in range(2)]
                total[couple] = merge(rows[0], rows[1], low1, 1) * (1.0 / VECS)
                if couple[0] == couple[1]:
                    total[couple] = total[couple] + RIDGE
            out = solve_rows(total, [total[s, SLOTS] for s in range(SLOTS)])
            for s in range(SLOTS):
                w_hold[s, pl.ds(pl.multiple_of(g * 8, 8), 8), :] = out[s]
            w_copy(g).start()
            return carry

        lax.fori_loop(0, SITES // 8, group, 0)
        for g in range(SITES // 8):
            w_copy(g).wait()

    stores = []

    def transpose_out(c, w):

        def one(k, carry):
            for x in range(NX):
                for half in range(NY // 8):
                    stage[c * KV + k, x, pl.ds(half * 8, 8), :] = w[
                        c, pl.ds(site_row(x, half * 8) + k, 8, stride=KV), :
                    ]
            return carry

        lax.fori_loop(0, KV, one, 0)
        part = pl.ds(c * KV, KV)
        store = pltpu.make_async_copy(stage.at[part], sm_out.at[part], out_sem.at[c])
        store.start()
        stores.append(store)

    loads[0].wait()
    transpose_in(0, (0, NX - 1))
    pl.semaphore_wait(barrier, greeted)
    send_x_faces(0, wa)
    coef_loads = []
    for n, part in enumerate((cx, cy, cz, sh)):
        load = pltpu.make_async_copy(part, coef.at[n], coef_sem.at[n])
        load.start()
        coef_loads.append(load)
    lists = []
    for n, part in enumerate((split, count, owner, local)):
        load = pltpu.make_async_copy(part, cells[n], list_sem.at[n])
        load.start()
        lists.append(load)

    transpose_in(0, range(1, NX - 1))
    send_y_faces(0, wa)
    for c in range(1, CHUNKS):
        loads[c].wait()
        transpose_in(c, range(NX))
        send_x_faces(c, wa)
        send_y_faces(c, wa)

    for load in coef_loads:
        load.wait()
    ax, ay, az = coef[0], coef[1], coef[2]
    scale = OMEGA / (2.0 * (ax + ay + az) + coef[3])
    ax, ay, az = ax * scale, ay * scale, az * scale
    lane = lax.broadcasted_iota(jnp.int32, az.shape, 2)
    before = jnp.where(lane == 0, 0.0, az)
    after = jnp.where(lane == ROWS - 1, 0.0, az)
    for x in range(NX):
        for y in range(NY):
            for held, value in ((ka, ax), (kb, ay), (km, before), (kp, after)):
                held[x, y] = jnp.broadcast_to(value[x, y : y + 1], (8, ROWS))

    for load in lists:
        load.wait()
    meta[...] = jnp.zeros_like(meta)
    slots = lax.broadcasted_iota(jnp.int32, (SLOTS, NY), 0)
    for x in range(NX):
        live = (cells[0][x] == 0) & (slots < cells[1][x])
        listed = jnp.where(live, cells[2][x] * SITES + cells[3][x], -1)
        for t in range(SLOTS):
            where = pl.ds((x % 2) * (ROWS // 2) + t * NY, NY)
            meta[x // 2 : x // 2 + 1, where] = listed[t : t + 1]
        meta[2:3, pl.ds(x * NY, NY)] = cells[0][x]
    blocks, targets, rank, ids, fine_ids, fine_rank = lists_of(meta[...], at)
    near[at["y"] * CORES + core] = jnp.broadcast_to(rank, (8, ROWS))
    for copy in gather_copies(0):
        copy.start()
    for p in range(2):
        block_cols[p] = jnp.broadcast_to(blocks[p], (ROWS, ROWS))
    idv[:COARSE] = ids
    idv[COARSE : COARSE + FINE] = fine_ids
    idv[COARSE + FINE :] = jnp.broadcast_to(fine_rank, (8, ROWS))
    part_sums[:, FINE] = jnp.zeros((len(PAIRS), 8, ROWS), F32)
    id_copies = [
        pltpu.make_async_copy(idv.at[pl.ds(0, COARSE)], id_s, smem_sem.at[0]),
        pltpu.make_async_copy(idv.at[pl.ds(COARSE, FINE)], fine_s, smem_sem.at[2]),
        pltpu.make_async_copy(idv.at[pl.ds(COARSE + FINE, 8)], spot_s, smem_sem.at[4]),
    ]
    for copy in id_copies:
        copy.start()
    tgt[...] = jnp.zeros_like(tgt)
    for c in range(CHUNKS):
        for h in range(2):
            tgt[2 * c + h : 2 * c + h + 1] = targets[c][h]
        rb[c][EMPTY] = jnp.zeros((KV, ROWS), BF16)
    tgt_copy = pltpu.make_async_copy(tgt, tgt_s, smem_sem.at[3])
    tgt_copy.start()

    for s in range(SWEEPS):
        src, dst = (wb, wa) if s % 2 else (wa, wb)
        for c in range(CHUNKS):
            fill_halo(s, c, src)
            sweep(s, c, src, dst)
            if s == SWEEPS - 1:
                if c == 0:
                    for copy in id_copies:
                        copy.wait()
                spread(c)
            if (s, c) in steps:
                steps[s, c]()
    drain(lines.at[:, pl.ds(0, 3)], table_sem.at[1])
    line_copy = pltpu.make_async_copy(lines, line_s, smem_sem.at[1])
    line_copy.start()
    cast(0)
    cast(1)
    cast(2)
    line_copy.wait()
    for c in range(CHUNKS):
        pass_on(c)
    for c in (1, 2, 0):
        reply(c, 0)
    for c in GRAM_ORDER:
        reply(c, 1)
    for c in range(CHUNKS):
        transpose_out(c, wb)
    drain(fxs, send_sem.at[0])
    drain(fys, send_sem.at[1])
    pair_copy().wait_send()
    drain(lines.at[:, pl.ds(0, 3)], table_sem.at[0])
    for step in range(3):
        drain(gathered(step), gather_sem.at[step, 0])
    for c in range(CHUNKS):
        drain(pg[c][0].at[pl.ds(0, 3)], near_sem.at[c, 0])
        for n in range(3):
            drain(pg[c][0], cast_send.at[c, n])
    tgt_copy.wait()
    for c in GRAM_ORDER:
        for part in range(len(PARTS)):
            answer(c, part, 0, 0).wait()
            drain(sb.at[c, pl.ds(0, 7 * PARTS[part][1] * SPOT)], ans_recv.at[c, part])
        add_products(c)
        for part in range(len(PARTS)):
            count = PARTS[part][1]
            drain(sb.at[c, pl.ds(0, 7 * count * SPOT)], ans_send.at[c, part])
    for store in stores:
        store.wait()
    finish()


def smooth(test_vectors, coef_x, coef_y, coef_z, shift, split, count, owner, local):
    vmem = pl.BlockSpec(memory_space=pltpu.VMEM)
    anywhere = pl.BlockSpec(memory_space=pl.ANY)
    cells = pltpu.VMEM((NX, NY, 8, ROWS), F32)
    rows = pltpu.VMEM((LINE, COARSE, KV, ROWS), BF16)
    dma = pltpu.SemaphoreType.DMA
    return pl.pallas_call(
        smooth_kernel,
        out_shape=(
            jax.ShapeDtypeStruct((VECS, NX, NY, ROWS), F32),
            jax.ShapeDtypeStruct((SLOTS, SITES, ROWS), F32),
        ),
        in_specs=[anywhere] * 9,
        out_specs=(anywhere, anywhere),
        scratch_shapes=[
            pltpu.VMEM((NX, 1, NY), jnp.int32),
            pltpu.VMEM((NX, 1, NY), jnp.int32),
            pltpu.VMEM((NX, SLOTS, NY), jnp.int32),
            pltpu.VMEM((NX, SLOTS, NY), jnp.int32),
            pltpu.VMEM((8, ROWS), jnp.int32),
            pltpu.VMEM((8, ROWS), jnp.int32),
            pltpu.SMEM((8, ROWS), jnp.int32),
            pltpu.VMEM((CHUNKS, SITES, KV, ROWS), BF16),
            *([pltpu.VMEM((EMPTY + 8, KV, ROWS), BF16)] * CHUNKS),
            pltpu.VMEM((len(PAIRS), SITES, 8, ROWS), F32),
            pltpu.VMEM((SLOTS, SITES, ROWS), F32),
            pltpu.VMEM((VECS, NX, NY, ROWS), F32),
            pltpu.VMEM((4, NX, NY, ROWS), F32),
            pltpu.VMEM((CHUNKS, EXT, ROWS), F32),
            pltpu.VMEM((CHUNKS, EXT, ROWS), F32),
            cells, cells, cells, cells,
            pltpu.VMEM((SWEEPS, CHUNKS, 2, NY * KV, ROWS), BF16),
            pltpu.VMEM((SWEEPS, CHUNKS, 2, NY * KV, ROWS), BF16),
            pltpu.VMEM((SWEEPS, CHUNKS, 2, NX * KV, ROWS), BF16),
            pltpu.VMEM((SWEEPS, CHUNKS, 2, NX * KV, ROWS), BF16),
            pltpu.VMEM((CORES, 2, 1, ROWS), jnp.int32),
            pltpu.VMEM((len(AXES), LINE, CORES, 2, 1, ROWS), jnp.int32),
            pltpu.VMEM((LINE * CORES, 8, ROWS), jnp.int32),
            pltpu.VMEM((LINE, LINE, LINE * CORES, ROWS), jnp.int32),
            pltpu.VMEM((2, ROWS, ROWS), jnp.int32),
            pltpu.VMEM((COARSE + FINE + 8, ROWS), jnp.int32),
            pltpu.SMEM((len(AXES), LINE, CORES, 2, 1, ROWS), jnp.int32),
            pltpu.SMEM((COARSE, ROWS), jnp.int32),
            pltpu.SMEM((FINE, ROWS), jnp.int32),
            pltpu.SMEM((8, ROWS), jnp.int32),
            *([rows] * (LINE * CHUNKS)),
            pltpu.VMEM((CHUNKS, EMPTY, KV, ROWS), BF16),
            dma((CHUNKS,)),
            dma((4,)),
            dma((CHUNKS,)),
            dma((2,)),
            dma((SWEEPS, CHUNKS, 2)),
            dma((2,)),
            dma((2,)),
            dma((3, 2)),
            dma((CHUNKS, 2)),
            dma((CHUNKS, 3)),
            dma((CHUNKS, 4)),
            dma((CHUNKS, len(PARTS))),
            dma((CHUNKS, len(PARTS))),
            dma((CHUNKS, len(PARTS))),
            dma((5,)),
            dma((4,)),
            dma((SITES // 8,)),
        ],
        compiler_params=pltpu.CompilerParams(
            collective_id=0, has_side_effects=True, vmem_limit_bytes=60 * 1024 * 1024
        ),
        name="smooth",
    )(test_vectors, coef_x, coef_y, coef_z, shift, split, count, owner, local)


def pass_kernel(w_in, sm_in, w_out, sm_out, w_hold, sm_hold, in_sem, out_sem):
    parts = [(w_in, w_hold, w_out)]
    for c in range(CHUNKS):
        part = pl.ds(c * KV, KV)
        parts.append((sm_in.at[part], sm_hold.at[part], sm_out.at[part]))
    ins = [pltpu.make_async_copy(a, b, in_sem.at[n]) for n, (a, b, _) in enumerate(parts)]
    outs = [pltpu.make_async_copy(b, d, out_sem.at[n]) for n, (_, b, d) in enumerate(parts)]
    for copy in ins:
        copy.start()
    for load, store in zip(ins, outs):
        load.wait()
        store.start()
    for store in outs:
        store.wait()


def pass_on_results(weights, sm):
    anywhere = pl.BlockSpec(memory_space=pl.ANY)
    dma = pltpu.SemaphoreType.DMA
    return pl.pallas_call(
        pass_kernel,
        out_shape=(
            jax.ShapeDtypeStruct(weights.shape, F32),
            jax.ShapeDtypeStruct(sm.shape, F32),
        ),
        in_specs=[anywhere, anywhere],
        out_specs=(anywhere, anywhere),
        scratch_shapes=[
            pltpu.VMEM(weights.shape, F32),
            pltpu.VMEM(sm.shape, F32),
            dma((CHUNKS + 1,)),
            dma((CHUNKS + 1,)),
        ],
        compiler_params=pltpu.CompilerParams(vmem_limit_bytes=60 * 1024 * 1024),
        name="fit",
    )(weights, sm)


def per_device(
    test_vectors, coef_x, coef_y, coef_z, shift, cf_split, nbr_count, nbr_owner, nbr_block
):
    sm, weights = smooth(
        test_vectors, coef_x, coef_y, coef_z, shift,
        jnp.swapaxes(cf_split, 1, 2),
        jnp.swapaxes(nbr_count, 1, 2),
        jnp.transpose(nbr_owner, (0, 2, 3, 1)).reshape(NX, SLOTS, NY),
        jnp.transpose(nbr_block, (0, 2, 3, 1)).reshape(NX, SLOTS, NY),
    )
    weights, smoothed = pass_on_results(weights.reshape(SLOTS, NX, NY, ROWS), sm)
    return (smoothed, weights)


def solution(mesh):
    cells = P("gx", "gy", None)
    lists = P("gx", "gy", None, None)
    vectors = P(None, "gx", "gy", None)
    return jax.shard_map(
        per_device,
        mesh=mesh,
        in_specs=(vectors, cells, cells, cells, cells, cells, cells, lists, lists),
        out_specs=(vectors, vectors),
        check_vma=False,
    )
```

```python
import jax
import jax.numpy as jnp
from jax import lax
from jax.experimental import pallas as pl
from jax.experimental.pallas import tpu as pltpu
from jax.sharding import PartitionSpec as P

SLOTS = 4
SWEEPS = 3
ROWS = 128
OMEGA = 0.8
RIDGE = 0.05
VECS = 48
CHUNKS = 3
KV = VECS // CHUNKS
NX = 4
NY = 16
SITES = NX * NY
XROW = (NY + 2) * KV
EXT = (NX + 2) * XROW
GX = 16
GY = 8
MESH = pl.DeviceIdType.MESH
F32 = jnp.float32
BF16 = jnp.bfloat16


def site_row(x, y):
    return (x + 1) * XROW + (y + 1) * KV


def solve_rows(gram, rhs):
    low = [[None] * SLOTS for _ in range(SLOTS)]
    inv = []
    for r in range(SLOTS):
        scaled = []
        diag = gram[r, r]
        for c in range(r):
            rest = gram[r, c]
            for m in range(c):
                rest = rest - scaled[m] * low[c][m]
            scaled.append(rest)
            low[r][c] = rest * inv[c]
            diag = diag - rest * low[r][c]
        inv.append(1.0 / diag)
    fwd = []
    for r in range(SLOTS):
        rest = rhs[r]
        for m in range(r):
            rest = rest - low[r][m] * fwd[m]
        fwd.append(rest)
    out = [None] * SLOTS
    for r in reversed(range(SLOTS)):
        rest = fwd[r] * inv[r]
        for m in range(r + 1, SLOTS):
            rest = rest - low[m][r] * out[m]
        out[r] = rest
    return out


PAIRS = [(s, t) for s in range(SLOTS) for t in range(s + 1)] + [(s, SLOTS) for s in range(SLOTS)]
AXES = "xyz"
LINE = 4
CORES = 2
COARSE = 16
FINE = 48
PLANE = LINE * LINE
ROUTES = (("x", "z", "y"), ("y", "x", "z"), ("z", "y", "x"))
BACKS = (0, 1, 3, 2)
EMPTY = LINE * CORES * PLANE * 2
SPOT = 2 * LINE
GRAM_ORDER = (1, 2, 0)
REPLY = PLANE * 2
PARTS = ((0, 3), (3, 1))


def lists_of(meta, here):
    lane = lax.broadcasted_iota(jnp.int32, (ROWS, ROWS), 1)
    sub = lax.broadcasted_iota(jnp.int32, (ROWS, ROWS), 0)
    diag = lane == sub
    none = 1 << 20

    def column(row):
        return jnp.sum(jnp.where(diag, row, 0), axis=1, keepdims=True)

    members, keys, owners = [], [], []
    for h in range(2):
        entry = meta[h : h + 1]
        owner = entry >> 6
        key = (lane[:1] + h * ROWS) * SITES + (entry & (SITES - 1))
        owners.append(owner)
        keys.append(key)
        members.append(owner == sub)
    first = jnp.minimum(*[jnp.where(m, k, none) for m, k in zip(members, keys)])
    first = jnp.min(first, axis=1, keepdims=True)
    first = jnp.where(first >= none, 0, first)
    second = jnp.maximum(*[jnp.where(m, k, 0) for m, k in zip(members, keys)])
    second = jnp.max(second, axis=1, keepdims=True)
    targets = [[] for _ in ROUTES]
    for h in range(2):
        own = owners[h]
        at_first = jnp.sum(jnp.where(members[h], first, 0), axis=0, keepdims=True)
        place = jnp.where(keys[h] == at_first, 0, 1)
        at = {"x": (own >> 5) & 3, "z": (own >> 3) & 3, "y": (own >> 1) & 3}
        for c, (a, u, v) in enumerate(ROUTES):
            back = (at[v] - here[v]) & 3
            spot = jnp.where(back == 2, 3, jnp.where(back == 3, 2, back))
            slot = ((at[a] * CORES + (own & 1)) * PLANE + spot * LINE + ((at[u] - here[u]) & 3)) * 2 + place
            targets[c].append(jnp.where(own < 0, EMPTY, slot))
    coarse = meta[2:3]
    rank = jnp.sum(jnp.where(sub < lane, column(coarse), 0), axis=0, keepdims=True)
    fine_rank = jnp.minimum(lane[:1] - rank, FINE)
    fine_rank = jnp.where(coarse > 0, FINE, fine_rank)

    def numbers(hit):
        found = jnp.sum(jnp.where(hit, lane[: hit.shape[0]], 0), axis=1, keepdims=True)
        return jnp.broadcast_to(found, hit.shape)

    ids = numbers((rank == sub[:COARSE]) & (coarse > 0))
    fine_ids = numbers((fine_rank == sub[:FINE]) & (lane[:1] < SITES))
    rank = jnp.minimum(rank, COARSE - 1)
    return (first, second), targets, rank, ids, fine_ids, fine_rank


def ranks_wanted(blocks, table):
    lane = lax.broadcasted_iota(jnp.int32, (ROWS, ROWS), 1)
    sub = lax.broadcasted_iota(jnp.int32, (ROWS, ROWS), 0)
    found = jnp.sum(
        jnp.where(lane == (blocks & (SITES - 1)), table, 0), axis=1, keepdims=True
    )
    return jnp.sum(jnp.where(lane == sub, found, 0), axis=0, keepdims=True)


def smooth_kernel(
    tv, cx, cy, cz, sh, split, count, owner, local, sm_out, w_out,
    split_v, count_v, owner_v, local_v, meta, tgt, tgt_s, blk, rb0, rb1, rb2, part_sums, w_hold,
    stage, coef, wa, wb, ka, kb, km, kp, fxs, fxr, fys, fyr,
    pair, lines, near, far, block_cols, idv, line_s, id_s, fine_s, spot_s, p00, p01, p02, p03, p10, p11, p12, p13, p20, p21, p22, p23, sb,
    in_sem, coef_sem, out_sem, send_sem, recv_sem, pair_sem, table_sem, gather_sem,
    near_sem, cast_send, cast_recv, ans_send, ans_recv, own_sem, smem_sem, list_sem, w_sem,
):
    cells = (split_v, count_v, owner_v, local_v)
    rb = (rb0, rb1, rb2)
    pg = ((p00, p01, p02, p03), (p10, p11, p12, p13), (p20, p21, p22, p23))
    i = lax.axis_index("gx")
    j = lax.axis_index("gy")
    core = lax.rem(j, CORES)
    at = {"x": i // LINE, "z": lax.rem(i, LINE), "y": j // CORES}
    peers = (
        (lax.rem(i + GX - 1, GX), j),
        (lax.rem(i + 1, GX), j),
        (i, lax.rem(j + GY - 1, GY)),
        (i, lax.rem(j + 1, GY)),
    )

    def device(axis, d, e):
        moved = dict(at)
        moved[axis] = lax.rem(at[axis] + d, LINE)
        return (moved["x"] * LINE + moved["z"], moved["y"] * CORES + lax.rem(core + e, CORES))

    def remote(src, dst, send, recv, peer):
        return pltpu.make_async_remote_copy(
            src_ref=src, dst_ref=dst, send_sem=send, recv_sem=recv,
            device_id=peer, device_id_type=MESH,
        )

    loads = []
    for c in range(CHUNKS):
        part = pl.ds(c * KV, KV)
        loads.append(pltpu.make_async_copy(tv.at[part], stage.at[part], in_sem.at[c]))
    loads[0].start()
    barrier = pltpu.get_barrier_semaphore()
    for peer in peers[:2]:
        pl.semaphore_signal(barrier, inc=1, device_id=peer, device_id_type=MESH)
    pl.semaphore_signal(barrier, inc=1, device_id=device("x", 0, 1), device_id_type=MESH)
    for axis in AXES:
        for d in range(1, LINE):
            for e in range(CORES):
                pl.semaphore_signal(
                    barrier, inc=1, device_id=device(axis, d, e), device_id_type=MESH
                )
    greeted = 3 + len(AXES) * (LINE - 1) * CORES
    for load in loads[1:]:
        load.start()
    coef_loads = []
    for n, part in enumerate((cx, cy, cz, sh)):
        load = pltpu.make_async_copy(part, coef.at[n], coef_sem.at[n])
        load.start()
        coef_loads.append(load)
    lists = []
    for n, part in enumerate((split, count, owner, local)):
        load = pltpu.make_async_copy(part, cells[n], list_sem.at[n])
        load.start()
        lists.append(load)

    keep = (
        (i > 0).astype(F32),
        (i < GX - 1).astype(F32),
        (j > 0).astype(F32),
        (j < GY - 1).astype(F32),
    )

    def drain(ref, sem):
        pltpu.make_async_copy(ref, ref, sem).wait()

    def copies(s, c):
        out = []
        for d in range(4):
            src, dst = (fxs, fxr) if d < 2 else (fys, fyr)
            out.append(
                remote(
                    src.at[s, c, d % 2], dst.at[s, c, 1 - d % 2],
                    send_sem.at[d // 2], recv_sem.at[s, c, d // 2], peers[d],
                )
            )
        return out

    def send_faces(s, c, w):
        for side in range(2):
            x = side * (NX - 1)
            fxs[s, c, side] = w[c, pl.ds(site_row(x, 0), NY * KV)].astype(BF16)
            y = side * (NY - 1)
            for x in range(NX):
                fys[s, c, side, pl.ds(x * KV, KV)] = w[c, pl.ds(site_row(x, y), KV)].astype(BF16)
        for copy in copies(s, c):
            copy.start()

    def fill_halo(s, c, w):
        drain(fxr.at[s, c], recv_sem.at[s, c, 0])
        drain(fyr.at[s, c], recv_sem.at[s, c, 1])
        for side in range(2):
            x = -1 if side == 0 else NX
            w[c, pl.ds(site_row(x, 0), NY * KV)] = fxr[s, c, side].astype(F32) * keep[side]
            y = -1 if side == 0 else NY
            for x in range(NX):
                w[c, pl.ds(site_row(x, y), KV)] = (
                    fyr[s, c, side, pl.ds(x * KV, KV)].astype(F32) * keep[2 + side]
                )

    def sweep(s, c, src, dst):
        last = s == SWEEPS - 1

        def plane(x, side):
            base = pl.multiple_of(x * XROW, 16)

            def cell(dx, y):
                return src[c, pl.ds(base + site_row(dx, y), KV)].reshape(2, 8, ROWS)

            below, here = cell(0, -1), cell(0, 0)
            for y in range(NY):
                above = cell(0, y + 1)
                new = (
                    ka[x, y] * (cell(-1, y) + cell(1, y))
                    + kb[x, y] * (below + above)
                    + km[x, y] * pltpu.roll(here, 1, 2)
                    + kp[x, y] * pltpu.roll(here, ROWS - 1, 2)
                    + (1.0 - OMEGA) * here
                ).reshape(KV, ROWS)
                dst[c, pl.ds(base + site_row(0, y), KV)] = new
                if last:
                    blk[c, x * NY + y] = new.astype(BF16)
                else:
                    if side is not None:
                        fxs[s + 1, c, side, pl.ds(y * KV, KV)] = new.astype(BF16)
                    if y in (0, NY - 1):
                        rows = pl.ds(pl.multiple_of(x * KV, KV), KV)
                        fys[s + 1, c, y // (NY - 1), rows] = new.astype(BF16)
                below, here = here, above

        def outer(n, carry):
            plane(n * (NX - 1), n)
            return carry

        def inner(n, carry):
            plane(n, None)
            return carry

        lax.fori_loop(0, 2, outer, 0)
        if not last:
            for copy in copies(s + 1, c)[:2]:
                copy.start()
        lax.fori_loop(1, NX - 1, inner, 0)
        if not last:
            for copy in copies(s + 1, c)[2:]:
                copy.start()

    def pair_copy():
        slot = pair.at[core]
        return remote(slot, slot, pair_sem.at[0], pair_sem.at[1], device("x", 0, 1))

    def line_copies():
        return [
            remote(
                pair, lines.at[n, at[axis]], table_sem.at[0], table_sem.at[1],
                device(axis, d, 0),
            )
            for n, axis in enumerate(AXES)
            for d in range(1, LINE)
        ]

    def gather_copies(step):
        send, recv = gather_sem.at[step, 0], gather_sem.at[step, 1]
        if step == 0:
            slot = near.at[at["y"] * CORES + core]
            return [
                remote(slot, slot, send, recv, device("y", d, e))
                for d in range(LINE)
                for e in range(CORES)
                if d or e
            ]
        slot = far.at[at["x"], at["z"]] if step == 1 else far.at[at["x"]]
        return [
            remote(slot, slot, send, recv, device("zx"[step - 1], d, 0)) for d in range(1, LINE)
        ]

    def gathered(step):
        if step == 0:
            return near.at[pl.ds(0, 7)]
        return far.at[0, pl.ds(0, 3)] if step == 1 else far.at[pl.ds(0, 3)]

    def gather_step(step):
        drain(gathered(step), gather_sem.at[step, 1])
        if step == 0:
            for n in range(LINE * CORES):
                far[at["x"], at["z"], n : n + 1] = near[n, 0:1]
        for copy in gather_copies(step + 1):
            copy.start()

    def ask():
        drain(gathered(2), gather_sem.at[2, 1])
        table = far[...].reshape(ROWS, ROWS)
        for p in range(2):
            pair[core, p] = ranks_wanted(block_cols[p], table)
        pair_copy().start()

    def ask_lines():
        pair_copy().wait_recv()
        for copy in line_copies():
            copy.start()
        for n, axis in enumerate(AXES):
            lines[n, at[axis]] = pair[...]

    steps = {
        (0, 1): lambda: gather_step(0),
        (1, 0): lambda: gather_step(1),
        (1, 2): ask,
        (2, 1): ask_lines,
    }

    def spread_copies(c):
        a, u, v = ROUTES[c]
        return [
            remote(
                pg[c][0].at[0], pg[c][0].at[LINE - d],
                near_sem.at[c, 0], near_sem.at[c, 1], device(u, d, 0),
            )
            for d in (2, 1, 3)
        ]

    def cast_copies(c):
        a, u, v = ROUTES[c]
        plan = (
            (0, 0, 2, 3, 1, 0, 0),
            (0, 2, 2, 1, 3, 1, 1),
            (0, 2, 2, 3, 1, 0, 2),
            (0, 0, 2, 1, 3, 1, 2),
            (3, 0, 2, 2, 1, 2, 3),
            (1, 2, 2, 2, 3, 2, 3),
        )
        return [
            remote(
                pg[c][src].at[pl.ds(first, size)], pg[c][dst].at[pl.ds(first, size)],
                cast_send.at[c, out], cast_recv.at[c, into], device(v, d, 0),
            )
            for src, first, size, dst, d, out, into in plan
        ]

    def piece(slot, part):
        first, count = PARTS[part]
        return pl.ds(slot * REPLY + first * SPOT, count * SPOT)

    def answer(c, part, d, e):
        a = ROUTES[c][0]
        slot = lax.rem(at[a] + d, LINE) * CORES + lax.rem(core + e, CORES)
        here = at[a] * CORES + core
        src = sb.at[c, piece(slot, part)]
        dst, peer = rb[c].at[piece(here, part)], device(a, d, e)
        if isinstance(d, int) and d == 0 and e == 0:
            return pltpu.make_async_copy(src, dst, own_sem.at[c, part])
        return remote(src, dst, ans_send.at[c, part], ans_recv.at[c, part], peer)

    order = [(d, e) for d in (2, 1, 3, 0) for e in range(CORES)]

    def spread(c):
        a, u, v = ROUTES[c]
        for r in range(COARSE):
            pg[c][0][0, r] = blk[c, id_s[r, 0] & (SITES - 1)]
        for copy in spread_copies(c):
            copy.start()

    def cast(c):
        drain(pg[c][1].at[pl.ds(0, 3)], near_sem.at[c, 1])
        for copy in cast_copies(c)[:4]:
            copy.start()

    def pass_on(c):
        for n in range(2):
            drain(pg[c][0].at[pl.ds(0, 2)], cast_recv.at[c, n])
            cast_copies(c)[4 + n].start()

    def pack(c, d, e, places):
        a, u, v = ROUTES[c]
        n = AXES.index(a)
        q, to = lax.rem(at[a] + d, LINE), lax.rem(core + e, CORES)
        slot = q * CORES + to
        for place in places:
            back = BACKS[place]
            tiles = []
            for ahead in range(LINE):
                whose = {
                    a: at[a],
                    u: lax.rem(at[u] + ahead, LINE),
                    v: lax.rem(at[v] + back, LINE),
                }
                owner = whose["x"] * 32 + whose["z"] * 8 + whose["y"] * 2 + core
                for p in range(2):
                    rank = line_s[n, q, to, p, 0, owner] & (COARSE - 1)
                    tiles.append(pg[c][back][ahead, rank])
            for t, tile in enumerate(tiles):
                sb[c, slot * REPLY + place * SPOT + t] = tile

    def reply(c, part):
        drain(pg[c][0], cast_recv.at[c, 2 + part])
        first, count = PARTS[part]
        places = range(first, first + count)

        def to_other_chip(n, carry):
            k, e = n // CORES, lax.rem(n, CORES)
            d = 2 - k + 3 * (k // 2)
            pack(c, d, e, places)
            answer(c, part, d, e).start()
            return carry

        lax.fori_loop(0, (LINE - 1) * CORES, to_other_chip, 0)
        for e in (1, 0):
            pack(c, 0, e, places)
            answer(c, part, 0, e).start()

    def transpose_in(c):
        loads[c].wait()

        def one(k, carry):
            for x in range(NX):
                for half in range(NY // 8):
                    wa[c, pl.ds(site_row(x, half * 8) + k, 8, stride=KV), :] = stage[
                        c * KV + k, x, pl.ds(half * 8, 8), :
                    ]
            return carry

        lax.fori_loop(0, KV, one, 0)

    def products(c, place):
        b = fine_s[place, 0] & (SITES - 1)
        column = ((b >> 4) & 1) * (ROWS // 2) + (b & (NY - 1))
        values = []
        for t in range(SLOTS):
            found = tgt_s[2 * c + (b >> 5), column + t * NY]
            values.append(rb[c][found].astype(F32))
        values.append(blk[c, b].astype(F32))
        for n, (p, q) in enumerate(PAIRS):
            product = values[p] * values[q]
            product = product[0:8] + product[8:16]
            if c != GRAM_ORDER[0]:
                product = product + part_sums[n, place]
            part_sums[n, place] = product

    def add_products(c):
        def step(g, carry):
            for m in range(4):
                products(c, g * 4 + m)
            return carry

        lax.fori_loop(0, FINE // 4, step, 0)

    def w_copy(g):
        rows = pl.ds(pl.multiple_of(g * 8, 8), 8)
        return pltpu.make_async_copy(w_hold.at[:, rows], w_out.at[:, rows], w_sem.at[g])

    def finish():
        sub = lax.broadcasted_iota(jnp.int32, (8, ROWS), 0)
        low4, low2, low1 = sub < 4, (sub & 2) == 0, (sub & 1) == 0

        def merge(first, second, keep_first, shift):
            first = first + pltpu.roll(first, 8 - shift, 0)
            second = second + pltpu.roll(second, shift, 0)
            return jnp.where(keep_first, first, second)

        def group(g, carry):
            total = {}
            spots = [spot_s[0, g * 8 + m] & (SITES - 1) for m in range(8)]
            for n, couple in enumerate(PAIRS):
                rows = [part_sums[n, spot] for spot in spots]
                rows = [
                    jnp.where(low4, rows[m], rows[m + 4])
                    + pltpu.roll(jnp.where(low4, rows[m + 4], rows[m]), 4, 0)
                    for m in range(4)
                ]
                rows = [merge(rows[m], rows[m + 2], low2, 2) for m in range(2)]
                total[couple] = merge(rows[0], rows[1], low1, 1) * (1.0 / VECS)
                if couple[0] == couple[1]:
                    total[couple] = total[couple] + RIDGE
            out = solve_rows(total, [total[s, SLOTS] for s in range(SLOTS)])
            for s in range(SLOTS):
                w_hold[s, pl.ds(pl.multiple_of(g * 8, 8), 8), :] = out[s]
            w_copy(g).start()
            return carry

        lax.fori_loop(0, SITES // 8, group, 0)
        for g in range(SITES // 8):
            w_copy(g).wait()

    stores = []

    def transpose_out(c, w):

        def one(k, carry):
            for x in range(NX):
                for half in range(NY // 8):
                    stage[c * KV + k, x, pl.ds(half * 8, 8), :] = w[
                        c, pl.ds(site_row(x, half * 8) + k, 8, stride=KV), :
                    ]
            return carry

        lax.fori_loop(0, KV, one, 0)
        part = pl.ds(c * KV, KV)
        store = pltpu.make_async_copy(stage.at[part], sm_out.at[part], out_sem.at[c])
        store.start()
        stores.append(store)

    for c in range(CHUNKS):
        transpose_in(c)
        if c == 0:
            pl.semaphore_wait(barrier, greeted)
        send_faces(0, c, wa)

    for load in coef_loads:
        load.wait()
    ax, ay, az = coef[0], coef[1], coef[2]
    scale = OMEGA / (2.0 * (ax + ay + az) + coef[3])
    ax, ay, az = ax * scale, ay * scale, az * scale
    lane = lax.broadcasted_iota(jnp.int32, az.shape, 2)
    before = jnp.where(lane == 0, 0.0, az)
    after = jnp.where(lane == ROWS - 1, 0.0, az)
    for x in range(NX):
        for y in range(NY):
            for held, value in ((ka, ax), (kb, ay), (km, before), (kp, after)):
                held[x, y] = jnp.broadcast_to(value[x, y : y + 1], (8, ROWS))

    for load in lists:
        load.wait()
    meta[...] = jnp.zeros_like(meta)
    slots = lax.broadcasted_iota(jnp.int32, (SLOTS, NY), 0)
    for x in range(NX):
        live = (cells[0][x] == 0) & (slots < cells[1][x])
        listed = jnp.where(live, cells[2][x] * SITES + cells[3][x], -1)
        for t in range(SLOTS):
            where = pl.ds((x % 2) * (ROWS // 2) + t * NY, NY)
            meta[x // 2 : x // 2 + 1, where] = listed[t : t + 1]
        meta[2:3, pl.ds(x * NY, NY)] = cells[0][x]
    blocks, targets, rank, ids, fine_ids, fine_rank = lists_of(meta[...], at)
    near[at["y"] * CORES + core] = jnp.broadcast_to(rank, (8, ROWS))
    for copy in gather_copies(0):
        copy.start()
    for p in range(2):
        block_cols[p] = jnp.broadcast_to(blocks[p], (ROWS, ROWS))
    idv[:COARSE] = ids
    idv[COARSE : COARSE + FINE] = fine_ids
    idv[COARSE + FINE :] = jnp.broadcast_to(fine_rank, (8, ROWS))
    part_sums[:, FINE] = jnp.zeros((len(PAIRS), 8, ROWS), F32)
    id_copies = [
        pltpu.make_async_copy(idv.at[pl.ds(0, COARSE)], id_s, smem_sem.at[0]),
        pltpu.make_async_copy(idv.at[pl.ds(COARSE, FINE)], fine_s, smem_sem.at[2]),
        pltpu.make_async_copy(idv.at[pl.ds(COARSE + FINE, 8)], spot_s, smem_sem.at[4]),
    ]
    for copy in id_copies:
        copy.start()
    tgt[...] = jnp.zeros_like(tgt)
    for c in range(CHUNKS):
        for h in range(2):
            tgt[2 * c + h : 2 * c + h + 1] = targets[c][h]
        rb[c][EMPTY] = jnp.zeros((KV, ROWS), BF16)
    tgt_copy = pltpu.make_async_copy(tgt, tgt_s, smem_sem.at[3])
    tgt_copy.start()

    for s in range(SWEEPS):
        src, dst = (wb, wa) if s % 2 else (wa, wb)
        for c in range(CHUNKS):
            fill_halo(s, c, src)
            sweep(s, c, src, dst)
            if s == SWEEPS - 1:
                if c == 0:
                    for copy in id_copies:
                        copy.wait()
                spread(c)
            if (s, c) in steps:
                steps[s, c]()
    drain(lines.at[:, pl.ds(0, 3)], table_sem.at[1])
    line_copy = pltpu.make_async_copy(lines, line_s, smem_sem.at[1])
    line_copy.start()
    cast(0)
    cast(1)
    cast(2)
    line_copy.wait()
    for c in range(CHUNKS):
        pass_on(c)
    for c in (1, 2, 0):
        reply(c, 0)
    for c in GRAM_ORDER:
        reply(c, 1)
    for c in range(CHUNKS):
        transpose_out(c, wb)
    drain(fxs, send_sem.at[0])
    drain(fys, send_sem.at[1])
    pair_copy().wait_send()
    drain(lines.at[:, pl.ds(0, 3)], table_sem.at[0])
    for step in range(3):
        drain(gathered(step), gather_sem.at[step, 0])
    for c in range(CHUNKS):
        drain(pg[c][0].at[pl.ds(0, 3)], near_sem.at[c, 0])
        for n in range(3):
            drain(pg[c][0], cast_send.at[c, n])
    tgt_copy.wait()
    for c in GRAM_ORDER:
        for part in range(len(PARTS)):
            answer(c, part, 0, 0).wait()
            drain(sb.at[c, pl.ds(0, 7 * PARTS[part][1] * SPOT)], ans_recv.at[c, part])
        add_products(c)
        for part in range(len(PARTS)):
            count = PARTS[part][1]
            drain(sb.at[c, pl.ds(0, 7 * count * SPOT)], ans_send.at[c, part])
    for store in stores:
        store.wait()
    finish()


def smooth(test_vectors, coef_x, coef_y, coef_z, shift, split, count, owner, local):
    vmem = pl.BlockSpec(memory_space=pltpu.VMEM)
    anywhere = pl.BlockSpec(memory_space=pl.ANY)
    cells = pltpu.VMEM((NX, NY, 8, ROWS), F32)
    rows = pltpu.VMEM((LINE, COARSE, KV, ROWS), BF16)
    dma = pltpu.SemaphoreType.DMA
    return pl.pallas_call(
        smooth_kernel,
        out_shape=(
            jax.ShapeDtypeStruct((VECS, NX, NY, ROWS), F32),
            jax.ShapeDtypeStruct((SLOTS, SITES, ROWS), F32),
        ),
        in_specs=[anywhere] * 9,
        out_specs=(anywhere, anywhere),
        scratch_shapes=[
            pltpu.VMEM((NX, 1, NY), jnp.int32),
            pltpu.VMEM((NX, 1, NY), jnp.int32),
            pltpu.VMEM((NX, SLOTS, NY), jnp.int32),
            pltpu.VMEM((NX, SLOTS, NY), jnp.int32),
            pltpu.VMEM((8, ROWS), jnp.int32),
            pltpu.VMEM((8, ROWS), jnp.int32),
            pltpu.SMEM((8, ROWS), jnp.int32),
            pltpu.VMEM((CHUNKS, SITES, KV, ROWS), BF16),
            *([pltpu.VMEM((EMPTY + 8, KV, ROWS), BF16)] * CHUNKS),
            pltpu.VMEM((len(PAIRS), SITES, 8, ROWS), F32),
            pltpu.VMEM((SLOTS, SITES, ROWS), F32),
            pltpu.VMEM((VECS, NX, NY, ROWS), F32),
            pltpu.VMEM((4, NX, NY, ROWS), F32),
            pltpu.VMEM((CHUNKS, EXT, ROWS), F32),
            pltpu.VMEM((CHUNKS, EXT, ROWS), F32),
            cells, cells, cells, cells,
            pltpu.VMEM((SWEEPS, CHUNKS, 2, NY * KV, ROWS), BF16),
            pltpu.VMEM((SWEEPS, CHUNKS, 2, NY * KV, ROWS), BF16),
            pltpu.VMEM((SWEEPS, CHUNKS, 2, NX * KV, ROWS), BF16),
            pltpu.VMEM((SWEEPS, CHUNKS, 2, NX * KV, ROWS), BF16),
            pltpu.VMEM((CORES, 2, 1, ROWS), jnp.int32),
            pltpu.VMEM((len(AXES), LINE, CORES, 2, 1, ROWS), jnp.int32),
            pltpu.VMEM((LINE * CORES, 8, ROWS), jnp.int32),
            pltpu.VMEM((LINE, LINE, LINE * CORES, ROWS), jnp.int32),
            pltpu.VMEM((2, ROWS, ROWS), jnp.int32),
            pltpu.VMEM((COARSE + FINE + 8, ROWS), jnp.int32),
            pltpu.SMEM((len(AXES), LINE, CORES, 2, 1, ROWS), jnp.int32),
            pltpu.SMEM((COARSE, ROWS), jnp.int32),
            pltpu.SMEM((FINE, ROWS), jnp.int32),
            pltpu.SMEM((8, ROWS), jnp.int32),
            *([rows] * (LINE * CHUNKS)),
            pltpu.VMEM((CHUNKS, EMPTY, KV, ROWS), BF16),
            dma((CHUNKS,)),
            dma((4,)),
            dma((CHUNKS,)),
            dma((2,)),
            dma((SWEEPS, CHUNKS, 2)),
            dma((2,)),
            dma((2,)),
            dma((3, 2)),
            dma((CHUNKS, 2)),
            dma((CHUNKS, 3)),
            dma((CHUNKS, 4)),
            dma((CHUNKS, len(PARTS))),
            dma((CHUNKS, len(PARTS))),
            dma((CHUNKS, len(PARTS))),
            dma((5,)),
            dma((4,)),
            dma((SITES // 8,)),
        ],
        compiler_params=pltpu.CompilerParams(
            collective_id=0, has_side_effects=True, vmem_limit_bytes=60 * 1024 * 1024
        ),
        name="smooth",
    )(test_vectors, coef_x, coef_y, coef_z, shift, split, count, owner, local)


def pass_kernel(w_in, sm_in, w_out, sm_out, w_hold, sm_hold, in_sem, out_sem):
    parts = [(w_in, w_hold, w_out)]
    for c in range(CHUNKS):
        part = pl.ds(c * KV, KV)
        parts.append((sm_in.at[part], sm_hold.at[part], sm_out.at[part]))
    ins = [pltpu.make_async_copy(a, b, in_sem.at[n]) for n, (a, b, _) in enumerate(parts)]
    outs = [pltpu.make_async_copy(b, d, out_sem.at[n]) for n, (_, b, d) in enumerate(parts)]
    for copy in ins:
        copy.start()
    for load, store in zip(ins, outs):
        load.wait()
        store.start()
    for store in outs:
        store.wait()


def pass_on_results(weights, sm):
    anywhere = pl.BlockSpec(memory_space=pl.ANY)
    dma = pltpu.SemaphoreType.DMA
    return pl.pallas_call(
        pass_kernel,
        out_shape=(
            jax.ShapeDtypeStruct(weights.shape, F32),
            jax.ShapeDtypeStruct(sm.shape, F32),
        ),
        in_specs=[anywhere, anywhere],
        out_specs=(anywhere, anywhere),
        scratch_shapes=[
            pltpu.VMEM(weights.shape, F32),
            pltpu.VMEM(sm.shape, F32),
            dma((CHUNKS + 1,)),
            dma((CHUNKS + 1,)),
        ],
        compiler_params=pltpu.CompilerParams(vmem_limit_bytes=60 * 1024 * 1024),
        name="fit",
    )(weights, sm)


def per_device(
    test_vectors, coef_x, coef_y, coef_z, shift, cf_split, nbr_count, nbr_owner, nbr_block
):
    sm, weights = smooth(
        test_vectors, coef_x, coef_y, coef_z, shift,
        jnp.swapaxes(cf_split, 1, 2),
        jnp.swapaxes(nbr_count, 1, 2),
        jnp.transpose(nbr_owner, (0, 2, 3, 1)).reshape(NX, SLOTS, NY),
        jnp.transpose(nbr_block, (0, 2, 3, 1)).reshape(NX, SLOTS, NY),
    )
    weights, smoothed = pass_on_results(weights.reshape(SLOTS, NX, NY, ROWS), sm)
    return (smoothed, weights)


def solution(mesh):
    cells = P("gx", "gy", None)
    lists = P("gx", "gy", None, None)
    vectors = P(None, "gx", "gy", None)
    return jax.shard_map(
        per_device,
        mesh=mesh,
        in_specs=(vectors, cells, cells, cells, cells, cells, cells, lists, lists),
        out_specs=(vectors, vectors),
        check_vma=False,
    )
```
